32 devices in a mesh: groups: 2 (over x), replica: 16 (over z, y, core).
Axes of the slice: x: 2, y: 2, z: 4, core: 2. Of those that a mesh axis runs over, the one named last changes fastest.
Arguments:
- hidden: bfloat16 [3, 64, 5120], P(None, ('groups', 'replica')), parts along dimension 1, may hold values from -6 to 6
- query_key_value_weight: bfloat16 [3, 5120, 5120], P(None, None, 'replica'), may hold values from -0.078125 to 0.078125
- adapter_down_maps: bfloat16 [64, 64, 5120], P('replica'), may hold values from -0.078125 to 0.078125
- adapter_up_maps: bfloat16 [64, 64, 5120], P(None, None, 'replica'), may hold values from -0.75 to 0.75
- adapter_storage_row: int32 [64], replicated, may hold values from 0 to 63, each once
- request_adapter: int32 [64], P('groups'), parts along dimension 0, may hold values from 0 to 63
- lengths: int32 [64], P('groups'), parts along dimension 0, may hold values from 1 to 128, as said below
- request_page_table: int32 [64, 32], P(('groups', 'replica')), parts along dimension 0, may hold values from 0 to 63, as said below
- key_value_pool: bfloat16 [2048, 4, 2, 5120], P(('groups', 'replica')), parts along dimension 0, may hold values from -220 to 220
Outputs:
- attn_out: bfloat16 [3, 64, 5120], P(None, ('groups', 'replica')), parts along dimension 1
The draws below stay inside these ranges and needn't reach their ends.
There are 2 independent parts, one for each index of `groups`. The reference program is written for one: setup_inputs(seed, part) draws one part's arguments, and reference() takes and returns one part's arrays. A program takes and returns all parts, laid end to end along the dimension named above; an argument that names none is the same for every part. Nothing has to cross between parts.
Inputs may be any that keep to these rules, and one draw needn't show every extreme that they name: `lengths`: requests 2 at a time belong to one replica, in replica order; cached keys were rotated at positions 0 to length - 1; replicas 2 j and 2 j + 1 form a pair in which one replica's requests all have 32 * 2 tokens or more and the other's all have 32 * 4 / 8 or fewer. `request_page_table`: local page numbers within the replica of the request; the rows of one replica name each of its 64 pages once.
All inputs are finite; a program needn't handle non-finite values.
Results may differ from the reference program's by a relative error of at most 0.012.
The reference program's roundings to bfloat16 on the way count: a program that leaves them out, or rounds other values in their place, can miss the bound.
Values may be sent and summed in bfloat16 or wider, within the bound.
No kernel may reach another device: no remote copies, remote signals or barrier semaphores. Data moves between devices by JAX's collectives and lax.ppermute only.
A program may use at most 128 MiB of HBM per device.

```python
import math
import jax
import jax.numpy as jnp
import numpy as np
from jax import lax

MODEL_WIDTH = 5120
HEADS = 40
HD = 128
ADAPTER_RANK = 64
STEPS = 3
PAGE = 4
MAXP = 32
REQ_DEV = 2
ADAPTER_TOTAL = 64
REQUESTS = 32
POOL = 64
KV_PAGES = 1024


def draw_lengths(key, part):
    key = jax.random.fold_in(key, 11)
    replicas = REQUESTS // REQ_DEV
    context = MAXP * PAGE
    replica_of_row = jnp.arange(REQUESTS) // REQ_DEV
    pair_coin = jax.random.randint(jax.random.fold_in(key, 1), (replicas // 2,), 0, 2)
    busy_member = jnp.repeat(pair_coin, 2)
    busy_replica = jnp.arange(replicas) % 2 == busy_member
    busy_rows = busy_replica[replica_of_row]
    long_length = jax.random.randint(jax.random.fold_in(key, 2), (REQUESTS,), context // 2, context + 1)
    short_length = jax.random.randint(jax.random.fold_in(key, 3), (REQUESTS,), 1, context // 8 + 1)
    drawn_lengths = jnp.where(busy_rows, long_length, short_length)
    first_slot = jnp.arange(REQUESTS) % REQ_DEV == 0
    first_pair = replica_of_row < 2
    drawn_lengths = jnp.where(first_slot & first_pair & busy_rows, context, drawn_lengths)
    drawn_lengths = jnp.where(first_slot & first_pair & jnp.logical_not(busy_rows), 1, drawn_lengths)
    return drawn_lengths.astype(jnp.int32)


def draw_request_page_table(key, part):
    key = jax.random.fold_in(key, 12)
    replicas = REQUESTS // REQ_DEV
    replica_keys = jax.random.split(key, replicas)
    shuffled = jax.vmap(lambda single_key: jax.random.permutation(single_key, POOL))(replica_keys)
    return shuffled.reshape(REQUESTS, MAXP).astype(jnp.int32)


def draw_key_value_pool(key, part):
    key = jax.random.fold_in(key, 13)
    shape_all = (KV_PAGES, PAGE, 2, MODEL_WIDTH)
    drawn_pool = jnp.clip(jax.random.normal(jax.random.fold_in(key, 1), shape_all, jnp.float32), -6.0, 6.0)
    return drawn_pool.astype(jnp.bfloat16)


def with_ends(result, key, low, top_value):
    longest = result.shape.index(max(result.shape))
    spots = []
    for shift in (0, 1):
        where = [jax.random.randint(jax.random.fold_in(key, axis), (), 0, length) for axis, length in enumerate(result.shape)]
        where[longest] = (where[longest] + shift) % result.shape[longest]
        spots.append(tuple(where))
    return result.at[spots[0]].set(low).at[spots[1]].set(top_value)


def levels(own_key, shape, pieces, low, largest):
    gain, own = 1.0, jax.random.fold_in(own_key, 6)
    for axis_at, shards_of in pieces:
        heights = jnp.exp(jax.random.uniform(jax.random.fold_in(own, axis_at), (shards_of,), jnp.float32, low / len(pieces), largest / len(pieces)))
        gain = gain * jnp.repeat(heights, shape[axis_at] // shards_of).reshape([-1 if axis == axis_at else 1 for axis in range(len(shape))])
    return gain


def cumulative_ranks(number_of, lean):
    loads = [(1 << 20) // math.isqrt(standing ** lean) + 1 for standing in range(1, number_of + 1)]
    deviation = 1 + sum(loads) // (1 << 30)
    return np.cumsum(np.array([max(1, weight // deviation) for weight in loads]))


def skewed_ids(stream_key, dims, amount, skew):
    grid = cumulative_ranks(amount, skew)
    pick = jax.random.randint(jax.random.fold_in(stream_key, 1), dims, 0, int(grid[amount - 1]))
    grade = jnp.searchsorted(jnp.asarray(grid, jnp.int32), pick, side="right")
    return jax.random.permutation(jax.random.fold_in(stream_key, 2), amount)[grade].astype(jnp.int32)


def centred(own_key, extent, deviation, reach, pieces=(), held_as=jnp.bfloat16):
    array = deviation * jax.random.normal(own_key, extent, jnp.float32)
    if pieces:
        array = array * levels(own_key, extent, pieces, -0.22, 0.18)
    return jnp.clip(array, -reach, reach).astype(held_as)


def setup_inputs(seed: int = 0, part: int = 0) -> dict:
    splits = jax.random.split(jax.random.key(seed), 10)
    part_splits = jax.random.split(jax.random.fold_in(splits[9], part), 10)
    return {
        "hidden": centred(part_splits[0], (STEPS, REQUESTS, MODEL_WIDTH), 1.0, 6.0, ((1, 16),)),
        "query_key_value_weight": centred(splits[1], (3, MODEL_WIDTH, MODEL_WIDTH), MODEL_WIDTH ** -0.5, 0.078125, ((2, 16),)),
        "adapter_down_maps": centred(splits[2], (ADAPTER_TOTAL, ADAPTER_RANK, MODEL_WIDTH), MODEL_WIDTH ** -0.5, 0.078125, ((0, 16),)),
        "adapter_up_maps": centred(splits[3], (ADAPTER_TOTAL, ADAPTER_RANK, MODEL_WIDTH), ADAPTER_RANK ** -0.5, 0.75, ((2, 16),)),
        "adapter_storage_row": jax.random.permutation(splits[4], ADAPTER_TOTAL).astype(jnp.int32),
        "request_adapter": with_ends(skewed_ids(part_splits[5], (REQUESTS,), ADAPTER_TOTAL, 2), jax.random.fold_in(part_splits[5], 3), 0, ADAPTER_TOTAL - 1).astype(jnp.int32),
        "lengths": draw_lengths(jax.random.fold_in(jax.random.fold_in(splits[9], part), 71), part),
        "request_page_table": draw_request_page_table(jax.random.fold_in(jax.random.fold_in(splits[9], part), 71), part),
        "key_value_pool": draw_key_value_pool(jax.random.fold_in(jax.random.fold_in(splits[9], part), 71), part),
    }


adapter_scale = 2.0
masked_score = -1e30


def narrow(value):
    return lax.optimization_barrier(value.astype(jnp.bfloat16))


def rotate(vectors, positions):
    half_dim = vectors.shape[-1] // 2
    frequency = jnp.exp(jnp.arange(half_dim, dtype=jnp.float32) * (-2.0 * jnp.log(10000.0) / vectors.shape[-1]))
    angles = positions.astype(jnp.float32)[:, None, None] * frequency[None, None, :]
    cosine = jnp.cos(angles)
    sine_part = jnp.sin(angles)
    first_half = vectors[..., :half_dim]
    second = vectors[..., half_dim:]
    return jnp.concatenate([first_half * cosine - second * sine_part, second * cosine + first_half * sine_part], axis=-1)


def reference(hidden, query_key_value_weight, adapter_down_maps, adapter_up_maps, adapter_storage_row, request_adapter, lengths, request_page_table, key_value_pool):
    stored_rows = adapter_storage_row[request_adapter]
    down_map_rows = adapter_down_maps[stored_rows]
    up_map_rows = adapter_up_maps[stored_rows]
    queries = []
    keys_new = []
    values_new = []
    for step_index in range(STEPS):
        current = hidden[step_index]
        projected_rows = [jnp.dot(current, query_key_value_weight[which], preferred_element_type=jnp.float32) for which in range(3)]
        reduced_state = narrow(jnp.einsum("rd,rkd->rk", current.astype(jnp.float32), down_map_rows.astype(jnp.float32)))
        adapter_update = jnp.einsum("uh,uhi->ui", reduced_state.astype(jnp.float32), up_map_rows.astype(jnp.float32))
        q_proj = narrow(projected_rows[0])
        k_proj = narrow(projected_rows[1])
        value_projection = (projected_rows[2] + adapter_scale * adapter_update).astype(jnp.bfloat16)
        positions = lengths + step_index
        queries.append(rotate(q_proj.astype(jnp.float32).reshape(REQUESTS, HEADS, HD), positions).astype(jnp.bfloat16))
        keys_new.append(rotate(k_proj.astype(jnp.float32).reshape(REQUESTS, HEADS, HD), positions).astype(jnp.bfloat16))
        values_new.append(value_projection.reshape(REQUESTS, HEADS, HD))
    queries = jnp.stack(queries, axis=1)
    keys_new = jnp.stack(keys_new, axis=1)
    values_new = jnp.stack(values_new, axis=1)
    page_rows = (jnp.arange(REQUESTS, dtype=jnp.int32) // REQ_DEV)[:, None] * POOL + request_page_table

    def attend(request_data):
        rows_now, length, query_now, key_fresh, value_fresh = request_data
        cached = key_value_pool[rows_now].reshape(MAXP * PAGE, 2, HEADS, HD)
        all_keys = jnp.concatenate([cached[:, 0], key_fresh], axis=0)
        values = jnp.concatenate([cached[:, 1], value_fresh], axis=0)
        scores = jnp.einsum("shd,chd->shc", query_now.astype(jnp.float32), all_keys.astype(jnp.float32)) * (HD ** -0.5)
        old_live = jnp.arange(MAXP * PAGE, dtype=jnp.int32) < length
        new_live = jnp.arange(STEPS)[None, :] <= jnp.arange(STEPS)[:, None]
        live_mask = jnp.concatenate([jnp.broadcast_to(old_live[None, :], (STEPS, MAXP * PAGE)), new_live], axis=1)
        scores = jnp.where(live_mask[:, None, :], scores, masked_score)
        row_top = jnp.max(scores, axis=-1, keepdims=True)
        weights = jnp.where(live_mask[:, None, :], jnp.exp(scores - row_top), 0.0)
        totals = jnp.sum(weights, axis=-1)
        mixed = jnp.einsum("shc,chd->shd", narrow(weights).astype(jnp.float32), values.astype(jnp.float32))
        return (mixed / totals[..., None]).astype(jnp.bfloat16).reshape(STEPS, MODEL_WIDTH)

    attended = lax.map(attend, (page_rows, lengths, queries, keys_new, values_new))
    return jnp.transpose(attended, (1, 0, 2))
```

```python
import functools

import jax
import jax.numpy as jnp
from jax import lax
from jax.experimental import pallas as pl
from jax.experimental.pallas import tpu as pltpu
from jax.sharding import PartitionSpec as P

HD = 128
ROWS = 8
HEAD_BLOCK = 8

adapter_scale = 2.0
masked_score = -1e30


def attention_kernel(steps, req_dev, q_ref, k_ref, v_ref, cos_ref, sin_ref, live_ref, kv_ref, out_ref, kn_ref, vn_ref):
    rows = steps * req_dev
    width = q_ref.shape[1]
    lanes = HEAD_BLOCK * HD
    group = rows * HEAD_BLOCK
    cosine = cos_ref[...]
    sine = sin_ref[...]

    def rotated(x):
        pieces = []
        for h in range(HEAD_BLOCK):
            head = x[:, h * HD : (h + 1) * HD]
            pieces.append(head * cosine + pltpu.roll(head, HD // 2, 1) * sine)
        return jnp.concatenate(pieces, axis=1)

    row_head = lax.broadcasted_iota(jnp.int32, (group, lanes), 0) % HEAD_BLOCK
    lane_head = lax.broadcasted_iota(jnp.int32, (group, lanes), 1) // HD
    own_head = row_head == lane_head
    row_j = lax.broadcasted_iota(jnp.int32, (group, 16), 0) // HEAD_BLOCK
    new_j = lax.broadcasted_iota(jnp.int32, (group, 16), 1)
    new_live = (new_j < rows) & (new_j % req_dev == row_j % req_dev) & (new_j // req_dev <= row_j // req_dev)
    live_all = live_ref[...]
    live = jnp.concatenate(
        [
            jnp.broadcast_to(live_all[j % req_dev : j % req_dev + 1], (HEAD_BLOCK, live_all.shape[1]))
            for j in range(rows)
        ],
        axis=0,
    )
    live = live > 0
    kn_ref[...] = jnp.zeros_like(kn_ref)
    vn_ref[...] = jnp.zeros_like(vn_ref)
    contract_lanes = (((1,), (1,)), ((), ()))
    for c in range(width // lanes):
        cols = slice(c * lanes, (c + 1) * lanes)
        query = rotated(q_ref[:, cols].astype(jnp.float32))
        key_new = rotated(k_ref[:, cols].astype(jnp.float32))
        kn_ref[0:8] = key_new
        vn_ref[0:8] = v_ref[:, cols].astype(jnp.float32)
        kn = kn_ref[...].astype(jnp.bfloat16)
        vn = vn_ref[...].astype(jnp.bfloat16)
        spread = jnp.concatenate(
            [jnp.broadcast_to(query[j : j + 1], (HEAD_BLOCK, lanes)) for j in range(rows)], axis=0
        )
        spread = jnp.where(own_head, spread, 0.0).astype(jnp.bfloat16)
        kv = kv_ref[:, cols]
        scores = lax.dot_general(spread, kv, contract_lanes, preferred_element_type=jnp.float32) * (HD**-0.5)
        scores = jnp.where(live, scores, masked_score)
        fresh = lax.dot_general(spread, kn, contract_lanes, preferred_element_type=jnp.float32) * (HD**-0.5)
        fresh = jnp.where(new_live, fresh, masked_score)
        top = jnp.maximum(jnp.max(scores, axis=1, keepdims=True), jnp.max(fresh, axis=1, keepdims=True))
        weights = jnp.where(live, jnp.exp(scores - top), 0.0)
        fresh = jnp.where(new_live, jnp.exp(fresh - top), 0.0)
        totals = jnp.sum(weights, axis=1, keepdims=True) + jnp.sum(fresh, axis=1, keepdims=True)
        weights = pltpu.roll(weights, 1, 1).astype(jnp.bfloat16)
        mixed = jnp.dot(weights, kv, preferred_element_type=jnp.float32)
        mixed = mixed + jnp.dot(fresh.astype(jnp.bfloat16), vn, preferred_element_type=jnp.float32)
        mixed = jnp.where(own_head, mixed / totals, 0.0)
        out = jnp.sum(mixed.reshape(rows, HEAD_BLOCK, lanes), axis=1)
        out_ref[:, cols] = out.astype(out_ref.dtype)


def attention(steps, req_dev, q, k, v, cosine, sine, live, kv):
    rows = steps * req_dev
    width = q.shape[1]
    vmem = pl.BlockSpec(memory_space=pltpu.VMEM)
    return pl.pallas_call(
        functools.partial(attention_kernel, steps, req_dev),
        out_shape=jax.ShapeDtypeStruct((rows, width), jnp.bfloat16),
        in_specs=[vmem] * 7,
        out_specs=vmem,
        scratch_shapes=[pltpu.VMEM((16, HEAD_BLOCK * HD), jnp.float32)] * 2,
        compiler_params=pltpu.CompilerParams(vmem_limit_bytes=32 * 2**20),
        cost_estimate=pl.CostEstimate(flops=10**9, bytes_accessed=6 * 10**6, transcendentals=0),
        name="attention",
    )(q, k, v, cosine, sine, live, kv)


def per_device(
    replicas,
    hidden,
    query_key_value_weight,
    adapter_down_maps,
    adapter_up_maps,
    adapter_storage_row,
    request_adapter,
    lengths,
    request_page_table,
    key_value_pool,
):
    my_index = lax.axis_index("replica")
    steps, req_dev, width = hidden.shape
    rows = steps * req_dev
    columns = query_key_value_weight.shape[2]
    holder_count, rank, _ = adapter_down_maps.shape
    pool_pages, page_len = key_value_pool.shape[:2]
    adapter_count = adapter_storage_row.shape[0]
    chips = replicas // 2
    total = replicas * ROWS

    block = jnp.pad(hidden.reshape(rows, width), ((0, ROWS - rows), (0, 0)))
    same_core = [[2 * chip + core for chip in range(chips)] for core in range(2)]
    mine = lax.all_to_all(
        jnp.broadcast_to(block[None], (chips, ROWS, width)),
        "replica",
        split_axis=0,
        concat_axis=0,
        axis_index_groups=same_core,
        tiled=True,
    )
    other = lax.ppermute(mine, "replica", [(i, i ^ 1) for i in range(replicas)])
    first = my_index % 2 == 0
    gathered = jnp.stack([jnp.where(first, mine, other), jnp.where(first, other, mine)])
    gathered = gathered.reshape(total, width)

    stored_rows = jnp.sum(
        jnp.where(
            request_adapter[:, None] == jnp.arange(adapter_count, dtype=jnp.int32)[None, :],
            adapter_storage_row[None, :],
            0,
        ),
        axis=1,
    )
    by_block = stored_rows.reshape(chips, 2, 1, req_dev).transpose(1, 0, 2, 3)
    by_block = jnp.broadcast_to(by_block, (2, chips, steps, req_dev)).reshape(2, chips, rows)
    row_stored = jnp.pad(by_block, ((0, 0), (0, 0), (0, ROWS - rows)), constant_values=-1).reshape(total)

    down = jnp.einsum("nd,hfd->nhf", gathered, adapter_down_maps, preferred_element_type=jnp.float32)
    slots = my_index * holder_count + jnp.arange(holder_count, dtype=jnp.int32)
    own = row_stored[:, None] == slots[None, :]
    low = jnp.sum(jnp.where(own[:, :, None], down, 0.0), axis=1).astype(jnp.bfloat16)
    low = jnp.concatenate([low[: total // 2], low[total // 2 :]], axis=1)
    low = lax.all_to_all(
        jnp.broadcast_to(low[None], (replicas,) + low.shape), "replica", split_axis=0, concat_axis=0, tiled=True
    )
    low = jnp.sum(low.astype(jnp.float32), axis=0)
    low = jnp.concatenate([low[:, :rank], low[:, rank:]], axis=0)

    projected = jnp.einsum("nd,idc->nic", gathered, query_key_value_weight, preferred_element_type=jnp.float32)

    def update(first_adapter, maps):
        held = maps.shape[0]
        which = first_adapter + jnp.arange(held, dtype=jnp.int32)
        wide = jnp.where((row_stored[:, None] == which[None, :])[:, :, None], low[:, None, :], 0.0)
        return jnp.dot(
            wide.astype(jnp.bfloat16).reshape(total, held * rank),
            maps.reshape(held * rank, columns),
            preferred_element_type=jnp.float32,
        )

    step_adapters = 64
    if adapter_count <= step_adapters:
        updated = update(0, adapter_up_maps)
    else:
        updated = lax.fori_loop(
            0,
            adapter_count // step_adapters,
            lambda i, sofar: sofar
            + update(
                i * step_adapters,
                lax.dynamic_slice_in_dim(adapter_up_maps, i * step_adapters, step_adapters, 0),
            ),
            jnp.zeros((total, columns), jnp.float32),
        )
    value = projected[:, 2] + adapter_scale * updated
    combined = jnp.concatenate([projected[:, 0], projected[:, 1], value], axis=1).astype(jnp.bfloat16)
    combined = combined.reshape(2, chips, ROWS, 3 * columns).transpose(1, 0, 2, 3)
    combined = combined.reshape(replicas, ROWS, 3 * columns)
    arrived = lax.all_to_all(combined, "replica", split_axis=0, concat_axis=0, tiled=True)
    arrived = arrived.reshape(replicas, ROWS, 3, columns).transpose(2, 1, 0, 3).reshape(3, ROWS, width)

    my_lengths = lax.dynamic_slice_in_dim(lengths, my_index * req_dev, req_dev)
    positions = (my_lengths[None, :] + jnp.arange(steps, dtype=jnp.int32)[:, None]).reshape(rows)
    positions = jnp.pad(positions, (0, ROWS - rows))
    half = HD // 2
    frequency = jnp.exp(jnp.arange(half, dtype=jnp.float32) * (-2.0 * jnp.log(10000.0) / HD))
    angles = positions.astype(jnp.float32)[:, None] * frequency[None, :]
    cosine = jnp.cos(angles)
    sine = jnp.sin(angles)
    cosine = jnp.concatenate([cosine, cosine], axis=1)
    sine = jnp.concatenate([-sine, sine], axis=1)

    pages = jnp.arange(pool_pages, dtype=jnp.int32)
    max_pages = request_page_table.shape[1]
    place = jnp.max(
        jnp.where(
            request_page_table[:, :, None] == pages[None, None, :],
            jnp.arange(max_pages, dtype=jnp.int32)[None, :, None],
            -1,
        ),
        axis=1,
    )
    token = place[:, :, None] * page_len + jnp.arange(page_len, dtype=jnp.int32)[None, None, :]
    alive = (place[:, :, None] >= 0) & (token < my_lengths[:, None, None])
    live = jnp.stack([alive, jnp.zeros_like(alive)], axis=-1).astype(jnp.int32)
    live = live.reshape(req_dev, pool_pages * page_len * 2)

    kv = key_value_pool.reshape(pool_pages * page_len * 2, width)
    out = attention(steps, req_dev, arrived[0], arrived[1], arrived[2], cosine, sine, live, kv)
    return out.reshape(steps, req_dev, width)


def solution(mesh):
    placed = (
        P(None, ("groups", "replica"), None),
        P(None, None, "replica"),
        P("replica", None, None),
        P(None, None, "replica"),
        P(),
        P("groups"),
        P("groups"),
        P(("groups", "replica"), None),
        P(("groups", "replica"), None, None, None),
    )
    return jax.shard_map(
        functools.partial(per_device, mesh.shape["replica"]),
        mesh=mesh,
        in_specs=placed,
        out_specs=P(None, ("groups", "replica"), None),
        check_vma=False,
    )
```

```python
import functools

import jax
import jax.numpy as jnp
from jax import lax
from jax.experimental import pallas as pl
from jax.experimental.pallas import tpu as pltpu
from jax.sharding import PartitionSpec as P

HD = 128
ROWS = 8
HEAD_BLOCK = 8

adapter_scale = 2.0
masked_score = -1e30


def attention_kernel(steps, req_dev, q_ref, k_ref, v_ref, cos_ref, sin_ref, live_ref, kv_ref, out_ref, kn_ref, vn_ref):
    rows = steps * req_dev
    width = q_ref.shape[1]
    lanes = HEAD_BLOCK * HD
    group = rows * HEAD_BLOCK
    cosine = cos_ref[...]
    sine = sin_ref[...]

    def rotated(x):
        pieces = []
        for h in range(HEAD_BLOCK):
            head = x[:, h * HD : (h + 1) * HD]
            pieces.append(head * cosine + pltpu.roll(head, HD // 2, 1) * sine)
        return jnp.concatenate(pieces, axis=1)

    row_head = lax.broadcasted_iota(jnp.int32, (group, lanes), 0) % HEAD_BLOCK
    lane_head = lax.broadcasted_iota(jnp.int32, (group, lanes), 1) // HD
    own_head = row_head == lane_head
    row_j = lax.broadcasted_iota(jnp.int32, (group, 16), 0) // HEAD_BLOCK
    new_j = lax.broadcasted_iota(jnp.int32, (group, 16), 1)
    new_live = (new_j < rows) & (new_j % req_dev == row_j % req_dev) & (new_j // req_dev <= row_j // req_dev)
    live_all = live_ref[...]
    live = jnp.concatenate(
        [
            jnp.broadcast_to(live_all[j % req_dev : j % req_dev + 1], (HEAD_BLOCK, live_all.shape[1]))
            for j in range(rows)
        ],
        axis=0,
    )
    live = live > 0
    kn_ref[...] = jnp.zeros_like(kn_ref)
    vn_ref[...] = jnp.zeros_like(vn_ref)
    contract_lanes = (((1,), (1,)), ((), ()))
    for c in range(width // lanes):
        cols = slice(c * lanes, (c + 1) * lanes)
        query = rotated(q_ref[:, cols].astype(jnp.float32))
        key_new = rotated(k_ref[:, cols].astype(jnp.float32))
        kn_ref[0:8] = key_new
        vn_ref[0:8] = v_ref[:, cols].astype(jnp.float32)
        kn = kn_ref[...].astype(jnp.bfloat16)
        vn = vn_ref[...].astype(jnp.bfloat16)
        spread = jnp.concatenate(
            [jnp.broadcast_to(query[j : j + 1], (HEAD_BLOCK, lanes)) for j in range(rows)], axis=0
        )
        spread = jnp.where(own_head, spread, 0.0).astype(jnp.bfloat16)
        kv = kv_ref[:, cols]
        scores = lax.dot_general(spread, kv, contract_lanes, preferred_element_type=jnp.float32) * (HD**-0.5)
        scores = jnp.where(live, scores, masked_score)
        fresh = lax.dot_general(spread, kn, contract_lanes, preferred_element_type=jnp.float32) * (HD**-0.5)
        fresh = jnp.where(new_live, fresh, masked_score)
        top = jnp.maximum(jnp.max(scores, axis=1, keepdims=True), jnp.max(fresh, axis=1, keepdims=True))
        weights = jnp.where(live, jnp.exp(scores - top), 0.0)
        fresh = jnp.where(new_live, jnp.exp(fresh - top), 0.0)
        totals = jnp.sum(weights, axis=1, keepdims=True) + jnp.sum(fresh, axis=1, keepdims=True)
        weights = pltpu.roll(weights, 1, 1).astype(jnp.bfloat16)
        mixed = jnp.dot(weights, kv, preferred_element_type=jnp.float32)
        mixed = mixed + jnp.dot(fresh.astype(jnp.bfloat16), vn, preferred_element_type=jnp.float32)
        mixed = jnp.where(own_head, mixed / totals, 0.0)
        out = jnp.sum(mixed.reshape(rows, HEAD_BLOCK, lanes), axis=1)
        out_ref[:, cols] = out.astype(out_ref.dtype)


def attention(steps, req_dev, q, k, v, cosine, sine, live, kv):
    rows = steps * req_dev
    width = q.shape[1]
    vmem = pl.BlockSpec(memory_space=pltpu.VMEM)
    return pl.pallas_call(
        functools.partial(attention_kernel, steps, req_dev),
        out_shape=jax.ShapeDtypeStruct((rows, width), jnp.bfloat16),
        in_specs=[vmem] * 7,
        out_specs=vmem,
        scratch_shapes=[pltpu.VMEM((16, HEAD_BLOCK * HD), jnp.float32)] * 2,
        compiler_params=pltpu.CompilerParams(vmem_limit_bytes=32 * 2**20),
        cost_estimate=pl.CostEstimate(flops=10**9, bytes_accessed=6 * 10**6, transcendentals=0),
        name="attention",
    )(q, k, v, cosine, sine, live, kv)


def rotation(my_lengths, steps):
    rows = steps * my_lengths.shape[0]
    positions = (my_lengths[None, :] + jnp.arange(steps, dtype=jnp.int32)[:, None]).reshape(rows)
    positions = jnp.pad(positions, (0, ROWS - rows))
    half = HD // 2
    frequency = jnp.exp(jnp.arange(half, dtype=jnp.float32) * (-2.0 * jnp.log(10000.0) / HD))
    angles = positions.astype(jnp.float32)[:, None] * frequency[None, :]
    cosine = jnp.cos(angles)
    sine = jnp.sin(angles)
    cosine = jnp.concatenate([cosine, cosine], axis=1)
    sine = jnp.concatenate([-sine, sine], axis=1)
    return cosine, sine


def live_rows(my_lengths, request_page_table, pool_pages, page_len):
    pages = jnp.arange(pool_pages, dtype=jnp.int32)
    max_pages = request_page_table.shape[1]
    place = jnp.max(
        jnp.where(
            request_page_table[:, :, None] == pages[None, None, :],
            jnp.arange(max_pages, dtype=jnp.int32)[None, :, None],
            -1,
        ),
        axis=1,
    )
    token = place[:, :, None] * page_len + jnp.arange(page_len, dtype=jnp.int32)[None, None, :]
    alive = (place[:, :, None] >= 0) & (token < my_lengths[:, None, None])
    live = jnp.stack([alive, jnp.zeros_like(alive)], axis=-1).astype(jnp.int32)
    return live.reshape(request_page_table.shape[0], pool_pages * page_len * 2)


def general_plan(
    replicas,
    hidden,
    query_key_value_weight,
    adapter_down_maps,
    adapter_up_maps,
    adapter_storage_row,
    request_adapter,
    lengths,
    request_page_table,
    key_value_pool,
):
    my_index = lax.axis_index("replica")
    steps, req_dev, width = hidden.shape
    rows = steps * req_dev
    columns = query_key_value_weight.shape[2]
    holder_count, rank, _ = adapter_down_maps.shape
    pool_pages, page_len = key_value_pool.shape[:2]
    adapter_count = adapter_storage_row.shape[0]
    chips = replicas // 2
    total = replicas * ROWS

    block = jnp.pad(hidden.reshape(rows, width), ((0, ROWS - rows), (0, 0)))
    same_core = [[2 * chip + core for chip in range(chips)] for core in range(2)]
    mine = lax.all_to_all(
        jnp.broadcast_to(block[None], (chips, ROWS, width)),
        "replica",
        split_axis=0,
        concat_axis=0,
        axis_index_groups=same_core,
        tiled=True,
    )
    other = lax.ppermute(mine, "replica", [(i, i ^ 1) for i in range(replicas)])
    first = my_index % 2 == 0
    gathered = jnp.stack([jnp.where(first, mine, other), jnp.where(first, other, mine)])
    gathered = gathered.reshape(total, width)

    stored_rows = jnp.sum(
        jnp.where(
            request_adapter[:, None] == jnp.arange(adapter_count, dtype=jnp.int32)[None, :],
            adapter_storage_row[None, :],
            0,
        ),
        axis=1,
    )
    by_block = stored_rows.reshape(chips, 2, 1, req_dev).transpose(1, 0, 2, 3)
    by_block = jnp.broadcast_to(by_block, (2, chips, steps, req_dev)).reshape(2, chips, rows)
    row_stored = jnp.pad(by_block, ((0, 0), (0, 0), (0, ROWS - rows)), constant_values=-1).reshape(total)

    down = jnp.einsum("nd,hfd->nhf", gathered, adapter_down_maps, preferred_element_type=jnp.float32)
    slots = my_index * holder_count + jnp.arange(holder_count, dtype=jnp.int32)
    own = row_stored[:, None] == slots[None, :]
    low = jnp.sum(jnp.where(own[:, :, None], down, 0.0), axis=1).astype(jnp.bfloat16)
    low = jnp.concatenate([low[: total // 2], low[total // 2 :]], axis=1)
    low = lax.all_to_all(
        jnp.broadcast_to(low[None], (replicas,) + low.shape), "replica", split_axis=0, concat_axis=0, tiled=True
    )
    low = jnp.sum(low.astype(jnp.float32), axis=0)
    low = jnp.concatenate([low[:, :rank], low[:, rank:]], axis=0)

    projected = jnp.einsum("nd,idc->nic", gathered, query_key_value_weight, preferred_element_type=jnp.float32)

    def update(first_adapter, maps):
        held = maps.shape[0]
        which = first_adapter + jnp.arange(held, dtype=jnp.int32)
        wide = jnp.where((row_stored[:, None] == which[None, :])[:, :, None], low[:, None, :], 0.0)
        return jnp.dot(
            wide.astype(jnp.bfloat16).reshape(total, held * rank),
            maps.reshape(held * rank, columns),
            preferred_element_type=jnp.float32,
        )

    step_adapters = 64
    if adapter_count <= step_adapters:
        updated = update(0, adapter_up_maps)
    else:
        updated = lax.fori_loop(
            0,
            adapter_count // step_adapters,
            lambda i, sofar: sofar
            + update(
                i * step_adapters,
                lax.dynamic_slice_in_dim(adapter_up_maps, i * step_adapters, step_adapters, 0),
            ),
            jnp.zeros((total, columns), jnp.float32),
        )
    value = projected[:, 2] + adapter_scale * updated
    combined = jnp.concatenate([projected[:, 0], projected[:, 1], value], axis=1).astype(jnp.bfloat16)
    combined = combined.reshape(2, chips, ROWS, 3 * columns).transpose(1, 0, 2, 3)
    combined = combined.reshape(replicas, ROWS, 3 * columns)
    arrived = lax.all_to_all(combined, "replica", split_axis=0, concat_axis=0, tiled=True)
    arrived = arrived.reshape(replicas, ROWS, 3, columns).transpose(2, 1, 0, 3).reshape(3, ROWS, width)

    my_lengths = lax.dynamic_slice_in_dim(lengths, my_index * req_dev, req_dev)
    cosine, sine = rotation(my_lengths, steps)
    live = live_rows(my_lengths, request_page_table, pool_pages, page_len)
    kv = key_value_pool.reshape(pool_pages * page_len * 2, width)
    out = attention(steps, req_dev, arrived[0], arrived[1], arrived[2], cosine, sine, live, kv)
    return out.reshape(steps, req_dev, width)


def trade(value, mask, count):
    return lax.ppermute(value, "replica", [(i, i ^ mask) for i in range(count)])


def cache_kernel(pool_ref, out_ref, sem):
    heads = out_ref.shape[0]
    copies = [pltpu.make_async_copy(pool_ref.at[:, h], out_ref.at[h], sem.at[h]) for h in range(heads)]
    for copy in copies:
        copy.start()
    for copy in copies:
        copy.wait()


def cache_by_head(pool):
    tokens, heads = pool.shape[:2]
    return pl.pallas_call(
        cache_kernel,
        out_shape=jax.ShapeDtypeStruct((heads, tokens, 2, HD), pool.dtype),
        in_specs=[pl.BlockSpec(memory_space=pl.ANY)],
        out_specs=pl.BlockSpec(memory_space=pltpu.VMEM),
        scratch_shapes=[pltpu.SemaphoreType.DMA((heads,))],
        compiler_params=pltpu.CompilerParams(vmem_limit_bytes=8 * 2**20),
        cost_estimate=pl.CostEstimate(flops=0, bytes_accessed=2 * pool.size * 2, transcendentals=0),
        name="cache_by_head",
    )(pool)


CONTRACT_LANES = (((1,), (1,)), ((), ()))


def lanes_of(x_ref):
    return jnp.concatenate([x_ref[c] for c in range(x_ref.shape[0])], axis=1)


def low_kernel(count, slot_ref, down_ref, *refs):
    blocks, (x_ref, low_ref, sem) = refs[:count], refs[count:]
    steps = blocks[0].shape[0]
    copies = []
    for k, block in enumerate(blocks):
        for t in range(steps):
            at = k * steps + t
            copies.append(pltpu.make_async_copy(block.at[t], x_ref.at[:, at], sem.at[at]))
    for copy in copies:
        copy.start()
    for copy in copies:
        copy.wait()
    chunks, pairs = x_ref.shape[:2]
    rows = 2 * pairs
    holders, rank, width = down_ref.shape
    x = lanes_of(x_ref.reshape(chunks, rows, HD))
    maps = down_ref.reshape(holders * rank, width)[...]
    made = lax.dot_general(x, maps, CONTRACT_LANES, preferred_element_type=jnp.float32)
    slot = slot_ref[...]
    low = jnp.zeros((rows, rank), jnp.float32)
    for h in range(holders):
        low = low + jnp.where(slot == h, made[:, h * rank : (h + 1) * rank], 0.0)
    low_ref[...] = jnp.concatenate([low[: rows // 2], low[rows // 2 :]], axis=1).astype(low_ref.dtype)


def low_of(blocks, slot, down):
    count = len(blocks)
    steps, chunks = blocks[0].shape[:2]
    rows = count * steps * 2
    rank = down.shape[1]
    vmem = pl.BlockSpec(memory_space=pltpu.VMEM)
    return pl.pallas_call(
        functools.partial(low_kernel, count),
        out_shape=(
            jax.ShapeDtypeStruct((chunks, rows // 2, 2, HD), jnp.bfloat16),
            jax.ShapeDtypeStruct((rows // 2, 2 * rank), jnp.bfloat16),
        ),
        in_specs=[vmem, vmem] + [pl.BlockSpec(memory_space=pl.ANY)] * count,
        out_specs=(vmem, vmem),
        scratch_shapes=[pltpu.SemaphoreType.DMA((count * steps,))],
        compiler_params=pltpu.CompilerParams(vmem_limit_bytes=16 * 2**20),
        cost_estimate=pl.CostEstimate(flops=10**8, bytes_accessed=4 * 10**6, transcendentals=0),
        name="low_rows",
    )(slot, down, *blocks)


def put_chunks(buf, first, value):
    wide = value.shape[1]
    for c in range(-(-wide // HD)):
        part = value[:, c * HD : min((c + 1) * HD, wide)]
        if part.shape[1] < HD:
            part = jnp.concatenate([part, jnp.zeros((part.shape[0], HD - part.shape[1]), part.dtype)], axis=1)
        buf[first + c] = part.astype(buf.dtype)


def send_blocks(buf, outs, sem):
    steps = outs[0].shape[1]
    copies = [
        pltpu.make_async_copy(buf.at[:, k * steps : (k + 1) * steps], out, sem.at[k]) for k, out in enumerate(outs)
    ]
    for copy in copies:
        copy.start()
    for copy in copies:
        copy.wait()


def project_kernel(count, x_ref, w_ref, base_ref, *refs):
    outs, (buf, sem) = refs[:count], refs[count:]
    chunks, pairs = x_ref.shape[:2]
    rows = 2 * pairs
    x = lanes_of(x_ref.reshape(chunks, rows, HD))
    columns = w_ref.shape[1]
    each = -(-columns // HD)
    flat = buf.reshape(buf.shape[0], rows, HD)
    for i in range(2):
        put_chunks(
            flat, i * each, lax.dot_general(x, w_ref[i], CONTRACT_LANES, preferred_element_type=jnp.float32)
        )
    send_blocks(buf, outs, sem)
    base_ref[...] = lax.dot_general(x, w_ref[2], CONTRACT_LANES, preferred_element_type=jnp.float32)


def project(x, weight, count):
    chunks, pairs = x.shape[:2]
    columns = weight.shape[1]
    each = -(-columns // HD)
    steps = pairs // count
    vmem = pl.BlockSpec(memory_space=pltpu.VMEM)
    any_place = pl.BlockSpec(memory_space=pl.ANY)
    piece = jax.ShapeDtypeStruct((2 * each, steps, 2, HD), jnp.bfloat16)
    made = pl.pallas_call(
        functools.partial(project_kernel, count),
        out_shape=(jax.ShapeDtypeStruct((2 * pairs, columns), jnp.float32),) + (piece,) * count,
        in_specs=[vmem, vmem],
        out_specs=(vmem,) + (any_place,) * count,
        scratch_shapes=[pltpu.VMEM((2 * each, pairs, 2, HD), jnp.bfloat16), pltpu.SemaphoreType.DMA((count,))],
        compiler_params=pltpu.CompilerParams(vmem_limit_bytes=24 * 2**20),
        cost_estimate=pl.CostEstimate(flops=10**9, bytes_accessed=11 * 10**6, transcendentals=0),
        name="project",
    )(x, weight)
    return made[0], made[1:]


def update_kernel(count, stored_ref, base_ref, up_ref, *refs):
    lows, outs, (buf, sem) = refs[:count], refs[count : 2 * count], refs[2 * count :]
    half, packed = lows[0].shape
    rank = packed // 2
    rows = 2 * half
    per = half // (count // 2)
    row = lax.broadcasted_iota(jnp.int32, (half, half), 0)
    col = lax.broadcasted_iota(jnp.int32, (half, half), 1)
    low = jnp.zeros((half, packed), jnp.float32)
    for s in range(count):
        piece = lows[s][...]
        if s >= count // 2:
            piece = jnp.concatenate([piece[:, rank:], piece[:, :rank]], axis=1)
        near = s % (count // 2)
        same = ((row // per) == ((col // per) ^ near)) & (row % per == col % per)
        low = low + jnp.dot(
            jnp.where(same, 1.0, 0.0).astype(jnp.bfloat16), piece, preferred_element_type=jnp.float32
        )
    low = jnp.concatenate([low[:, :rank], low[:, rank:]], axis=0)
    adapters = up_ref.shape[0] // rank
    batch = 256 // rank
    spread = jnp.concatenate([low] * batch, axis=1)
    which = lax.broadcasted_iota(jnp.int32, (rows, batch * rank), 1) // rank
    ahead = stored_ref[...] - which
    total = jnp.zeros(base_ref.shape, jnp.float32)
    for a in range(0, adapters, batch):
        wide = jnp.where(ahead == a, spread, 0.0).astype(jnp.bfloat16)
        total = total + jnp.dot(wide, up_ref[a * rank : (a + batch) * rank], preferred_element_type=jnp.float32)
    put_chunks(buf.reshape(buf.shape[0], rows, HD), 0, base_ref[...] + adapter_scale * total)
    send_blocks(buf, outs, sem)


def update_values(stored, base, up, lows):
    count = len(lows)
    rows, columns = base.shape
    each = -(-columns // HD)
    pairs = rows // 2
    vmem = pl.BlockSpec(memory_space=pltpu.VMEM)
    any_place = pl.BlockSpec(memory_space=pl.ANY)
    piece = jax.ShapeDtypeStruct((each, pairs // count, 2, HD), jnp.bfloat16)
    return pl.pallas_call(
        functools.partial(update_kernel, count),
        out_shape=(piece,) * count,
        in_specs=[vmem] * (3 + count),
        out_specs=(any_place,) * count,
        scratch_shapes=[pltpu.VMEM((each, pairs, 2, HD), jnp.bfloat16), pltpu.SemaphoreType.DMA((count,))],
        compiler_params=pltpu.CompilerParams(vmem_limit_bytes=16 * 2**20),
        cost_estimate=pl.CostEstimate(flops=3 * 10**8, bytes_accessed=4 * 10**6, transcendentals=0),
        name="update_values",
    )(stored, base, up, *lows)


def attend_kernel(count, me_ref, cos_ref, sin_ref, live_ref, cache_ref, *refs):
    pieces, fresh_values = refs[:count], refs[count : 2 * count]
    out_ref, kn_ref, vn_ref = refs[2 * count :]
    steps = pieces[0].shape[1]
    rows = 2 * steps
    each = fresh_values[0].shape[0]
    heads = 2 * out_ref.shape[1] // count
    lanes = heads * HD
    group = rows * HEAD_BLOCK
    me = me_ref[0]
    first_core = me % 2 == 0
    cosine = cos_ref[...][:rows]
    sine = sin_ref[...][:rows]
    left = lax.broadcasted_iota(jnp.int32, (rows, HD), 1) < HD // 2

    def chip_columns(near, far, at):
        mine = [near[at + c].reshape(rows, HD).astype(jnp.float32) for c in range(each)]
        theirs = [far[at + c].reshape(rows, HD).astype(jnp.float32) for c in range(each)]
        low = [jnp.where(first_core, a, b) for a, b in zip(mine, theirs)]
        high = [pltpu.roll(jnp.where(first_core, b, a), HD // 2, 1) for a, b in zip(mine, theirs)]
        whole = low[:-1] + [jnp.where(left, low[-1], high[0])]
        return whole + [jnp.where(left, a, b) for a, b in zip(high[:-1], high[1:])]

    def rotated(parts):
        return [x * cosine + pltpu.roll(x, HD // 2, 1) * sine for x in parts]

    row_head = lax.broadcasted_iota(jnp.int32, (group, lanes), 0) % HEAD_BLOCK
    lane_head = lax.broadcasted_iota(jnp.int32, (group, lanes), 1) // HD
    own_head = row_head == lane_head
    row_j = lax.broadcasted_iota(jnp.int32, (group, 16), 0) // HEAD_BLOCK
    new_j = lax.broadcasted_iota(jnp.int32, (group, 16), 1)
    new_live = (new_j < rows) & (new_j % 2 == row_j % 2) & (new_j // 2 <= row_j // 2)
    live = jnp.concatenate(
        [
            jnp.broadcast_to(live_ref[j % 2 : j % 2 + 1, :], (HEAD_BLOCK, live_ref.shape[1]))
            for j in range(rows)
        ],
        axis=0,
    )
    live = live > 0
    kn_ref[...] = jnp.zeros_like(kn_ref)
    vn_ref[...] = jnp.zeros_like(vn_ref)
    tokens = cache_ref.shape[1] * 2
    cache = cache_ref.reshape(cache_ref.shape[0], tokens, HD)
    for pair in range(count // 2):
        base = ((me // 2) ^ pair) * heads
        near, far = pieces[2 * pair], pieces[2 * pair + 1]
        query = jnp.concatenate(rotated(chip_columns(near, far, 0)), axis=1)
        key_new = jnp.concatenate(rotated(chip_columns(near, far, each)), axis=1)
        value_new = jnp.concatenate(chip_columns(fresh_values[2 * pair], fresh_values[2 * pair + 1], 0), axis=1)
        kn_ref[0:rows] = key_new
        vn_ref[0:rows] = value_new
        kn = kn_ref[...].astype(jnp.bfloat16)
        vn = vn_ref[...].astype(jnp.bfloat16)
        spread = jnp.concatenate(
            [jnp.broadcast_to(query[j : j + 1], (HEAD_BLOCK, lanes)) for j in range(rows)], axis=0
        )
        spread = jnp.where(own_head, spread, 0.0).astype(jnp.bfloat16)
        kv = jnp.concatenate([cache[base + h] for h in range(heads)], axis=1)
        scores = lax.dot_general(spread, kv, CONTRACT_LANES, preferred_element_type=jnp.float32) * (HD**-0.5)
        scores = jnp.where(live, scores, masked_score)
        fresh = lax.dot_general(spread, kn, CONTRACT_LANES, preferred_element_type=jnp.float32) * (HD**-0.5)
        fresh = jnp.where(new_live, fresh, masked_score)
        top = jnp.maximum(jnp.max(scores, axis=1, keepdims=True), jnp.max(fresh, axis=1, keepdims=True))
        weights = jnp.where(live, jnp.exp(scores - top), 0.0)
        fresh = jnp.where(new_live, jnp.exp(fresh - top), 0.0)
        totals = jnp.sum(weights, axis=1, keepdims=True) + jnp.sum(fresh, axis=1, keepdims=True)
        weights = pltpu.roll(weights, 1, 1).astype(jnp.bfloat16)
        mixed = jnp.dot(weights, kv, preferred_element_type=jnp.float32)
        mixed = mixed + jnp.dot(fresh.astype(jnp.bfloat16), vn, preferred_element_type=jnp.float32)
        mixed = jnp.where(own_head, mixed / totals, 0.0)
        out = jnp.sum(mixed.reshape(rows, HEAD_BLOCK, lanes), axis=1).astype(out_ref.dtype)
        for t in range(steps):
            for h in range(heads):
                out_ref[t, base + h] = out[2 * t : 2 * t + 2, h * HD : (h + 1) * HD]


def attend(me, cosine, sine, live, cache, pieces, fresh_values):
    count = len(pieces)
    steps = pieces[0].shape[1]
    heads = cache.shape[0]
    lanes = 2 * heads // count * HD
    vmem = pl.BlockSpec(memory_space=pltpu.VMEM)
    return pl.pallas_call(
        functools.partial(attend_kernel, count),
        out_shape=jax.ShapeDtypeStruct((steps, heads, 2, HD), jnp.bfloat16),
        in_specs=[pl.BlockSpec(memory_space=pltpu.SMEM)] + [vmem] * (4 + 2 * count),
        out_specs=vmem,
        scratch_shapes=[pltpu.VMEM((16, lanes), jnp.float32)] * 2,
        compiler_params=pltpu.CompilerParams(vmem_limit_bytes=16 * 2**20),
        cost_estimate=pl.CostEstimate(flops=10**9, bytes_accessed=6 * 10**6, transcendentals=0),
        name="attention",
    )(me, cosine, sine, live, cache, *pieces, *fresh_values)


def chip_plan(
    count,
    hidden,
    query_key_value_weight,
    adapter_down_maps,
    adapter_up_maps,
    adapter_storage_row,
    request_adapter,
    lengths,
    request_page_table,
    key_value_pool,
):
    me = lax.axis_index("replica")
    steps, req_dev, width = hidden.shape
    heads = width // HD
    holder_count, rank, _ = adapter_down_maps.shape
    pool_pages, page_len = key_value_pool.shape[:2]
    adapter_count = adapter_storage_row.shape[0]
    request_count = request_adapter.shape[0]

    held = {0: hidden}
    for masks in (range(4, count, 4), (2,), (1,)):
        held.update({k ^ m: trade(v, m, count) for k, v in list(held.items()) for m in masks})
    blocks = [
        held[k].reshape(steps, req_dev, heads, HD).transpose(0, 2, 1, 3) for k in range(count)
    ]

    owner = me ^ jnp.arange(count, dtype=jnp.int32)
    request = owner[:, None] * req_dev + jnp.arange(req_dev, dtype=jnp.int32)[None, :]
    request = jnp.broadcast_to(request[:, None, :], (count, steps, req_dev)).reshape(-1, 1)
    adapter = jnp.sum(
        jnp.where(request == jnp.arange(request_count, dtype=jnp.int32)[None, :], request_adapter[None, :], 0),
        axis=1,
        keepdims=True,
    )
    stored = jnp.sum(
        jnp.where(adapter == jnp.arange(adapter_count, dtype=jnp.int32)[None, :], adapter_storage_row[None, :], 0),
        axis=1,
        keepdims=True,
    )

    tokens = pool_pages * page_len
    cache = cache_by_head(key_value_pool.reshape(tokens, 2, heads, HD).transpose(0, 2, 1, 3))

    x, low = low_of(blocks, stored - me * holder_count, adapter_down_maps)
    lows = [low] + [trade(low, k, count) for k in range(1, count)]
    base, pieces = project(x, query_key_value_weight.transpose(0, 2, 1), count)
    pieces = [pieces[0]] + [trade(pieces[k], k, count) for k in range(1, count)]
    values = update_values(stored, base, adapter_up_maps.reshape(adapter_count * rank, -1), lows)
    values = [values[0]] + [trade(values[k], k, count) for k in range(1, count)]

    my_lengths = lax.dynamic_slice_in_dim(lengths, me * req_dev, req_dev)
    cosine, sine = rotation(my_lengths, steps)
    live = live_rows(my_lengths, request_page_table, pool_pages, page_len)
    out = attend(me.astype(jnp.int32).reshape(1), cosine, sine, live, cache, pieces, values)
    return out.transpose(0, 2, 1, 3).reshape(steps, req_dev, width)


def per_device(replicas, *arrays):
    columns = arrays[1].shape[2]
    whole_heads = replicas % 4 == 0 and (2 * columns) % HD == 0 and columns % HD == HD // 2
    plan = chip_plan if whole_heads and arrays[0].shape[1] == 2 else general_plan
    return plan(replicas, *arrays)


def solution(mesh):
    placed = (
        P(None, ("groups", "replica"), None),
        P(None, None, "replica"),
        P("replica", None, None),
        P(None, None, "replica"),
        P(),
        P("groups"),
        P("groups"),
        P(("groups", "replica"), None),
        P(("groups", "replica"), None, None, None),
    )
    return jax.shard_map(
        functools.partial(per_device, mesh.shape["replica"]),
        mesh=mesh,
        in_specs=placed,
        out_specs=P(None, ("groups", "replica"), None),
        check_vma=False,
    )
```

```python
import functools

import jax
import jax.numpy as jnp
from jax import lax
from jax.experimental import pallas as pl
from jax.experimental.pallas import tpu as pltpu
from jax.sharding import PartitionSpec as P

HD = 128
ROWS = 8
HEAD_BLOCK = 8

adapter_scale = 2.0
masked_score = -1e30


def attention_kernel(steps, req_dev, q_ref, k_ref, v_ref, cos_ref, sin_ref, live_ref, kv_ref, out_ref, kn_ref, vn_ref):
    rows = steps * req_dev
    width = q_ref.shape[1]
    lanes = HEAD_BLOCK * HD
    group = rows * HEAD_BLOCK
    cosine = cos_ref[...]
    sine = sin_ref[...]

    def rotated(x):
        pieces = []
        for h in range(HEAD_BLOCK):
            head = x[:, h * HD : (h + 1) * HD]
            pieces.append(head * cosine + pltpu.roll(head, HD // 2, 1) * sine)
        return jnp.concatenate(pieces, axis=1)

    row_head = lax.broadcasted_iota(jnp.int32, (group, lanes), 0) % HEAD_BLOCK
    lane_head = lax.broadcasted_iota(jnp.int32, (group, lanes), 1) // HD
    own_head = row_head == lane_head
    row_j = lax.broadcasted_iota(jnp.int32, (group, 16), 0) // HEAD_BLOCK
    new_j = lax.broadcasted_iota(jnp.int32, (group, 16), 1)
    new_live = (new_j < rows) & (new_j % req_dev == row_j % req_dev) & (new_j // req_dev <= row_j // req_dev)
    live_all = live_ref[...]
    live = jnp.concatenate(
        [
            jnp.broadcast_to(live_all[j % req_dev : j % req_dev + 1], (HEAD_BLOCK, live_all.shape[1]))
            for j in range(rows)
        ],
        axis=0,
    )
    live = live > 0
    kn_ref[...] = jnp.zeros_like(kn_ref)
    vn_ref[...] = jnp.zeros_like(vn_ref)
    contract_lanes = (((1,), (1,)), ((), ()))
    for c in range(width // lanes):
        cols = slice(c * lanes, (c + 1) * lanes)
        query = rotated(q_ref[:, cols].astype(jnp.float32))
        key_new = rotated(k_ref[:, cols].astype(jnp.float32))
        kn_ref[0:8] = key_new
        vn_ref[0:8] = v_ref[:, cols].astype(jnp.float32)
        kn = kn_ref[...].astype(jnp.bfloat16)
        vn = vn_ref[...].astype(jnp.bfloat16)
        spread = jnp.concatenate(
            [jnp.broadcast_to(query[j : j + 1], (HEAD_BLOCK, lanes)) for j in range(rows)], axis=0
        )
        spread = jnp.where(own_head, spread, 0.0).astype(jnp.bfloat16)
        kv = kv_ref[:, cols]
        scores = lax.dot_general(spread, kv, contract_lanes, preferred_element_type=jnp.float32) * (HD**-0.5)
        scores = jnp.where(live, scores, masked_score)
        fresh = lax.dot_general(spread, kn, contract_lanes, preferred_element_type=jnp.float32) * (HD**-0.5)
        fresh = jnp.where(new_live, fresh, masked_score)
        top = jnp.maximum(jnp.max(scores, axis=1, keepdims=True), jnp.max(fresh, axis=1, keepdims=True))
        weights = jnp.where(live, jnp.exp(scores - top), 0.0)
        fresh = jnp.where(new_live, jnp.exp(fresh - top), 0.0)
        totals = jnp.sum(weights, axis=1, keepdims=True) + jnp.sum(fresh, axis=1, keepdims=True)
        weights = pltpu.roll(weights, 1, 1).astype(jnp.bfloat16)
        mixed = jnp.dot(weights, kv, preferred_element_type=jnp.float32)
        mixed = mixed + jnp.dot(fresh.astype(jnp.bfloat16), vn, preferred_element_type=jnp.float32)
        mixed = jnp.where(own_head, mixed / totals, 0.0)
        out = jnp.sum(mixed.reshape(rows, HEAD_BLOCK, lanes), axis=1)
        out_ref[:, cols] = out.astype(out_ref.dtype)


def attention(steps, req_dev, q, k, v, cosine, sine, live, kv):
    rows = steps * req_dev
    width = q.shape[1]
    vmem = pl.BlockSpec(memory_space=pltpu.VMEM)
    return pl.pallas_call(
        functools.partial(attention_kernel, steps, req_dev),
        out_shape=jax.ShapeDtypeStruct((rows, width), jnp.bfloat16),
        in_specs=[vmem] * 7,
        out_specs=vmem,
        scratch_shapes=[pltpu.VMEM((16, HEAD_BLOCK * HD), jnp.float32)] * 2,
        compiler_params=pltpu.CompilerParams(vmem_limit_bytes=32 * 2**20),
        cost_estimate=pl.CostEstimate(flops=10**9, bytes_accessed=6 * 10**6, transcendentals=0),
        name="attention",
    )(q, k, v, cosine, sine, live, kv)


def rotation(my_lengths, steps):
    rows = steps * my_lengths.shape[0]
    positions = (my_lengths[None, :] + jnp.arange(steps, dtype=jnp.int32)[:, None]).reshape(rows)
    positions = jnp.pad(positions, (0, ROWS - rows))
    half = HD // 2
    frequency = jnp.exp(jnp.arange(half, dtype=jnp.float32) * (-2.0 * jnp.log(10000.0) / HD))
    angles = positions.astype(jnp.float32)[:, None] * frequency[None, :]
    cosine = jnp.cos(angles)
    sine = jnp.sin(angles)
    cosine = jnp.concatenate([cosine, cosine], axis=1)
    sine = jnp.concatenate([-sine, sine], axis=1)
    return cosine, sine


def live_tokens(my_lengths, request_page_table, pool_pages, page_len):
    pages = jnp.arange(pool_pages, dtype=jnp.int32)
    max_pages = request_page_table.shape[1]
    place = jnp.max(
        jnp.where(
            request_page_table[:, :, None] == pages[None, None, :],
            jnp.arange(max_pages, dtype=jnp.int32)[None, :, None],
            -1,
        ),
        axis=1,
    )
    token = place[:, :, None] * page_len + jnp.arange(page_len, dtype=jnp.int32)[None, None, :]
    return (place[:, :, None] >= 0) & (token < my_lengths[:, None, None])


def live_rows(my_lengths, request_page_table, pool_pages, page_len):
    alive = live_tokens(my_lengths, request_page_table, pool_pages, page_len)
    live = jnp.stack([alive, jnp.zeros_like(alive)], axis=-1).astype(jnp.int32)
    return live.reshape(request_page_table.shape[0], pool_pages * page_len * 2)


def general_plan(
    replicas,
    hidden,
    query_key_value_weight,
    adapter_down_maps,
    adapter_up_maps,
    adapter_storage_row,
    request_adapter,
    lengths,
    request_page_table,
    key_value_pool,
):
    my_index = lax.axis_index("replica")
    steps, req_dev, width = hidden.shape
    rows = steps * req_dev
    columns = query_key_value_weight.shape[2]
    holder_count, rank, _ = adapter_down_maps.shape
    pool_pages, page_len = key_value_pool.shape[:2]
    adapter_count = adapter_storage_row.shape[0]
    chips = replicas // 2
    total = replicas * ROWS

    block = jnp.pad(hidden.reshape(rows, width), ((0, ROWS - rows), (0, 0)))
    same_core = [[2 * chip + core for chip in range(chips)] for core in range(2)]
    mine = lax.all_to_all(
        jnp.broadcast_to(block[None], (chips, ROWS, width)),
        "replica",
        split_axis=0,
        concat_axis=0,
        axis_index_groups=same_core,
        tiled=True,
    )
    other = lax.ppermute(mine, "replica", [(i, i ^ 1) for i in range(replicas)])
    first = my_index % 2 == 0
    gathered = jnp.stack([jnp.where(first, mine, other), jnp.where(first, other, mine)])
    gathered = gathered.reshape(total, width)

    stored_rows = jnp.sum(
        jnp.where(
            request_adapter[:, None] == jnp.arange(adapter_count, dtype=jnp.int32)[None, :],
            adapter_storage_row[None, :],
            0,
        ),
        axis=1,
    )
    by_block = stored_rows.reshape(chips, 2, 1, req_dev).transpose(1, 0, 2, 3)
    by_block = jnp.broadcast_to(by_block, (2, chips, steps, req_dev)).reshape(2, chips, rows)
    row_stored = jnp.pad(by_block, ((0, 0), (0, 0), (0, ROWS - rows)), constant_values=-1).reshape(total)

    down = jnp.einsum("nd,hfd->nhf", gathered, adapter_down_maps, preferred_element_type=jnp.float32)
    slots = my_index * holder_count + jnp.arange(holder_count, dtype=jnp.int32)
    own = row_stored[:, None] == slots[None, :]
    low = jnp.sum(jnp.where(own[:, :, None], down, 0.0), axis=1).astype(jnp.bfloat16)
    low = jnp.concatenate([low[: total // 2], low[total // 2 :]], axis=1)
    low = lax.all_to_all(
        jnp.broadcast_to(low[None], (replicas,) + low.shape), "replica", split_axis=0, concat_axis=0, tiled=True
    )
    low = jnp.sum(low.astype(jnp.float32), axis=0)
    low = jnp.concatenate([low[:, :rank], low[:, rank:]], axis=0)

    projected = jnp.einsum("nd,idc->nic", gathered, query_key_value_weight, preferred_element_type=jnp.float32)

    def update(first_adapter, maps):
        held = maps.shape[0]
        which = first_adapter + jnp.arange(held, dtype=jnp.int32)
        wide = jnp.where((row_stored[:, None] == which[None, :])[:, :, None], low[:, None, :], 0.0)
        return jnp.dot(
            wide.astype(jnp.bfloat16).reshape(total, held * rank),
            maps.reshape(held * rank, columns),
            preferred_element_type=jnp.float32,
        )

    step_adapters = 64
    if adapter_count <= step_adapters:
        updated = update(0, adapter_up_maps)
    else:
        updated = lax.fori_loop(
            0,
            adapter_count // step_adapters,
            lambda i, sofar: sofar
            + update(
                i * step_adapters,
                lax.dynamic_slice_in_dim(adapter_up_maps, i * step_adapters, step_adapters, 0),
            ),
            jnp.zeros((total, columns), jnp.float32),
        )
    value = projected[:, 2] + adapter_scale * updated
    combined = jnp.concatenate([projected[:, 0], projected[:, 1], value], axis=1).astype(jnp.bfloat16)
    combined = combined.reshape(2, chips, ROWS, 3 * columns).transpose(1, 0, 2, 3)
    combined = combined.reshape(replicas, ROWS, 3 * columns)
    arrived = lax.all_to_all(combined, "replica", split_axis=0, concat_axis=0, tiled=True)
    arrived = arrived.reshape(replicas, ROWS, 3, columns).transpose(2, 1, 0, 3).reshape(3, ROWS, width)

    my_lengths = lax.dynamic_slice_in_dim(lengths, my_index * req_dev, req_dev)
    cosine, sine = rotation(my_lengths, steps)
    live = live_rows(my_lengths, request_page_table, pool_pages, page_len)
    kv = key_value_pool.reshape(pool_pages * page_len * 2, width)
    out = attention(steps, req_dev, arrived[0], arrived[1], arrived[2], cosine, sine, live, kv)
    return out.reshape(steps, req_dev, width)


def trade(value, mask, count):
    return lax.ppermute(value, "replica", [(i, i ^ mask) for i in range(count)])


CONTRACT_LANES = (((1,), (1,)), ((), ()))
SPLIT_BUFFERS = 4


def cache_kernel(pool_ref, keys_ref, values_ref, raw, wide, sem):
    heads, tokens = raw.shape[:2]
    copies = [pltpu.make_async_copy(pool_ref.at[:, h], raw.at[h], sem.at[h]) for h in range(heads)]
    for copy in copies:
        copy.start()
    rows = raw.reshape(heads, 2 * tokens, HD)
    for h in range(heads):
        copies[h].wait()
        both = wide.at[h % SPLIT_BUFFERS]
        both[...] = rows[h].astype(jnp.float32)
        keys_ref[h] = both[pl.ds(0, tokens, stride=2), :].astype(jnp.bfloat16)
        values_ref[h] = both[pl.ds(1, tokens, stride=2), :].astype(jnp.bfloat16)


def cache_by_head(pool):
    tokens, heads = pool.shape[:2]
    vmem = pl.BlockSpec(memory_space=pltpu.VMEM)
    part = jax.ShapeDtypeStruct((heads, tokens, HD), pool.dtype)
    return pl.pallas_call(
        cache_kernel,
        out_shape=(part, part),
        in_specs=[pl.BlockSpec(memory_space=pltpu.HBM)],
        out_specs=(vmem, vmem),
        scratch_shapes=[
            pltpu.VMEM((heads, tokens, 2, HD), pool.dtype),
            pltpu.VMEM((SPLIT_BUFFERS, 2 * tokens, HD), jnp.float32),
            pltpu.SemaphoreType.DMA((heads,)),
        ],
        compiler_params=pltpu.CompilerParams(vmem_limit_bytes=20 * 2**20),
        cost_estimate=pl.CostEstimate(flops=0, bytes_accessed=3 * pool.size * 2, transcendentals=0),
        name="cache_by_head",
    )(pool)


def lanes_of(x_ref):
    return jnp.concatenate([x_ref[c] for c in range(x_ref.shape[0])], axis=1)


def low_kernel(count, me_ref, slot_ref, down_ref, *refs):
    blocks, (x_ref, low_ref, made_ref, sem, low_sem) = refs[:count], refs[count:]
    me = me_ref[0]
    steps = blocks[0].shape[0]
    copies = []
    for k, block in enumerate(blocks):
        for t in range(steps):
            copies.append(
                pltpu.make_async_copy(block.at[t], x_ref.at[:, (me ^ k) * steps + t], sem.at[k * steps + t])
            )
    for copy in copies:
        copy.start()
    for copy in copies:
        copy.wait()
    chunks, pairs = x_ref.shape[:2]
    rows = 2 * pairs
    holders, rank, width = down_ref.shape
    x = lanes_of(x_ref.reshape(chunks, rows, HD))
    maps = down_ref.reshape(holders * rank, width)[...]
    made = lax.dot_general(maps, x, CONTRACT_LANES, preferred_element_type=jnp.float32)
    slot = slot_ref[...]
    low = jnp.zeros((rank, rows), jnp.float32)
    for h in range(holders):
        low = low + jnp.where(slot == h, made[h * rank : (h + 1) * rank], 0.0)
    low = low.T
    made_ref[...] = jnp.concatenate([low[: rows // 2], low[rows // 2 :]], axis=1).astype(made_ref.dtype)
    copies = [pltpu.make_async_copy(made_ref, low_ref.at[k], low_sem.at[k]) for k in range(count)]
    for copy in copies:
        copy.start()
    for copy in copies:
        copy.wait()


def low_of(me, blocks, slot, down):
    count = len(blocks)
    steps, chunks = blocks[0].shape[:2]
    rows = count * steps * 2
    rank = down.shape[1]
    vmem = pl.BlockSpec(memory_space=pltpu.VMEM)
    any_place = pl.BlockSpec(memory_space=pl.ANY)
    return pl.pallas_call(
        functools.partial(low_kernel, count),
        out_shape=(
            jax.ShapeDtypeStruct((chunks, rows // 2, 2, HD), jnp.bfloat16),
            jax.ShapeDtypeStruct((count, rows // 2, 2 * rank), jnp.bfloat16),
        ),
        in_specs=[pl.BlockSpec(memory_space=pltpu.SMEM), vmem, vmem] + [any_place] * count,
        out_specs=(vmem, any_place),
        scratch_shapes=[
            pltpu.VMEM((rows // 2, 2 * rank), jnp.bfloat16),
            pltpu.SemaphoreType.DMA((count * steps,)),
            pltpu.SemaphoreType.DMA((count,)),
        ],
        compiler_params=pltpu.CompilerParams(vmem_limit_bytes=16 * 2**20),
        cost_estimate=pl.CostEstimate(flops=10**8, bytes_accessed=4 * 10**6, transcendentals=0),
        name="low_rows",
    )(me, slot, down, *blocks)


def project_kernel(x_ref, w_ref, out_ref):
    chunks, pairs = x_ref.shape[:2]
    x = lanes_of(x_ref.reshape(chunks, 2 * pairs, HD))
    for i in range(3):
        out_ref[i] = lax.dot_general(w_ref[i], x, CONTRACT_LANES, preferred_element_type=jnp.float32).T


def project(x, weight):
    pairs = x.shape[1]
    columns = weight.shape[1]
    vmem = pl.BlockSpec(memory_space=pltpu.VMEM)
    return pl.pallas_call(
        project_kernel,
        out_shape=jax.ShapeDtypeStruct((3, 2 * pairs, columns), jnp.float32),
        in_specs=[vmem, vmem],
        out_specs=vmem,
        compiler_params=pltpu.CompilerParams(vmem_limit_bytes=16 * 2**20),
        cost_estimate=pl.CostEstimate(flops=10**9, bytes_accessed=11 * 10**6, transcendentals=0),
        name="project",
    )(x, weight)


def put_chunks(buf, first, value):
    wide = value.shape[1]
    for c in range(-(-wide // HD)):
        part = value[:, c * HD : min((c + 1) * HD, wide)]
        if part.shape[1] < HD:
            part = jnp.concatenate([part, jnp.zeros((part.shape[0], HD - part.shape[1]), part.dtype)], axis=1)
        buf[first + c] = part.astype(buf.dtype)


def update_kernel(stored_ref, base_ref, up_ref, low_ref, out_ref, buf, sem):
    count, half, packed = low_ref.shape
    rank = packed // 2
    rows = 2 * half
    low = low_ref[0].astype(jnp.float32)
    for s in range(1, count):
        low = low + low_ref[s].astype(jnp.float32)
    low = jnp.concatenate([low[:, :rank], low[:, rank:]], axis=0)
    adapters = up_ref.shape[0] // rank
    batch = 256 // rank
    spread = jnp.concatenate([low] * batch, axis=1)
    which = lax.broadcasted_iota(jnp.int32, (rows, batch * rank), 1) // rank
    ahead = stored_ref[...] - which
    total = jnp.zeros(base_ref.shape[1:], jnp.float32)
    for a in range(0, adapters, batch):
        wide = jnp.where(ahead == a, spread, 0.0).astype(jnp.bfloat16)
        total = total + jnp.dot(wide, up_ref[a * rank : (a + batch) * rank], preferred_element_type=jnp.float32)
    flat = buf.reshape(buf.shape[0], rows, HD)
    each = buf.shape[0] // 3
    put_chunks(flat, 0, base_ref[0])
    put_chunks(flat, each, base_ref[1])
    put_chunks(flat, 2 * each, base_ref[2] + adapter_scale * total)
    steps = out_ref.shape[2]
    copies = [
        pltpu.make_async_copy(buf.at[:, k * steps : (k + 1) * steps], out_ref.at[k], sem.at[k]) for k in range(count)
    ]
    for copy in copies:
        copy.start()
    for copy in copies:
        copy.wait()


def update_values(stored, base, up, lows):
    count = lows.shape[0]
    rows, columns = base.shape[1:]
    chunks = 3 * -(-columns // HD)
    pairs = rows // 2
    vmem = pl.BlockSpec(memory_space=pltpu.VMEM)
    return pl.pallas_call(
        update_kernel,
        out_shape=jax.ShapeDtypeStruct((count, chunks, pairs // count, 2, HD), jnp.bfloat16),
        in_specs=[vmem] * 4,
        out_specs=pl.BlockSpec(memory_space=pl.ANY),
        scratch_shapes=[pltpu.VMEM((chunks, pairs, 2, HD), jnp.bfloat16), pltpu.SemaphoreType.DMA((count,))],
        compiler_params=pltpu.CompilerParams(vmem_limit_bytes=16 * 2**20),
        cost_estimate=pl.CostEstimate(flops=3 * 10**8, bytes_accessed=4 * 10**6, transcendentals=0),
        name="update_values",
    )(stored, base, up, lows)


def attend_kernel(cos_ref, sin_ref, live_ref, keys_ref, values_ref, pieces_ref, out_ref, kn_ref, vn_ref):
    count, _, steps = pieces_ref.shape[:3]
    rows = 2 * steps
    each = pieces_ref.shape[1] // 3
    heads = 2 * out_ref.shape[1] // count
    lanes = heads * HD
    group = rows * HEAD_BLOCK
    cosine = cos_ref[...][:rows]
    sine = sin_ref[...][:rows]
    left = lax.broadcasted_iota(jnp.int32, (rows, HD), 1) < HD // 2

    def chip_columns(chip, at):
        low = [pieces_ref[2 * chip, at + c].reshape(rows, HD).astype(jnp.float32) for c in range(each)]
        high = [pieces_ref[2 * chip + 1, at + c].reshape(rows, HD).astype(jnp.float32) for c in range(each)]
        high = [pltpu.roll(x, HD // 2, 1) for x in high]
        whole = low[:-1] + [jnp.where(left, low[-1], high[0])]
        return whole + [jnp.where(left, a, b) for a, b in zip(high[:-1], high[1:])]

    def rotated(parts):
        return [x * cosine + pltpu.roll(x, HD // 2, 1) * sine for x in parts]

    row_head = lax.broadcasted_iota(jnp.int32, (group, lanes), 0) % HEAD_BLOCK
    lane_head = lax.broadcasted_iota(jnp.int32, (group, lanes), 1) // HD
    own_head = row_head == lane_head
    row_j = lax.broadcasted_iota(jnp.int32, (group, 16), 0) // HEAD_BLOCK
    new_j = lax.broadcasted_iota(jnp.int32, (group, 16), 1)
    new_live = (new_j < rows) & (new_j % 2 == row_j % 2) & (new_j // 2 <= row_j // 2)
    live = jnp.concatenate(
        [
            jnp.broadcast_to(live_ref[j % 2 : j % 2 + 1, :], (HEAD_BLOCK, live_ref.shape[1]))
            for j in range(rows)
        ],
        axis=0,
    )
    live = live > 0
    kn_ref[...] = jnp.zeros_like(kn_ref)
    vn_ref[...] = jnp.zeros_like(vn_ref)
    for chip in range(count // 2):
        base = chip * heads
        query = jnp.concatenate(rotated(chip_columns(chip, 0)), axis=1)
        kn_ref[0:rows] = jnp.concatenate(rotated(chip_columns(chip, each)), axis=1)
        vn_ref[0:rows] = jnp.concatenate(chip_columns(chip, 2 * each), axis=1)
        kn = kn_ref[...].astype(jnp.bfloat16)
        vn = vn_ref[...].astype(jnp.bfloat16)
        spread = jnp.concatenate(
            [jnp.broadcast_to(query[j : j + 1], (HEAD_BLOCK, lanes)) for j in range(rows)], axis=0
        )
        spread = jnp.where(own_head, spread, 0.0).astype(jnp.bfloat16)
        keys = jnp.concatenate([keys_ref[base + h] for h in range(heads)], axis=1)
        values = jnp.concatenate([values_ref[base + h] for h in range(heads)], axis=1)
        scores = lax.dot_general(spread, keys, CONTRACT_LANES, preferred_element_type=jnp.float32) * (HD**-0.5)
        scores = jnp.where(live, scores, masked_score)
        fresh = lax.dot_general(spread, kn, CONTRACT_LANES, preferred_element_type=jnp.float32) * (HD**-0.5)
        fresh = jnp.where(new_live, fresh, masked_score)
        top = jnp.maximum(jnp.max(scores, axis=1, keepdims=True), jnp.max(fresh, axis=1, keepdims=True))
        weights = jnp.where(live, jnp.exp(scores - top), 0.0)
        fresh = jnp.where(new_live, jnp.exp(fresh - top), 0.0)
        totals = jnp.sum(weights, axis=1, keepdims=True) + jnp.sum(fresh, axis=1, keepdims=True)
        mixed = jnp.dot(weights.astype(jnp.bfloat16), values, preferred_element_type=jnp.float32)
        mixed = mixed + jnp.dot(fresh.astype(jnp.bfloat16), vn, preferred_element_type=jnp.float32)
        mixed = jnp.where(own_head, mixed / totals, 0.0)
        out = jnp.sum(mixed.reshape(rows, HEAD_BLOCK, lanes), axis=1).astype(out_ref.dtype)
        for t in range(steps):
            for h in range(heads):
                out_ref[t, base + h] = out[2 * t : 2 * t + 2, h * HD : (h + 1) * HD]


def attend(cosine, sine, live, keys, values, pieces):
    count, _, steps = pieces.shape[:3]
    heads = keys.shape[0]
    lanes = 2 * heads // count * HD
    vmem = pl.BlockSpec(memory_space=pltpu.VMEM)
    return pl.pallas_call(
        attend_kernel,
        out_shape=jax.ShapeDtypeStruct((steps, heads, 2, HD), jnp.bfloat16),
        in_specs=[vmem] * 6,
        out_specs=vmem,
        scratch_shapes=[pltpu.VMEM((16, lanes), jnp.float32)] * 2,
        compiler_params=pltpu.CompilerParams(vmem_limit_bytes=16 * 2**20),
        cost_estimate=pl.CostEstimate(flops=10**9, bytes_accessed=6 * 10**6, transcendentals=0),
        name="attention",
    )(cosine, sine, live, keys, values, pieces)


def chip_plan(
    count,
    hidden,
    query_key_value_weight,
    adapter_down_maps,
    adapter_up_maps,
    adapter_storage_row,
    request_adapter,
    lengths,
    request_page_table,
    key_value_pool,
):
    me = lax.axis_index("replica")
    steps, req_dev, width = hidden.shape
    heads = width // HD
    holder_count, rank, _ = adapter_down_maps.shape
    pool_pages, page_len = key_value_pool.shape[:2]
    adapter_count = adapter_storage_row.shape[0]

    held = {0: hidden}
    for masks in (range(4, count, 4), (2,), (1,)):
        held.update({k ^ m: trade(v, m, count) for k, v in list(held.items()) for m in masks})
    blocks = [
        held[k].reshape(steps, req_dev, heads, HD).transpose(0, 2, 1, 3) for k in range(count)
    ]

    stored = jnp.sum(
        jnp.where(
            request_adapter[:, None] == jnp.arange(adapter_count, dtype=jnp.int32)[None, :],
            adapter_storage_row[None, :],
            0,
        ),
        axis=1,
    )
    stored = jnp.broadcast_to(stored.reshape(count, 1, req_dev), (count, steps, req_dev)).reshape(-1)

    tokens = pool_pages * page_len
    keys, values = cache_by_head(key_value_pool.reshape(tokens, 2, heads, HD).transpose(0, 2, 1, 3))

    x, lows = low_of(
        me.astype(jnp.int32).reshape(1), blocks, (stored - me * holder_count)[None, :], adapter_down_maps
    )
    lows = lax.all_to_all(lows, "replica", split_axis=0, concat_axis=0, tiled=True)
    base = project(x, query_key_value_weight.transpose(0, 2, 1))
    pieces = update_values(stored[:, None], base, adapter_up_maps.reshape(adapter_count * rank, -1), lows)
    pieces = lax.all_to_all(pieces, "replica", split_axis=0, concat_axis=0, tiled=True)

    my_lengths = lax.dynamic_slice_in_dim(lengths, me * req_dev, req_dev)
    cosine, sine = rotation(my_lengths, steps)
    live = live_tokens(my_lengths, request_page_table, pool_pages, page_len).astype(jnp.int32)
    out = attend(cosine, sine, live.reshape(req_dev, tokens), keys, values, pieces)
    return out.transpose(0, 2, 1, 3).reshape(steps, req_dev, width)


def per_device(replicas, *arrays):
    columns = arrays[1].shape[2]
    whole_heads = replicas % 4 == 0 and (2 * columns) % HD == 0 and columns % HD == HD // 2
    plan = chip_plan if whole_heads and arrays[0].shape[1] == 2 else general_plan
    return plan(replicas, *arrays)


def solution(mesh):
    placed = (
        P(None, ("groups", "replica"), None),
        P(None, None, "replica"),
        P("replica", None, None),
        P(None, None, "replica"),
        P(),
        P("groups"),
        P("groups"),
        P(("groups", "replica"), None),
        P(("groups", "replica"), None, None, None),
    )
    return jax.shard_map(
        functools.partial(per_device, mesh.shape["replica"]),
        mesh=mesh,
        in_specs=placed,
        out_specs=P(None, ("groups", "replica"), None),
        check_vma=False,
    )
```

```python
import functools

import jax
import jax.numpy as jnp
from jax import lax
from jax.experimental import pallas as pl
from jax.experimental.pallas import tpu as pltpu
from jax.sharding import PartitionSpec as P

HD = 128
ROWS = 8
HEAD_BLOCK = 8

adapter_scale = 2.0
masked_score = -1e30


def attention_kernel(steps, req_dev, q_ref, k_ref, v_ref, cos_ref, sin_ref, live_ref, kv_ref, out_ref, kn_ref, vn_ref):
    rows = steps * req_dev
    width = q_ref.shape[1]
    lanes = HEAD_BLOCK * HD
    group = rows * HEAD_BLOCK
    cosine = cos_ref[...]
    sine = sin_ref[...]

    def rotated(x):
        pieces = []
        for h in range(HEAD_BLOCK):
            head = x[:, h * HD : (h + 1) * HD]
            pieces.append(head * cosine + pltpu.roll(head, HD // 2, 1) * sine)
        return jnp.concatenate(pieces, axis=1)

    row_head = lax.broadcasted_iota(jnp.int32, (group, lanes), 0) % HEAD_BLOCK
    lane_head = lax.broadcasted_iota(jnp.int32, (group, lanes), 1) // HD
    own_head = row_head == lane_head
    row_j = lax.broadcasted_iota(jnp.int32, (group, 16), 0) // HEAD_BLOCK
    new_j = lax.broadcasted_iota(jnp.int32, (group, 16), 1)
    new_live = (new_j < rows) & (new_j % req_dev == row_j % req_dev) & (new_j // req_dev <= row_j // req_dev)
    live_all = live_ref[...]
    live = jnp.concatenate(
        [
            jnp.broadcast_to(live_all[j % req_dev : j % req_dev + 1], (HEAD_BLOCK, live_all.shape[1]))
            for j in range(rows)
        ],
        axis=0,
    )
    live = live > 0
    kn_ref[...] = jnp.zeros_like(kn_ref)
    vn_ref[...] = jnp.zeros_like(vn_ref)
    contract_lanes = (((1,), (1,)), ((), ()))
    for c in range(width // lanes):
        cols = slice(c * lanes, (c + 1) * lanes)
        query = rotated(q_ref[:, cols].astype(jnp.float32))
        key_new = rotated(k_ref[:, cols].astype(jnp.float32))
        kn_ref[0:8] = key_new
        vn_ref[0:8] = v_ref[:, cols].astype(jnp.float32)
        kn = kn_ref[...].astype(jnp.bfloat16)
        vn = vn_ref[...].astype(jnp.bfloat16)
        spread = jnp.concatenate(
            [jnp.broadcast_to(query[j : j + 1], (HEAD_BLOCK, lanes)) for j in range(rows)], axis=0
        )
        spread = jnp.where(own_head, spread, 0.0).astype(jnp.bfloat16)
        kv = kv_ref[:, cols]
        scores = lax.dot_general(spread, kv, contract_lanes, preferred_element_type=jnp.float32) * (HD**-0.5)
        scores = jnp.where(live, scores, masked_score)
        fresh = lax.dot_general(spread, kn, contract_lanes, preferred_element_type=jnp.float32) * (HD**-0.5)
        fresh = jnp.where(new_live, fresh, masked_score)
        top = jnp.maximum(jnp.max(scores, axis=1, keepdims=True), jnp.max(fresh, axis=1, keepdims=True))
        weights = jnp.where(live, jnp.exp(scores - top), 0.0)
        fresh = jnp.where(new_live, jnp.exp(fresh - top), 0.0)
        totals = jnp.sum(weights, axis=1, keepdims=True) + jnp.sum(fresh, axis=1, keepdims=True)
        weights = pltpu.roll(weights, 1, 1).astype(jnp.bfloat16)
        mixed = jnp.dot(weights, kv, preferred_element_type=jnp.float32)
        mixed = mixed + jnp.dot(fresh.astype(jnp.bfloat16), vn, preferred_element_type=jnp.float32)
        mixed = jnp.where(own_head, mixed / totals, 0.0)
        out = jnp.sum(mixed.reshape(rows, HEAD_BLOCK, lanes), axis=1)
        out_ref[:, cols] = out.astype(out_ref.dtype)


def attention(steps, req_dev, q, k, v, cosine, sine, live, kv):
    rows = steps * req_dev
    width = q.shape[1]
    vmem = pl.BlockSpec(memory_space=pltpu.VMEM)
    return pl.pallas_call(
        functools.partial(attention_kernel, steps, req_dev),
        out_shape=jax.ShapeDtypeStruct((rows, width), jnp.bfloat16),
        in_specs=[vmem] * 7,
        out_specs=vmem,
        scratch_shapes=[pltpu.VMEM((16, HEAD_BLOCK * HD), jnp.float32)] * 2,
        compiler_params=pltpu.CompilerParams(vmem_limit_bytes=32 * 2**20),
        cost_estimate=pl.CostEstimate(flops=10**9, bytes_accessed=6 * 10**6, transcendentals=0),
        name="attention",
    )(q, k, v, cosine, sine, live, kv)


def rotation(my_lengths, steps):
    rows = steps * my_lengths.shape[0]
    positions = (my_lengths[None, :] + jnp.arange(steps, dtype=jnp.int32)[:, None]).reshape(rows)
    positions = jnp.pad(positions, (0, ROWS - rows))
    half = HD // 2
    frequency = jnp.exp(jnp.arange(half, dtype=jnp.float32) * (-2.0 * jnp.log(10000.0) / HD))
    angles = positions.astype(jnp.float32)[:, None] * frequency[None, :]
    cosine = jnp.cos(angles)
    sine = jnp.sin(angles)
    cosine = jnp.concatenate([cosine, cosine], axis=1)
    sine = jnp.concatenate([-sine, sine], axis=1)
    return cosine, sine


def live_tokens(my_lengths, request_page_table, pool_pages, page_len):
    pages = jnp.arange(pool_pages, dtype=jnp.int32)
    max_pages = request_page_table.shape[1]
    place = jnp.max(
        jnp.where(
            request_page_table[:, :, None] == pages[None, None, :],
            jnp.arange(max_pages, dtype=jnp.int32)[None, :, None],
            -1,
        ),
        axis=1,
    )
    token = place[:, :, None] * page_len + jnp.arange(page_len, dtype=jnp.int32)[None, None, :]
    return (place[:, :, None] >= 0) & (token < my_lengths[:, None, None])


def live_rows(my_lengths, request_page_table, pool_pages, page_len):
    alive = live_tokens(my_lengths, request_page_table, pool_pages, page_len)
    live = jnp.stack([alive, jnp.zeros_like(alive)], axis=-1).astype(jnp.int32)
    return live.reshape(request_page_table.shape[0], pool_pages * page_len * 2)


def general_plan(
    replicas,
    hidden,
    query_key_value_weight,
    adapter_down_maps,
    adapter_up_maps,
    adapter_storage_row,
    request_adapter,
    lengths,
    request_page_table,
    key_value_pool,
):
    my_index = lax.axis_index("replica")
    steps, req_dev, width = hidden.shape
    rows = steps * req_dev
    columns = query_key_value_weight.shape[2]
    holder_count, rank, _ = adapter_down_maps.shape
    pool_pages, page_len = key_value_pool.shape[:2]
    adapter_count = adapter_storage_row.shape[0]
    chips = replicas // 2
    total = replicas * ROWS

    block = jnp.pad(hidden.reshape(rows, width), ((0, ROWS - rows), (0, 0)))
    same_core = [[2 * chip + core for chip in range(chips)] for core in range(2)]
    mine = lax.all_to_all(
        jnp.broadcast_to(block[None], (chips, ROWS, width)),
        "replica",
        split_axis=0,
        concat_axis=0,
        axis_index_groups=same_core,
        tiled=True,
    )
    other = lax.ppermute(mine, "replica", [(i, i ^ 1) for i in range(replicas)])
    first = my_index % 2 == 0
    gathered = jnp.stack([jnp.where(first, mine, other), jnp.where(first, other, mine)])
    gathered = gathered.reshape(total, width)

    stored_rows = jnp.sum(
        jnp.where(
            request_adapter[:, None] == jnp.arange(adapter_count, dtype=jnp.int32)[None, :],
            adapter_storage_row[None, :],
            0,
        ),
        axis=1,
    )
    by_block = stored_rows.reshape(chips, 2, 1, req_dev).transpose(1, 0, 2, 3)
    by_block = jnp.broadcast_to(by_block, (2, chips, steps, req_dev)).reshape(2, chips, rows)
    row_stored = jnp.pad(by_block, ((0, 0), (0, 0), (0, ROWS - rows)), constant_values=-1).reshape(total)

    down = jnp.einsum("nd,hfd->nhf", gathered, adapter_down_maps, preferred_element_type=jnp.float32)
    slots = my_index * holder_count + jnp.arange(holder_count, dtype=jnp.int32)
    own = row_stored[:, None] == slots[None, :]
    low = jnp.sum(jnp.where(own[:, :, None], down, 0.0), axis=1).astype(jnp.bfloat16)
    low = jnp.concatenate([low[: total // 2], low[total // 2 :]], axis=1)
    low = lax.all_to_all(
        jnp.broadcast_to(low[None], (replicas,) + low.shape), "replica", split_axis=0, concat_axis=0, tiled=True
    )
    low = jnp.sum(low.astype(jnp.float32), axis=0)
    low = jnp.concatenate([low[:, :rank], low[:, rank:]], axis=0)

    projected = jnp.einsum("nd,idc->nic", gathered, query_key_value_weight, preferred_element_type=jnp.float32)

    def update(first_adapter, maps):
        held = maps.shape[0]
        which = first_adapter + jnp.arange(held, dtype=jnp.int32)
        wide = jnp.where((row_stored[:, None] == which[None, :])[:, :, None], low[:, None, :], 0.0)
        return jnp.dot(
            wide.astype(jnp.bfloat16).reshape(total, held * rank),
            maps.reshape(held * rank, columns),
            preferred_element_type=jnp.float32,
        )

    step_adapters = 64
    if adapter_count <= step_adapters:
        updated = update(0, adapter_up_maps)
    else:
        updated = lax.fori_loop(
            0,
            adapter_count // step_adapters,
            lambda i, sofar: sofar
            + update(
                i * step_adapters,
                lax.dynamic_slice_in_dim(adapter_up_maps, i * step_adapters, step_adapters, 0),
            ),
            jnp.zeros((total, columns), jnp.float32),
        )
    value = projected[:, 2] + adapter_scale * updated
    combined = jnp.concatenate([projected[:, 0], projected[:, 1], value], axis=1).astype(jnp.bfloat16)
    combined = combined.reshape(2, chips, ROWS, 3 * columns).transpose(1, 0, 2, 3)
    combined = combined.reshape(replicas, ROWS, 3 * columns)
    arrived = lax.all_to_all(combined, "replica", split_axis=0, concat_axis=0, tiled=True)
    arrived = arrived.reshape(replicas, ROWS, 3, columns).transpose(2, 1, 0, 3).reshape(3, ROWS, width)

    my_lengths = lax.dynamic_slice_in_dim(lengths, my_index * req_dev, req_dev)
    cosine, sine = rotation(my_lengths, steps)
    live = live_rows(my_lengths, request_page_table, pool_pages, page_len)
    kv = key_value_pool.reshape(pool_pages * page_len * 2, width)
    out = attention(steps, req_dev, arrived[0], arrived[1], arrived[2], cosine, sine, live, kv)
    return out.reshape(steps, req_dev, width)


def trade(value, mask, count):
    return lax.ppermute(value, "replica", [(i, i ^ mask) for i in range(count)])


CONTRACT_LANES = (((1,), (1,)), ((), ()))
SPLIT_BUFFERS = 4


def in_hbm(x):
    return pltpu.with_memory_space_constraint(x, pltpu.HBM)


VMEM = pl.BlockSpec(memory_space=pltpu.VMEM)
HBM = pl.BlockSpec(memory_space=pltpu.HBM)
SMEM = pl.BlockSpec(memory_space=pltpu.SMEM)
ANY = pl.BlockSpec(memory_space=pl.ANY)


def start_all(copies):
    for copy in copies:
        copy.start()
    return copies


def wait_all(copies):
    for copy in copies:
        copy.wait()


def cache_kernel(first, pool_ref, keys_ref, values_ref, raw, wide, keys, values, sem, out_sem):
    heads, tokens = raw.shape[:2]
    copies = start_all(
        [pltpu.make_async_copy(pool_ref.at[:, first + h], raw.at[h], sem.at[h]) for h in range(heads)]
    )
    rows = raw.reshape(heads, 2 * tokens, HD)
    sent = []
    for h in range(heads):
        copies[h].wait()
        both = wide.at[h % SPLIT_BUFFERS]
        both[...] = rows[h].astype(jnp.float32)
        keys[h] = both[pl.ds(0, tokens, stride=2), :].astype(jnp.bfloat16)
        values[h] = both[pl.ds(1, tokens, stride=2), :].astype(jnp.bfloat16)
        sent += start_all(
            [
                pltpu.make_async_copy(keys.at[h], keys_ref.at[h], out_sem.at[0, h]),
                pltpu.make_async_copy(values.at[h], values_ref.at[h], out_sem.at[1, h]),
            ]
        )
    wait_all(sent)


def cache_by_head(pool, first, heads):
    tokens = pool.shape[0]
    part = pltpu.HBM((heads, tokens, HD), pool.dtype)
    return pl.pallas_call(
        functools.partial(cache_kernel, first),
        out_shape=(part, part),
        in_specs=[HBM],
        out_specs=(HBM, HBM),
        scratch_shapes=[
            pltpu.VMEM((heads, tokens, 2, HD), pool.dtype),
            pltpu.VMEM((SPLIT_BUFFERS, 2 * tokens, HD), jnp.float32),
            pltpu.VMEM((heads, tokens, HD), pool.dtype),
            pltpu.VMEM((heads, tokens, HD), pool.dtype),
            pltpu.SemaphoreType.DMA((heads,)),
            pltpu.SemaphoreType.DMA((2, heads)),
        ],
        compiler_params=pltpu.CompilerParams(vmem_limit_bytes=16 * 2**20),
        cost_estimate=pl.CostEstimate(flops=0, bytes_accessed=12 * 10**6, transcendentals=0),
        name="cache_by_head",
    )(pool)


def lanes_of(x):
    return jnp.concatenate([x[c] for c in range(x.shape[0])], axis=1)


def low_kernel(count, me_ref, slot_ref, down_ref, *refs):
    blocks, (x_ref, low_ref, x_buf, maps, made_ref, sem, low_sem, own_sem) = refs[:count], refs[count:]
    me = me_ref[0]
    steps = blocks[0].shape[0]
    holders, rank, width = down_ref.shape
    fetch = pltpu.make_async_copy(down_ref, maps, own_sem.at[0])
    fetch.start()
    copies = []
    for k, block in enumerate(blocks):
        for t in range(steps):
            copies.append(
                pltpu.make_async_copy(block.at[t], x_buf.at[:, (me ^ k) * steps + t], sem.at[k * steps + t])
            )
    wait_all(start_all(copies))
    keep = pltpu.make_async_copy(x_buf, x_ref, own_sem.at[1])
    keep.start()
    chunks, pairs = x_buf.shape[:2]
    rows = 2 * pairs
    x = lanes_of(x_buf.reshape(chunks, rows, HD))
    fetch.wait()
    made = lax.dot_general(
        maps.reshape(holders * rank, width)[...], x, CONTRACT_LANES, preferred_element_type=jnp.float32
    )
    slot = slot_ref[...]
    low = jnp.zeros((rank, rows), jnp.float32)
    for h in range(holders):
        low = low + jnp.where(slot == h, made[h * rank : (h + 1) * rank], 0.0)
    low = low.T
    made_ref[...] = jnp.concatenate([low[: rows // 2], low[rows // 2 :]], axis=1).astype(made_ref.dtype)
    wait_all(start_all([pltpu.make_async_copy(made_ref, low_ref.at[k], low_sem.at[k]) for k in range(count)]))
    keep.wait()


def low_of(me, blocks, slot, down):
    count = len(blocks)
    steps, chunks = blocks[0].shape[:2]
    rows = count * steps * 2
    rank = down.shape[1]
    return pl.pallas_call(
        functools.partial(low_kernel, count),
        out_shape=(
            pltpu.HBM((chunks, rows // 2, 2, HD), jnp.bfloat16),
            pltpu.HBM((count, rows // 2, 2 * rank), jnp.bfloat16),
        ),
        in_specs=[SMEM, VMEM, HBM] + [ANY] * count,
        out_specs=(HBM, HBM),
        scratch_shapes=[
            pltpu.VMEM((chunks, rows // 2, 2, HD), jnp.bfloat16),
            pltpu.VMEM(down.shape, jnp.bfloat16),
            pltpu.VMEM((rows // 2, 2 * rank), jnp.bfloat16),
            pltpu.SemaphoreType.DMA((count * steps,)),
            pltpu.SemaphoreType.DMA((count,)),
            pltpu.SemaphoreType.DMA((2,)),
        ],
        compiler_params=pltpu.CompilerParams(vmem_limit_bytes=16 * 2**20),
        cost_estimate=pl.CostEstimate(flops=10**8, bytes_accessed=4 * 10**6, transcendentals=0),
        name="low_rows",
    )(me, slot, in_hbm(down), *blocks)


def put_chunks(buf, first, value):
    wide = value.shape[1]
    for c in range(-(-wide // HD)):
        part = value[:, c * HD : min((c + 1) * HD, wide)]
        if part.shape[1] < HD:
            part = jnp.concatenate([part, jnp.zeros((part.shape[0], HD - part.shape[1]), part.dtype)], axis=1)
        buf[first + c] = part.astype(buf.dtype)


def send_blocks(buf, out_ref, first, sem):
    count, _, steps = out_ref.shape[:3]
    chunks = buf.shape[0]
    return start_all(
        [
            pltpu.make_async_copy(
                buf.at[:, k * steps : (k + 1) * steps], out_ref.at[k, first : first + chunks], sem.at[k]
            )
            for k in range(count)
        ]
    )


PROJECT_CHUNK = 1024


def project_kernel(x_ref, w_ref, send_ref, base_ref, x_buf, w_buf, total, buf, base, x_sem, w_sem, sem, base_sem):
    chunks, pairs = x_buf.shape[:2]
    rows = 2 * pairs
    columns, width = w_ref.shape[1:]
    parts = width // PROJECT_CHUNK
    per = PROJECT_CHUNK // HD
    fetch_x = pltpu.make_async_copy(x_ref, x_buf, x_sem)
    fetch_x.start()
    fetches = start_all(
        [
            pltpu.make_async_copy(
                w_ref.at[:, :, p * PROJECT_CHUNK : (p + 1) * PROJECT_CHUNK], w_buf.at[p], w_sem.at[p]
            )
            for p in range(parts)
        ]
    )
    fetch_x.wait()
    x_rows = x_buf.reshape(chunks, rows, HD)
    for p in range(parts):
        fetches[p].wait()
        x = jnp.concatenate([x_rows[c] for c in range(p * per, (p + 1) * per)], axis=1)
        for i in range(3):
            made = lax.dot_general(w_buf[p, i], x, CONTRACT_LANES, preferred_element_type=jnp.float32)
            total[i] = made if p == 0 else total[i] + made
    each = buf.shape[0] // 2
    flat = buf.reshape(buf.shape[0], rows, HD)
    for i in range(2):
        put_chunks(flat, i * each, total[i].T)
    sent = send_blocks(buf, send_ref, 0, sem)
    base[...] = total[2].T
    keep = pltpu.make_async_copy(base, base_ref, base_sem)
    keep.start()
    wait_all(sent)
    keep.wait()


def project(x, weight, count):
    chunks, pairs = x.shape[:2]
    columns, width = weight.shape[1:]
    each = -(-columns // HD)
    parts = width // PROJECT_CHUNK
    return pl.pallas_call(
        project_kernel,
        out_shape=(
            pltpu.HBM((count, 3 * each, pairs // count, 2, HD), jnp.bfloat16),
            pltpu.HBM((2 * pairs, columns), jnp.float32),
        ),
        in_specs=[HBM, HBM],
        out_specs=(HBM, HBM),
        scratch_shapes=[
            pltpu.VMEM(x.shape, jnp.bfloat16),
            pltpu.VMEM((parts, 3, columns, PROJECT_CHUNK), jnp.bfloat16),
            pltpu.VMEM((3, columns, 2 * pairs), jnp.float32),
            pltpu.VMEM((2 * each, pairs, 2, HD), jnp.bfloat16),
            pltpu.VMEM((2 * pairs, columns), jnp.float32),
            pltpu.SemaphoreType.DMA,
            pltpu.SemaphoreType.DMA((parts,)),
            pltpu.SemaphoreType.DMA((count,)),
            pltpu.SemaphoreType.DMA,
        ],
        compiler_params=pltpu.CompilerParams(vmem_limit_bytes=24 * 2**20),
        cost_estimate=pl.CostEstimate(flops=10**9, bytes_accessed=11 * 10**6, transcendentals=0),
        name="project",
    )(in_hbm(x), in_hbm(weight))


UPDATE_PARTS = 4


def update_kernel(stored_ref, low_ref, base_ref, up_ref, send_in, send_ref, base, up, buf, base_sem, up_sem, sem):
    count, half, packed = low_ref.shape
    rank = packed // 2
    rows = 2 * half
    height = up_ref.shape[0] // UPDATE_PARTS
    fetches = start_all(
        [
            pltpu.make_async_copy(up_ref.at[p * height : (p + 1) * height], up.at[p], up_sem.at[p])
            for p in range(UPDATE_PARTS)
        ]
    )
    fetch_base = pltpu.make_async_copy(base_ref, base, base_sem)
    fetch_base.start()
    low = low_ref[0].astype(jnp.float32)
    for s in range(1, count):
        low = low + low_ref[s].astype(jnp.float32)
    low = jnp.concatenate([low[:, :rank], low[:, rank:]], axis=0)
    batch = 256 // rank
    spread = jnp.concatenate([low] * batch, axis=1)
    which = lax.broadcasted_iota(jnp.int32, (rows, batch * rank), 1) // rank
    ahead = stored_ref[...] - which
    total = jnp.zeros(base.shape, jnp.float32)
    for p in range(UPDATE_PARTS):
        fetches[p].wait()
        for a in range(0, height // rank, batch):
            wide = jnp.where(ahead == p * (height // rank) + a, spread, 0.0).astype(jnp.bfloat16)
            total = total + jnp.dot(
                wide, up[p, a * rank : (a + batch) * rank], preferred_element_type=jnp.float32
            )
    fetch_base.wait()
    put_chunks(buf.reshape(buf.shape[0], rows, HD), 0, base[...] + adapter_scale * total)
    wait_all(send_blocks(buf, send_ref, send_ref.shape[1] - buf.shape[0], sem))


def update_values(stored, lows, base, up, send):
    count, chunks = send.shape[:2]
    rows, columns = base.shape
    height = up.shape[0] // UPDATE_PARTS
    return pl.pallas_call(
        update_kernel,
        out_shape=pltpu.HBM(send.shape, send.dtype),
        in_specs=[VMEM, VMEM, HBM, HBM, HBM],
        out_specs=HBM,
        scratch_shapes=[
            pltpu.VMEM(base.shape, jnp.float32),
            pltpu.VMEM((UPDATE_PARTS, height, columns), jnp.bfloat16),
            pltpu.VMEM((chunks // 3, rows // 2, 2, HD), jnp.bfloat16),
            pltpu.SemaphoreType.DMA,
            pltpu.SemaphoreType.DMA((UPDATE_PARTS,)),
            pltpu.SemaphoreType.DMA((count,)),
        ],
        input_output_aliases={4: 0},
        compiler_params=pltpu.CompilerParams(vmem_limit_bytes=16 * 2**20),
        cost_estimate=pl.CostEstimate(flops=3 * 10**8, bytes_accessed=4 * 10**6, transcendentals=0),
        name="update_values",
    )(stored, lows, in_hbm(base), in_hbm(up), in_hbm(send))


def attend_kernel(halves, cos_ref, sin_ref, live_ref, pieces_ref, *refs):
    key_refs, value_refs = refs[:halves], refs[halves : 2 * halves]
    out_ref, keys_buf, values_buf, kn_ref, vn_ref, sem = refs[2 * halves :]
    count, _, steps = pieces_ref.shape[:3]
    rows = 2 * steps
    each = pieces_ref.shape[1] // 3
    heads = 2 * out_ref.shape[1] // count
    lanes = heads * HD
    group = rows * HEAD_BLOCK
    chips = count // 2
    fetches = []
    for chip in range(chips):
        half, at = divmod(chip, chips // halves)
        span = slice(at * heads, (at + 1) * heads)
        fetches.append(
            start_all(
                [
                    pltpu.make_async_copy(key_refs[half].at[span], keys_buf.at[chip], sem.at[0, chip]),
                    pltpu.make_async_copy(value_refs[half].at[span], values_buf.at[chip], sem.at[1, chip]),
                ]
            )
        )
    cosine = cos_ref[...][:rows]
    sine = sin_ref[...][:rows]
    left = lax.broadcasted_iota(jnp.int32, (rows, HD), 1) < HD // 2

    def chip_columns(chip, at):
        low = [pieces_ref[2 * chip, at + c].reshape(rows, HD).astype(jnp.float32) for c in range(each)]
        high = [pieces_ref[2 * chip + 1, at + c].reshape(rows, HD).astype(jnp.float32) for c in range(each)]
        high = [pltpu.roll(x, HD // 2, 1) for x in high]
        whole = low[:-1] + [jnp.where(left, low[-1], high[0])]
        return whole + [jnp.where(left, a, b) for a, b in zip(high[:-1], high[1:])]

    def rotated(parts):
        return [x * cosine + pltpu.roll(x, HD // 2, 1) * sine for x in parts]

    row_head = lax.broadcasted_iota(jnp.int32, (group, lanes), 0) % HEAD_BLOCK
    lane_head = lax.broadcasted_iota(jnp.int32, (group, lanes), 1) // HD
    own_head = row_head == lane_head
    row_j = lax.broadcasted_iota(jnp.int32, (group, 16), 0) // HEAD_BLOCK
    new_j = lax.broadcasted_iota(jnp.int32, (group, 16), 1)
    new_live = (new_j < rows) & (new_j % 2 == row_j % 2) & (new_j // 2 <= row_j // 2)
    live = jnp.concatenate(
        [
            jnp.broadcast_to(live_ref[j % 2 : j % 2 + 1, :], (HEAD_BLOCK, live_ref.shape[1]))
            for j in range(rows)
        ],
        axis=0,
    )
    live = live > 0
    kn_ref[...] = jnp.zeros_like(kn_ref)
    vn_ref[...] = jnp.zeros_like(vn_ref)
    for chip in range(chips):
        query = jnp.concatenate(rotated(chip_columns(chip, 0)), axis=1)
        kn_ref[0:rows] = jnp.concatenate(rotated(chip_columns(chip, each)), axis=1)
        vn_ref[0:rows] = jnp.concatenate(chip_columns(chip, 2 * each), axis=1)
        kn = kn_ref[...].astype(jnp.bfloat16)
        vn = vn_ref[...].astype(jnp.bfloat16)
        spread = jnp.concatenate(
            [jnp.broadcast_to(query[j : j + 1], (HEAD_BLOCK, lanes)) for j in range(rows)], axis=0
        )
        spread = jnp.where(own_head, spread, 0.0).astype(jnp.bfloat16)
        wait_all(fetches[chip])
        keys = lanes_of(keys_buf[chip])
        values = lanes_of(values_buf[chip])
        scores = lax.dot_general(spread, keys, CONTRACT_LANES, preferred_element_type=jnp.float32) * (HD**-0.5)
        scores = jnp.where(live, scores, masked_score)
        fresh = lax.dot_general(spread, kn, CONTRACT_LANES, preferred_element_type=jnp.float32) * (HD**-0.5)
        fresh = jnp.where(new_live, fresh, masked_score)
        top = jnp.maximum(jnp.max(scores, axis=1, keepdims=True), jnp.max(fresh, axis=1, keepdims=True))
        weights = jnp.where(live, jnp.exp(scores - top), 0.0)
        fresh = jnp.where(new_live, jnp.exp(fresh - top), 0.0)
        totals = jnp.sum(weights, axis=1, keepdims=True) + jnp.sum(fresh, axis=1, keepdims=True)
        mixed = jnp.dot(weights.astype(jnp.bfloat16), values, preferred_element_type=jnp.float32)
        mixed = mixed + jnp.dot(fresh.astype(jnp.bfloat16), vn, preferred_element_type=jnp.float32)
        mixed = jnp.where(own_head, mixed / totals, 0.0)
        out = jnp.sum(mixed.reshape(rows, HEAD_BLOCK, lanes), axis=1).astype(out_ref.dtype)
        for t in range(steps):
            for h in range(heads):
                out_ref[t, chip * heads + h] = out[2 * t : 2 * t + 2, h * HD : (h + 1) * HD]


def attend(cosine, sine, live, pieces, keys, values):
    count, _, steps = pieces.shape[:3]
    halves = len(keys)
    heads = halves * keys[0].shape[0]
    tokens = keys[0].shape[1]
    per = 2 * heads // count
    return pl.pallas_call(
        functools.partial(attend_kernel, halves),
        out_shape=jax.ShapeDtypeStruct((steps, heads, 2, HD), jnp.bfloat16),
        in_specs=[VMEM] * 4 + [HBM] * (2 * halves),
        out_specs=VMEM,
        scratch_shapes=[pltpu.VMEM((count // 2, per, tokens, HD), jnp.bfloat16)] * 2
        + [pltpu.VMEM((16, per * HD), jnp.float32)] * 2
        + [pltpu.SemaphoreType.DMA((2, count // 2))],
        compiler_params=pltpu.CompilerParams(vmem_limit_bytes=16 * 2**20),
        cost_estimate=pl.CostEstimate(flops=10**9, bytes_accessed=6 * 10**6, transcendentals=0),
        name="attention",
    )(cosine, sine, live, pieces, *[in_hbm(x) for x in keys], *[in_hbm(x) for x in values])


def chip_plan(
    count,
    hidden,
    query_key_value_weight,
    adapter_down_maps,
    adapter_up_maps,
    adapter_storage_row,
    request_adapter,
    lengths,
    request_page_table,
    key_value_pool,
):
    me = lax.axis_index("replica")
    steps, req_dev, width = hidden.shape
    heads = width // HD
    holder_count, rank, _ = adapter_down_maps.shape
    pool_pages, page_len = key_value_pool.shape[:2]
    adapter_count = adapter_storage_row.shape[0]

    tokens = pool_pages * page_len
    pool = in_hbm(key_value_pool.reshape(tokens, 2, heads, HD).transpose(0, 2, 1, 3))
    first_half = cache_by_head(pool, 0, heads // 2)
    second_half = cache_by_head(pool, heads // 2, heads // 2)

    held = {0: hidden}
    held.update({m: trade(hidden, m, count) for m in range(4, count, 4)})
    held, first_half = lax.optimization_barrier((held, first_half))
    for mask in (2, 1):
        held.update({k ^ mask: trade(v, mask, count) for k, v in list(held.items())})
    blocks = [
        held[k].reshape(steps, req_dev, heads, HD).transpose(0, 2, 1, 3) for k in range(count)
    ]
    blocks[0] = in_hbm(blocks[0])

    stored = jnp.sum(
        jnp.where(
            request_adapter[:, None] == jnp.arange(adapter_count, dtype=jnp.int32)[None, :],
            adapter_storage_row[None, :],
            0,
        ),
        axis=1,
    )
    stored = jnp.broadcast_to(stored.reshape(count, 1, req_dev), (count, steps, req_dev)).reshape(-1)

    x, lows = low_of(
        me.astype(jnp.int32).reshape(1), blocks, (stored - me * holder_count)[None, :], adapter_down_maps
    )
    lows = lax.all_to_all(lows, "replica", split_axis=0, concat_axis=0, tiled=True)
    send, base = project(x, query_key_value_weight.transpose(0, 2, 1), count)
    send = update_values(stored[:, None], lows, base, adapter_up_maps.reshape(adapter_count * rank, -1), send)
    pieces = lax.all_to_all(send, "replica", split_axis=0, concat_axis=0, tiled=True)

    my_lengths = lax.dynamic_slice_in_dim(lengths, me * req_dev, req_dev)
    cosine, sine = rotation(my_lengths, steps)
    live = live_tokens(my_lengths, request_page_table, pool_pages, page_len).astype(jnp.int32)
    keys, values = zip(first_half, second_half)
    out = attend(cosine, sine, live.reshape(req_dev, tokens), pieces, keys, values)
    return out.transpose(0, 2, 1, 3).reshape(steps, req_dev, width)


def per_device(replicas, *arrays):
    columns = arrays[1].shape[2]
    whole_heads = replicas % 4 == 0 and (2 * columns) % HD == 0 and columns % HD == HD // 2
    plan = chip_plan if whole_heads and arrays[0].shape[1] == 2 else general_plan
    return plan(replicas, *arrays)


def solution(mesh):
    placed = (
        P(None, ("groups", "replica"), None),
        P(None, None, "replica"),
        P("replica", None, None),
        P(None, None, "replica"),
        P(),
        P("groups"),
        P("groups"),
        P(("groups", "replica"), None),
        P(("groups", "replica"), None, None, None),
    )
    return jax.shard_map(
        functools.partial(per_device, mesh.shape["replica"]),
        mesh=mesh,
        in_specs=placed,
        out_specs=P(None, ("groups", "replica"), None),
        check_vma=False,
    )
```

```python
import functools

import jax
import jax.numpy as jnp
from jax import lax
from jax.experimental import pallas as pl
from jax.experimental.pallas import tpu as pltpu
from jax.sharding import PartitionSpec as P

HD = 128
ROWS = 8
HEAD_BLOCK = 8

adapter_scale = 2.0
masked_score = -1e30


def attention_kernel(steps, req_dev, q_ref, k_ref, v_ref, cos_ref, sin_ref, live_ref, kv_ref, out_ref, kn_ref, vn_ref):
    rows = steps * req_dev
    width = q_ref.shape[1]
    lanes = HEAD_BLOCK * HD
    group = rows * HEAD_BLOCK
    cosine = cos_ref[...]
    sine = sin_ref[...]

    def rotated(x):
        pieces = []
        for h in range(HEAD_BLOCK):
            head = x[:, h * HD : (h + 1) * HD]
            pieces.append(head * cosine + pltpu.roll(head, HD // 2, 1) * sine)
        return jnp.concatenate(pieces, axis=1)

    row_head = lax.broadcasted_iota(jnp.int32, (group, lanes), 0) % HEAD_BLOCK
    lane_head = lax.broadcasted_iota(jnp.int32, (group, lanes), 1) // HD
    own_head = row_head == lane_head
    row_j = lax.broadcasted_iota(jnp.int32, (group, 16), 0) // HEAD_BLOCK
    new_j = lax.broadcasted_iota(jnp.int32, (group, 16), 1)
    new_live = (new_j < rows) & (new_j % req_dev == row_j % req_dev) & (new_j // req_dev <= row_j // req_dev)
    live_all = live_ref[...]
    live = jnp.concatenate(
        [
            jnp.broadcast_to(live_all[j % req_dev : j % req_dev + 1], (HEAD_BLOCK, live_all.shape[1]))
            for j in range(rows)
        ],
        axis=0,
    )
    live = live > 0
    kn_ref[...] = jnp.zeros_like(kn_ref)
    vn_ref[...] = jnp.zeros_like(vn_ref)
    contract_lanes = (((1,), (1,)), ((), ()))
    for c in range(width // lanes):
        cols = slice(c * lanes, (c + 1) * lanes)
        query = rotated(q_ref[:, cols].astype(jnp.float32))
        key_new = rotated(k_ref[:, cols].astype(jnp.float32))
        kn_ref[0:8] = key_new
        vn_ref[0:8] = v_ref[:, cols].astype(jnp.float32)
        kn = kn_ref[...].astype(jnp.bfloat16)
        vn = vn_ref[...].astype(jnp.bfloat16)
        spread = jnp.concatenate(
            [jnp.broadcast_to(query[j : j + 1], (HEAD_BLOCK, lanes)) for j in range(rows)], axis=0
        )
        spread = jnp.where(own_head, spread, 0.0).astype(jnp.bfloat16)
        kv = kv_ref[:, cols]
        scores = lax.dot_general(spread, kv, contract_lanes, preferred_element_type=jnp.float32) * (HD**-0.5)
        scores = jnp.where(live, scores, masked_score)
        fresh = lax.dot_general(spread, kn, contract_lanes, preferred_element_type=jnp.float32) * (HD**-0.5)
        fresh = jnp.where(new_live, fresh, masked_score)
        top = jnp.maximum(jnp.max(scores, axis=1, keepdims=True), jnp.max(fresh, axis=1, keepdims=True))
        weights = jnp.where(live, jnp.exp(scores - top), 0.0)
        fresh = jnp.where(new_live, jnp.exp(fresh - top), 0.0)
        totals = jnp.sum(weights, axis=1, keepdims=True) + jnp.sum(fresh, axis=1, keepdims=True)
        weights = pltpu.roll(weights, 1, 1).astype(jnp.bfloat16)
        mixed = jnp.dot(weights, kv, preferred_element_type=jnp.float32)
        mixed = mixed + jnp.dot(fresh.astype(jnp.bfloat16), vn, preferred_element_type=jnp.float32)
        mixed = jnp.where(own_head, mixed / totals, 0.0)
        out = jnp.sum(mixed.reshape(rows, HEAD_BLOCK, lanes), axis=1)
        out_ref[:, cols] = out.astype(out_ref.dtype)


def attention(steps, req_dev, q, k, v, cosine, sine, live, kv):
    rows = steps * req_dev
    width = q.shape[1]
    vmem = pl.BlockSpec(memory_space=pltpu.VMEM)
    return pl.pallas_call(
        functools.partial(attention_kernel, steps, req_dev),
        out_shape=jax.ShapeDtypeStruct((rows, width), jnp.bfloat16),
        in_specs=[vmem] * 7,
        out_specs=vmem,
        scratch_shapes=[pltpu.VMEM((16, HEAD_BLOCK * HD), jnp.float32)] * 2,
        compiler_params=pltpu.CompilerParams(vmem_limit_bytes=32 * 2**20),
        cost_estimate=pl.CostEstimate(flops=10**9, bytes_accessed=6 * 10**6, transcendentals=0),
        name="attention",
    )(q, k, v, cosine, sine, live, kv)


def rotation(my_lengths, steps):
    rows = steps * my_lengths.shape[0]
    positions = (my_lengths[None, :] + jnp.arange(steps, dtype=jnp.int32)[:, None]).reshape(rows)
    positions = jnp.pad(positions, (0, ROWS - rows))
    half = HD // 2
    frequency = jnp.exp(jnp.arange(half, dtype=jnp.float32) * (-2.0 * jnp.log(10000.0) / HD))
    angles = positions.astype(jnp.float32)[:, None] * frequency[None, :]
    cosine = jnp.cos(angles)
    sine = jnp.sin(angles)
    cosine = jnp.concatenate([cosine, cosine], axis=1)
    sine = jnp.concatenate([-sine, sine], axis=1)
    return cosine, sine


def live_tokens(my_lengths, request_page_table, pool_pages, page_len):
    pages = jnp.arange(pool_pages, dtype=jnp.int32)
    max_pages = request_page_table.shape[1]
    place = jnp.max(
        jnp.where(
            request_page_table[:, :, None] == pages[None, None, :],
            jnp.arange(max_pages, dtype=jnp.int32)[None, :, None],
            -1,
        ),
        axis=1,
    )
    token = place[:, :, None] * page_len + jnp.arange(page_len, dtype=jnp.int32)[None, None, :]
    return (place[:, :, None] >= 0) & (token < my_lengths[:, None, None])


def live_rows(my_lengths, request_page_table, pool_pages, page_len):
    alive = live_tokens(my_lengths, request_page_table, pool_pages, page_len)
    live = jnp.stack([alive, jnp.zeros_like(alive)], axis=-1).astype(jnp.int32)
    return live.reshape(request_page_table.shape[0], pool_pages * page_len * 2)


def general_plan(
    replicas,
    hidden,
    query_key_value_weight,
    adapter_down_maps,
    adapter_up_maps,
    adapter_storage_row,
    request_adapter,
    lengths,
    request_page_table,
    key_value_pool,
):
    my_index = lax.axis_index("replica")
    steps, req_dev, width = hidden.shape
    rows = steps * req_dev
    columns = query_key_value_weight.shape[2]
    holder_count, rank, _ = adapter_down_maps.shape
    pool_pages, page_len = key_value_pool.shape[:2]
    adapter_count = adapter_storage_row.shape[0]
    chips = replicas // 2
    total = replicas * ROWS

    block = jnp.pad(hidden.reshape(rows, width), ((0, ROWS - rows), (0, 0)))
    same_core = [[2 * chip + core for chip in range(chips)] for core in range(2)]
    mine = lax.all_to_all(
        jnp.broadcast_to(block[None], (chips, ROWS, width)),
        "replica",
        split_axis=0,
        concat_axis=0,
        axis_index_groups=same_core,
        tiled=True,
    )
    other = lax.ppermute(mine, "replica", [(i, i ^ 1) for i in range(replicas)])
    first = my_index % 2 == 0
    gathered = jnp.stack([jnp.where(first, mine, other), jnp.where(first, other, mine)])
    gathered = gathered.reshape(total, width)

    stored_rows = jnp.sum(
        jnp.where(
            request_adapter[:, None] == jnp.arange(adapter_count, dtype=jnp.int32)[None, :],
            adapter_storage_row[None, :],
            0,
        ),
        axis=1,
    )
    by_block = stored_rows.reshape(chips, 2, 1, req_dev).transpose(1, 0, 2, 3)
    by_block = jnp.broadcast_to(by_block, (2, chips, steps, req_dev)).reshape(2, chips, rows)
    row_stored = jnp.pad(by_block, ((0, 0), (0, 0), (0, ROWS - rows)), constant_values=-1).reshape(total)

    down = jnp.einsum("nd,hfd->nhf", gathered, adapter_down_maps, preferred_element_type=jnp.float32)
    slots = my_index * holder_count + jnp.arange(holder_count, dtype=jnp.int32)
    own = row_stored[:, None] == slots[None, :]
    low = jnp.sum(jnp.where(own[:, :, None], down, 0.0), axis=1).astype(jnp.bfloat16)
    low = jnp.concatenate([low[: total // 2], low[total // 2 :]], axis=1)
    low = lax.all_to_all(
        jnp.broadcast_to(low[None], (replicas,) + low.shape), "replica", split_axis=0, concat_axis=0, tiled=True
    )
    low = jnp.sum(low.astype(jnp.float32), axis=0)
    low = jnp.concatenate([low[:, :rank], low[:, rank:]], axis=0)

    projected = jnp.einsum("nd,idc->nic", gathered, query_key_value_weight, preferred_element_type=jnp.float32)

    def update(first_adapter, maps):
        held = maps.shape[0]
        which = first_adapter + jnp.arange(held, dtype=jnp.int32)
        wide = jnp.where((row_stored[:, None] == which[None, :])[:, :, None], low[:, None, :], 0.0)
        return jnp.dot(
            wide.astype(jnp.bfloat16).reshape(total, held * rank),
            maps.reshape(held * rank, columns),
            preferred_element_type=jnp.float32,
        )

    step_adapters = 64
    if adapter_count <= step_adapters:
        updated = update(0, adapter_up_maps)
    else:
        updated = lax.fori_loop(
            0,
            adapter_count // step_adapters,
            lambda i, sofar: sofar
            + update(
                i * step_adapters,
                lax.dynamic_slice_in_dim(adapter_up_maps, i * step_adapters, step_adapters, 0),
            ),
            jnp.zeros((total, columns), jnp.float32),
        )
    value = projected[:, 2] + adapter_scale * updated
    combined = jnp.concatenate([projected[:, 0], projected[:, 1], value], axis=1).astype(jnp.bfloat16)
    combined = combined.reshape(2, chips, ROWS, 3 * columns).transpose(1, 0, 2, 3)
    combined = combined.reshape(replicas, ROWS, 3 * columns)
    arrived = lax.all_to_all(combined, "replica", split_axis=0, concat_axis=0, tiled=True)
    arrived = arrived.reshape(replicas, ROWS, 3, columns).transpose(2, 1, 0, 3).reshape(3, ROWS, width)

    my_lengths = lax.dynamic_slice_in_dim(lengths, my_index * req_dev, req_dev)
    cosine, sine = rotation(my_lengths, steps)
    live = live_rows(my_lengths, request_page_table, pool_pages, page_len)
    kv = key_value_pool.reshape(pool_pages * page_len * 2, width)
    out = attention(steps, req_dev, arrived[0], arrived[1], arrived[2], cosine, sine, live, kv)
    return out.reshape(steps, req_dev, width)


def trade(value, mask, count):
    return lax.ppermute(value, "replica", [(i, i ^ mask) for i in range(count)])


CONTRACT_LANES = (((1,), (1,)), ((), ()))
SPLIT_BUFFERS = 4
FETCH_AHEAD = 2


def in_hbm(x):
    return pltpu.with_memory_space_constraint(x, pltpu.HBM)


VMEM = pl.BlockSpec(memory_space=pltpu.VMEM)
HBM = pl.BlockSpec(memory_space=pltpu.HBM)
SMEM = pl.BlockSpec(memory_space=pltpu.SMEM)
ANY = pl.BlockSpec(memory_space=pl.ANY)


def start_all(copies):
    for copy in copies:
        copy.start()
    return copies


def wait_all(copies):
    for copy in copies:
        copy.wait()


def cache_kernel(first, extra, pool_ref, *refs):
    sources, refs = refs[:extra], refs[extra:]
    keys_ref, values_ref = refs[:2]
    places = refs[2 : 2 + extra]
    raw, wide, keys, values, sem, out_sem, place_sem = refs[2 + extra :]
    heads, tokens = raw.shape[:2]
    copies = start_all(
        [pltpu.make_async_copy(pool_ref.at[:, first + h], raw.at[h], sem.at[h]) for h in range(heads)]
    )
    brought = start_all(
        [pltpu.make_async_copy(a, b, place_sem.at[i]) for i, (a, b) in enumerate(zip(sources, places))]
    )
    rows = raw.reshape(heads, 2 * tokens, HD)
    sent = []
    for h in range(heads):
        copies[h].wait()
        both = wide.at[h % SPLIT_BUFFERS]
        both[...] = rows[h].astype(jnp.float32)
        keys[h] = both[pl.ds(0, tokens, stride=2), :].astype(jnp.bfloat16)
        values[h] = both[pl.ds(1, tokens, stride=2), :].astype(jnp.bfloat16)
        sent += start_all(
            [
                pltpu.make_async_copy(keys.at[h], keys_ref.at[h], out_sem.at[0, h]),
                pltpu.make_async_copy(values.at[h], values_ref.at[h], out_sem.at[1, h]),
            ]
        )
    wait_all(sent)
    wait_all(brought)


def cache_by_head(pool, first, heads, bring=()):
    tokens = pool.shape[0]
    part = pltpu.HBM((heads, tokens, HD), pool.dtype)
    return pl.pallas_call(
        functools.partial(cache_kernel, first, len(bring)),
        out_shape=(part, part) + tuple(pltpu.VMEM(x.shape, x.dtype) for x in bring),
        in_specs=[HBM] + [HBM] * len(bring),
        out_specs=(HBM, HBM) + (VMEM,) * len(bring),
        scratch_shapes=[
            pltpu.VMEM((heads, tokens, 2, HD), pool.dtype),
            pltpu.VMEM((SPLIT_BUFFERS, 2 * tokens, HD), jnp.float32),
            pltpu.VMEM((heads, tokens, HD), pool.dtype),
            pltpu.VMEM((heads, tokens, HD), pool.dtype),
            pltpu.SemaphoreType.DMA((heads,)),
            pltpu.SemaphoreType.DMA((2, heads)),
            pltpu.SemaphoreType.DMA((max(len(bring), 1),)),
        ],
        compiler_params=pltpu.CompilerParams(vmem_limit_bytes=(12 + 24 * bool(bring)) * 2**20),
        cost_estimate=pl.CostEstimate(flops=0, bytes_accessed=12 * 10**6, transcendentals=0),
        name="cache_by_head",
    )(in_hbm(pool), *[in_hbm(x) for x in bring])


def lanes_of(x):
    return jnp.concatenate([x[c] for c in range(x.shape[0])], axis=1)


def low_kernel(count, me_ref, slot_ref, down_ref, *refs):
    blocks, (x_ref, low_ref, maps, sem, own_sem) = refs[:count], refs[count:]
    me = me_ref[0]
    steps = blocks[0].shape[0]
    holders, rank, width = down_ref.shape
    fetch = pltpu.make_async_copy(down_ref, maps, own_sem)
    fetch.start()
    copies = []
    for k, block in enumerate(blocks):
        for t in range(steps):
            copies.append(
                pltpu.make_async_copy(block.at[t], x_ref.at[:, (me ^ k) * steps + t], sem.at[k * steps + t])
            )
    wait_all(start_all(copies))
    chunks, pairs = x_ref.shape[:2]
    rows = 2 * pairs
    x = lanes_of(x_ref.reshape(chunks, rows, HD))
    fetch.wait()
    made = lax.dot_general(
        maps.reshape(holders * rank, width)[...], x, CONTRACT_LANES, preferred_element_type=jnp.float32
    )
    slot = slot_ref[...]
    low = jnp.zeros((rank, rows), jnp.float32)
    for h in range(holders):
        low = low + jnp.where(slot == h, made[h * rank : (h + 1) * rank], 0.0)
    low = low.T
    low_ref[...] = jnp.concatenate([low[: rows // 2], low[rows // 2 :]], axis=1).astype(low_ref.dtype)


def low_of(me, blocks, slot, down):
    count = len(blocks)
    steps, chunks = blocks[0].shape[:2]
    rows = count * steps * 2
    rank = down.shape[1]
    return pl.pallas_call(
        functools.partial(low_kernel, count),
        out_shape=(
            jax.ShapeDtypeStruct((chunks, rows // 2, 2, HD), jnp.bfloat16),
            jax.ShapeDtypeStruct((rows // 2, 2 * rank), jnp.bfloat16),
        ),
        in_specs=[SMEM, VMEM, HBM] + [ANY] * count,
        out_specs=(VMEM, VMEM),
        scratch_shapes=[
            pltpu.VMEM(down.shape, jnp.bfloat16),
            pltpu.SemaphoreType.DMA((count * steps,)),
            pltpu.SemaphoreType.DMA,
        ],
        compiler_params=pltpu.CompilerParams(vmem_limit_bytes=8 * 2**20),
        cost_estimate=pl.CostEstimate(flops=10**6, bytes_accessed=10**5, transcendentals=0),
        name="low_rows",
    )(me, slot, in_hbm(down), *blocks)


def put_chunks(buf, first, value):
    wide = value.shape[1]
    for c in range(-(-wide // HD)):
        part = value[:, c * HD : min((c + 1) * HD, wide)]
        if part.shape[1] < HD:
            part = jnp.concatenate([part, jnp.zeros((part.shape[0], HD - part.shape[1]), part.dtype)], axis=1)
        buf[first + c] = part.astype(buf.dtype)


def send_blocks(buf, out_ref, first, sem):
    count, _, steps = out_ref.shape[:3]
    chunks = buf.shape[0]
    return start_all(
        [
            pltpu.make_async_copy(
                buf.at[:, k * steps : (k + 1) * steps], out_ref.at[k, first : first + chunks], sem.at[k]
            )
            for k in range(count)
        ]
    )


def rows_of(x_ref):
    chunks, pairs = x_ref.shape[:2]
    return lanes_of(x_ref.reshape(chunks, 2 * pairs, HD))


def query_key_kernel(x_ref, w_ref, up_ref, send_ref, up_out, buf, sem, up_sem):
    bring = pltpu.make_async_copy(up_ref, up_out, up_sem)
    bring.start()
    x = rows_of(x_ref)
    each = buf.shape[0] // 2
    flat = buf.reshape(buf.shape[0], x.shape[0], HD)
    for i in range(2):
        put_chunks(
            flat, i * each, lax.dot_general(w_ref[i], x, CONTRACT_LANES, preferred_element_type=jnp.float32).T
        )
    wait_all(send_blocks(buf, send_ref, 0, sem))
    bring.wait()


def project_query_key(x, weight, up, count):
    pairs = x.shape[1]
    each = -(-weight.shape[1] // HD)
    return pl.pallas_call(
        query_key_kernel,
        out_shape=(
            pltpu.HBM((count, 3 * each, pairs // count, 2, HD), jnp.bfloat16),
            pltpu.VMEM(up.shape, up.dtype),
        ),
        in_specs=[VMEM, VMEM, HBM],
        out_specs=(HBM, VMEM),
        scratch_shapes=[
            pltpu.VMEM((2 * each, pairs, 2, HD), jnp.bfloat16),
            pltpu.SemaphoreType.DMA((count,)),
            pltpu.SemaphoreType.DMA,
        ],
        compiler_params=pltpu.CompilerParams(vmem_limit_bytes=24 * 2**20),
        cost_estimate=pl.CostEstimate(flops=10**9, bytes_accessed=8 * 10**6, transcendentals=0),
        name="project_query_key",
    )(x, weight, in_hbm(up))


def value_kernel(x_ref, w_ref, base_ref):
    base_ref[...] = lax.dot_general(
        w_ref[2], rows_of(x_ref), CONTRACT_LANES, preferred_element_type=jnp.float32
    ).T


def project_value(x, weight):
    return pl.pallas_call(
        value_kernel,
        out_shape=jax.ShapeDtypeStruct((2 * x.shape[1], weight.shape[1]), jnp.float32),
        in_specs=[VMEM, VMEM],
        out_specs=VMEM,
        compiler_params=pltpu.CompilerParams(vmem_limit_bytes=16 * 2**20),
        cost_estimate=pl.CostEstimate(flops=5 * 10**8, bytes_accessed=4 * 10**6, transcendentals=0),
        name="project_value",
    )(x, weight)


def update_kernel(stored_ref, base_ref, up_ref, send_in, *refs):
    lows, (send_ref, buf, sem) = refs[:-3], refs[-3:]
    rank = lows[0].shape[1] // 2
    rows = 2 * lows[0].shape[0]
    low = lows[0][...].astype(jnp.float32)
    for more in lows[1:]:
        low = low + more[...].astype(jnp.float32)
    low = jnp.concatenate([low[:, :rank], low[:, rank:]], axis=0)
    batch = 256 // rank
    spread = jnp.concatenate([low] * batch, axis=1)
    which = lax.broadcasted_iota(jnp.int32, (rows, batch * rank), 1) // rank
    ahead = stored_ref[...] - which
    total = jnp.zeros(base_ref.shape, jnp.float32)
    for a in range(0, up_ref.shape[0] // rank, batch):
        wide = jnp.where(ahead == a, spread, 0.0).astype(jnp.bfloat16)
        total = total + jnp.dot(wide, up_ref[a * rank : (a + batch) * rank], preferred_element_type=jnp.float32)
    put_chunks(buf.reshape(buf.shape[0], rows, HD), 0, base_ref[...] + adapter_scale * total)
    wait_all(send_blocks(buf, send_ref, send_ref.shape[1] - buf.shape[0], sem))


def update_values(stored, base, up, send, lows):
    count, chunks = send.shape[:2]
    rows = base.shape[0]
    return pl.pallas_call(
        update_kernel,
        out_shape=pltpu.HBM(send.shape, send.dtype),
        in_specs=[VMEM, VMEM, VMEM, HBM] + [VMEM] * len(lows),
        out_specs=HBM,
        scratch_shapes=[
            pltpu.VMEM((chunks // 3, rows // 2, 2, HD), jnp.bfloat16),
            pltpu.SemaphoreType.DMA((count,)),
        ],
        input_output_aliases={3: 0},
        compiler_params=pltpu.CompilerParams(vmem_limit_bytes=8 * 2**20),
        cost_estimate=pl.CostEstimate(flops=3 * 10**8, bytes_accessed=4 * 10**6, transcendentals=0),
        name="update_values",
    )(stored, base, up, in_hbm(send), *lows)


def attend_kernel(halves, cos_ref, sin_ref, live_ref, pieces_ref, *refs):
    key_refs, value_refs = refs[:halves], refs[halves : 2 * halves]
    out_ref, keys_buf, values_buf, kn_ref, vn_ref, sem = refs[2 * halves :]
    count, _, steps = pieces_ref.shape[:3]
    rows = 2 * steps
    each = pieces_ref.shape[1] // 3
    heads = 2 * out_ref.shape[1] // count
    lanes = heads * HD
    group = rows * HEAD_BLOCK
    chips = count // 2
    fetches = []
    for chip in range(chips):
        half, at = divmod(chip, chips // halves)
        span = slice(at * heads, (at + 1) * heads)
        fetches.append(
            [
                pltpu.make_async_copy(key_refs[half].at[span], keys_buf.at[chip], sem.at[0, chip]),
                pltpu.make_async_copy(value_refs[half].at[span], values_buf.at[chip], sem.at[1, chip]),
            ]
        )
    for chip in range(FETCH_AHEAD):
        start_all(fetches[chip])
    cosine = cos_ref[...][:rows]
    sine = sin_ref[...][:rows]
    left = lax.broadcasted_iota(jnp.int32, (rows, HD), 1) < HD // 2

    def chip_columns(chip, at):
        low = [pieces_ref[2 * chip, at + c].reshape(rows, HD).astype(jnp.float32) for c in range(each)]
        high = [pieces_ref[2 * chip + 1, at + c].reshape(rows, HD).astype(jnp.float32) for c in range(each)]
        high = [pltpu.roll(x, HD // 2, 1) for x in high]
        whole = low[:-1] + [jnp.where(left, low[-1], high[0])]
        return whole + [jnp.where(left, a, b) for a, b in zip(high[:-1], high[1:])]

    def rotated(parts):
        return [x * cosine + pltpu.roll(x, HD // 2, 1) * sine for x in parts]

    row_head = lax.broadcasted_iota(jnp.int32, (group, lanes), 0) % HEAD_BLOCK
    lane_head = lax.broadcasted_iota(jnp.int32, (group, lanes), 1) // HD
    own_head = row_head == lane_head
    row_j = lax.broadcasted_iota(jnp.int32, (group, 16), 0) // HEAD_BLOCK
    new_j = lax.broadcasted_iota(jnp.int32, (group, 16), 1)
    new_live = (new_j < rows) & (new_j % 2 == row_j % 2) & (new_j // 2 <= row_j // 2)
    live = jnp.concatenate(
        [
            jnp.broadcast_to(live_ref[j % 2 : j % 2 + 1, :], (HEAD_BLOCK, live_ref.shape[1]))
            for j in range(rows)
        ],
        axis=0,
    )
    live = live > 0
    kn_ref[...] = jnp.zeros_like(kn_ref)
    vn_ref[...] = jnp.zeros_like(vn_ref)
    for chip in range(chips):
        query = jnp.concatenate(rotated(chip_columns(chip, 0)), axis=1)
        kn_ref[0:rows] = jnp.concatenate(rotated(chip_columns(chip, each)), axis=1)
        vn_ref[0:rows] = jnp.concatenate(chip_columns(chip, 2 * each), axis=1)
        kn = kn_ref[...].astype(jnp.bfloat16)
        vn = vn_ref[...].astype(jnp.bfloat16)
        spread = jnp.concatenate(
            [jnp.broadcast_to(query[j : j + 1], (HEAD_BLOCK, lanes)) for j in range(rows)], axis=0
        )
        spread = jnp.where(own_head, spread, 0.0).astype(jnp.bfloat16)
        wait_all(fetches[chip])
        if chip + FETCH_AHEAD < chips:
            start_all(fetches[chip + FETCH_AHEAD])
        keys = lanes_of(keys_buf[chip])
        values = lanes_of(values_buf[chip])
        scores = lax.dot_general(spread, keys, CONTRACT_LANES, preferred_element_type=jnp.float32) * (HD**-0.5)
        scores = jnp.where(live, scores, masked_score)
        fresh = lax.dot_general(spread, kn, CONTRACT_LANES, preferred_element_type=jnp.float32) * (HD**-0.5)
        fresh = jnp.where(new_live, fresh, masked_score)
        top = jnp.maximum(jnp.max(scores, axis=1, keepdims=True), jnp.max(fresh, axis=1, keepdims=True))
        weights = jnp.where(live, jnp.exp(scores - top), 0.0)
        fresh = jnp.where(new_live, jnp.exp(fresh - top), 0.0)
        totals = jnp.sum(weights, axis=1, keepdims=True) + jnp.sum(fresh, axis=1, keepdims=True)
        mixed = jnp.dot(weights.astype(jnp.bfloat16), values, preferred_element_type=jnp.float32)
        mixed = mixed + jnp.dot(fresh.astype(jnp.bfloat16), vn, preferred_element_type=jnp.float32)
        mixed = jnp.where(own_head, mixed / totals, 0.0)
        out = jnp.sum(mixed.reshape(rows, HEAD_BLOCK, lanes), axis=1).astype(out_ref.dtype)
        for t in range(steps):
            for h in range(heads):
                out_ref[t, chip * heads + h] = out[2 * t : 2 * t + 2, h * HD : (h + 1) * HD]


def attend(cosine, sine, live, pieces, keys, values):
    count, _, steps = pieces.shape[:3]
    halves = len(keys)
    heads = halves * keys[0].shape[0]
    tokens = keys[0].shape[1]
    per = 2 * heads // count
    return pl.pallas_call(
        functools.partial(attend_kernel, halves),
        out_shape=jax.ShapeDtypeStruct((steps, heads, 2, HD), jnp.bfloat16),
        in_specs=[VMEM] * 4 + [HBM] * (2 * halves),
        out_specs=VMEM,
        scratch_shapes=[pltpu.VMEM((count // 2, per, tokens, HD), jnp.bfloat16)] * 2
        + [pltpu.VMEM((16, per * HD), jnp.float32)] * 2
        + [pltpu.SemaphoreType.DMA((2, count // 2))],
        compiler_params=pltpu.CompilerParams(vmem_limit_bytes=16 * 2**20),
        cost_estimate=pl.CostEstimate(flops=10**9, bytes_accessed=6 * 10**6, transcendentals=0),
        name="attention",
    )(cosine, sine, live, pieces, *[in_hbm(x) for x in keys], *[in_hbm(x) for x in values])


def chip_plan(
    count,
    hidden,
    query_key_value_weight,
    adapter_down_maps,
    adapter_up_maps,
    adapter_storage_row,
    request_adapter,
    lengths,
    request_page_table,
    key_value_pool,
):
    me = lax.axis_index("replica")
    steps, req_dev, width = hidden.shape
    heads = width // HD
    holder_count, rank, _ = adapter_down_maps.shape
    pool_pages, page_len = key_value_pool.shape[:2]
    adapter_count = adapter_storage_row.shape[0]

    tokens = pool_pages * page_len
    pool = key_value_pool.reshape(tokens, 2, heads, HD).transpose(0, 2, 1, 3)
    weight = query_key_value_weight.transpose(0, 2, 1)
    *first_half, weight = cache_by_head(pool, 0, heads // 2, [weight])
    second_half = cache_by_head(pool, heads // 2, heads // 2)

    held = {0: hidden}
    held.update({m: trade(hidden, m, count) for m in range(count - 4, 0, -4)})
    held[4], first_half, weight = lax.optimization_barrier((held[4], first_half, weight))
    for mask in (2, 1):
        held.update({k ^ mask: trade(v, mask, count) for k, v in list(held.items())})
    blocks = [
        held[k].reshape(steps, req_dev, heads, HD).transpose(0, 2, 1, 3) for k in range(count)
    ]
    blocks[0] = in_hbm(blocks[0])

    stored = jnp.sum(
        jnp.where(
            request_adapter[:, None] == jnp.arange(adapter_count, dtype=jnp.int32)[None, :],
            adapter_storage_row[None, :],
            0,
        ),
        axis=1,
    )
    stored = jnp.broadcast_to(stored.reshape(count, 1, req_dev), (count, steps, req_dev)).reshape(-1)

    x, low = low_of(
        me.astype(jnp.int32).reshape(1), blocks, (stored - me * holder_count)[None, :], adapter_down_maps
    )
    arrived = trade(low, 1, count)
    send, up = project_query_key(x, weight, adapter_up_maps.reshape(adapter_count * rank, -1), count)
    arrived, send = lax.optimization_barrier((arrived, send))
    low = low + arrived
    arrived = trade(low, 2, count)
    base = project_value(x, weight)
    arrived, base = lax.optimization_barrier((arrived, base))
    low = low + arrived
    lows = [low] + [trade(low, m, count) for m in range(4, count, 4)]
    send = update_values(stored[:, None], base, up, send, lows)
    pieces = lax.all_to_all(send, "replica", split_axis=0, concat_axis=0, tiled=True)

    my_lengths = lax.dynamic_slice_in_dim(lengths, me * req_dev, req_dev)
    cosine, sine = rotation(my_lengths, steps)
    live = live_tokens(my_lengths, request_page_table, pool_pages, page_len).astype(jnp.int32)
    keys, values = zip(first_half, second_half)
    out = attend(cosine, sine, live.reshape(req_dev, tokens), pieces, keys, values)
    return out.transpose(0, 2, 1, 3).reshape(steps, req_dev, width)


def per_device(replicas, *arrays):
    columns = arrays[1].shape[2]
    whole_heads = replicas % 4 == 0 and (2 * columns) % HD == 0 and columns % HD == HD // 2
    plan = chip_plan if whole_heads and arrays[0].shape[1] == 2 else general_plan
    return plan(replicas, *arrays)


def solution(mesh):
    placed = (
        P(None, ("groups", "replica"), None),
        P(None, None, "replica"),
        P("replica", None, None),
        P(None, None, "replica"),
        P(),
        P("groups"),
        P("groups"),
        P(("groups", "replica"), None),
        P(("groups", "replica"), None, None, None),
    )
    return jax.shard_map(
        functools.partial(per_device, mesh.shape["replica"]),
        mesh=mesh,
        in_specs=placed,
        out_specs=P(None, ("groups", "replica"), None),
        check_vma=False,
    )
```

```python
import functools

import jax
import jax.numpy as jnp
from jax import lax
from jax.experimental import pallas as pl
from jax.experimental.pallas import tpu as pltpu
from jax.sharding import PartitionSpec as P

HD = 128
ROWS = 8
HEAD_BLOCK = 8

adapter_scale = 2.0
masked_score = -1e30


def attention_kernel(steps, req_dev, q_ref, k_ref, v_ref, cos_ref, sin_ref, live_ref, kv_ref, out_ref, kn_ref, vn_ref):
    rows = steps * req_dev
    width = q_ref.shape[1]
    lanes = HEAD_BLOCK * HD
    group = rows * HEAD_BLOCK
    cosine = cos_ref[...]
    sine = sin_ref[...]

    def rotated(x):
        pieces = []
        for h in range(HEAD_BLOCK):
            head = x[:, h * HD : (h + 1) * HD]
            pieces.append(head * cosine + pltpu.roll(head, HD // 2, 1) * sine)
        return jnp.concatenate(pieces, axis=1)

    row_head = lax.broadcasted_iota(jnp.int32, (group, lanes), 0) % HEAD_BLOCK
    lane_head = lax.broadcasted_iota(jnp.int32, (group, lanes), 1) // HD
    own_head = row_head == lane_head
    row_j = lax.broadcasted_iota(jnp.int32, (group, 16), 0) // HEAD_BLOCK
    new_j = lax.broadcasted_iota(jnp.int32, (group, 16), 1)
    new_live = (new_j < rows) & (new_j % req_dev == row_j % req_dev) & (new_j // req_dev <= row_j // req_dev)
    live_all = live_ref[...]
    live = jnp.concatenate(
        [
            jnp.broadcast_to(live_all[j % req_dev : j % req_dev + 1], (HEAD_BLOCK, live_all.shape[1]))
            for j in range(rows)
        ],
        axis=0,
    )
    live = live > 0
    kn_ref[...] = jnp.zeros_like(kn_ref)
    vn_ref[...] = jnp.zeros_like(vn_ref)
    contract_lanes = (((1,), (1,)), ((), ()))
    for c in range(width // lanes):
        cols = slice(c * lanes, (c + 1) * lanes)
        query = rotated(q_ref[:, cols].astype(jnp.float32))
        key_new = rotated(k_ref[:, cols].astype(jnp.float32))
        kn_ref[0:8] = key_new
        vn_ref[0:8] = v_ref[:, cols].astype(jnp.float32)
        kn = kn_ref[...].astype(jnp.bfloat16)
        vn = vn_ref[...].astype(jnp.bfloat16)
        spread = jnp.concatenate(
            [jnp.broadcast_to(query[j : j + 1], (HEAD_BLOCK, lanes)) for j in range(rows)], axis=0
        )
        spread = jnp.where(own_head, spread, 0.0).astype(jnp.bfloat16)
        kv = kv_ref[:, cols]
        scores = lax.dot_general(spread, kv, contract_lanes, preferred_element_type=jnp.float32) * (HD**-0.5)
        scores = jnp.where(live, scores, masked_score)
        fresh = lax.dot_general(spread, kn, contract_lanes, preferred_element_type=jnp.float32) * (HD**-0.5)
        fresh = jnp.where(new_live, fresh, masked_score)
        top = jnp.maximum(jnp.max(scores, axis=1, keepdims=True), jnp.max(fresh, axis=1, keepdims=True))
        weights = jnp.where(live, jnp.exp(scores - top), 0.0)
        fresh = jnp.where(new_live, jnp.exp(fresh - top), 0.0)
        totals = jnp.sum(weights, axis=1, keepdims=True) + jnp.sum(fresh, axis=1, keepdims=True)
        weights = pltpu.roll(weights, 1, 1).astype(jnp.bfloat16)
        mixed = jnp.dot(weights, kv, preferred_element_type=jnp.float32)
        mixed = mixed + jnp.dot(fresh.astype(jnp.bfloat16), vn, preferred_element_type=jnp.float32)
        mixed = jnp.where(own_head, mixed / totals, 0.0)
        out = jnp.sum(mixed.reshape(rows, HEAD_BLOCK, lanes), axis=1)
        out_ref[:, cols] = out.astype(out_ref.dtype)


def attention(steps, req_dev, q, k, v, cosine, sine, live, kv):
    rows = steps * req_dev
    width = q.shape[1]
    vmem = pl.BlockSpec(memory_space=pltpu.VMEM)
    return pl.pallas_call(
        functools.partial(attention_kernel, steps, req_dev),
        out_shape=jax.ShapeDtypeStruct((rows, width), jnp.bfloat16),
        in_specs=[vmem] * 7,
        out_specs=vmem,
        scratch_shapes=[pltpu.VMEM((16, HEAD_BLOCK * HD), jnp.float32)] * 2,
        compiler_params=pltpu.CompilerParams(vmem_limit_bytes=32 * 2**20),
        cost_estimate=pl.CostEstimate(flops=10**9, bytes_accessed=6 * 10**6, transcendentals=0),
        name="attention",
    )(q, k, v, cosine, sine, live, kv)


def rotation(my_lengths, steps):
    rows = steps * my_lengths.shape[0]
    positions = (my_lengths[None, :] + jnp.arange(steps, dtype=jnp.int32)[:, None]).reshape(rows)
    positions = jnp.pad(positions, (0, ROWS - rows))
    half = HD // 2
    frequency = jnp.exp(jnp.arange(half, dtype=jnp.float32) * (-2.0 * jnp.log(10000.0) / HD))
    angles = positions.astype(jnp.float32)[:, None] * frequency[None, :]
    cosine = jnp.cos(angles)
    sine = jnp.sin(angles)
    cosine = jnp.concatenate([cosine, cosine], axis=1)
    sine = jnp.concatenate([-sine, sine], axis=1)
    return cosine, sine


def live_tokens(my_lengths, request_page_table, pool_pages, page_len):
    pages = jnp.arange(pool_pages, dtype=jnp.int32)
    max_pages = request_page_table.shape[1]
    place = jnp.max(
        jnp.where(
            request_page_table[:, :, None] == pages[None, None, :],
            jnp.arange(max_pages, dtype=jnp.int32)[None, :, None],
            -1,
        ),
        axis=1,
    )
    token = place[:, :, None] * page_len + jnp.arange(page_len, dtype=jnp.int32)[None, None, :]
    return (place[:, :, None] >= 0) & (token < my_lengths[:, None, None])


def live_rows(my_lengths, request_page_table, pool_pages, page_len):
    alive = live_tokens(my_lengths, request_page_table, pool_pages, page_len)
    live = jnp.stack([alive, jnp.zeros_like(alive)], axis=-1).astype(jnp.int32)
    return live.reshape(request_page_table.shape[0], pool_pages * page_len * 2)


def general_plan(
    replicas,
    hidden,
    query_key_value_weight,
    adapter_down_maps,
    adapter_up_maps,
    adapter_storage_row,
    request_adapter,
    lengths,
    request_page_table,
    key_value_pool,
):
    my_index = lax.axis_index("replica")
    steps, req_dev, width = hidden.shape
    rows = steps * req_dev
    columns = query_key_value_weight.shape[2]
    holder_count, rank, _ = adapter_down_maps.shape
    pool_pages, page_len = key_value_pool.shape[:2]
    adapter_count = adapter_storage_row.shape[0]
    chips = replicas // 2
    total = replicas * ROWS

    block = jnp.pad(hidden.reshape(rows, width), ((0, ROWS - rows), (0, 0)))
    same_core = [[2 * chip + core for chip in range(chips)] for core in range(2)]
    mine = lax.all_to_all(
        jnp.broadcast_to(block[None], (chips, ROWS, width)),
        "replica",
        split_axis=0,
        concat_axis=0,
        axis_index_groups=same_core,
        tiled=True,
    )
    other = lax.ppermute(mine, "replica", [(i, i ^ 1) for i in range(replicas)])
    first = my_index % 2 == 0
    gathered = jnp.stack([jnp.where(first, mine, other), jnp.where(first, other, mine)])
    gathered = gathered.reshape(total, width)

    stored_rows = jnp.sum(
        jnp.where(
            request_adapter[:, None] == jnp.arange(adapter_count, dtype=jnp.int32)[None, :],
            adapter_storage_row[None, :],
            0,
        ),
        axis=1,
    )
    by_block = stored_rows.reshape(chips, 2, 1, req_dev).transpose(1, 0, 2, 3)
    by_block = jnp.broadcast_to(by_block, (2, chips, steps, req_dev)).reshape(2, chips, rows)
    row_stored = jnp.pad(by_block, ((0, 0), (0, 0), (0, ROWS - rows)), constant_values=-1).reshape(total)

    down = jnp.einsum("nd,hfd->nhf", gathered, adapter_down_maps, preferred_element_type=jnp.float32)
    slots = my_index * holder_count + jnp.arange(holder_count, dtype=jnp.int32)
    own = row_stored[:, None] == slots[None, :]
    low = jnp.sum(jnp.where(own[:, :, None], down, 0.0), axis=1).astype(jnp.bfloat16)
    low = jnp.concatenate([low[: total // 2], low[total // 2 :]], axis=1)
    low = lax.all_to_all(
        jnp.broadcast_to(low[None], (replicas,) + low.shape), "replica", split_axis=0, concat_axis=0, tiled=True
    )
    low = jnp.sum(low.astype(jnp.float32), axis=0)
    low = jnp.concatenate([low[:, :rank], low[:, rank:]], axis=0)

    projected = jnp.einsum("nd,idc->nic", gathered, query_key_value_weight, preferred_element_type=jnp.float32)

    def update(first_adapter, maps):
        held = maps.shape[0]
        which = first_adapter + jnp.arange(held, dtype=jnp.int32)
        wide = jnp.where((row_stored[:, None] == which[None, :])[:, :, None], low[:, None, :], 0.0)
        return jnp.dot(
            wide.astype(jnp.bfloat16).reshape(total, held * rank),
            maps.reshape(held * rank, columns),
            preferred_element_type=jnp.float32,
        )

    step_adapters = 64
    if adapter_count <= step_adapters:
        updated = update(0, adapter_up_maps)
    else:
        updated = lax.fori_loop(
            0,
            adapter_count // step_adapters,
            lambda i, sofar: sofar
            + update(
                i * step_adapters,
                lax.dynamic_slice_in_dim(adapter_up_maps, i * step_adapters, step_adapters, 0),
            ),
            jnp.zeros((total, columns), jnp.float32),
        )
    value = projected[:, 2] + adapter_scale * updated
    combined = jnp.concatenate([projected[:, 0], projected[:, 1], value], axis=1).astype(jnp.bfloat16)
    combined = combined.reshape(2, chips, ROWS, 3 * columns).transpose(1, 0, 2, 3)
    combined = combined.reshape(replicas, ROWS, 3 * columns)
    arrived = lax.all_to_all(combined, "replica", split_axis=0, concat_axis=0, tiled=True)
    arrived = arrived.reshape(replicas, ROWS, 3, columns).transpose(2, 1, 0, 3).reshape(3, ROWS, width)

    my_lengths = lax.dynamic_slice_in_dim(lengths, my_index * req_dev, req_dev)
    cosine, sine = rotation(my_lengths, steps)
    live = live_rows(my_lengths, request_page_table, pool_pages, page_len)
    kv = key_value_pool.reshape(pool_pages * page_len * 2, width)
    out = attention(steps, req_dev, arrived[0], arrived[1], arrived[2], cosine, sine, live, kv)
    return out.reshape(steps, req_dev, width)


def trade(value, mask, count):
    return lax.ppermute(value, "replica", [(i, i ^ mask) for i in range(count)])


CONTRACT_LANES = (((1,), (1,)), ((), ()))


def in_hbm(x):
    return pltpu.with_memory_space_constraint(x, pltpu.HBM)


VMEM = pl.BlockSpec(memory_space=pltpu.VMEM)
HBM = pl.BlockSpec(memory_space=pltpu.HBM)
SMEM = pl.BlockSpec(memory_space=pltpu.SMEM)
ANY = pl.BlockSpec(memory_space=pl.ANY)


def start_all(copies):
    for copy in copies:
        copy.start()
    return copies


def wait_all(copies):
    for copy in copies:
        copy.wait()


CACHE_AHEAD = 16


def cache_kernel(pool_ref, keys_ref, values_ref, raw, values, sem, out_sem):
    heads, tokens = raw.shape[:2]
    copies = [pltpu.make_async_copy(pool_ref.at[:, h], raw.at[h], sem.at[h]) for h in range(heads)]
    start_all(copies[:CACHE_AHEAD])
    rows = raw.reshape(heads, 2 * tokens, HD)
    to = lax.broadcasted_iota(jnp.int32, (2 * tokens, 2 * tokens), 0)
    source = lax.broadcasted_iota(jnp.int32, (2 * tokens, 2 * tokens), 1)
    wanted = jnp.where(to < tokens, 2 * to, 2 * (to - tokens) + 1)
    pick = jnp.where(source == wanted, 1.0, 0.0).astype(jnp.bfloat16)
    sent = []
    for h in range(0, heads, 2):
        for ahead in range(h + CACHE_AHEAD, min(h + CACHE_AHEAD + 2, heads)):
            copies[ahead].start()
        wait_all(copies[h : h + 2])
        both = jnp.concatenate([rows[h], rows[h + 1]], axis=1)
        made = jnp.dot(pick, both, preferred_element_type=jnp.float32).astype(jnp.bfloat16)
        for i in range(2):
            keys_ref[h + i] = made[:tokens, i * HD : (i + 1) * HD]
            values[h + i] = made[tokens:, i * HD : (i + 1) * HD]
        sent += start_all([pltpu.make_async_copy(values.at[h : h + 2], values_ref.at[h : h + 2], out_sem.at[h // 2])])
    wait_all(sent)


def cache_by_head(pool):
    tokens, heads = pool.shape[:2]
    return pl.pallas_call(
        cache_kernel,
        out_shape=(
            jax.ShapeDtypeStruct((heads, tokens, HD), pool.dtype),
            pltpu.HBM((heads, tokens, HD), pool.dtype),
        ),
        in_specs=[HBM],
        out_specs=(VMEM, HBM),
        scratch_shapes=[
            pltpu.VMEM((heads, tokens, 2, HD), pool.dtype),
            pltpu.VMEM((heads, tokens, HD), pool.dtype),
            pltpu.SemaphoreType.DMA((heads,)),
            pltpu.SemaphoreType.DMA((heads // 2,)),
        ],
        compiler_params=pltpu.CompilerParams(vmem_limit_bytes=16 * 2**20),
        cost_estimate=pl.CostEstimate(flops=0, bytes_accessed=12 * 10**6, transcendentals=0),
        name="cache_by_head",
    )(in_hbm(pool))


def lanes_of(x):
    return jnp.concatenate([x[c] for c in range(x.shape[0])], axis=1)


def low_kernel(count, me_ref, slot_ref, down_ref, *refs):
    blocks, (x_ref, low_ref, x_buf, maps, made_ref, sem, low_sem, own_sem) = refs[:count], refs[count:]
    me = me_ref[0]
    steps = blocks[0].shape[0]
    holders, rank, width = down_ref.shape
    fetch = pltpu.make_async_copy(down_ref, maps, own_sem.at[0])
    fetch.start()
    copies = []
    for k, block in enumerate(blocks):
        for t in range(steps):
            copies.append(
                pltpu.make_async_copy(block.at[t], x_buf.at[:, (me ^ k) * steps + t], sem.at[k * steps + t])
            )
    wait_all(start_all(copies))
    keep = pltpu.make_async_copy(x_buf, x_ref, own_sem.at[1])
    keep.start()
    chunks, pairs = x_buf.shape[:2]
    rows = 2 * pairs
    x = lanes_of(x_buf.reshape(chunks, rows, HD))
    fetch.wait()
    made = lax.dot_general(
        maps.reshape(holders * rank, width)[...], x, CONTRACT_LANES, preferred_element_type=jnp.float32
    )
    slot = slot_ref[...]
    low = jnp.zeros((rank, rows), jnp.float32)
    for h in range(holders):
        low = low + jnp.where(slot == h, made[h * rank : (h + 1) * rank], 0.0)
    low = low.T
    made_ref[...] = jnp.concatenate([low[: rows // 2], low[rows // 2 :]], axis=1).astype(made_ref.dtype)
    wait_all(start_all([pltpu.make_async_copy(made_ref, low_ref.at[k], low_sem.at[k]) for k in range(count)]))
    keep.wait()


def low_of(me, blocks, slot, down):
    count = len(blocks)
    steps, chunks = blocks[0].shape[:2]
    rows = count * steps * 2
    rank = down.shape[1]
    return pl.pallas_call(
        functools.partial(low_kernel, count),
        out_shape=(
            pltpu.HBM((chunks, rows // 2, 2, HD), jnp.bfloat16),
            pltpu.HBM((count, rows // 2, 2 * rank), jnp.bfloat16),
        ),
        in_specs=[SMEM, VMEM, HBM] + [ANY] * count,
        out_specs=(HBM, HBM),
        scratch_shapes=[
            pltpu.VMEM((chunks, rows // 2, 2, HD), jnp.bfloat16),
            pltpu.VMEM(down.shape, jnp.bfloat16),
            pltpu.VMEM((rows // 2, 2 * rank), jnp.bfloat16),
            pltpu.SemaphoreType.DMA((count * steps,)),
            pltpu.SemaphoreType.DMA((count,)),
            pltpu.SemaphoreType.DMA((2,)),
        ],
        compiler_params=pltpu.CompilerParams(vmem_limit_bytes=16 * 2**20),
        cost_estimate=pl.CostEstimate(flops=10**8, bytes_accessed=4 * 10**6, transcendentals=0),
        name="low_rows",
    )(me, slot, in_hbm(down), *blocks)


def put_chunks(buf, first, value):
    wide = value.shape[1]
    for c in range(-(-wide // HD)):
        part = value[:, c * HD : min((c + 1) * HD, wide)]
        if part.shape[1] < HD:
            part = jnp.concatenate([part, jnp.zeros((part.shape[0], HD - part.shape[1]), part.dtype)], axis=1)
        buf[first + c] = part.astype(buf.dtype)


def send_blocks(buf, out_ref, first, sem):
    count, _, steps = out_ref.shape[:3]
    chunks = buf.shape[0]
    return start_all(
        [
            pltpu.make_async_copy(
                buf.at[:, k * steps : (k + 1) * steps], out_ref.at[k, first : first + chunks], sem.at[k]
            )
            for k in range(count)
        ]
    )


PROJECT_CHUNK = 512
PROJECT_AHEAD = 3


def project_kernel(x_ref, w_ref, send_ref, base_ref, x_buf, w_buf, total, buf, base, x_sem, w_sem, sem, base_sem):
    chunks, pairs = x_buf.shape[:2]
    rows = 2 * pairs
    columns, width = w_ref.shape[1:]
    parts = width // PROJECT_CHUNK
    per = PROJECT_CHUNK // HD
    fetch_x = pltpu.make_async_copy(x_ref, x_buf, x_sem)
    fetch_x.start()
    fetches = [
        pltpu.make_async_copy(w_ref.at[:, :, p * PROJECT_CHUNK : (p + 1) * PROJECT_CHUNK], w_buf.at[p], w_sem.at[p])
        for p in range(parts)
    ]
    start_all(fetches[:PROJECT_AHEAD])
    fetch_x.wait()
    x_rows = x_buf.reshape(chunks, rows, HD)
    for p in range(parts):
        fetches[p].wait()
        start_all(fetches[p + PROJECT_AHEAD : p + PROJECT_AHEAD + 1])
        x = jnp.concatenate([x_rows[c] for c in range(p * per, (p + 1) * per)], axis=1)
        for i in range(3):
            made = lax.dot_general(w_buf[p, i], x, CONTRACT_LANES, preferred_element_type=jnp.float32)
            total[i] = made if p == 0 else total[i] + made
    each = buf.shape[0] // 2
    flat = buf.reshape(buf.shape[0], rows, HD)
    for i in range(2):
        put_chunks(flat, i * each, total[i].T)
    sent = send_blocks(buf, send_ref, 0, sem)
    base[...] = total[2].T
    keep = pltpu.make_async_copy(base, base_ref, base_sem)
    keep.start()
    wait_all(sent)
    keep.wait()


def project(x, weight, count):
    chunks, pairs = x.shape[:2]
    columns, width = weight.shape[1:]
    each = -(-columns // HD)
    parts = width // PROJECT_CHUNK
    return pl.pallas_call(
        project_kernel,
        out_shape=(
            pltpu.HBM((count, 3 * each, pairs // count, 2, HD), jnp.bfloat16),
            pltpu.HBM((2 * pairs, columns), jnp.float32),
        ),
        in_specs=[HBM, HBM],
        out_specs=(HBM, HBM),
        scratch_shapes=[
            pltpu.VMEM(x.shape, jnp.bfloat16),
            pltpu.VMEM((parts, 3, columns, PROJECT_CHUNK), jnp.bfloat16),
            pltpu.VMEM((3, columns, 2 * pairs), jnp.float32),
            pltpu.VMEM((2 * each, pairs, 2, HD), jnp.bfloat16),
            pltpu.VMEM((2 * pairs, columns), jnp.float32),
            pltpu.SemaphoreType.DMA,
            pltpu.SemaphoreType.DMA((parts,)),
            pltpu.SemaphoreType.DMA((count,)),
            pltpu.SemaphoreType.DMA,
        ],
        compiler_params=pltpu.CompilerParams(vmem_limit_bytes=24 * 2**20),
        cost_estimate=pl.CostEstimate(flops=10**9, bytes_accessed=11 * 10**6, transcendentals=0),
        name="project",
    )(in_hbm(x), in_hbm(weight))


UPDATE_PARTS = 8
UPDATE_AHEAD = 4


def update_kernel(stored_ref, low_ref, base_ref, up_ref, send_in, send_ref, base, up, buf, base_sem, up_sem, sem):
    count, half, packed = low_ref.shape
    rank = packed // 2
    rows = 2 * half
    height = up_ref.shape[0] // UPDATE_PARTS
    fetches = [
        pltpu.make_async_copy(up_ref.at[p * height : (p + 1) * height], up.at[p], up_sem.at[p])
        for p in range(UPDATE_PARTS)
    ]
    start_all(fetches[:UPDATE_AHEAD])
    fetch_base = pltpu.make_async_copy(base_ref, base, base_sem)
    fetch_base.start()
    low = low_ref[0].astype(jnp.float32)
    for s in range(1, count):
        low = low + low_ref[s].astype(jnp.float32)
    low = jnp.concatenate([low[:, :rank], low[:, rank:]], axis=0)
    batch = 256 // rank
    spread = jnp.concatenate([low] * batch, axis=1)
    which = lax.broadcasted_iota(jnp.int32, (rows, batch * rank), 1) // rank
    ahead = stored_ref[...] - which
    total = jnp.zeros(base.shape, jnp.float32)
    for p in range(UPDATE_PARTS):
        fetches[p].wait()
        start_all(fetches[p + UPDATE_AHEAD : p + UPDATE_AHEAD + 1])
        for a in range(0, height // rank, batch):
            wide = jnp.where(ahead == p * (height // rank) + a, spread, 0.0).astype(jnp.bfloat16)
            total = total + jnp.dot(
                wide, up[p, a * rank : (a + batch) * rank], preferred_element_type=jnp.float32
            )
    fetch_base.wait()
    put_chunks(buf.reshape(buf.shape[0], rows, HD), 0, base[...] + adapter_scale * total)
    wait_all(send_blocks(buf, send_ref, send_ref.shape[1] - buf.shape[0], sem))


def update_values(stored, lows, base, up, send):
    count, chunks = send.shape[:2]
    rows, columns = base.shape
    height = up.shape[0] // UPDATE_PARTS
    return pl.pallas_call(
        update_kernel,
        out_shape=pltpu.HBM(send.shape, send.dtype),
        in_specs=[VMEM, VMEM, HBM, HBM, HBM],
        out_specs=HBM,
        scratch_shapes=[
            pltpu.VMEM(base.shape, jnp.float32),
            pltpu.VMEM((UPDATE_PARTS, height, columns), jnp.bfloat16),
            pltpu.VMEM((chunks // 3, rows // 2, 2, HD), jnp.bfloat16),
            pltpu.SemaphoreType.DMA,
            pltpu.SemaphoreType.DMA((UPDATE_PARTS,)),
            pltpu.SemaphoreType.DMA((count,)),
        ],
        input_output_aliases={4: 0},
        compiler_params=pltpu.CompilerParams(vmem_limit_bytes=16 * 2**20),
        cost_estimate=pl.CostEstimate(flops=3 * 10**8, bytes_accessed=4 * 10**6, transcendentals=0),
        name="update_values",
    )(stored, lows, in_hbm(base), in_hbm(up), in_hbm(send))


def attend_kernel(cos_ref, sin_ref, live_ref, pieces_ref, keys_ref, values_ref, out_ref, values_buf, kn_ref, vn_ref, sem):
    count, _, steps = pieces_ref.shape[:3]
    rows = 2 * steps
    each = pieces_ref.shape[1] // 3
    heads = 2 * out_ref.shape[1] // count
    lanes = heads * HD
    group = rows * HEAD_BLOCK
    chips = range(count // 2)
    fetches = start_all(
        [
            pltpu.make_async_copy(values_ref.at[c * heads : (c + 1) * heads], values_buf.at[c], sem.at[c])
            for c in chips
        ]
    )
    cosine = cos_ref[...][:rows]
    sine = sin_ref[...][:rows]
    left = lax.broadcasted_iota(jnp.int32, (rows, HD), 1) < HD // 2

    def chip_columns(chip, at):
        low = [pieces_ref[2 * chip, at + c].reshape(rows, HD).astype(jnp.float32) for c in range(each)]
        high = [pieces_ref[2 * chip + 1, at + c].reshape(rows, HD).astype(jnp.float32) for c in range(each)]
        high = [pltpu.roll(x, HD // 2, 1) for x in high]
        whole = low[:-1] + [jnp.where(left, low[-1], high[0])]
        return whole + [jnp.where(left, a, b) for a, b in zip(high[:-1], high[1:])]

    def rotated(parts):
        return [x * cosine + pltpu.roll(x, HD // 2, 1) * sine for x in parts]

    row_head = lax.broadcasted_iota(jnp.int32, (group, lanes), 0) % HEAD_BLOCK
    lane_head = lax.broadcasted_iota(jnp.int32, (group, lanes), 1) // HD
    own_head = row_head == lane_head
    row_j = lax.broadcasted_iota(jnp.int32, (group, 16), 0) // HEAD_BLOCK
    new_j = lax.broadcasted_iota(jnp.int32, (group, 16), 1)
    new_live = (new_j < rows) & (new_j % 2 == row_j % 2) & (new_j // 2 <= row_j // 2)
    live = jnp.concatenate(
        [
            jnp.broadcast_to(live_ref[j % 2 : j % 2 + 1, :], (HEAD_BLOCK, live_ref.shape[1]))
            for j in range(rows)
        ],
        axis=0,
    )
    live = live > 0
    kn_ref[...] = jnp.zeros_like(kn_ref)
    vn_ref[...] = jnp.zeros_like(vn_ref)
    spreads = []
    for c in chips:
        query = jnp.concatenate(rotated(chip_columns(c, 0)), axis=1)
        kn_ref[c, 0:rows] = jnp.concatenate(rotated(chip_columns(c, each)), axis=1)
        vn_ref[c, 0:rows] = jnp.concatenate(chip_columns(c, 2 * each), axis=1)
        spread = jnp.concatenate(
            [jnp.broadcast_to(query[j : j + 1], (HEAD_BLOCK, lanes)) for j in range(rows)], axis=0
        )
        spreads.append(jnp.where(own_head, spread, 0.0).astype(jnp.bfloat16))
    scores, fresh = [], []
    for c in chips:
        keys = jnp.concatenate([keys_ref[c * heads + h] for h in range(heads)], axis=1)
        kn = kn_ref[c].astype(jnp.bfloat16)
        scores.append(lax.dot_general(spreads[c], keys, CONTRACT_LANES, preferred_element_type=jnp.float32))
        fresh.append(lax.dot_general(spreads[c], kn, CONTRACT_LANES, preferred_element_type=jnp.float32))
    weights, fresh_weights, totals = [], [], []
    for c in chips:
        old = jnp.where(live, scores[c] * (HD**-0.5), masked_score)
        new = jnp.where(new_live, fresh[c] * (HD**-0.5), masked_score)
        top = jnp.maximum(jnp.max(old, axis=1, keepdims=True), jnp.max(new, axis=1, keepdims=True))
        old = jnp.where(live, jnp.exp(old - top), 0.0)
        new = jnp.where(new_live, jnp.exp(new - top), 0.0)
        totals.append(jnp.sum(old, axis=1, keepdims=True) + jnp.sum(new, axis=1, keepdims=True))
        weights.append(old.astype(jnp.bfloat16))
        fresh_weights.append(new.astype(jnp.bfloat16))
    wait_all(fetches)
    for c in chips:
        values = lanes_of(values_buf[c])
        vn = vn_ref[c].astype(jnp.bfloat16)
        mixed = jnp.dot(weights[c], values, preferred_element_type=jnp.float32)
        mixed = mixed + jnp.dot(fresh_weights[c], vn, preferred_element_type=jnp.float32)
        mixed = jnp.where(own_head, mixed / totals[c], 0.0)
        out = jnp.sum(mixed.reshape(rows, HEAD_BLOCK, lanes), axis=1).astype(out_ref.dtype)
        for t in range(steps):
            for h in range(heads):
                out_ref[t, c * heads + h] = out[2 * t : 2 * t + 2, h * HD : (h + 1) * HD]


def attend(cosine, sine, live, pieces, keys, values):
    count, _, steps = pieces.shape[:3]
    heads, tokens = keys.shape[:2]
    chips = count // 2
    per = heads // chips
    return pl.pallas_call(
        attend_kernel,
        out_shape=jax.ShapeDtypeStruct((steps, heads, 2, HD), jnp.bfloat16),
        in_specs=[VMEM] * 5 + [HBM],
        out_specs=VMEM,
        scratch_shapes=[pltpu.VMEM((chips, per, tokens, HD), jnp.bfloat16)]
        + [pltpu.VMEM((chips, 16, per * HD), jnp.float32)] * 2
        + [pltpu.SemaphoreType.DMA((chips,))],
        compiler_params=pltpu.CompilerParams(vmem_limit_bytes=16 * 2**20),
        cost_estimate=pl.CostEstimate(flops=10**9, bytes_accessed=6 * 10**6, transcendentals=0),
        name="attention",
    )(cosine, sine, live, pieces, keys, in_hbm(values))


def chip_plan(
    count,
    hidden,
    query_key_value_weight,
    adapter_down_maps,
    adapter_up_maps,
    adapter_storage_row,
    request_adapter,
    lengths,
    request_page_table,
    key_value_pool,
):
    me = lax.axis_index("replica")
    steps, req_dev, width = hidden.shape
    heads = width // HD
    holder_count, rank, _ = adapter_down_maps.shape
    pool_pages, page_len = key_value_pool.shape[:2]
    adapter_count = adapter_storage_row.shape[0]

    tokens = pool_pages * page_len
    keys, values = cache_by_head(key_value_pool.reshape(tokens, 2, heads, HD).transpose(0, 2, 1, 3))

    held = {0: hidden}
    for masks in (range(4, count, 4), (2,), (1,)):
        held.update({k ^ m: trade(v, m, count) for k, v in list(held.items()) for m in masks})
    blocks = [
        held[k].reshape(steps, req_dev, heads, HD).transpose(0, 2, 1, 3) for k in range(count)
    ]
    blocks[0] = in_hbm(blocks[0])

    stored = jnp.sum(
        jnp.where(
            request_adapter[:, None] == jnp.arange(adapter_count, dtype=jnp.int32)[None, :],
            adapter_storage_row[None, :],
            0,
        ),
        axis=1,
    )
    stored = jnp.broadcast_to(stored.reshape(count, 1, req_dev), (count, steps, req_dev)).reshape(-1)

    x, lows = low_of(
        me.astype(jnp.int32).reshape(1), blocks, (stored - me * holder_count)[None, :], adapter_down_maps
    )
    lows = lax.all_to_all(lows, "replica", split_axis=0, concat_axis=0, tiled=True)
    send, base = project(x, query_key_value_weight.transpose(0, 2, 1), count)
    send = update_values(stored[:, None], lows, base, adapter_up_maps.reshape(adapter_count * rank, -1), send)
    pieces = lax.all_to_all(send, "replica", split_axis=0, concat_axis=0, tiled=True)

    my_lengths = lax.dynamic_slice_in_dim(lengths, me * req_dev, req_dev)
    cosine, sine = rotation(my_lengths, steps)
    live = live_tokens(my_lengths, request_page_table, pool_pages, page_len).astype(jnp.int32)
    out = attend(cosine, sine, live.reshape(req_dev, tokens), pieces, keys, values)
    return out.transpose(0, 2, 1, 3).reshape(steps, req_dev, width)


def per_device(replicas, *arrays):
    columns = arrays[1].shape[2]
    whole_heads = replicas % 4 == 0 and (2 * columns) % HD == 0 and columns % HD == HD // 2
    plan = chip_plan if whole_heads and arrays[0].shape[1] == 2 else general_plan
    return plan(replicas, *arrays)


def solution(mesh):
    placed = (
        P(None, ("groups", "replica"), None),
        P(None, None, "replica"),
        P("replica", None, None),
        P(None, None, "replica"),
        P(),
        P("groups"),
        P("groups"),
        P(("groups", "replica"), None),
        P(("groups", "replica"), None, None, None),
    )
    return jax.shard_map(
        functools.partial(per_device, mesh.shape["replica"]),
        mesh=mesh,
        in_specs=placed,
        out_specs=P(None, ("groups", "replica"), None),
        check_vma=False,
    )
```

```python
import functools

import jax
import jax.numpy as jnp
from jax import lax
from jax.experimental import pallas as pl
from jax.experimental.pallas import tpu as pltpu
from jax.sharding import PartitionSpec as P

HD = 128
ROWS = 8
HEAD_BLOCK = 8

adapter_scale = 2.0
masked_score = -1e30


def attention_kernel(steps, req_dev, q_ref, k_ref, v_ref, cos_ref, sin_ref, live_ref, kv_ref, out_ref, kn_ref, vn_ref):
    rows = steps * req_dev
    width = q_ref.shape[1]
    lanes = HEAD_BLOCK * HD
    group = rows * HEAD_BLOCK
    cosine = cos_ref[...]
    sine = sin_ref[...]

    def rotated(x):
        pieces = []
        for h in range(HEAD_BLOCK):
            head = x[:, h * HD : (h + 1) * HD]
            pieces.append(head * cosine + pltpu.roll(head, HD // 2, 1) * sine)
        return jnp.concatenate(pieces, axis=1)

    row_head = lax.broadcasted_iota(jnp.int32, (group, lanes), 0) % HEAD_BLOCK
    lane_head = lax.broadcasted_iota(jnp.int32, (group, lanes), 1) // HD
    own_head = row_head == lane_head
    row_j = lax.broadcasted_iota(jnp.int32, (group, 16), 0) // HEAD_BLOCK
    new_j = lax.broadcasted_iota(jnp.int32, (group, 16), 1)
    new_live = (new_j < rows) & (new_j % req_dev == row_j % req_dev) & (new_j // req_dev <= row_j // req_dev)
    live_all = live_ref[...]
    live = jnp.concatenate(
        [
            jnp.broadcast_to(live_all[j % req_dev : j % req_dev + 1], (HEAD_BLOCK, live_all.shape[1]))
            for j in range(rows)
        ],
        axis=0,
    )
    live = live > 0
    kn_ref[...] = jnp.zeros_like(kn_ref)
    vn_ref[...] = jnp.zeros_like(vn_ref)
    contract_lanes = (((1,), (1,)), ((), ()))
    for c in range(width // lanes):
        cols = slice(c * lanes, (c + 1) * lanes)
        query = rotated(q_ref[:, cols].astype(jnp.float32))
        key_new = rotated(k_ref[:, cols].astype(jnp.float32))
        kn_ref[0:8] = key_new
        vn_ref[0:8] = v_ref[:, cols].astype(jnp.float32)
        kn = kn_ref[...].astype(jnp.bfloat16)
        vn = vn_ref[...].astype(jnp.bfloat16)
        spread = jnp.concatenate(
            [jnp.broadcast_to(query[j : j + 1], (HEAD_BLOCK, lanes)) for j in range(rows)], axis=0
        )
        spread = jnp.where(own_head, spread, 0.0).astype(jnp.bfloat16)
        kv = kv_ref[:, cols]
        scores = lax.dot_general(spread, kv, contract_lanes, preferred_element_type=jnp.float32) * (HD**-0.5)
        scores = jnp.where(live, scores, masked_score)
        fresh = lax.dot_general(spread, kn, contract_lanes, preferred_element_type=jnp.float32) * (HD**-0.5)
        fresh = jnp.where(new_live, fresh, masked_score)
        top = jnp.maximum(jnp.max(scores, axis=1, keepdims=True), jnp.max(fresh, axis=1, keepdims=True))
        weights = jnp.where(live, jnp.exp(scores - top), 0.0)
        fresh = jnp.where(new_live, jnp.exp(fresh - top), 0.0)
        totals = jnp.sum(weights, axis=1, keepdims=True) + jnp.sum(fresh, axis=1, keepdims=True)
        weights = pltpu.roll(weights, 1, 1).astype(jnp.bfloat16)
        mixed = jnp.dot(weights, kv, preferred_element_type=jnp.float32)
        mixed = mixed + jnp.dot(fresh.astype(jnp.bfloat16), vn, preferred_element_type=jnp.float32)
        mixed = jnp.where(own_head, mixed / totals, 0.0)
        out = jnp.sum(mixed.reshape(rows, HEAD_BLOCK, lanes), axis=1)
        out_ref[:, cols] = out.astype(out_ref.dtype)


def attention(steps, req_dev, q, k, v, cosine, sine, live, kv):
    rows = steps * req_dev
    width = q.shape[1]
    vmem = pl.BlockSpec(memory_space=pltpu.VMEM)
    return pl.pallas_call(
        functools.partial(attention_kernel, steps, req_dev),
        out_shape=jax.ShapeDtypeStruct((rows, width), jnp.bfloat16),
        in_specs=[vmem] * 7,
        out_specs=vmem,
        scratch_shapes=[pltpu.VMEM((16, HEAD_BLOCK * HD), jnp.float32)] * 2,
        compiler_params=pltpu.CompilerParams(vmem_limit_bytes=32 * 2**20),
        cost_estimate=pl.CostEstimate(flops=10**9, bytes_accessed=6 * 10**6, transcendentals=0),
        name="attention",
    )(q, k, v, cosine, sine, live, kv)


def rotation(my_lengths, steps):
    rows = steps * my_lengths.shape[0]
    positions = (my_lengths[None, :] + jnp.arange(steps, dtype=jnp.int32)[:, None]).reshape(rows)
    positions = jnp.pad(positions, (0, ROWS - rows))
    half = HD // 2
    frequency = jnp.exp(jnp.arange(half, dtype=jnp.float32) * (-2.0 * jnp.log(10000.0) / HD))
    angles = positions.astype(jnp.float32)[:, None] * frequency[None, :]
    cosine = jnp.cos(angles)
    sine = jnp.sin(angles)
    cosine = jnp.concatenate([cosine, cosine], axis=1)
    sine = jnp.concatenate([-sine, sine], axis=1)
    return cosine, sine


def live_tokens(my_lengths, request_page_table, pool_pages, page_len):
    pages = jnp.arange(pool_pages, dtype=jnp.int32)
    max_pages = request_page_table.shape[1]
    place = jnp.max(
        jnp.where(
            request_page_table[:, :, None] == pages[None, None, :],
            jnp.arange(max_pages, dtype=jnp.int32)[None, :, None],
            -1,
        ),
        axis=1,
    )
    token = place[:, :, None] * page_len + jnp.arange(page_len, dtype=jnp.int32)[None, None, :]
    return (place[:, :, None] >= 0) & (token < my_lengths[:, None, None])


def live_rows(my_lengths, request_page_table, pool_pages, page_len):
    alive = live_tokens(my_lengths, request_page_table, pool_pages, page_len)
    live = jnp.stack([alive, jnp.zeros_like(alive)], axis=-1).astype(jnp.int32)
    return live.reshape(request_page_table.shape[0], pool_pages * page_len * 2)


def general_plan(
    replicas,
    hidden,
    query_key_value_weight,
    adapter_down_maps,
    adapter_up_maps,
    adapter_storage_row,
    request_adapter,
    lengths,
    request_page_table,
    key_value_pool,
):
    my_index = lax.axis_index("replica")
    steps, req_dev, width = hidden.shape
    rows = steps * req_dev
    columns = query_key_value_weight.shape[2]
    holder_count, rank, _ = adapter_down_maps.shape
    pool_pages, page_len = key_value_pool.shape[:2]
    adapter_count = adapter_storage_row.shape[0]
    chips = replicas // 2
    total = replicas * ROWS

    block = jnp.pad(hidden.reshape(rows, width), ((0, ROWS - rows), (0, 0)))
    same_core = [[2 * chip + core for chip in range(chips)] for core in range(2)]
    mine = lax.all_to_all(
        jnp.broadcast_to(block[None], (chips, ROWS, width)),
        "replica",
        split_axis=0,
        concat_axis=0,
        axis_index_groups=same_core,
        tiled=True,
    )
    other = lax.ppermute(mine, "replica", [(i, i ^ 1) for i in range(replicas)])
    first = my_index % 2 == 0
    gathered = jnp.stack([jnp.where(first, mine, other), jnp.where(first, other, mine)])
    gathered = gathered.reshape(total, width)

    stored_rows = jnp.sum(
        jnp.where(
            request_adapter[:, None] == jnp.arange(adapter_count, dtype=jnp.int32)[None, :],
            adapter_storage_row[None, :],
            0,
        ),
        axis=1,
    )
    by_block = stored_rows.reshape(chips, 2, 1, req_dev).transpose(1, 0, 2, 3)
    by_block = jnp.broadcast_to(by_block, (2, chips, steps, req_dev)).reshape(2, chips, rows)
    row_stored = jnp.pad(by_block, ((0, 0), (0, 0), (0, ROWS - rows)), constant_values=-1).reshape(total)

    down = jnp.einsum("nd,hfd->nhf", gathered, adapter_down_maps, preferred_element_type=jnp.float32)
    slots = my_index * holder_count + jnp.arange(holder_count, dtype=jnp.int32)
    own = row_stored[:, None] == slots[None, :]
    low = jnp.sum(jnp.where(own[:, :, None], down, 0.0), axis=1).astype(jnp.bfloat16)
    low = jnp.concatenate([low[: total // 2], low[total // 2 :]], axis=1)
    low = lax.all_to_all(
        jnp.broadcast_to(low[None], (replicas,) + low.shape), "replica", split_axis=0, concat_axis=0, tiled=True
    )
    low = jnp.sum(low.astype(jnp.float32), axis=0)
    low = jnp.concatenate([low[:, :rank], low[:, rank:]], axis=0)

    projected = jnp.einsum("nd,idc->nic", gathered, query_key_value_weight, preferred_element_type=jnp.float32)

    def update(first_adapter, maps):
        held = maps.shape[0]
        which = first_adapter + jnp.arange(held, dtype=jnp.int32)
        wide = jnp.where((row_stored[:, None] == which[None, :])[:, :, None], low[:, None, :], 0.0)
        return jnp.dot(
            wide.astype(jnp.bfloat16).reshape(total, held * rank),
            maps.reshape(held * rank, columns),
            preferred_element_type=jnp.float32,
        )

    step_adapters = 64
    if adapter_count <= step_adapters:
        updated = update(0, adapter_up_maps)
    else:
        updated = lax.fori_loop(
            0,
            adapter_count // step_adapters,
            lambda i, sofar: sofar
            + update(
                i * step_adapters,
                lax.dynamic_slice_in_dim(adapter_up_maps, i * step_adapters, step_adapters, 0),
            ),
            jnp.zeros((total, columns), jnp.float32),
        )
    value = projected[:, 2] + adapter_scale * updated
    combined = jnp.concatenate([projected[:, 0], projected[:, 1], value], axis=1).astype(jnp.bfloat16)
    combined = combined.reshape(2, chips, ROWS, 3 * columns).transpose(1, 0, 2, 3)
    combined = combined.reshape(replicas, ROWS, 3 * columns)
    arrived = lax.all_to_all(combined, "replica", split_axis=0, concat_axis=0, tiled=True)
    arrived = arrived.reshape(replicas, ROWS, 3, columns).transpose(2, 1, 0, 3).reshape(3, ROWS, width)

    my_lengths = lax.dynamic_slice_in_dim(lengths, my_index * req_dev, req_dev)
    cosine, sine = rotation(my_lengths, steps)
    live = live_rows(my_lengths, request_page_table, pool_pages, page_len)
    kv = key_value_pool.reshape(pool_pages * page_len * 2, width)
    out = attention(steps, req_dev, arrived[0], arrived[1], arrived[2], cosine, sine, live, kv)
    return out.reshape(steps, req_dev, width)


def trade(value, mask, count):
    return lax.ppermute(value, "replica", [(i, i ^ mask) for i in range(count)])


CONTRACT_LANES = (((1,), (1,)), ((), ()))


def in_hbm(x):
    return pltpu.with_memory_space_constraint(x, pltpu.HBM)


VMEM = pl.BlockSpec(memory_space=pltpu.VMEM)
HBM = pl.BlockSpec(memory_space=pltpu.HBM)
SMEM = pl.BlockSpec(memory_space=pltpu.SMEM)
ANY = pl.BlockSpec(memory_space=pl.ANY)


def start_all(copies):
    for copy in copies:
        copy.start()
    return copies


def rows_copies(source, place, sem, pieces):
    step = source.shape[0] // pieces
    return [
        pltpu.make_async_copy(source.at[p * step : (p + 1) * step], place.at[p * step : (p + 1) * step], sem.at[p])
        for p in range(pieces)
    ]


def wait_all(copies):
    for copy in copies:
        copy.wait()


def cache_kernel(pool_ref, keys_ref, values_ref, raw, values, sem, out_sem):
    heads, tokens = raw.shape[:2]
    copies = start_all([pltpu.make_async_copy(pool_ref.at[:, h], raw.at[h], sem.at[h]) for h in range(heads)])
    rows = raw.reshape(heads, 2 * tokens, HD)
    to = lax.broadcasted_iota(jnp.int32, (2 * tokens, 2 * tokens), 0)
    source = lax.broadcasted_iota(jnp.int32, (2 * tokens, 2 * tokens), 1)
    wanted = jnp.where(to < tokens, 2 * to, 2 * (to - tokens) + 1)
    pick = jnp.where(source == wanted, 1.0, 0.0).astype(jnp.bfloat16)
    sent = []
    for h in range(0, heads, 2):
        wait_all(copies[h : h + 2])
        both = jnp.concatenate([rows[h], rows[h + 1]], axis=1)
        made = jnp.dot(pick, both, preferred_element_type=jnp.float32).astype(jnp.bfloat16)
        for i in range(2):
            keys_ref[h + i] = made[:tokens, i * HD : (i + 1) * HD]
            values[h + i] = made[tokens:, i * HD : (i + 1) * HD]
        sent += start_all([pltpu.make_async_copy(values.at[h : h + 2], values_ref.at[h : h + 2], out_sem.at[h // 2])])
    wait_all(sent)


def cache_by_head(pool):
    tokens, heads = pool.shape[:2]
    return pl.pallas_call(
        cache_kernel,
        out_shape=(
            jax.ShapeDtypeStruct((heads, tokens, HD), pool.dtype),
            pltpu.HBM((heads, tokens, HD), pool.dtype),
        ),
        in_specs=[HBM],
        out_specs=(VMEM, HBM),
        scratch_shapes=[
            pltpu.VMEM((heads, tokens, 2, HD), pool.dtype),
            pltpu.VMEM((heads, tokens, HD), pool.dtype),
            pltpu.SemaphoreType.DMA((heads,)),
            pltpu.SemaphoreType.DMA((heads // 2,)),
        ],
        compiler_params=pltpu.CompilerParams(vmem_limit_bytes=16 * 2**20),
        cost_estimate=pl.CostEstimate(flops=0, bytes_accessed=12 * 10**6, transcendentals=0),
        name="cache_by_head",
    )(in_hbm(pool))


def lanes_of(x):
    return jnp.concatenate([x[c] for c in range(x.shape[0])], axis=1)


DOWN_PIECES = 4
X_PIECES = 8


def low_kernel(count, me_ref, slot_ref, down_ref, *refs):
    blocks, (x_ref, low_ref, x_buf, maps, made_ref, sem, low_sem, x_sem, down_sem) = refs[:count], refs[count:]
    me = me_ref[0]
    steps = blocks[0].shape[0]
    holders, rank, width = down_ref.shape
    fetches = []
    for h in range(holders):
        fetches += start_all(rows_copies(down_ref.at[h], maps.at[h], down_sem.at[h], DOWN_PIECES))
    copies = []
    for k, block in enumerate(blocks):
        for t in range(steps):
            copies.append(
                pltpu.make_async_copy(block.at[t], x_buf.at[:, (me ^ k) * steps + t], sem.at[k * steps + t])
            )
    wait_all(start_all(copies))
    keep = start_all(rows_copies(x_buf, x_ref, x_sem, X_PIECES))
    chunks, pairs = x_buf.shape[:2]
    rows = 2 * pairs
    x = lanes_of(x_buf.reshape(chunks, rows, HD))
    wait_all(fetches)
    made = lax.dot_general(
        maps.reshape(holders * rank, width)[...], x, CONTRACT_LANES, preferred_element_type=jnp.float32
    )
    slot = slot_ref[...]
    low = jnp.zeros((rank, rows), jnp.float32)
    for h in range(holders):
        low = low + jnp.where(slot == h, made[h * rank : (h + 1) * rank], 0.0)
    low = low.T
    made_ref[...] = jnp.concatenate([low[: rows // 2], low[rows // 2 :]], axis=1).astype(made_ref.dtype)
    wait_all(start_all([pltpu.make_async_copy(made_ref, low_ref.at[k], low_sem.at[k]) for k in range(count)]))
    wait_all(keep)


def low_of(me, blocks, slot, down):
    count = len(blocks)
    steps, chunks = blocks[0].shape[:2]
    rows = count * steps * 2
    rank = down.shape[1]
    return pl.pallas_call(
        functools.partial(low_kernel, count),
        out_shape=(
            pltpu.HBM((chunks, rows // 2, 2, HD), jnp.bfloat16),
            pltpu.HBM((count, rows // 2, 2 * rank), jnp.bfloat16),
        ),
        in_specs=[SMEM, VMEM, HBM] + [ANY] * count,
        out_specs=(HBM, HBM),
        scratch_shapes=[
            pltpu.VMEM((chunks, rows // 2, 2, HD), jnp.bfloat16),
            pltpu.VMEM(down.shape, jnp.bfloat16),
            pltpu.VMEM((rows // 2, 2 * rank), jnp.bfloat16),
            pltpu.SemaphoreType.DMA((count * steps,)),
            pltpu.SemaphoreType.DMA((count,)),
            pltpu.SemaphoreType.DMA((X_PIECES,)),
            pltpu.SemaphoreType.DMA((down.shape[0], DOWN_PIECES)),
        ],
        compiler_params=pltpu.CompilerParams(vmem_limit_bytes=16 * 2**20),
        cost_estimate=pl.CostEstimate(flops=10**8, bytes_accessed=4 * 10**6, transcendentals=0),
        name="low_rows",
    )(me, slot, in_hbm(down), *blocks)


def put_chunks(buf, first, value):
    wide = value.shape[1]
    for c in range(-(-wide // HD)):
        part = value[:, c * HD : min((c + 1) * HD, wide)]
        if part.shape[1] < HD:
            part = jnp.concatenate([part, jnp.zeros((part.shape[0], HD - part.shape[1]), part.dtype)], axis=1)
        buf[first + c] = part.astype(buf.dtype)


def send_blocks(buf, out_ref, first, sem):
    count, _, steps = out_ref.shape[:3]
    chunks = buf.shape[0]
    return start_all(
        [
            pltpu.make_async_copy(
                buf.at[:, k * steps : (k + 1) * steps], out_ref.at[k, first : first + chunks], sem.at[k]
            )
            for k in range(count)
        ]
    )


PROJECT_CHUNK = 512
PROJECT_AHEAD = 4
PROJECT_PIECES = 2


def project_kernel(x_ref, w_ref, send_ref, base_ref, x_buf, w_buf, total, buf, base, x_sem, w_sem, sem, base_sem):
    chunks, pairs = x_buf.shape[:2]
    rows = 2 * pairs
    columns, width = w_ref.shape[1:]
    parts = width // PROJECT_CHUNK
    per = PROJECT_CHUNK // HD
    fetch_x = start_all(rows_copies(x_ref, x_buf, x_sem, X_PIECES))
    fetches = []
    for p in range(parts):
        span = slice(p * PROJECT_CHUNK, (p + 1) * PROJECT_CHUNK)
        fetches.append([])
        for i in range(3):
            fetches[p] += rows_copies(w_ref.at[i, :, span], w_buf.at[p, i], w_sem.at[p, i], PROJECT_PIECES)
    for ahead in fetches[:PROJECT_AHEAD]:
        start_all(ahead)
    wait_all(fetch_x)
    x_rows = x_buf.reshape(chunks, rows, HD)
    for p in range(parts):
        wait_all(fetches[p])
        for ahead in fetches[p + PROJECT_AHEAD : p + PROJECT_AHEAD + 1]:
            start_all(ahead)
        x = jnp.concatenate([x_rows[c] for c in range(p * per, (p + 1) * per)], axis=1)
        for i in range(3):
            made = lax.dot_general(w_buf[p, i], x, CONTRACT_LANES, preferred_element_type=jnp.float32)
            total[i] = made if p == 0 else total[i] + made
    each = buf.shape[0] // 2
    flat = buf.reshape(buf.shape[0], rows, HD)
    for i in range(2):
        put_chunks(flat, i * each, total[i].T)
    sent = send_blocks(buf, send_ref, 0, sem)
    base[...] = total[2].T
    keep = pltpu.make_async_copy(base, base_ref, base_sem)
    keep.start()
    wait_all(sent)
    keep.wait()


def project(x, weight, count):
    chunks, pairs = x.shape[:2]
    columns, width = weight.shape[1:]
    each = -(-columns // HD)
    parts = width // PROJECT_CHUNK
    return pl.pallas_call(
        project_kernel,
        out_shape=(
            pltpu.HBM((count, 3 * each, pairs // count, 2, HD), jnp.bfloat16),
            pltpu.HBM((2 * pairs, columns), jnp.float32),
        ),
        in_specs=[HBM, HBM],
        out_specs=(HBM, HBM),
        scratch_shapes=[
            pltpu.VMEM(x.shape, jnp.bfloat16),
            pltpu.VMEM((parts, 3, columns, PROJECT_CHUNK), jnp.bfloat16),
            pltpu.VMEM((3, columns, 2 * pairs), jnp.float32),
            pltpu.VMEM((2 * each, pairs, 2, HD), jnp.bfloat16),
            pltpu.VMEM((2 * pairs, columns), jnp.float32),
            pltpu.SemaphoreType.DMA((X_PIECES,)),
            pltpu.SemaphoreType.DMA((parts, 3, PROJECT_PIECES)),
            pltpu.SemaphoreType.DMA((count,)),
            pltpu.SemaphoreType.DMA,
        ],
        compiler_params=pltpu.CompilerParams(vmem_limit_bytes=24 * 2**20),
        cost_estimate=pl.CostEstimate(flops=10**9, bytes_accessed=11 * 10**6, transcendentals=0),
        name="project",
    )(in_hbm(x), in_hbm(weight))


UPDATE_PARTS = 16
UPDATE_AHEAD = 16


def update_kernel(stored_ref, low_ref, base_ref, up_ref, send_in, send_ref, base, up, buf, base_sem, up_sem, sem):
    count, half, packed = low_ref.shape
    rank = packed // 2
    rows = 2 * half
    height = up_ref.shape[0] // UPDATE_PARTS
    fetches = [
        pltpu.make_async_copy(up_ref.at[p * height : (p + 1) * height], up.at[p], up_sem.at[p])
        for p in range(UPDATE_PARTS)
    ]
    start_all(fetches[:UPDATE_AHEAD])
    fetch_base = pltpu.make_async_copy(base_ref, base, base_sem)
    fetch_base.start()
    low = low_ref[0].astype(jnp.float32)
    for s in range(1, count):
        low = low + low_ref[s].astype(jnp.float32)
    low = jnp.concatenate([low[:, :rank], low[:, rank:]], axis=0)
    batch = 256 // rank
    spread = jnp.concatenate([low] * batch, axis=1)
    which = lax.broadcasted_iota(jnp.int32, (rows, batch * rank), 1) // rank
    ahead = stored_ref[...] - which
    total = jnp.zeros(base.shape, jnp.float32)
    for p in range(UPDATE_PARTS):
        fetches[p].wait()
        start_all(fetches[p + UPDATE_AHEAD : p + UPDATE_AHEAD + 1])
        for a in range(0, height // rank, batch):
            wide = jnp.where(ahead == p * (height // rank) + a, spread, 0.0).astype(jnp.bfloat16)
            total = total + jnp.dot(
                wide, up[p, a * rank : (a + batch) * rank], preferred_element_type=jnp.float32
            )
    fetch_base.wait()
    put_chunks(buf.reshape(buf.shape[0], rows, HD), 0, base[...] + adapter_scale * total)
    wait_all(send_blocks(buf, send_ref, send_ref.shape[1] - buf.shape[0], sem))


def update_values(stored, lows, base, up, send):
    count, chunks = send.shape[:2]
    rows, columns = base.shape
    height = up.shape[0] // UPDATE_PARTS
    return pl.pallas_call(
        update_kernel,
        out_shape=pltpu.HBM(send.shape, send.dtype),
        in_specs=[VMEM, VMEM, HBM, HBM, HBM],
        out_specs=HBM,
        scratch_shapes=[
            pltpu.VMEM(base.shape, jnp.float32),
            pltpu.VMEM((UPDATE_PARTS, height, columns), jnp.bfloat16),
            pltpu.VMEM((chunks // 3, rows // 2, 2, HD), jnp.bfloat16),
            pltpu.SemaphoreType.DMA,
            pltpu.SemaphoreType.DMA((UPDATE_PARTS,)),
            pltpu.SemaphoreType.DMA((count,)),
        ],
        input_output_aliases={4: 0},
        compiler_params=pltpu.CompilerParams(vmem_limit_bytes=16 * 2**20),
        cost_estimate=pl.CostEstimate(flops=3 * 10**8, bytes_accessed=4 * 10**6, transcendentals=0),
        name="update_values",
    )(stored, lows, in_hbm(base), in_hbm(up), in_hbm(send))


def attend_kernel(cos_ref, sin_ref, live_ref, pieces_ref, keys_ref, values_ref, out_ref, values_buf, kn_ref, vn_ref, sem):
    count, _, steps = pieces_ref.shape[:3]
    rows = 2 * steps
    each = pieces_ref.shape[1] // 3
    heads = 2 * out_ref.shape[1] // count
    lanes = heads * HD
    group = rows * HEAD_BLOCK
    chips = range(count // 2)
    fetches = start_all(
        [
            pltpu.make_async_copy(values_ref.at[c * heads : (c + 1) * heads], values_buf.at[c], sem.at[c])
            for c in chips
        ]
    )
    cosine = cos_ref[...][:rows]
    sine = sin_ref[...][:rows]
    left = lax.broadcasted_iota(jnp.int32, (rows, HD), 1) < HD // 2

    def chip_columns(chip, at):
        low = [pieces_ref[2 * chip, at + c].reshape(rows, HD).astype(jnp.float32) for c in range(each)]
        high = [pieces_ref[2 * chip + 1, at + c].reshape(rows, HD).astype(jnp.float32) for c in range(each)]
        high = [pltpu.roll(x, HD // 2, 1) for x in high]
        whole = low[:-1] + [jnp.where(left, low[-1], high[0])]
        return whole + [jnp.where(left, a, b) for a, b in zip(high[:-1], high[1:])]

    def rotated(parts):
        return [x * cosine + pltpu.roll(x, HD // 2, 1) * sine for x in parts]

    row_head = lax.broadcasted_iota(jnp.int32, (group, lanes), 0) % HEAD_BLOCK
    lane_head = lax.broadcasted_iota(jnp.int32, (group, lanes), 1) // HD
    own_head = row_head == lane_head
    row_j = lax.broadcasted_iota(jnp.int32, (group, 16), 0) // HEAD_BLOCK
    new_j = lax.broadcasted_iota(jnp.int32, (group, 16), 1)
    new_live = (new_j < rows) & (new_j % 2 == row_j % 2) & (new_j // 2 <= row_j // 2)
    live = jnp.concatenate(
        [
            jnp.broadcast_to(live_ref[j % 2 : j % 2 + 1, :], (HEAD_BLOCK, live_ref.shape[1]))
            for j in range(rows)
        ],
        axis=0,
    )
    live = live > 0
    kn_ref[...] = jnp.zeros_like(kn_ref)
    vn_ref[...] = jnp.zeros_like(vn_ref)
    spreads = []
    for c in chips:
        query = jnp.concatenate(rotated(chip_columns(c, 0)), axis=1)
        kn_ref[c, 0:rows] = jnp.concatenate(rotated(chip_columns(c, each)), axis=1)
        vn_ref[c, 0:rows] = jnp.concatenate(chip_columns(c, 2 * each), axis=1)
        spread = jnp.concatenate(
            [jnp.broadcast_to(query[j : j + 1], (HEAD_BLOCK, lanes)) for j in range(rows)], axis=0
        )
        spreads.append(jnp.where(own_head, spread, 0.0).astype(jnp.bfloat16))
    scores, fresh = [], []
    for c in chips:
        keys = jnp.concatenate([keys_ref[c * heads + h] for h in range(heads)], axis=1)
        kn = kn_ref[c].astype(jnp.bfloat16)
        scores.append(lax.dot_general(spreads[c], keys, CONTRACT_LANES, preferred_element_type=jnp.float32))
        fresh.append(lax.dot_general(spreads[c], kn, CONTRACT_LANES, preferred_element_type=jnp.float32))
    weights, fresh_weights, totals = [], [], []
    for c in chips:
        old = jnp.where(live, scores[c] * (HD**-0.5), masked_score)
        new = jnp.where(new_live, fresh[c] * (HD**-0.5), masked_score)
        top = jnp.maximum(jnp.max(old, axis=1, keepdims=True), jnp.max(new, axis=1, keepdims=True))
        old = jnp.where(live, jnp.exp(old - top), 0.0)
        new = jnp.where(new_live, jnp.exp(new - top), 0.0)
        totals.append(jnp.sum(old, axis=1, keepdims=True) + jnp.sum(new, axis=1, keepdims=True))
        weights.append(old.astype(jnp.bfloat16))
        fresh_weights.append(new.astype(jnp.bfloat16))
    wait_all(fetches)
    for c in chips:
        values = lanes_of(values_buf[c])
        vn = vn_ref[c].astype(jnp.bfloat16)
        mixed = jnp.dot(weights[c], values, preferred_element_type=jnp.float32)
        mixed = mixed + jnp.dot(fresh_weights[c], vn, preferred_element_type=jnp.float32)
        mixed = jnp.where(own_head, mixed / totals[c], 0.0)
        out = jnp.sum(mixed.reshape(rows, HEAD_BLOCK, lanes), axis=1).astype(out_ref.dtype)
        for t in range(steps):
            for h in range(heads):
                out_ref[t, c * heads + h] = out[2 * t : 2 * t + 2, h * HD : (h + 1) * HD]


def attend(cosine, sine, live, pieces, keys, values):
    count, _, steps = pieces.shape[:3]
    heads, tokens = keys.shape[:2]
    chips = count // 2
    per = heads // chips
    return pl.pallas_call(
        attend_kernel,
        out_shape=jax.ShapeDtypeStruct((steps, heads, 2, HD), jnp.bfloat16),
        in_specs=[VMEM] * 5 + [HBM],
        out_specs=VMEM,
        scratch_shapes=[pltpu.VMEM((chips, per, tokens, HD), jnp.bfloat16)]
        + [pltpu.VMEM((chips, 16, per * HD), jnp.float32)] * 2
        + [pltpu.SemaphoreType.DMA((chips,))],
        compiler_params=pltpu.CompilerParams(vmem_limit_bytes=16 * 2**20),
        cost_estimate=pl.CostEstimate(flops=10**9, bytes_accessed=6 * 10**6, transcendentals=0),
        name="attention",
    )(cosine, sine, live, pieces, keys, in_hbm(values))


def chip_plan(
    count,
    hidden,
    query_key_value_weight,
    adapter_down_maps,
    adapter_up_maps,
    adapter_storage_row,
    request_adapter,
    lengths,
    request_page_table,
    key_value_pool,
):
    me = lax.axis_index("replica")
    steps, req_dev, width = hidden.shape
    heads = width // HD
    holder_count, rank, _ = adapter_down_maps.shape
    pool_pages, page_len = key_value_pool.shape[:2]
    adapter_count = adapter_storage_row.shape[0]

    tokens = pool_pages * page_len
    keys, values = cache_by_head(key_value_pool.reshape(tokens, 2, heads, HD).transpose(0, 2, 1, 3))

    stored = jnp.sum(
        jnp.where(
            request_adapter[:, None] == jnp.arange(adapter_count, dtype=jnp.int32)[None, :],
            adapter_storage_row[None, :],
            0,
        ),
        axis=1,
    )
    stored = jnp.broadcast_to(stored.reshape(count, 1, req_dev), (count, steps, req_dev)).reshape(-1)
    my_lengths = lax.dynamic_slice_in_dim(lengths, me * req_dev, req_dev)

    held = {0: hidden}
    for masks in (range(4, count, 4), (2,), (1,)):
        held.update({k ^ m: trade(v, m, count) for k, v in list(held.items()) for m in masks})
    blocks = [
        held[k].reshape(steps, req_dev, heads, HD).transpose(0, 2, 1, 3) for k in range(count)
    ]
    blocks[0] = in_hbm(blocks[0])

    x, lows = low_of(
        me.astype(jnp.int32).reshape(1), blocks, (stored - me * holder_count)[None, :], adapter_down_maps
    )
    lows = lax.all_to_all(lows, "replica", split_axis=0, concat_axis=0, tiled=True)
    send, base = project(x, query_key_value_weight.transpose(0, 2, 1), count)
    send = update_values(stored[:, None], lows, base, adapter_up_maps.reshape(adapter_count * rank, -1), send)
    pieces = lax.all_to_all(send, "replica", split_axis=0, concat_axis=0, tiled=True)

    cosine, sine = rotation(my_lengths, steps)
    live = live_tokens(my_lengths, request_page_table, pool_pages, page_len).astype(jnp.int32)
    out = attend(cosine, sine, live.reshape(req_dev, tokens), pieces, keys, values)
    return out.transpose(0, 2, 1, 3).reshape(steps, req_dev, width)


def per_device(replicas, *arrays):
    columns = arrays[1].shape[2]
    whole_heads = replicas % 4 == 0 and (2 * columns) % HD == 0 and columns % HD == HD // 2
    plan = chip_plan if whole_heads and arrays[0].shape[1] == 2 else general_plan
    return plan(replicas, *arrays)


def solution(mesh):
    placed = (
        P(None, ("groups", "replica"), None),
        P(None, None, "replica"),
        P("replica", None, None),
        P(None, None, "replica"),
        P(),
        P("groups"),
        P("groups"),
        P(("groups", "replica"), None),
        P(("groups", "replica"), None, None, None),
    )
    return jax.shard_map(
        functools.partial(per_device, mesh.shape["replica"]),
        mesh=mesh,
        in_specs=placed,
        out_specs=P(None, ("groups", "replica"), None),
        check_vma=False,
    )
```

```python
import functools

import jax
import jax.numpy as jnp
from jax import lax
from jax.experimental import pallas as pl
from jax.experimental.pallas import tpu as pltpu
from jax.sharding import PartitionSpec as P

HD = 128
ROWS = 8
HEAD_BLOCK = 8

adapter_scale = 2.0
masked_score = -1e30


def attention_kernel(steps, req_dev, q_ref, k_ref, v_ref, cos_ref, sin_ref, live_ref, kv_ref, out_ref, kn_ref, vn_ref):
    rows = steps * req_dev
    width = q_ref.shape[1]
    lanes = HEAD_BLOCK * HD
    group = rows * HEAD_BLOCK
    cosine = cos_ref[...]
    sine = sin_ref[...]

    def rotated(x):
        pieces = []
        for h in range(HEAD_BLOCK):
            head = x[:, h * HD : (h + 1) * HD]
            pieces.append(head * cosine + pltpu.roll(head, HD // 2, 1) * sine)
        return jnp.concatenate(pieces, axis=1)

    row_head = lax.broadcasted_iota(jnp.int32, (group, lanes), 0) % HEAD_BLOCK
    lane_head = lax.broadcasted_iota(jnp.int32, (group, lanes), 1) // HD
    own_head = row_head == lane_head
    row_j = lax.broadcasted_iota(jnp.int32, (group, 16), 0) // HEAD_BLOCK
    new_j = lax.broadcasted_iota(jnp.int32, (group, 16), 1)
    new_live = (new_j < rows) & (new_j % req_dev == row_j % req_dev) & (new_j // req_dev <= row_j // req_dev)
    live_all = live_ref[...]
    live = jnp.concatenate(
        [
            jnp.broadcast_to(live_all[j % req_dev : j % req_dev + 1], (HEAD_BLOCK, live_all.shape[1]))
            for j in range(rows)
        ],
        axis=0,
    )
    live = live > 0
    kn_ref[...] = jnp.zeros_like(kn_ref)
    vn_ref[...] = jnp.zeros_like(vn_ref)
    contract_lanes = (((1,), (1,)), ((), ()))
    for c in range(width // lanes):
        cols = slice(c * lanes, (c + 1) * lanes)
        query = rotated(q_ref[:, cols].astype(jnp.float32))
        key_new = rotated(k_ref[:, cols].astype(jnp.float32))
        kn_ref[0:8] = key_new
        vn_ref[0:8] = v_ref[:, cols].astype(jnp.float32)
        kn = kn_ref[...].astype(jnp.bfloat16)
        vn = vn_ref[...].astype(jnp.bfloat16)
        spread = jnp.concatenate(
            [jnp.broadcast_to(query[j : j + 1], (HEAD_BLOCK, lanes)) for j in range(rows)], axis=0
        )
        spread = jnp.where(own_head, spread, 0.0).astype(jnp.bfloat16)
        kv = kv_ref[:, cols]
        scores = lax.dot_general(spread, kv, contract_lanes, preferred_element_type=jnp.float32) * (HD**-0.5)
        scores = jnp.where(live, scores, masked_score)
        fresh = lax.dot_general(spread, kn, contract_lanes, preferred_element_type=jnp.float32) * (HD**-0.5)
        fresh = jnp.where(new_live, fresh, masked_score)
        top = jnp.maximum(jnp.max(scores, axis=1, keepdims=True), jnp.max(fresh, axis=1, keepdims=True))
        weights = jnp.where(live, jnp.exp(scores - top), 0.0)
        fresh = jnp.where(new_live, jnp.exp(fresh - top), 0.0)
        totals = jnp.sum(weights, axis=1, keepdims=True) + jnp.sum(fresh, axis=1, keepdims=True)
        weights = pltpu.roll(weights, 1, 1).astype(jnp.bfloat16)
        mixed = jnp.dot(weights, kv, preferred_element_type=jnp.float32)
        mixed = mixed + jnp.dot(fresh.astype(jnp.bfloat16), vn, preferred_element_type=jnp.float32)
        mixed = jnp.where(own_head, mixed / totals, 0.0)
        out = jnp.sum(mixed.reshape(rows, HEAD_BLOCK, lanes), axis=1)
        out_ref[:, cols] = out.astype(out_ref.dtype)


def attention(steps, req_dev, q, k, v, cosine, sine, live, kv):
    rows = steps * req_dev
    width = q.shape[1]
    vmem = pl.BlockSpec(memory_space=pltpu.VMEM)
    return pl.pallas_call(
        functools.partial(attention_kernel, steps, req_dev),
        out_shape=jax.ShapeDtypeStruct((rows, width), jnp.bfloat16),
        in_specs=[vmem] * 7,
        out_specs=vmem,
        scratch_shapes=[pltpu.VMEM((16, HEAD_BLOCK * HD), jnp.float32)] * 2,
        compiler_params=pltpu.CompilerParams(vmem_limit_bytes=32 * 2**20),
        cost_estimate=pl.CostEstimate(flops=10**9, bytes_accessed=6 * 10**6, transcendentals=0),
        name="attention",
    )(q, k, v, cosine, sine, live, kv)


def rotation(my_lengths, steps):
    rows = steps * my_lengths.shape[0]
    positions = (my_lengths[None, :] + jnp.arange(steps, dtype=jnp.int32)[:, None]).reshape(rows)
    positions = jnp.pad(positions, (0, ROWS - rows))
    half = HD // 2
    frequency = jnp.exp(jnp.arange(half, dtype=jnp.float32) * (-2.0 * jnp.log(10000.0) / HD))
    angles = positions.astype(jnp.float32)[:, None] * frequency[None, :]
    cosine = jnp.cos(angles)
    sine = jnp.sin(angles)
    cosine = jnp.concatenate([cosine, cosine], axis=1)
    sine = jnp.concatenate([-sine, sine], axis=1)
    return cosine, sine


def live_tokens(my_lengths, request_page_table, pool_pages, page_len):
    pages = jnp.arange(pool_pages, dtype=jnp.int32)
    max_pages = request_page_table.shape[1]
    place = jnp.max(
        jnp.where(
            request_page_table[:, :, None] == pages[None, None, :],
            jnp.arange(max_pages, dtype=jnp.int32)[None, :, None],
            -1,
        ),
        axis=1,
    )
    token = place[:, :, None] * page_len + jnp.arange(page_len, dtype=jnp.int32)[None, None, :]
    return (place[:, :, None] >= 0) & (token < my_lengths[:, None, None])


def live_rows(my_lengths, request_page_table, pool_pages, page_len):
    alive = live_tokens(my_lengths, request_page_table, pool_pages, page_len)
    live = jnp.stack([alive, jnp.zeros_like(alive)], axis=-1).astype(jnp.int32)
    return live.reshape(request_page_table.shape[0], pool_pages * page_len * 2)


def general_plan(
    replicas,
    hidden,
    query_key_value_weight,
    adapter_down_maps,
    adapter_up_maps,
    adapter_storage_row,
    request_adapter,
    lengths,
    request_page_table,
    key_value_pool,
):
    my_index = lax.axis_index("replica")
    steps, req_dev, width = hidden.shape
    rows = steps * req_dev
    columns = query_key_value_weight.shape[2]
    holder_count, rank, _ = adapter_down_maps.shape
    pool_pages, page_len = key_value_pool.shape[:2]
    adapter_count = adapter_storage_row.shape[0]
    chips = replicas // 2
    total = replicas * ROWS

    block = jnp.pad(hidden.reshape(rows, width), ((0, ROWS - rows), (0, 0)))
    same_core = [[2 * chip + core for chip in range(chips)] for core in range(2)]
    mine = lax.all_to_all(
        jnp.broadcast_to(block[None], (chips, ROWS, width)),
        "replica",
        split_axis=0,
        concat_axis=0,
        axis_index_groups=same_core,
        tiled=True,
    )
    other = lax.ppermute(mine, "replica", [(i, i ^ 1) for i in range(replicas)])
    first = my_index % 2 == 0
    gathered = jnp.stack([jnp.where(first, mine, other), jnp.where(first, other, mine)])
    gathered = gathered.reshape(total, width)

    stored_rows = jnp.sum(
        jnp.where(
            request_adapter[:, None] == jnp.arange(adapter_count, dtype=jnp.int32)[None, :],
            adapter_storage_row[None, :],
            0,
        ),
        axis=1,
    )
    by_block = stored_rows.reshape(chips, 2, 1, req_dev).transpose(1, 0, 2, 3)
    by_block = jnp.broadcast_to(by_block, (2, chips, steps, req_dev)).reshape(2, chips, rows)
    row_stored = jnp.pad(by_block, ((0, 0), (0, 0), (0, ROWS - rows)), constant_values=-1).reshape(total)

    down = jnp.einsum("nd,hfd->nhf", gathered, adapter_down_maps, preferred_element_type=jnp.float32)
    slots = my_index * holder_count + jnp.arange(holder_count, dtype=jnp.int32)
    own = row_stored[:, None] == slots[None, :]
    low = jnp.sum(jnp.where(own[:, :, None], down, 0.0), axis=1).astype(jnp.bfloat16)
    low = jnp.concatenate([low[: total // 2], low[total // 2 :]], axis=1)
    low = lax.all_to_all(
        jnp.broadcast_to(low[None], (replicas,) + low.shape), "replica", split_axis=0, concat_axis=0, tiled=True
    )
    low = jnp.sum(low.astype(jnp.float32), axis=0)
    low = jnp.concatenate([low[:, :rank], low[:, rank:]], axis=0)

    projected = jnp.einsum("nd,idc->nic", gathered, query_key_value_weight, preferred_element_type=jnp.float32)

    def update(first_adapter, maps):
        held = maps.shape[0]
        which = first_adapter + jnp.arange(held, dtype=jnp.int32)
        wide = jnp.where((row_stored[:, None] == which[None, :])[:, :, None], low[:, None, :], 0.0)
        return jnp.dot(
            wide.astype(jnp.bfloat16).reshape(total, held * rank),
            maps.reshape(held * rank, columns),
            preferred_element_type=jnp.float32,
        )

    step_adapters = 64
    if adapter_count <= step_adapters:
        updated = update(0, adapter_up_maps)
    else:
        updated = lax.fori_loop(
            0,
            adapter_count // step_adapters,
            lambda i, sofar: sofar
            + update(
                i * step_adapters,
                lax.dynamic_slice_in_dim(adapter_up_maps, i * step_adapters, step_adapters, 0),
            ),
            jnp.zeros((total, columns), jnp.float32),
        )
    value = projected[:, 2] + adapter_scale * updated
    combined = jnp.concatenate([projected[:, 0], projected[:, 1], value], axis=1).astype(jnp.bfloat16)
    combined = combined.reshape(2, chips, ROWS, 3 * columns).transpose(1, 0, 2, 3)
    combined = combined.reshape(replicas, ROWS, 3 * columns)
    arrived = lax.all_to_all(combined, "replica", split_axis=0, concat_axis=0, tiled=True)
    arrived = arrived.reshape(replicas, ROWS, 3, columns).transpose(2, 1, 0, 3).reshape(3, ROWS, width)

    my_lengths = lax.dynamic_slice_in_dim(lengths, my_index * req_dev, req_dev)
    cosine, sine = rotation(my_lengths, steps)
    live = live_rows(my_lengths, request_page_table, pool_pages, page_len)
    kv = key_value_pool.reshape(pool_pages * page_len * 2, width)
    out = attention(steps, req_dev, arrived[0], arrived[1], arrived[2], cosine, sine, live, kv)
    return out.reshape(steps, req_dev, width)


def trade(value, mask, count):
    return lax.ppermute(value, "replica", [(i, i ^ mask) for i in range(count)])


CONTRACT_LANES = (((1,), (1,)), ((), ()))


def in_hbm(x):
    return pltpu.with_memory_space_constraint(x, pltpu.HBM)


VMEM = pl.BlockSpec(memory_space=pltpu.VMEM)
HBM = pl.BlockSpec(memory_space=pltpu.HBM)
SMEM = pl.BlockSpec(memory_space=pltpu.SMEM)
ANY = pl.BlockSpec(memory_space=pl.ANY)


def start_all(copies):
    for copy in copies:
        copy.start()
    return copies


def wait_all(copies):
    for copy in copies:
        copy.wait()


CACHE_PARTS = 4


def cache_kernel(pool_ref, keys_ref, values_ref, raw, values, sem, out_sem):
    heads, tokens = raw.shape[:2]
    copies = start_all([pltpu.make_async_copy(pool_ref.at[:, h], raw.at[h], sem.at[h]) for h in range(heads)])
    rows = raw.reshape(heads, 2 * tokens, HD)
    to = lax.broadcasted_iota(jnp.int32, (2 * tokens, 2 * tokens), 0)
    source = lax.broadcasted_iota(jnp.int32, (2 * tokens, 2 * tokens), 1)
    wanted = jnp.where(to < tokens, 2 * to, 2 * (to - tokens) + 1)
    pick = jnp.where(source == wanted, 1.0, 0.0).astype(jnp.bfloat16)
    sent = []
    part = heads // CACHE_PARTS
    for p in range(CACHE_PARTS):
        wait_all(copies[p * part : (p + 1) * part])
        for h in range(p * part, (p + 1) * part, 2):
            both = jnp.concatenate([rows[h], rows[h + 1]], axis=1)
            made = jnp.dot(pick, both, preferred_element_type=jnp.float32).astype(jnp.bfloat16)
            for i in range(2):
                keys_ref[h + i] = made[:tokens, i * HD : (i + 1) * HD]
                values[h + i] = made[tokens:, i * HD : (i + 1) * HD]
        span = slice(p * part, (p + 1) * part)
        sent += start_all([pltpu.make_async_copy(values.at[span], values_ref.at[span], out_sem.at[p])])
    wait_all(sent)


def cache_by_head(pool):
    tokens, heads = pool.shape[:2]
    return pl.pallas_call(
        cache_kernel,
        out_shape=(
            jax.ShapeDtypeStruct((heads, tokens, HD), pool.dtype),
            pltpu.HBM((heads, tokens, HD), pool.dtype),
        ),
        in_specs=[HBM],
        out_specs=(VMEM, HBM),
        scratch_shapes=[
            pltpu.VMEM((heads, tokens, 2, HD), pool.dtype),
            pltpu.VMEM((heads, tokens, HD), pool.dtype),
            pltpu.SemaphoreType.DMA((heads,)),
            pltpu.SemaphoreType.DMA((CACHE_PARTS,)),
        ],
        compiler_params=pltpu.CompilerParams(vmem_limit_bytes=16 * 2**20),
        cost_estimate=pl.CostEstimate(flops=0, bytes_accessed=12 * 10**6, transcendentals=0),
        name="cache_by_head",
    )(in_hbm(pool))


def lanes_of(x):
    return jnp.concatenate([x[c] for c in range(x.shape[0])], axis=1)


def low_kernel(count, me_ref, slot_ref, down_ref, *refs):
    blocks, (x_ref, low_ref, x_buf, maps, made_ref, sem, low_sem, down_sem, own_sem) = refs[:count], refs[count:]
    me = me_ref[0]
    steps = blocks[0].shape[0]
    holders, rank, width = down_ref.shape
    fetches = start_all(
        [pltpu.make_async_copy(down_ref.at[h], maps.at[h], down_sem.at[h]) for h in range(holders)]
    )
    copies = []
    for k, block in enumerate(blocks):
        for t in range(steps):
            copies.append(
                pltpu.make_async_copy(block.at[t], x_buf.at[:, (me ^ k) * steps + t], sem.at[k * steps + t])
            )
    wait_all(start_all(copies))
    keep = pltpu.make_async_copy(x_buf, x_ref, own_sem)
    keep.start()
    chunks, pairs = x_buf.shape[:2]
    rows = 2 * pairs
    x = lanes_of(x_buf.reshape(chunks, rows, HD))
    wait_all(fetches)
    made = lax.dot_general(
        maps.reshape(holders * rank, width)[...], x, CONTRACT_LANES, preferred_element_type=jnp.float32
    )
    slot = slot_ref[...]
    low = jnp.zeros((rank, rows), jnp.float32)
    for h in range(holders):
        low = low + jnp.where(slot == h, made[h * rank : (h + 1) * rank], 0.0)
    low = low.T
    made_ref[...] = jnp.concatenate([low[: rows // 2], low[rows // 2 :]], axis=1).astype(made_ref.dtype)
    wait_all(start_all([pltpu.make_async_copy(made_ref, low_ref.at[k], low_sem.at[k]) for k in range(count)]))
    keep.wait()


def low_of(me, blocks, slot, down):
    count = len(blocks)
    steps, chunks = blocks[0].shape[:2]
    rows = count * steps * 2
    rank = down.shape[1]
    return pl.pallas_call(
        functools.partial(low_kernel, count),
        out_shape=(
            pltpu.HBM((chunks, rows // 2, 2, HD), jnp.bfloat16),
            pltpu.HBM((count, rows // 2, 2 * rank), jnp.bfloat16),
        ),
        in_specs=[SMEM, VMEM, HBM] + [ANY] * count,
        out_specs=(HBM, HBM),
        scratch_shapes=[
            pltpu.VMEM((chunks, rows // 2, 2, HD), jnp.bfloat16),
            pltpu.VMEM(down.shape, jnp.bfloat16),
            pltpu.VMEM((rows // 2, 2 * rank), jnp.bfloat16),
            pltpu.SemaphoreType.DMA((count * steps,)),
            pltpu.SemaphoreType.DMA((count,)),
            pltpu.SemaphoreType.DMA((down.shape[0],)),
            pltpu.SemaphoreType.DMA,
        ],
        compiler_params=pltpu.CompilerParams(vmem_limit_bytes=16 * 2**20),
        cost_estimate=pl.CostEstimate(flops=10**8, bytes_accessed=4 * 10**6, transcendentals=0),
        name="low_rows",
    )(me, slot, in_hbm(down), *blocks)


def put_chunks(buf, first, value):
    wide = value.shape[1]
    for c in range(-(-wide // HD)):
        part = value[:, c * HD : min((c + 1) * HD, wide)]
        if part.shape[1] < HD:
            part = jnp.concatenate([part, jnp.zeros((part.shape[0], HD - part.shape[1]), part.dtype)], axis=1)
        buf[first + c] = part.astype(buf.dtype)


def send_blocks(buf, out_ref, first, sem):
    count, _, steps = out_ref.shape[:3]
    chunks = buf.shape[0]
    return start_all(
        [
            pltpu.make_async_copy(
                buf.at[:, k * steps : (k + 1) * steps], out_ref.at[k, first : first + chunks], sem.at[k]
            )
            for k in range(count)
        ]
    )


PROJECT_CHUNK = 512
PROJECT_AHEAD = 3


def project_kernel(
    stored_ref, x_ref, w_ref, up_ref, send_ref, base_ref, maps_ref, x_buf, w_buf, total, buf, base, x_sem, w_sem, sem, base_sem, up_sem
):
    chunks, pairs = x_buf.shape[:2]
    rows = 2 * pairs
    columns, width = w_ref.shape[1:]
    parts = width // PROJECT_CHUNK
    per = PROJECT_CHUNK // HD
    fetch_x = pltpu.make_async_copy(x_ref, x_buf, x_sem)
    fetch_x.start()
    fetches = [
        pltpu.make_async_copy(w_ref.at[:, :, p * PROJECT_CHUNK : (p + 1) * PROJECT_CHUNK], w_buf.at[p], w_sem.at[p])
        for p in range(parts)
    ]
    start_all(fetches[:PROJECT_AHEAD])
    rank = up_ref.shape[1]
    maps = start_all(
        [
            pltpu.make_async_copy(up_ref.at[stored_ref[q]], maps_ref.at[q * rank : (q + 1) * rank], up_sem.at[q])
            for q in range(stored_ref.shape[0])
        ]
    )
    fetch_x.wait()
    x_rows = x_buf.reshape(chunks, rows, HD)
    for p in range(parts):
        fetches[p].wait()
        start_all(fetches[p + PROJECT_AHEAD : p + PROJECT_AHEAD + 1])
        x = jnp.concatenate([x_rows[c] for c in range(p * per, (p + 1) * per)], axis=1)
        for i in range(3):
            made = lax.dot_general(w_buf[p, i], x, CONTRACT_LANES, preferred_element_type=jnp.float32)
            total[i] = made if p == 0 else total[i] + made
    each = buf.shape[0] // 2
    flat = buf.reshape(buf.shape[0], rows, HD)
    for i in range(2):
        put_chunks(flat, i * each, total[i].T)
    sent = send_blocks(buf, send_ref, 0, sem)
    base[...] = total[2].T
    keep = pltpu.make_async_copy(base, base_ref, base_sem)
    keep.start()
    wait_all(sent)
    keep.wait()
    wait_all(maps)


def project(stored, x, weight, up, count):
    chunks, pairs = x.shape[:2]
    columns, width = weight.shape[1:]
    each = -(-columns // HD)
    parts = width // PROJECT_CHUNK
    return pl.pallas_call(
        project_kernel,
        out_shape=(
            pltpu.HBM((count, 3 * each, pairs // count, 2, HD), jnp.bfloat16),
            pltpu.HBM((2 * pairs, columns), jnp.float32),
            pltpu.VMEM((stored.shape[0] * up.shape[1], columns), up.dtype),
        ),
        in_specs=[SMEM, HBM, HBM, HBM],
        out_specs=(HBM, HBM, VMEM),
        scratch_shapes=[
            pltpu.VMEM(x.shape, jnp.bfloat16),
            pltpu.VMEM((parts, 3, columns, PROJECT_CHUNK), jnp.bfloat16),
            pltpu.VMEM((3, columns, 2 * pairs), jnp.float32),
            pltpu.VMEM((2 * each, pairs, 2, HD), jnp.bfloat16),
            pltpu.VMEM((2 * pairs, columns), jnp.float32),
            pltpu.SemaphoreType.DMA,
            pltpu.SemaphoreType.DMA((parts,)),
            pltpu.SemaphoreType.DMA((count,)),
            pltpu.SemaphoreType.DMA,
            pltpu.SemaphoreType.DMA((stored.shape[0],)),
        ],
        compiler_params=pltpu.CompilerParams(vmem_limit_bytes=24 * 2**20),
        cost_estimate=pl.CostEstimate(flops=10**9, bytes_accessed=11 * 10**6, transcendentals=0),
        name="project",
    )(stored, in_hbm(x), in_hbm(weight), in_hbm(up))


def update_kernel(low_ref, base_ref, maps_ref, send_in, send_ref, base, buf, base_sem, sem):
    count, half, packed = low_ref.shape
    rank = packed // 2
    rows = 2 * half
    per = rows // count
    fetch_base = pltpu.make_async_copy(base_ref, base, base_sem)
    fetch_base.start()
    low = low_ref[0].astype(jnp.float32)
    for s in range(1, count):
        low = low + low_ref[s].astype(jnp.float32)
    low = jnp.concatenate([low[:, :rank], low[:, rank:]], axis=0)
    batch = 256 // rank
    spread = jnp.concatenate([low] * batch, axis=1)
    row = lax.broadcasted_iota(jnp.int32, (rows, batch * rank), 0)
    which = lax.broadcasted_iota(jnp.int32, (rows, batch * rank), 1) // rank
    ahead = (row // per) * 2 + row % 2 - which
    total = jnp.zeros(base.shape, jnp.float32)
    for a in range(0, maps_ref.shape[0] // rank, batch):
        wide = jnp.where(ahead == a, spread, 0.0).astype(jnp.bfloat16)
        total = total + jnp.dot(wide, maps_ref[a * rank : (a + batch) * rank], preferred_element_type=jnp.float32)
    fetch_base.wait()
    put_chunks(buf.reshape(buf.shape[0], rows, HD), 0, base[...] + adapter_scale * total)
    wait_all(send_blocks(buf, send_ref, send_ref.shape[1] - buf.shape[0], sem))


def update_values(lows, base, maps, send):
    count, chunks = send.shape[:2]
    rows, columns = base.shape
    return pl.pallas_call(
        update_kernel,
        out_shape=pltpu.HBM(send.shape, send.dtype),
        in_specs=[VMEM, HBM, VMEM, HBM],
        out_specs=HBM,
        scratch_shapes=[
            pltpu.VMEM(base.shape, jnp.float32),
            pltpu.VMEM((chunks // 3, rows // 2, 2, HD), jnp.bfloat16),
            pltpu.SemaphoreType.DMA,
            pltpu.SemaphoreType.DMA((count,)),
        ],
        input_output_aliases={3: 0},
        compiler_params=pltpu.CompilerParams(vmem_limit_bytes=8 * 2**20),
        cost_estimate=pl.CostEstimate(flops=3 * 10**8, bytes_accessed=4 * 10**6, transcendentals=0),
        name="update_values",
    )(lows, in_hbm(base), maps, in_hbm(send))


def attend_kernel(cos_ref, sin_ref, live_ref, pieces_ref, keys_ref, values_ref, out_ref, values_buf, kn_ref, vn_ref, sem):
    count, _, steps = pieces_ref.shape[:3]
    rows = 2 * steps
    each = pieces_ref.shape[1] // 3
    heads = 2 * out_ref.shape[1] // count
    lanes = heads * HD
    group = rows * HEAD_BLOCK
    chips = range(count // 2)
    fetches = start_all(
        [
            pltpu.make_async_copy(values_ref.at[c * heads : (c + 1) * heads], values_buf.at[c], sem.at[c])
            for c in chips
        ]
    )
    cosine = cos_ref[...][:rows]
    sine = sin_ref[...][:rows]
    left = lax.broadcasted_iota(jnp.int32, (rows, HD), 1) < HD // 2

    def chip_columns(chip, at):
        low = [pieces_ref[2 * chip, at + c].reshape(rows, HD).astype(jnp.float32) for c in range(each)]
        high = [pieces_ref[2 * chip + 1, at + c].reshape(rows, HD).astype(jnp.float32) for c in range(each)]
        high = [pltpu.roll(x, HD // 2, 1) for x in high]
        whole = low[:-1] + [jnp.where(left, low[-1], high[0])]
        return whole + [jnp.where(left, a, b) for a, b in zip(high[:-1], high[1:])]

    def rotated(parts):
        return [x * cosine + pltpu.roll(x, HD // 2, 1) * sine for x in parts]

    row_head = lax.broadcasted_iota(jnp.int32, (group, lanes), 0) % HEAD_BLOCK
    lane_head = lax.broadcasted_iota(jnp.int32, (group, lanes), 1) // HD
    own_head = row_head == lane_head
    row_j = lax.broadcasted_iota(jnp.int32, (group, 16), 0) // HEAD_BLOCK
    new_j = lax.broadcasted_iota(jnp.int32, (group, 16), 1)
    new_live = (new_j < rows) & (new_j % 2 == row_j % 2) & (new_j // 2 <= row_j // 2)
    live = jnp.concatenate(
        [
            jnp.broadcast_to(live_ref[j % 2 : j % 2 + 1, :], (HEAD_BLOCK, live_ref.shape[1]))
            for j in range(rows)
        ],
        axis=0,
    )
    live = live > 0
    kn_ref[...] = jnp.zeros_like(kn_ref)
    vn_ref[...] = jnp.zeros_like(vn_ref)
    spreads = []
    for c in chips:
        query = jnp.concatenate(rotated(chip_columns(c, 0)), axis=1)
        kn_ref[c, 0:rows] = jnp.concatenate(rotated(chip_columns(c, each)), axis=1)
        vn_ref[c, 0:rows] = jnp.concatenate(chip_columns(c, 2 * each), axis=1)
        spread = jnp.concatenate(
            [jnp.broadcast_to(query[j : j + 1], (HEAD_BLOCK, lanes)) for j in range(rows)], axis=0
        )
        spreads.append(jnp.where(own_head, spread, 0.0).astype(jnp.bfloat16))
    scores, fresh = [], []
    for c in chips:
        keys = jnp.concatenate([keys_ref[c * heads + h] for h in range(heads)], axis=1)
        kn = kn_ref[c].astype(jnp.bfloat16)
        scores.append(lax.dot_general(spreads[c], keys, CONTRACT_LANES, preferred_element_type=jnp.float32))
        fresh.append(lax.dot_general(spreads[c], kn, CONTRACT_LANES, preferred_element_type=jnp.float32))
    weights, fresh_weights, totals = [], [], []
    for c in chips:
        old = jnp.where(live, scores[c] * (HD**-0.5), masked_score)
        new = jnp.where(new_live, fresh[c] * (HD**-0.5), masked_score)
        top = jnp.maximum(jnp.max(old, axis=1, keepdims=True), jnp.max(new, axis=1, keepdims=True))
        old = jnp.where(live, jnp.exp(old - top), 0.0)
        new = jnp.where(new_live, jnp.exp(new - top), 0.0)
        totals.append(jnp.sum(old, axis=1, keepdims=True) + jnp.sum(new, axis=1, keepdims=True))
        weights.append(old.astype(jnp.bfloat16))
        fresh_weights.append(new.astype(jnp.bfloat16))
    wait_all(fetches)
    for c in chips:
        values = lanes_of(values_buf[c])
        vn = vn_ref[c].astype(jnp.bfloat16)
        mixed = jnp.dot(weights[c], values, preferred_element_type=jnp.float32)
        mixed = mixed + jnp.dot(fresh_weights[c], vn, preferred_element_type=jnp.float32)
        mixed = jnp.where(own_head, mixed / totals[c], 0.0)
        out = jnp.sum(mixed.reshape(rows, HEAD_BLOCK, lanes), axis=1).astype(out_ref.dtype)
        for t in range(steps):
            for h in range(heads):
                out_ref[t, c * heads + h] = out[2 * t : 2 * t + 2, h * HD : (h + 1) * HD]


def attend(cosine, sine, live, pieces, keys, values):
    count, _, steps = pieces.shape[:3]
    heads, tokens = keys.shape[:2]
    chips = count // 2
    per = heads // chips
    return pl.pallas_call(
        attend_kernel,
        out_shape=jax.ShapeDtypeStruct((steps, heads, 2, HD), jnp.bfloat16),
        in_specs=[VMEM] * 5 + [HBM],
        out_specs=VMEM,
        scratch_shapes=[pltpu.VMEM((chips, per, tokens, HD), jnp.bfloat16)]
        + [pltpu.VMEM((chips, 16, per * HD), jnp.float32)] * 2
        + [pltpu.SemaphoreType.DMA((chips,))],
        compiler_params=pltpu.CompilerParams(vmem_limit_bytes=16 * 2**20),
        cost_estimate=pl.CostEstimate(flops=10**9, bytes_accessed=6 * 10**6, transcendentals=0),
        name="attention",
    )(cosine, sine, live, pieces, keys, in_hbm(values))


def chip_plan(
    count,
    hidden,
    query_key_value_weight,
    adapter_down_maps,
    adapter_up_maps,
    adapter_storage_row,
    request_adapter,
    lengths,
    request_page_table,
    key_value_pool,
):
    me = lax.axis_index("replica")
    steps, req_dev, width = hidden.shape
    heads = width // HD
    holder_count, rank, _ = adapter_down_maps.shape
    pool_pages, page_len = key_value_pool.shape[:2]
    adapter_count = adapter_storage_row.shape[0]

    tokens = pool_pages * page_len
    keys, values = cache_by_head(key_value_pool.reshape(tokens, 2, heads, HD).transpose(0, 2, 1, 3))

    held = {m: trade(hidden, m, count) for m in range(8, count, 4)}
    held[1] = trade(hidden, 1, count)
    held[0], held[1] = lax.optimization_barrier((hidden, held[1]))
    held[4] = trade(held[0], 4, count)
    held[2] = trade(held[0], 2, count)
    held.update({m | 2: trade(held[m], 2, count) for m in range(4, count, 4)})
    held.update({m | 1: trade(held[m], 1, count) for m in range(2, count, 2)})
    blocks = [
        held[k].reshape(steps, req_dev, heads, HD).transpose(0, 2, 1, 3) for k in range(count)
    ]
    blocks[0] = in_hbm(blocks[0])

    stored = jnp.sum(
        jnp.where(
            request_adapter[:, None] == jnp.arange(adapter_count, dtype=jnp.int32)[None, :],
            adapter_storage_row[None, :],
            0,
        ),
        axis=1,
    )
    slot = (stored - me * holder_count).reshape(count, 1, req_dev)
    slot = jnp.broadcast_to(slot, (count, steps, req_dev)).reshape(1, -1)

    x, lows = low_of(me.astype(jnp.int32).reshape(1), blocks, slot, adapter_down_maps)
    lows = lax.all_to_all(lows, "replica", split_axis=0, concat_axis=0, tiled=True)
    send, base, maps = project(stored, x, query_key_value_weight.transpose(0, 2, 1), adapter_up_maps, count)
    send = update_values(lows, base, maps, send)
    pieces = lax.all_to_all(send, "replica", split_axis=0, concat_axis=0, tiled=True)

    my_lengths = lax.dynamic_slice_in_dim(lengths, me * req_dev, req_dev)
    cosine, sine = rotation(my_lengths, steps)
    live = live_tokens(my_lengths, request_page_table, pool_pages, page_len).astype(jnp.int32)
    out = attend(cosine, sine, live.reshape(req_dev, tokens), pieces, keys, values)
    return out.transpose(0, 2, 1, 3).reshape(steps, req_dev, width)


def per_device(replicas, *arrays):
    columns = arrays[1].shape[2]
    whole_heads = replicas % 4 == 0 and (2 * columns) % HD == 0 and columns % HD == HD // 2
    plan = chip_plan if whole_heads and arrays[0].shape[1] == 2 else general_plan
    return plan(replicas, *arrays)


def solution(mesh):
    placed = (
        P(None, ("groups", "replica"), None),
        P(None, None, "replica"),
        P("replica", None, None),
        P(None, None, "replica"),
        P(),
        P("groups"),
        P("groups"),
        P(("groups", "replica"), None),
        P(("groups", "replica"), None, None, None),
    )
    return jax.shard_map(
        functools.partial(per_device, mesh.shape["replica"]),
        mesh=mesh,
        in_specs=placed,
        out_specs=P(None, ("groups", "replica"), None),
        check_vma=False,
    )
```

```python
import functools

import jax
import jax.numpy as jnp
from jax import lax
from jax.experimental import pallas as pl
from jax.experimental.pallas import tpu as pltpu
from jax.sharding import PartitionSpec as P

HD = 128
ROWS = 8
HEAD_BLOCK = 8

adapter_scale = 2.0
masked_score = -1e30


def attention_kernel(steps, req_dev, q_ref, k_ref, v_ref, cos_ref, sin_ref, live_ref, kv_ref, out_ref, kn_ref, vn_ref):
    rows = steps * req_dev
    width = q_ref.shape[1]
    lanes = HEAD_BLOCK * HD
    group = rows * HEAD_BLOCK
    cosine = cos_ref[...]
    sine = sin_ref[...]

    def rotated(x):
        pieces = []
        for h in range(HEAD_BLOCK):
            head = x[:, h * HD : (h + 1) * HD]
            pieces.append(head * cosine + pltpu.roll(head, HD // 2, 1) * sine)
        return jnp.concatenate(pieces, axis=1)

    row_head = lax.broadcasted_iota(jnp.int32, (group, lanes), 0) % HEAD_BLOCK
    lane_head = lax.broadcasted_iota(jnp.int32, (group, lanes), 1) // HD
    own_head = row_head == lane_head
    row_j = lax.broadcasted_iota(jnp.int32, (group, 16), 0) // HEAD_BLOCK
    new_j = lax.broadcasted_iota(jnp.int32, (group, 16), 1)
    new_live = (new_j < rows) & (new_j % req_dev == row_j % req_dev) & (new_j // req_dev <= row_j // req_dev)
    live_all = live_ref[...]
    live = jnp.concatenate(
        [
            jnp.broadcast_to(live_all[j % req_dev : j % req_dev + 1], (HEAD_BLOCK, live_all.shape[1]))
            for j in range(rows)
        ],
        axis=0,
    )
    live = live > 0
    kn_ref[...] = jnp.zeros_like(kn_ref)
    vn_ref[...] = jnp.zeros_like(vn_ref)
    contract_lanes = (((1,), (1,)), ((), ()))
    for c in range(width // lanes):
        cols = slice(c * lanes, (c + 1) * lanes)
        query = rotated(q_ref[:, cols].astype(jnp.float32))
        key_new = rotated(k_ref[:, cols].astype(jnp.float32))
        kn_ref[0:8] = key_new
        vn_ref[0:8] = v_ref[:, cols].astype(jnp.float32)
        kn = kn_ref[...].astype(jnp.bfloat16)
        vn = vn_ref[...].astype(jnp.bfloat16)
        spread = jnp.concatenate(
            [jnp.broadcast_to(query[j : j + 1], (HEAD_BLOCK, lanes)) for j in range(rows)], axis=0
        )
        spread = jnp.where(own_head, spread, 0.0).astype(jnp.bfloat16)
        kv = kv_ref[:, cols]
        scores = lax.dot_general(spread, kv, contract_lanes, preferred_element_type=jnp.float32) * (HD**-0.5)
        scores = jnp.where(live, scores, masked_score)
        fresh = lax.dot_general(spread, kn, contract_lanes, preferred_element_type=jnp.float32) * (HD**-0.5)
        fresh = jnp.where(new_live, fresh, masked_score)
        top = jnp.maximum(jnp.max(scores, axis=1, keepdims=True), jnp.max(fresh, axis=1, keepdims=True))
        weights = jnp.where(live, jnp.exp(scores - top), 0.0)
        fresh = jnp.where(new_live, jnp.exp(fresh - top), 0.0)
        totals = jnp.sum(weights, axis=1, keepdims=True) + jnp.sum(fresh, axis=1, keepdims=True)
        weights = pltpu.roll(weights, 1, 1).astype(jnp.bfloat16)
        mixed = jnp.dot(weights, kv, preferred_element_type=jnp.float32)
        mixed = mixed + jnp.dot(fresh.astype(jnp.bfloat16), vn, preferred_element_type=jnp.float32)
        mixed = jnp.where(own_head, mixed / totals, 0.0)
        out = jnp.sum(mixed.reshape(rows, HEAD_BLOCK, lanes), axis=1)
        out_ref[:, cols] = out.astype(out_ref.dtype)


def attention(steps, req_dev, q, k, v, cosine, sine, live, kv):
    rows = steps * req_dev
    width = q.shape[1]
    vmem = pl.BlockSpec(memory_space=pltpu.VMEM)
    return pl.pallas_call(
        functools.partial(attention_kernel, steps, req_dev),
        out_shape=jax.ShapeDtypeStruct((rows, width), jnp.bfloat16),
        in_specs=[vmem] * 7,
        out_specs=vmem,
        scratch_shapes=[pltpu.VMEM((16, HEAD_BLOCK * HD), jnp.float32)] * 2,
        compiler_params=pltpu.CompilerParams(vmem_limit_bytes=32 * 2**20),
        cost_estimate=pl.CostEstimate(flops=10**9, bytes_accessed=6 * 10**6, transcendentals=0),
        name="attention",
    )(q, k, v, cosine, sine, live, kv)


def rotation(my_lengths, steps):
    rows = steps * my_lengths.shape[0]
    positions = (my_lengths[None, :] + jnp.arange(steps, dtype=jnp.int32)[:, None]).reshape(rows)
    positions = jnp.pad(positions, (0, ROWS - rows))
    half = HD // 2
    frequency = jnp.exp(jnp.arange(half, dtype=jnp.float32) * (-2.0 * jnp.log(10000.0) / HD))
    angles = positions.astype(jnp.float32)[:, None] * frequency[None, :]
    cosine = jnp.cos(angles)
    sine = jnp.sin(angles)
    cosine = jnp.concatenate([cosine, cosine], axis=1)
    sine = jnp.concatenate([-sine, sine], axis=1)
    return cosine, sine


def live_tokens(my_lengths, request_page_table, pool_pages, page_len):
    pages = jnp.arange(pool_pages, dtype=jnp.int32)
    max_pages = request_page_table.shape[1]
    place = jnp.max(
        jnp.where(
            request_page_table[:, :, None] == pages[None, None, :],
            jnp.arange(max_pages, dtype=jnp.int32)[None, :, None],
            -1,
        ),
        axis=1,
    )
    token = place[:, :, None] * page_len + jnp.arange(page_len, dtype=jnp.int32)[None, None, :]
    return (place[:, :, None] >= 0) & (token < my_lengths[:, None, None])


def live_rows(my_lengths, request_page_table, pool_pages, page_len):
    alive = live_tokens(my_lengths, request_page_table, pool_pages, page_len)
    live = jnp.stack([alive, jnp.zeros_like(alive)], axis=-1).astype(jnp.int32)
    return live.reshape(request_page_table.shape[0], pool_pages * page_len * 2)


def general_plan(
    replicas,
    hidden,
    query_key_value_weight,
    adapter_down_maps,
    adapter_up_maps,
    adapter_storage_row,
    request_adapter,
    lengths,
    request_page_table,
    key_value_pool,
):
    my_index = lax.axis_index("replica")
    steps, req_dev, width = hidden.shape
    rows = steps * req_dev
    columns = query_key_value_weight.shape[2]
    holder_count, rank, _ = adapter_down_maps.shape
    pool_pages, page_len = key_value_pool.shape[:2]
    adapter_count = adapter_storage_row.shape[0]
    chips = replicas // 2
    total = replicas * ROWS

    block = jnp.pad(hidden.reshape(rows, width), ((0, ROWS - rows), (0, 0)))
    same_core = [[2 * chip + core for chip in range(chips)] for core in range(2)]
    mine = lax.all_to_all(
        jnp.broadcast_to(block[None], (chips, ROWS, width)),
        "replica",
        split_axis=0,
        concat_axis=0,
        axis_index_groups=same_core,
        tiled=True,
    )
    other = lax.ppermute(mine, "replica", [(i, i ^ 1) for i in range(replicas)])
    first = my_index % 2 == 0
    gathered = jnp.stack([jnp.where(first, mine, other), jnp.where(first, other, mine)])
    gathered = gathered.reshape(total, width)

    stored_rows = jnp.sum(
        jnp.where(
            request_adapter[:, None] == jnp.arange(adapter_count, dtype=jnp.int32)[None, :],
            adapter_storage_row[None, :],
            0,
        ),
        axis=1,
    )
    by_block = stored_rows.reshape(chips, 2, 1, req_dev).transpose(1, 0, 2, 3)
    by_block = jnp.broadcast_to(by_block, (2, chips, steps, req_dev)).reshape(2, chips, rows)
    row_stored = jnp.pad(by_block, ((0, 0), (0, 0), (0, ROWS - rows)), constant_values=-1).reshape(total)

    down = jnp.einsum("nd,hfd->nhf", gathered, adapter_down_maps, preferred_element_type=jnp.float32)
    slots = my_index * holder_count + jnp.arange(holder_count, dtype=jnp.int32)
    own = row_stored[:, None] == slots[None, :]
    low = jnp.sum(jnp.where(own[:, :, None], down, 0.0), axis=1).astype(jnp.bfloat16)
    low = jnp.concatenate([low[: total // 2], low[total // 2 :]], axis=1)
    low = lax.all_to_all(
        jnp.broadcast_to(low[None], (replicas,) + low.shape), "replica", split_axis=0, concat_axis=0, tiled=True
    )
    low = jnp.sum(low.astype(jnp.float32), axis=0)
    low = jnp.concatenate([low[:, :rank], low[:, rank:]], axis=0)

    projected = jnp.einsum("nd,idc->nic", gathered, query_key_value_weight, preferred_element_type=jnp.float32)

    def update(first_adapter, maps):
        held = maps.shape[0]
        which = first_adapter + jnp.arange(held, dtype=jnp.int32)
        wide = jnp.where((row_stored[:, None] == which[None, :])[:, :, None], low[:, None, :], 0.0)
        return jnp.dot(
            wide.astype(jnp.bfloat16).reshape(total, held * rank),
            maps.reshape(held * rank, columns),
            preferred_element_type=jnp.float32,
        )

    step_adapters = 64
    if adapter_count <= step_adapters:
        updated = update(0, adapter_up_maps)
    else:
        updated = lax.fori_loop(
            0,
            adapter_count // step_adapters,
            lambda i, sofar: sofar
            + update(
                i * step_adapters,
                lax.dynamic_slice_in_dim(adapter_up_maps, i * step_adapters, step_adapters, 0),
            ),
            jnp.zeros((total, columns), jnp.float32),
        )
    value = projected[:, 2] + adapter_scale * updated
    combined = jnp.concatenate([projected[:, 0], projected[:, 1], value], axis=1).astype(jnp.bfloat16)
    combined = combined.reshape(2, chips, ROWS, 3 * columns).transpose(1, 0, 2, 3)
    combined = combined.reshape(replicas, ROWS, 3 * columns)
    arrived = lax.all_to_all(combined, "replica", split_axis=0, concat_axis=0, tiled=True)
    arrived = arrived.reshape(replicas, ROWS, 3, columns).transpose(2, 1, 0, 3).reshape(3, ROWS, width)

    my_lengths = lax.dynamic_slice_in_dim(lengths, my_index * req_dev, req_dev)
    cosine, sine = rotation(my_lengths, steps)
    live = live_rows(my_lengths, request_page_table, pool_pages, page_len)
    kv = key_value_pool.reshape(pool_pages * page_len * 2, width)
    out = attention(steps, req_dev, arrived[0], arrived[1], arrived[2], cosine, sine, live, kv)
    return out.reshape(steps, req_dev, width)


def trade(value, mask, count):
    return lax.ppermute(value, "replica", [(i, i ^ mask) for i in range(count)])


CONTRACT_LANES = (((1,), (1,)), ((), ()))


def in_hbm(x):
    return pltpu.with_memory_space_constraint(x, pltpu.HBM)


VMEM = pl.BlockSpec(memory_space=pltpu.VMEM)
HBM = pl.BlockSpec(memory_space=pltpu.HBM)
SMEM = pl.BlockSpec(memory_space=pltpu.SMEM)
ANY = pl.BlockSpec(memory_space=pl.ANY)


def start_all(copies):
    for copy in copies:
        copy.start()
    return copies


def wait_all(copies):
    for copy in copies:
        copy.wait()


CACHE_PARTS = 4


def cache_kernel(pool_ref, keys_ref, values_ref, raw, values, sem, out_sem):
    heads, tokens = raw.shape[:2]
    copies = start_all([pltpu.make_async_copy(pool_ref.at[:, h], raw.at[h], sem.at[h]) for h in range(heads)])
    rows = raw.reshape(heads, 2 * tokens, HD)
    to = lax.broadcasted_iota(jnp.int32, (2 * tokens, 2 * tokens), 0)
    source = lax.broadcasted_iota(jnp.int32, (2 * tokens, 2 * tokens), 1)
    wanted = jnp.where(to < tokens, 2 * to, 2 * (to - tokens) + 1)
    pick = jnp.where(source == wanted, 1.0, 0.0).astype(jnp.bfloat16)
    sent = []
    part = heads // CACHE_PARTS
    for p in range(CACHE_PARTS):
        wait_all(copies[p * part : (p + 1) * part])
        for h in range(p * part, (p + 1) * part, 2):
            both = jnp.concatenate([rows[h], rows[h + 1]], axis=1)
            made = jnp.dot(pick, both, preferred_element_type=jnp.float32).astype(jnp.bfloat16)
            for i in range(2):
                keys_ref[h + i] = made[:tokens, i * HD : (i + 1) * HD]
                values[h + i] = made[tokens:, i * HD : (i + 1) * HD]
        span = slice(p * part, (p + 1) * part)
        sent += start_all([pltpu.make_async_copy(values.at[span], values_ref.at[span], out_sem.at[p])])
    wait_all(sent)


def cache_by_head(pool):
    tokens, heads = pool.shape[:2]
    return pl.pallas_call(
        cache_kernel,
        out_shape=(
            jax.ShapeDtypeStruct((heads, tokens, HD), pool.dtype),
            pltpu.HBM((heads, tokens, HD), pool.dtype),
        ),
        in_specs=[HBM],
        out_specs=(VMEM, HBM),
        scratch_shapes=[
            pltpu.VMEM((heads, tokens, 2, HD), pool.dtype),
            pltpu.VMEM((heads, tokens, HD), pool.dtype),
            pltpu.SemaphoreType.DMA((heads,)),
            pltpu.SemaphoreType.DMA((CACHE_PARTS,)),
        ],
        compiler_params=pltpu.CompilerParams(vmem_limit_bytes=16 * 2**20),
        cost_estimate=pl.CostEstimate(flops=0, bytes_accessed=12 * 10**6, transcendentals=0),
        name="cache_by_head",
    )(in_hbm(pool))


def lanes_of(x):
    return jnp.concatenate([x[c] for c in range(x.shape[0])], axis=1)


def step_rows(x, first, chunks):
    steps, _, count = x.shape[:3]
    flat = x.reshape(steps, x.shape[1], 2 * count, HD)
    return jnp.concatenate(
        [jnp.concatenate([flat[t, c] for c in range(first, first + chunks)], axis=1) for t in range(steps)], axis=0
    )


def low_kernel(count, me_ref, slot_ref, down_ref, *refs):
    blocks, (x_ref, low_ref, x_buf, maps, made_ref, sem, down_sem, x_sem, low_sem) = refs[:count], refs[count:]
    me = me_ref[0]
    holders, rank, width = down_ref.shape
    fetch = pltpu.make_async_copy(down_ref, maps, down_sem)
    fetch.start()
    wait_all(
        start_all(
            [pltpu.make_async_copy(block, x_buf.at[:, :, me ^ k], sem.at[k]) for k, block in enumerate(blocks)]
        )
    )
    keep = pltpu.make_async_copy(x_buf, x_ref, x_sem)
    keep.start()
    x = step_rows(x_buf, 0, x_buf.shape[1])
    rows = x.shape[0]
    fetch.wait()
    made = lax.dot_general(
        maps.reshape(holders * rank, width)[...], x, CONTRACT_LANES, preferred_element_type=jnp.float32
    )
    slot = slot_ref[...]
    low = jnp.zeros((rank, rows), jnp.float32)
    for h in range(holders):
        low = low + jnp.where(slot == h, made[h * rank : (h + 1) * rank], 0.0)
    low = low.T
    low = jnp.concatenate([low[: rows // 2], low[rows // 2 :]], axis=1).astype(made_ref.dtype)
    for k in range(count):
        made_ref[k] = low
    send = pltpu.make_async_copy(made_ref, low_ref, low_sem)
    send.start()
    send.wait()
    keep.wait()


def low_of(me, blocks, slot, down):
    count = len(blocks)
    steps, chunks = blocks[0].shape[:2]
    rows = count * steps * 2
    rank = down.shape[1]
    return pl.pallas_call(
        functools.partial(low_kernel, count),
        out_shape=(
            pltpu.HBM((steps, chunks, count, 2, HD), jnp.bfloat16),
            pltpu.HBM((count, rows // 2, 2 * rank), jnp.bfloat16),
        ),
        in_specs=[SMEM, VMEM, HBM] + [ANY] * count,
        out_specs=(HBM, HBM),
        scratch_shapes=[
            pltpu.VMEM((steps, chunks, count, 2, HD), jnp.bfloat16),
            pltpu.VMEM(down.shape, jnp.bfloat16),
            pltpu.VMEM((count, rows // 2, 2 * rank), jnp.bfloat16),
            pltpu.SemaphoreType.DMA((count,)),
            pltpu.SemaphoreType.DMA,
            pltpu.SemaphoreType.DMA,
            pltpu.SemaphoreType.DMA,
        ],
        compiler_params=pltpu.CompilerParams(vmem_limit_bytes=16 * 2**20),
        cost_estimate=pl.CostEstimate(flops=10**8, bytes_accessed=4 * 10**6, transcendentals=0),
        name="low_rows",
    )(me, slot, in_hbm(down), *blocks)


def put_chunks(buf, first, value):
    steps, count = buf.shape[1:3]
    flat = buf.reshape(buf.shape[0], steps, 2 * count, HD)
    wide = value.shape[1]
    for c in range(-(-wide // HD)):
        part = value[:, c * HD : min((c + 1) * HD, wide)]
        if part.shape[1] < HD:
            part = jnp.concatenate([part, jnp.zeros((part.shape[0], HD - part.shape[1]), part.dtype)], axis=1)
        part = part.astype(buf.dtype)
        for t in range(steps):
            flat[first + c, t] = part[t * 2 * count : (t + 1) * 2 * count]


PROJECT_CHUNK = 1024
PROJECT_AHEAD = 2


def project_kernel(
    stored_ref, x_ref, w_ref, up_ref, early_ref, base_ref, maps_ref, x_buf, w_buf, total, x_sem, w_sem, up_sem
):
    columns, width = w_ref.shape[1:]
    parts = width // PROJECT_CHUNK
    per = PROJECT_CHUNK // HD
    fetch_x = pltpu.make_async_copy(x_ref, x_buf, x_sem)
    fetch_x.start()
    fetches = [
        pltpu.make_async_copy(w_ref.at[:, :, p * PROJECT_CHUNK : (p + 1) * PROJECT_CHUNK], w_buf.at[p], w_sem.at[p])
        for p in range(parts)
    ]
    start_all(fetches[:PROJECT_AHEAD])
    rank = up_ref.shape[1]
    maps = start_all(
        [
            pltpu.make_async_copy(up_ref.at[stored_ref[q]], maps_ref.at[q * rank : (q + 1) * rank], up_sem.at[q])
            for q in range(stored_ref.shape[0])
        ]
    )
    fetch_x.wait()
    for p in range(parts):
        fetches[p].wait()
        start_all(fetches[p + PROJECT_AHEAD : p + PROJECT_AHEAD + 1])
        x = step_rows(x_buf, p * per, per)
        for i in range(3):
            made = lax.dot_general(w_buf[p, i], x, CONTRACT_LANES, preferred_element_type=jnp.float32)
            total[i] = made if p == 0 else total[i] + made
    each = early_ref.shape[0] // 2
    for i in range(2):
        put_chunks(early_ref, i * each, total[i].T)
    base_ref[...] = total[2].T
    wait_all(maps)


def project(stored, x, weight, up):
    steps, _, count = x.shape[:3]
    columns, width = weight.shape[1:]
    each = -(-columns // HD)
    rows = 2 * steps * count
    parts = width // PROJECT_CHUNK
    return pl.pallas_call(
        project_kernel,
        out_shape=(
            pltpu.VMEM((2 * each, steps, count, 2, HD), jnp.bfloat16),
            pltpu.VMEM((rows, columns), jnp.float32),
            pltpu.VMEM((stored.shape[0] * up.shape[1], columns), up.dtype),
        ),
        in_specs=[SMEM, HBM, HBM, HBM],
        out_specs=(VMEM, VMEM, VMEM),
        scratch_shapes=[
            pltpu.VMEM(x.shape, jnp.bfloat16),
            pltpu.VMEM((parts, 3, columns, PROJECT_CHUNK), jnp.bfloat16),
            pltpu.VMEM((3, columns, rows), jnp.float32),
            pltpu.SemaphoreType.DMA,
            pltpu.SemaphoreType.DMA((parts,)),
            pltpu.SemaphoreType.DMA((stored.shape[0],)),
        ],
        compiler_params=pltpu.CompilerParams(vmem_limit_bytes=24 * 2**20),
        cost_estimate=pl.CostEstimate(flops=10**9, bytes_accessed=11 * 10**6, transcendentals=0),
        name="project",
    )(stored, in_hbm(x), in_hbm(weight), in_hbm(up))


def update_kernel(low_ref, early_ref, base_ref, maps_ref, send_ref, buf, sem):
    count, half, packed = low_ref.shape
    rank = packed // 2
    rows = 2 * half
    low = low_ref[0].astype(jnp.float32)
    for s in range(1, count):
        low = low + low_ref[s].astype(jnp.float32)
    low = jnp.concatenate([low[:, :rank], low[:, rank:]], axis=0)
    batch = 256 // rank
    requests = maps_ref.shape[0] // rank
    spread = jnp.concatenate([low] * batch, axis=1)
    row = lax.broadcasted_iota(jnp.int32, (rows, batch * rank), 0)
    which = lax.broadcasted_iota(jnp.int32, (rows, batch * rank), 1) // rank
    ahead = row % requests - which
    total = jnp.zeros(base_ref.shape, jnp.float32)
    for a in range(0, requests, batch):
        wide = jnp.where(ahead == a, spread, 0.0).astype(jnp.bfloat16)
        total = total + jnp.dot(wide, maps_ref[a * rank : (a + batch) * rank], preferred_element_type=jnp.float32)
    early = early_ref.shape[0]
    buf[:early] = early_ref[...]
    put_chunks(buf, early, base_ref[...] + adapter_scale * total)
    wait_all(
        start_all([pltpu.make_async_copy(buf.at[:, :, k], send_ref.at[k], sem.at[k]) for k in range(count)])
    )


def update_values(lows, early, base, maps):
    chunks, steps, count = early.shape[:3]
    chunks = chunks * 3 // 2
    return pl.pallas_call(
        update_kernel,
        out_shape=pltpu.HBM((count, chunks, steps, 2, HD), early.dtype),
        in_specs=[VMEM, VMEM, VMEM, VMEM],
        out_specs=HBM,
        scratch_shapes=[
            pltpu.VMEM((chunks, steps, count, 2, HD), early.dtype),
            pltpu.SemaphoreType.DMA((count,)),
        ],
        compiler_params=pltpu.CompilerParams(vmem_limit_bytes=8 * 2**20),
        cost_estimate=pl.CostEstimate(flops=3 * 10**8, bytes_accessed=4 * 10**6, transcendentals=0),
        name="update_values",
    )(lows, early, base, maps)


def attend_kernel(cos_ref, sin_ref, live_ref, pieces_ref, keys_ref, values_ref, out_ref, values_buf, kn_ref, vn_ref, sem):
    count, _, steps = pieces_ref.shape[:3]
    rows = 2 * steps
    each = pieces_ref.shape[1] // 3
    heads = 2 * out_ref.shape[1] // count
    lanes = heads * HD
    group = rows * HEAD_BLOCK
    chips = range(count // 2)
    fetches = start_all(
        [
            pltpu.make_async_copy(values_ref.at[c * heads : (c + 1) * heads], values_buf.at[c], sem.at[c])
            for c in chips
        ]
    )
    cosine = cos_ref[...][:rows]
    sine = sin_ref[...][:rows]
    left = lax.broadcasted_iota(jnp.int32, (rows, HD), 1) < HD // 2

    def chip_columns(chip, at):
        low = [pieces_ref[2 * chip, at + c].reshape(rows, HD).astype(jnp.float32) for c in range(each)]
        high = [pieces_ref[2 * chip + 1, at + c].reshape(rows, HD).astype(jnp.float32) for c in range(each)]
        high = [pltpu.roll(x, HD // 2, 1) for x in high]
        whole = low[:-1] + [jnp.where(left, low[-1], high[0])]
        return whole + [jnp.where(left, a, b) for a, b in zip(high[:-1], high[1:])]

    def rotated(parts):
        return [x * cosine + pltpu.roll(x, HD // 2, 1) * sine for x in parts]

    row_head = lax.broadcasted_iota(jnp.int32, (group, lanes), 0) % HEAD_BLOCK
    lane_head = lax.broadcasted_iota(jnp.int32, (group, lanes), 1) // HD
    own_head = row_head == lane_head
    row_j = lax.broadcasted_iota(jnp.int32, (group, 16), 0) // HEAD_BLOCK
    new_j = lax.broadcasted_iota(jnp.int32, (group, 16), 1)
    new_live = (new_j < rows) & (new_j % 2 == row_j % 2) & (new_j // 2 <= row_j // 2)
    live = jnp.concatenate(
        [
            jnp.broadcast_to(live_ref[j % 2 : j % 2 + 1, :], (HEAD_BLOCK, live_ref.shape[1]))
            for j in range(rows)
        ],
        axis=0,
    )
    live = live > 0
    kn_ref[...] = jnp.zeros_like(kn_ref)
    vn_ref[...] = jnp.zeros_like(vn_ref)
    spreads = []
    for c in chips:
        query = jnp.concatenate(rotated(chip_columns(c, 0)), axis=1)
        kn_ref[c, 0:rows] = jnp.concatenate(rotated(chip_columns(c, each)), axis=1)
        vn_ref[c, 0:rows] = jnp.concatenate(chip_columns(c, 2 * each), axis=1)
        spread = jnp.concatenate(
            [jnp.broadcast_to(query[j : j + 1], (HEAD_BLOCK, lanes)) for j in range(rows)], axis=0
        )
        spreads.append(jnp.where(own_head, spread, 0.0).astype(jnp.bfloat16))
    scores, fresh = [], []
    for c in chips:
        keys = jnp.concatenate([keys_ref[c * heads + h] for h in range(heads)], axis=1)
        kn = kn_ref[c].astype(jnp.bfloat16)
        scores.append(lax.dot_general(spreads[c], keys, CONTRACT_LANES, preferred_element_type=jnp.float32))
        fresh.append(lax.dot_general(spreads[c], kn, CONTRACT_LANES, preferred_element_type=jnp.float32))
    weights, fresh_weights, totals = [], [], []
    for c in chips:
        old = jnp.where(live, scores[c] * (HD**-0.5), masked_score)
        new = jnp.where(new_live, fresh[c] * (HD**-0.5), masked_score)
        top = jnp.maximum(jnp.max(old, axis=1, keepdims=True), jnp.max(new, axis=1, keepdims=True))
        old = jnp.where(live, jnp.exp(old - top), 0.0)
        new = jnp.where(new_live, jnp.exp(new - top), 0.0)
        totals.append(jnp.sum(old, axis=1, keepdims=True) + jnp.sum(new, axis=1, keepdims=True))
        weights.append(old.astype(jnp.bfloat16))
        fresh_weights.append(new.astype(jnp.bfloat16))
    wait_all(fetches)
    for c in chips:
        values = lanes_of(values_buf[c])
        vn = vn_ref[c].astype(jnp.bfloat16)
        mixed = jnp.dot(weights[c], values, preferred_element_type=jnp.float32)
        mixed = mixed + jnp.dot(fresh_weights[c], vn, preferred_element_type=jnp.float32)
        mixed = jnp.where(own_head, mixed / totals[c], 0.0)
        out = jnp.sum(mixed.reshape(rows, HEAD_BLOCK, lanes), axis=1).astype(out_ref.dtype)
        for t in range(steps):
            for h in range(heads):
                out_ref[t, c * heads + h] = out[2 * t : 2 * t + 2, h * HD : (h + 1) * HD]


def attend(cosine, sine, live, pieces, keys, values):
    count, _, steps = pieces.shape[:3]
    heads, tokens = keys.shape[:2]
    chips = count // 2
    per = heads // chips
    return pl.pallas_call(
        attend_kernel,
        out_shape=jax.ShapeDtypeStruct((steps, heads, 2, HD), jnp.bfloat16),
        in_specs=[VMEM] * 5 + [HBM],
        out_specs=VMEM,
        scratch_shapes=[pltpu.VMEM((chips, per, tokens, HD), jnp.bfloat16)]
        + [pltpu.VMEM((chips, 16, per * HD), jnp.float32)] * 2
        + [pltpu.SemaphoreType.DMA((chips,))],
        compiler_params=pltpu.CompilerParams(vmem_limit_bytes=16 * 2**20),
        cost_estimate=pl.CostEstimate(flops=10**9, bytes_accessed=6 * 10**6, transcendentals=0),
        name="attention",
    )(cosine, sine, live, pieces, keys, in_hbm(values))


def chip_plan(
    count,
    hidden,
    query_key_value_weight,
    adapter_down_maps,
    adapter_up_maps,
    adapter_storage_row,
    request_adapter,
    lengths,
    request_page_table,
    key_value_pool,
):
    me = lax.axis_index("replica")
    steps, req_dev, width = hidden.shape
    heads = width // HD
    holder_count, rank, _ = adapter_down_maps.shape
    pool_pages, page_len = key_value_pool.shape[:2]
    adapter_count = adapter_storage_row.shape[0]

    tokens = pool_pages * page_len
    keys, values = cache_by_head(key_value_pool.reshape(tokens, 2, heads, HD).transpose(0, 2, 1, 3))

    held = {m: trade(hidden, m, count) for m in range(8, count, 4)}
    held[1] = trade(hidden, 1, count)
    held[0], held[1] = lax.optimization_barrier((hidden, held[1]))
    held[4] = trade(held[0], 4, count)
    held[2] = trade(held[0], 2, count)
    held.update({m | 2: trade(held[m], 2, count) for m in range(4, count, 4)})
    held.update({m | 1: trade(held[m], 1, count) for m in range(2, count, 2)})
    blocks = [
        held[k].reshape(steps, req_dev, heads, HD).transpose(0, 2, 1, 3) for k in range(count)
    ]
    blocks[0] = in_hbm(blocks[0])

    stored = jnp.sum(
        jnp.where(
            request_adapter[:, None] == jnp.arange(adapter_count, dtype=jnp.int32)[None, :],
            adapter_storage_row[None, :],
            0,
        ),
        axis=1,
    )
    slot = jnp.concatenate([stored - me * holder_count] * steps)[None, :]

    x, lows = low_of(me.astype(jnp.int32).reshape(1), blocks, slot, adapter_down_maps)
    lows = lax.all_to_all(lows, "replica", split_axis=0, concat_axis=0, tiled=True)
    early, base, maps = project(stored, x, query_key_value_weight.transpose(0, 2, 1), adapter_up_maps)
    send = update_values(lows, early, base, maps)
    pieces = lax.all_to_all(send, "replica", split_axis=0, concat_axis=0, tiled=True)

    my_lengths = lax.dynamic_slice_in_dim(lengths, me * req_dev, req_dev)
    cosine, sine = rotation(my_lengths, steps)
    live = live_tokens(my_lengths, request_page_table, pool_pages, page_len).astype(jnp.int32)
    out = attend(cosine, sine, live.reshape(req_dev, tokens), pieces, keys, values)
    return out.transpose(0, 2, 1, 3).reshape(steps, req_dev, width)


def per_device(replicas, *arrays):
    columns = arrays[1].shape[2]
    whole_heads = replicas % 4 == 0 and (2 * columns) % HD == 0 and columns % HD == HD // 2
    plan = chip_plan if whole_heads and arrays[0].shape[1] == 2 else general_plan
    return plan(replicas, *arrays)


def solution(mesh):
    placed = (
        P(None, ("groups", "replica"), None),
        P(None, None, "replica"),
        P("replica", None, None),
        P(None, None, "replica"),
        P(),
        P("groups"),
        P("groups"),
        P(("groups", "replica"), None),
        P(("groups", "replica"), None, None, None),
    )
    return jax.shard_map(
        functools.partial(per_device, mesh.shape["replica"]),
        mesh=mesh,
        in_specs=placed,
        out_specs=P(None, ("groups", "replica"), None),
        check_vma=False,
    )
```

```python
import functools

import jax
import jax.numpy as jnp
from jax import lax
from jax.experimental import pallas as pl
from jax.experimental.pallas import tpu as pltpu
from jax.sharding import PartitionSpec as P

HD = 128
ROWS = 8
HEAD_BLOCK = 8

adapter_scale = 2.0
masked_score = -1e30


def attention_kernel(steps, req_dev, q_ref, k_ref, v_ref, cos_ref, sin_ref, live_ref, kv_ref, out_ref, kn_ref, vn_ref):
    rows = steps * req_dev
    width = q_ref.shape[1]
    lanes = HEAD_BLOCK * HD
    group = rows * HEAD_BLOCK
    cosine = cos_ref[...]
    sine = sin_ref[...]

    def rotated(x):
        pieces = []
        for h in range(HEAD_BLOCK):
            head = x[:, h * HD : (h + 1) * HD]
            pieces.append(head * cosine + pltpu.roll(head, HD // 2, 1) * sine)
        return jnp.concatenate(pieces, axis=1)

    row_head = lax.broadcasted_iota(jnp.int32, (group, lanes), 0) % HEAD_BLOCK
    lane_head = lax.broadcasted_iota(jnp.int32, (group, lanes), 1) // HD
    own_head = row_head == lane_head
    row_j = lax.broadcasted_iota(jnp.int32, (group, 16), 0) // HEAD_BLOCK
    new_j = lax.broadcasted_iota(jnp.int32, (group, 16), 1)
    new_live = (new_j < rows) & (new_j % req_dev == row_j % req_dev) & (new_j // req_dev <= row_j // req_dev)
    live_all = live_ref[...]
    live = jnp.concatenate(
        [
            jnp.broadcast_to(live_all[j % req_dev : j % req_dev + 1], (HEAD_BLOCK, live_all.shape[1]))
            for j in range(rows)
        ],
        axis=0,
    )
    live = live > 0
    kn_ref[...] = jnp.zeros_like(kn_ref)
    vn_ref[...] = jnp.zeros_like(vn_ref)
    contract_lanes = (((1,), (1,)), ((), ()))
    for c in range(width // lanes):
        cols = slice(c * lanes, (c + 1) * lanes)
        query = rotated(q_ref[:, cols].astype(jnp.float32))
        key_new = rotated(k_ref[:, cols].astype(jnp.float32))
        kn_ref[0:8] = key_new
        vn_ref[0:8] = v_ref[:, cols].astype(jnp.float32)
        kn = kn_ref[...].astype(jnp.bfloat16)
        vn = vn_ref[...].astype(jnp.bfloat16)
        spread = jnp.concatenate(
            [jnp.broadcast_to(query[j : j + 1], (HEAD_BLOCK, lanes)) for j in range(rows)], axis=0
        )
        spread = jnp.where(own_head, spread, 0.0).astype(jnp.bfloat16)
        kv = kv_ref[:, cols]
        scores = lax.dot_general(spread, kv, contract_lanes, preferred_element_type=jnp.float32) * (HD**-0.5)
        scores = jnp.where(live, scores, masked_score)
        fresh = lax.dot_general(spread, kn, contract_lanes, preferred_element_type=jnp.float32) * (HD**-0.5)
        fresh = jnp.where(new_live, fresh, masked_score)
        top = jnp.maximum(jnp.max(scores, axis=1, keepdims=True), jnp.max(fresh, axis=1, keepdims=True))
        weights = jnp.where(live, jnp.exp(scores - top), 0.0)
        fresh = jnp.where(new_live, jnp.exp(fresh - top), 0.0)
        totals = jnp.sum(weights, axis=1, keepdims=True) + jnp.sum(fresh, axis=1, keepdims=True)
        weights = pltpu.roll(weights, 1, 1).astype(jnp.bfloat16)
        mixed = jnp.dot(weights, kv, preferred_element_type=jnp.float32)
        mixed = mixed + jnp.dot(fresh.astype(jnp.bfloat16), vn, preferred_element_type=jnp.float32)
        mixed = jnp.where(own_head, mixed / totals, 0.0)
        out = jnp.sum(mixed.reshape(rows, HEAD_BLOCK, lanes), axis=1)
        out_ref[:, cols] = out.astype(out_ref.dtype)


def attention(steps, req_dev, q, k, v, cosine, sine, live, kv):
    rows = steps * req_dev
    width = q.shape[1]
    vmem = pl.BlockSpec(memory_space=pltpu.VMEM)
    return pl.pallas_call(
        functools.partial(attention_kernel, steps, req_dev),
        out_shape=jax.ShapeDtypeStruct((rows, width), jnp.bfloat16),
        in_specs=[vmem] * 7,
        out_specs=vmem,
        scratch_shapes=[pltpu.VMEM((16, HEAD_BLOCK * HD), jnp.float32)] * 2,
        compiler_params=pltpu.CompilerParams(vmem_limit_bytes=32 * 2**20),
        cost_estimate=pl.CostEstimate(flops=10**9, bytes_accessed=6 * 10**6, transcendentals=0),
        name="attention",
    )(q, k, v, cosine, sine, live, kv)


def rotation(my_lengths, steps):
    rows = steps * my_lengths.shape[0]
    positions = (my_lengths[None, :] + jnp.arange(steps, dtype=jnp.int32)[:, None]).reshape(rows)
    positions = jnp.pad(positions, (0, ROWS - rows))
    half = HD // 2
    frequency = jnp.exp(jnp.arange(half, dtype=jnp.float32) * (-2.0 * jnp.log(10000.0) / HD))
    angles = positions.astype(jnp.float32)[:, None] * frequency[None, :]
    cosine = jnp.cos(angles)
    sine = jnp.sin(angles)
    cosine = jnp.concatenate([cosine, cosine], axis=1)
    sine = jnp.concatenate([-sine, sine], axis=1)
    return cosine, sine


def live_tokens(my_lengths, request_page_table, pool_pages, page_len):
    pages = jnp.arange(pool_pages, dtype=jnp.int32)
    max_pages = request_page_table.shape[1]
    place = jnp.max(
        jnp.where(
            request_page_table[:, :, None] == pages[None, None, :],
            jnp.arange(max_pages, dtype=jnp.int32)[None, :, None],
            -1,
        ),
        axis=1,
    )
    token = place[:, :, None] * page_len + jnp.arange(page_len, dtype=jnp.int32)[None, None, :]
    return (place[:, :, None] >= 0) & (token < my_lengths[:, None, None])


def live_rows(my_lengths, request_page_table, pool_pages, page_len):
    alive = live_tokens(my_lengths, request_page_table, pool_pages, page_len)
    live = jnp.stack([alive, jnp.zeros_like(alive)], axis=-1).astype(jnp.int32)
    return live.reshape(request_page_table.shape[0], pool_pages * page_len * 2)


def general_plan(
    replicas,
    hidden,
    query_key_value_weight,
    adapter_down_maps,
    adapter_up_maps,
    adapter_storage_row,
    request_adapter,
    lengths,
    request_page_table,
    key_value_pool,
):
    my_index = lax.axis_index("replica")
    steps, req_dev, width = hidden.shape
    rows = steps * req_dev
    columns = query_key_value_weight.shape[2]
    holder_count, rank, _ = adapter_down_maps.shape
    pool_pages, page_len = key_value_pool.shape[:2]
    adapter_count = adapter_storage_row.shape[0]
    chips = replicas // 2
    total = replicas * ROWS

    block = jnp.pad(hidden.reshape(rows, width), ((0, ROWS - rows), (0, 0)))
    same_core = [[2 * chip + core for chip in range(chips)] for core in range(2)]
    mine = lax.all_to_all(
        jnp.broadcast_to(block[None], (chips, ROWS, width)),
        "replica",
        split_axis=0,
        concat_axis=0,
        axis_index_groups=same_core,
        tiled=True,
    )
    other = lax.ppermute(mine, "replica", [(i, i ^ 1) for i in range(replicas)])
    first = my_index % 2 == 0
    gathered = jnp.stack([jnp.where(first, mine, other), jnp.where(first, other, mine)])
    gathered = gathered.reshape(total, width)

    stored_rows = jnp.sum(
        jnp.where(
            request_adapter[:, None] == jnp.arange(adapter_count, dtype=jnp.int32)[None, :],
            adapter_storage_row[None, :],
            0,
        ),
        axis=1,
    )
    by_block = stored_rows.reshape(chips, 2, 1, req_dev).transpose(1, 0, 2, 3)
    by_block = jnp.broadcast_to(by_block, (2, chips, steps, req_dev)).reshape(2, chips, rows)
    row_stored = jnp.pad(by_block, ((0, 0), (0, 0), (0, ROWS - rows)), constant_values=-1).reshape(total)

    down = jnp.einsum("nd,hfd->nhf", gathered, adapter_down_maps, preferred_element_type=jnp.float32)
    slots = my_index * holder_count + jnp.arange(holder_count, dtype=jnp.int32)
    own = row_stored[:, None] == slots[None, :]
    low = jnp.sum(jnp.where(own[:, :, None], down, 0.0), axis=1).astype(jnp.bfloat16)
    low = jnp.concatenate([low[: total // 2], low[total // 2 :]], axis=1)
    low = lax.all_to_all(
        jnp.broadcast_to(low[None], (replicas,) + low.shape), "replica", split_axis=0, concat_axis=0, tiled=True
    )
    low = jnp.sum(low.astype(jnp.float32), axis=0)
    low = jnp.concatenate([low[:, :rank], low[:, rank:]], axis=0)

    projected = jnp.einsum("nd,idc->nic", gathered, query_key_value_weight, preferred_element_type=jnp.float32)

    def update(first_adapter, maps):
        held = maps.shape[0]
        which = first_adapter + jnp.arange(held, dtype=jnp.int32)
        wide = jnp.where((row_stored[:, None] == which[None, :])[:, :, None], low[:, None, :], 0.0)
        return jnp.dot(
            wide.astype(jnp.bfloat16).reshape(total, held * rank),
            maps.reshape(held * rank, columns),
            preferred_element_type=jnp.float32,
        )

    step_adapters = 64
    if adapter_count <= step_adapters:
        updated = update(0, adapter_up_maps)
    else:
        updated = lax.fori_loop(
            0,
            adapter_count // step_adapters,
            lambda i, sofar: sofar
            + update(
                i * step_adapters,
                lax.dynamic_slice_in_dim(adapter_up_maps, i * step_adapters, step_adapters, 0),
            ),
            jnp.zeros((total, columns), jnp.float32),
        )
    value = projected[:, 2] + adapter_scale * updated
    combined = jnp.concatenate([projected[:, 0], projected[:, 1], value], axis=1).astype(jnp.bfloat16)
    combined = combined.reshape(2, chips, ROWS, 3 * columns).transpose(1, 0, 2, 3)
    combined = combined.reshape(replicas, ROWS, 3 * columns)
    arrived = lax.all_to_all(combined, "replica", split_axis=0, concat_axis=0, tiled=True)
    arrived = arrived.reshape(replicas, ROWS, 3, columns).transpose(2, 1, 0, 3).reshape(3, ROWS, width)

    my_lengths = lax.dynamic_slice_in_dim(lengths, my_index * req_dev, req_dev)
    cosine, sine = rotation(my_lengths, steps)
    live = live_rows(my_lengths, request_page_table, pool_pages, page_len)
    kv = key_value_pool.reshape(pool_pages * page_len * 2, width)
    out = attention(steps, req_dev, arrived[0], arrived[1], arrived[2], cosine, sine, live, kv)
    return out.reshape(steps, req_dev, width)


def trade(value, mask, count):
    return lax.ppermute(value, "replica", [(i, i ^ mask) for i in range(count)])


CONTRACT_LANES = (((1,), (1,)), ((), ()))


def in_hbm(x):
    return pltpu.with_memory_space_constraint(x, pltpu.HBM)


VMEM = pl.BlockSpec(memory_space=pltpu.VMEM)
HBM = pl.BlockSpec(memory_space=pltpu.HBM)
SMEM = pl.BlockSpec(memory_space=pltpu.SMEM)
ANY = pl.BlockSpec(memory_space=pl.ANY)


def start_all(copies):
    for copy in copies:
        copy.start()
    return copies


def wait_all(copies):
    for copy in copies:
        copy.wait()


CACHE_PARTS = 4


def cache_kernel(pool_ref, keys_ref, values_ref, raw, values, sem, out_sem):
    heads, tokens = raw.shape[:2]
    copies = start_all([pltpu.make_async_copy(pool_ref.at[:, h], raw.at[h], sem.at[h]) for h in range(heads)])
    rows = raw.reshape(heads, 2 * tokens, HD)
    to = lax.broadcasted_iota(jnp.int32, (2 * tokens, 2 * tokens), 0)
    source = lax.broadcasted_iota(jnp.int32, (2 * tokens, 2 * tokens), 1)
    wanted = jnp.where(to < tokens, 2 * to, 2 * (to - tokens) + 1)
    pick = jnp.where(source == wanted, 1.0, 0.0).astype(jnp.bfloat16)
    sent = []
    part = heads // CACHE_PARTS
    for p in range(CACHE_PARTS):
        wait_all(copies[p * part : (p + 1) * part])
        for h in range(p * part, (p + 1) * part, 2):
            both = jnp.concatenate([rows[h], rows[h + 1]], axis=1)
            made = jnp.dot(pick, both, preferred_element_type=jnp.float32).astype(jnp.bfloat16)
            for i in range(2):
                keys_ref[h + i] = made[:tokens, i * HD : (i + 1) * HD]
                values[h + i] = made[tokens:, i * HD : (i + 1) * HD]
        span = slice(p * part, (p + 1) * part)
        sent += start_all([pltpu.make_async_copy(values.at[span], values_ref.at[span], out_sem.at[p])])
    wait_all(sent)


def cache_by_head(pool):
    tokens, heads = pool.shape[:2]
    return pl.pallas_call(
        cache_kernel,
        out_shape=(
            jax.ShapeDtypeStruct((heads, tokens, HD), pool.dtype),
            pltpu.HBM((heads, tokens, HD), pool.dtype),
        ),
        in_specs=[HBM],
        out_specs=(VMEM, HBM),
        scratch_shapes=[
            pltpu.VMEM((heads, tokens, 2, HD), pool.dtype),
            pltpu.VMEM((heads, tokens, HD), pool.dtype),
            pltpu.SemaphoreType.DMA((heads,)),
            pltpu.SemaphoreType.DMA((CACHE_PARTS,)),
        ],
        compiler_params=pltpu.CompilerParams(vmem_limit_bytes=16 * 2**20),
        cost_estimate=pl.CostEstimate(flops=0, bytes_accessed=12 * 10**6, transcendentals=0),
        name="cache_by_head",
    )(in_hbm(pool))


def lanes_of(x):
    return jnp.concatenate([x[c] for c in range(x.shape[0])], axis=1)


def step_rows(x, first, chunks):
    steps, _, count = x.shape[:3]
    flat = x.reshape(steps, x.shape[1], 2 * count, HD)
    return jnp.concatenate(
        [jnp.concatenate([flat[t, c] for c in range(first, first + chunks)], axis=1) for t in range(steps)], axis=0
    )


def index_kernel(me_ref, stored_ref, slot_ref, column_ref):
    requests = stored_ref.shape[1]
    steps = slot_ref.shape[1] // requests
    row = jnp.concatenate([stored_ref[...]] * steps, axis=1)
    slot_ref[...] = row - me_ref[0]
    wide = jnp.concatenate([row, jnp.zeros((1, HD - row.shape[1]), row.dtype)], axis=1)
    column_ref[...] = jnp.broadcast_to(wide.astype(jnp.float32), (HD, HD)).T[: row.shape[1], :1].astype(jnp.int32)


def index_work(first, stored, steps):
    rows = stored.shape[0] * steps
    return pl.pallas_call(
        index_kernel,
        out_shape=(jax.ShapeDtypeStruct((1, rows), jnp.int32), jax.ShapeDtypeStruct((rows, 1), jnp.int32)),
        in_specs=[SMEM, VMEM],
        out_specs=(VMEM, VMEM),
        compiler_params=pltpu.CompilerParams(vmem_limit_bytes=2 * 2**20),
        cost_estimate=pl.CostEstimate(flops=2 * 10**10, bytes_accessed=10**4, transcendentals=0),
        name="index_work",
    )(first, stored[None, :])


def low_kernel(count, me_ref, slot_ref, down_ref, *refs):
    blocks, (x_ref, low_ref, sem) = refs[:count], refs[count:]
    me = me_ref[0]
    holders, rank, width = down_ref.shape
    wait_all(
        start_all(
            [pltpu.make_async_copy(block, x_ref.at[:, :, me ^ k], sem.at[k]) for k, block in enumerate(blocks)]
        )
    )
    x = step_rows(x_ref, 0, x_ref.shape[1])
    rows = x.shape[0]
    made = lax.dot_general(
        down_ref.reshape(holders * rank, width)[...], x, CONTRACT_LANES, preferred_element_type=jnp.float32
    )
    slot = slot_ref[...]
    low = jnp.zeros((rank, rows), jnp.float32)
    for h in range(holders):
        low = low + jnp.where(slot == h, made[h * rank : (h + 1) * rank], 0.0)
    low = low.T
    low_ref[...] = jnp.concatenate([low[: rows // 2], low[rows // 2 :]], axis=1).astype(low_ref.dtype)


def low_of(me, blocks, slot, down):
    count = len(blocks)
    steps, chunks = blocks[0].shape[:2]
    rows = count * steps * 2
    rank = down.shape[1]
    return pl.pallas_call(
        functools.partial(low_kernel, count),
        out_shape=(
            jax.ShapeDtypeStruct((steps, chunks, count, 2, HD), jnp.bfloat16),
            jax.ShapeDtypeStruct((rows // 2, 2 * rank), jnp.bfloat16),
        ),
        in_specs=[SMEM, VMEM, VMEM] + [ANY] * count,
        out_specs=(VMEM, VMEM),
        scratch_shapes=[pltpu.SemaphoreType.DMA((count,))],
        compiler_params=pltpu.CompilerParams(vmem_limit_bytes=12 * 2**20),
        cost_estimate=pl.CostEstimate(flops=10**8, bytes_accessed=4 * 10**6, transcendentals=0),
        name="low_rows",
    )(me, slot, down, *blocks)


def put_chunks(buf, first, value):
    steps, count = buf.shape[1:3]
    flat = buf.reshape(buf.shape[0], steps, 2 * count, HD)
    wide = value.shape[1]
    for c in range(-(-wide // HD)):
        part = value[:, c * HD : min((c + 1) * HD, wide)]
        if part.shape[1] < HD:
            part = jnp.concatenate([part, jnp.zeros((part.shape[0], HD - part.shape[1]), part.dtype)], axis=1)
        part = part.astype(buf.dtype)
        for t in range(steps):
            flat[first + c, t] = part[t * 2 * count : (t + 1) * 2 * count]


def project_kernel(which, x_ref, w_ref, out_ref):
    x = step_rows(x_ref, 0, x_ref.shape[1])
    made = lax.dot_general(w_ref[which], x, CONTRACT_LANES, preferred_element_type=jnp.float32).T
    if which < 2:
        put_chunks(out_ref, 0, made)
    else:
        out_ref[...] = made


def project(which, x, weight):
    steps, _, count = x.shape[:3]
    columns = weight.shape[1]
    chunks = jax.ShapeDtypeStruct((-(-columns // HD), steps, count, 2, HD), jnp.bfloat16)
    base = jax.ShapeDtypeStruct((2 * steps * count, columns), jnp.float32)
    return pl.pallas_call(
        functools.partial(project_kernel, which),
        out_shape=chunks if which < 2 else base,
        in_specs=[VMEM, VMEM],
        out_specs=VMEM,
        compiler_params=pltpu.CompilerParams(vmem_limit_bytes=16 * 2**20),
        cost_estimate=pl.CostEstimate(flops=5 * 10**8, bytes_accessed=4 * 10**6, transcendentals=0),
        name="project",
    )(x, weight)


def update_kernel(stored_ref, query_ref, key_ref, base_ref, up_ref, low_ref, more_ref, send_ref, buf, sem):
    half, packed = low_ref.shape
    rank = packed // 2
    rows = 2 * half
    count = send_ref.shape[0]
    low = low_ref[...].astype(jnp.float32) + more_ref[...].astype(jnp.float32)
    low = jnp.concatenate([low[:, :rank], low[:, rank:]], axis=0)
    batch = 256 // rank
    spread = jnp.concatenate([low] * batch, axis=1)
    ahead = stored_ref[...] - lax.broadcasted_iota(jnp.int32, (rows, batch * rank), 1) // rank
    total = jnp.zeros(base_ref.shape, jnp.float32)
    for a in range(0, up_ref.shape[0] // rank, batch):
        wide = jnp.where(ahead == a, spread, 0.0).astype(jnp.bfloat16)
        total = total + jnp.dot(wide, up_ref[a * rank : (a + batch) * rank], preferred_element_type=jnp.float32)
    each = query_ref.shape[0]
    buf[:each] = query_ref[...]
    buf[each : 2 * each] = key_ref[...]
    put_chunks(buf, 2 * each, base_ref[...] + adapter_scale * total)
    wait_all(
        start_all([pltpu.make_async_copy(buf.at[:, :, k], send_ref.at[k], sem.at[k]) for k in range(count)])
    )


def update_values(stored, query, key, base, up, low, more):
    chunks, steps, count = query.shape[:3]
    return pl.pallas_call(
        update_kernel,
        out_shape=pltpu.HBM((count, 3 * chunks, steps, 2, HD), query.dtype),
        in_specs=[VMEM] * 7,
        out_specs=HBM,
        scratch_shapes=[
            pltpu.VMEM((3 * chunks, steps, count, 2, HD), query.dtype),
            pltpu.SemaphoreType.DMA((count,)),
        ],
        compiler_params=pltpu.CompilerParams(vmem_limit_bytes=8 * 2**20),
        cost_estimate=pl.CostEstimate(flops=3 * 10**8, bytes_accessed=4 * 10**6, transcendentals=0),
        name="update_values",
    )(stored, query, key, base, up, low, more)


def attend_kernel(cos_ref, sin_ref, live_ref, pieces_ref, keys_ref, values_ref, out_ref, values_buf, kn_ref, vn_ref, sem):
    count, _, steps = pieces_ref.shape[:3]
    rows = 2 * steps
    each = pieces_ref.shape[1] // 3
    heads = 2 * out_ref.shape[1] // count
    lanes = heads * HD
    group = rows * HEAD_BLOCK
    chips = range(count // 2)
    fetches = start_all(
        [
            pltpu.make_async_copy(values_ref.at[c * heads : (c + 1) * heads], values_buf.at[c], sem.at[c])
            for c in chips
        ]
    )
    cosine = cos_ref[...][:rows]
    sine = sin_ref[...][:rows]
    left = lax.broadcasted_iota(jnp.int32, (rows, HD), 1) < HD // 2

    def chip_columns(chip, at):
        low = [pieces_ref[2 * chip, at + c].reshape(rows, HD).astype(jnp.float32) for c in range(each)]
        high = [pieces_ref[2 * chip + 1, at + c].reshape(rows, HD).astype(jnp.float32) for c in range(each)]
        high = [pltpu.roll(x, HD // 2, 1) for x in high]
        whole = low[:-1] + [jnp.where(left, low[-1], high[0])]
        return whole + [jnp.where(left, a, b) for a, b in zip(high[:-1], high[1:])]

    def rotated(parts):
        return [x * cosine + pltpu.roll(x, HD // 2, 1) * sine for x in parts]

    row_head = lax.broadcasted_iota(jnp.int32, (group, lanes), 0) % HEAD_BLOCK
    lane_head = lax.broadcasted_iota(jnp.int32, (group, lanes), 1) // HD
    own_head = row_head == lane_head
    row_j = lax.broadcasted_iota(jnp.int32, (group, 16), 0) // HEAD_BLOCK
    new_j = lax.broadcasted_iota(jnp.int32, (group, 16), 1)
    new_live = (new_j < rows) & (new_j % 2 == row_j % 2) & (new_j // 2 <= row_j // 2)
    live = jnp.concatenate(
        [
            jnp.broadcast_to(live_ref[j % 2 : j % 2 + 1, :], (HEAD_BLOCK, live_ref.shape[1]))
            for j in range(rows)
        ],
        axis=0,
    )
    live = live > 0
    kn_ref[...] = jnp.zeros_like(kn_ref)
    vn_ref[...] = jnp.zeros_like(vn_ref)
    spreads = []
    for c in chips:
        query = jnp.concatenate(rotated(chip_columns(c, 0)), axis=1)
        kn_ref[c, 0:rows] = jnp.concatenate(rotated(chip_columns(c, each)), axis=1)
        vn_ref[c, 0:rows] = jnp.concatenate(chip_columns(c, 2 * each), axis=1)
        spread = jnp.concatenate(
            [jnp.broadcast_to(query[j : j + 1], (HEAD_BLOCK, lanes)) for j in range(rows)], axis=0
        )
        spreads.append(jnp.where(own_head, spread, 0.0).astype(jnp.bfloat16))
    scores, fresh = [], []
    for c in chips:
        keys = jnp.concatenate([keys_ref[c * heads + h] for h in range(heads)], axis=1)
        kn = kn_ref[c].astype(jnp.bfloat16)
        scores.append(lax.dot_general(spreads[c], keys, CONTRACT_LANES, preferred_element_type=jnp.float32))
        fresh.append(lax.dot_general(spreads[c], kn, CONTRACT_LANES, preferred_element_type=jnp.float32))
    weights, fresh_weights, totals = [], [], []
    for c in chips:
        old = jnp.where(live, scores[c] * (HD**-0.5), masked_score)
        new = jnp.where(new_live, fresh[c] * (HD**-0.5), masked_score)
        top = jnp.maximum(jnp.max(old, axis=1, keepdims=True), jnp.max(new, axis=1, keepdims=True))
        old = jnp.where(live, jnp.exp(old - top), 0.0)
        new = jnp.where(new_live, jnp.exp(new - top), 0.0)
        totals.append(jnp.sum(old, axis=1, keepdims=True) + jnp.sum(new, axis=1, keepdims=True))
        weights.append(old.astype(jnp.bfloat16))
        fresh_weights.append(new.astype(jnp.bfloat16))
    wait_all(fetches)
    for c in chips:
        values = lanes_of(values_buf[c])
        vn = vn_ref[c].astype(jnp.bfloat16)
        mixed = jnp.dot(weights[c], values, preferred_element_type=jnp.float32)
        mixed = mixed + jnp.dot(fresh_weights[c], vn, preferred_element_type=jnp.float32)
        mixed = jnp.where(own_head, mixed / totals[c], 0.0)
        out = jnp.sum(mixed.reshape(rows, HEAD_BLOCK, lanes), axis=1).astype(out_ref.dtype)
        for t in range(steps):
            for h in range(heads):
                out_ref[t, c * heads + h] = out[2 * t : 2 * t + 2, h * HD : (h + 1) * HD]


def attend(cosine, sine, live, pieces, keys, values):
    count, _, steps = pieces.shape[:3]
    heads, tokens = keys.shape[:2]
    chips = count // 2
    per = heads // chips
    return pl.pallas_call(
        attend_kernel,
        out_shape=jax.ShapeDtypeStruct((steps, heads, 2, HD), jnp.bfloat16),
        in_specs=[VMEM] * 5 + [HBM],
        out_specs=VMEM,
        scratch_shapes=[pltpu.VMEM((chips, per, tokens, HD), jnp.bfloat16)]
        + [pltpu.VMEM((chips, 16, per * HD), jnp.float32)] * 2
        + [pltpu.SemaphoreType.DMA((chips,))],
        compiler_params=pltpu.CompilerParams(vmem_limit_bytes=16 * 2**20),
        cost_estimate=pl.CostEstimate(flops=10**9, bytes_accessed=6 * 10**6, transcendentals=0),
        name="attention",
    )(cosine, sine, live, pieces, keys, in_hbm(values))


def chip_plan(
    count,
    hidden,
    query_key_value_weight,
    adapter_down_maps,
    adapter_up_maps,
    adapter_storage_row,
    request_adapter,
    lengths,
    request_page_table,
    key_value_pool,
):
    me = lax.axis_index("replica")
    steps, req_dev, width = hidden.shape
    heads = width // HD
    holder_count, rank, _ = adapter_down_maps.shape
    pool_pages, page_len = key_value_pool.shape[:2]
    adapter_count = adapter_storage_row.shape[0]

    tokens = pool_pages * page_len
    keys, values = cache_by_head(key_value_pool.reshape(tokens, 2, heads, HD).transpose(0, 2, 1, 3))

    held = {m: trade(hidden, m, count) for m in range(8, count, 4)}
    held[1] = trade(hidden, 1, count)
    held[0], held[1] = lax.optimization_barrier((hidden, held[1]))
    held[4] = trade(held[0], 4, count)
    held[2] = trade(held[0], 2, count)
    held.update({m | 2: trade(held[m], 2, count) for m in range(4, count, 4)})
    held.update({m | 1: trade(held[m], 1, count) for m in range(2, count, 2)})
    blocks = [
        held[k].reshape(steps, req_dev, heads, HD).transpose(0, 2, 1, 3) for k in range(count)
    ]
    blocks[0] = in_hbm(blocks[0])

    stored = jnp.sum(
        jnp.where(
            request_adapter[:, None] == jnp.arange(adapter_count, dtype=jnp.int32)[None, :],
            adapter_storage_row[None, :],
            0,
        ),
        axis=1,
    )
    slot, column = index_work((me * holder_count).astype(jnp.int32).reshape(1), stored, steps)

    held = {m: trade(hidden, m, count) for m in range(8, count, 4)}
    held[1] = trade(hidden, 1, count)
    held[0], held[1] = lax.optimization_barrier((hidden, held[1]))
    held[4] = trade(held[0], 4, count)
    held[2] = trade(held[0], 2, count)
    held.update({m | 2: trade(held[m], 2, count) for m in range(4, count, 4)})
    held.update({m | 1: trade(held[m], 1, count) for m in range(2, count, 2)})
    blocks = [
        held[k].reshape(steps, req_dev, heads, HD).transpose(0, 2, 1, 3) for k in range(count)
    ]
    blocks[0] = in_hbm(blocks[0])

    stored = jnp.sum(
        jnp.where(
            request_adapter[:, None] == jnp.arange(adapter_count, dtype=jnp.int32)[None, :],
            adapter_storage_row[None, :],
            0,
        ),
        axis=1,
    )
    slot = jnp.concatenate([stored - me * holder_count] * steps)[None, :]

    x, low = low_of(me.astype(jnp.int32).reshape(1), blocks, slot, adapter_down_maps)
    weight = query_key_value_weight.transpose(0, 2, 1)
    parts = []
    hops = [1 << i for i in range(count.bit_length() - 1)]
    for i, mask in enumerate(hops):
        arrived = trade(low, mask, count)
        if i < 3:
            part = project(i, x, weight)
            arrived, part = lax.optimization_barrier((arrived, part))
            parts.append(part)
        if mask != hops[-1]:
            low = low + arrived
    send = update_values(column, *parts, adapter_up_maps.reshape(adapter_count * rank, -1), low, arrived)
    pieces = lax.all_to_all(send, "replica", split_axis=0, concat_axis=0, tiled=True)

    my_lengths = lax.dynamic_slice_in_dim(lengths, me * req_dev, req_dev)
    cosine, sine = rotation(my_lengths, steps)
    live = live_tokens(my_lengths, request_page_table, pool_pages, page_len).astype(jnp.int32)
    out = attend(cosine, sine, live.reshape(req_dev, tokens), pieces, keys, values)
    return out.transpose(0, 2, 1, 3).reshape(steps, req_dev, width)


def per_device(replicas, *arrays):
    columns = arrays[1].shape[2]
    whole_heads = replicas % 4 == 0 and (2 * columns) % HD == 0 and columns % HD == HD // 2
    plan = chip_plan if whole_heads and arrays[0].shape[1] == 2 else general_plan
    return plan(replicas, *arrays)


def solution(mesh):
    placed = (
        P(None, ("groups", "replica"), None),
        P(None, None, "replica"),
        P("replica", None, None),
        P(None, None, "replica"),
        P(),
        P("groups"),
        P("groups"),
        P(("groups", "replica"), None),
        P(("groups", "replica"), None, None, None),
    )
    return jax.shard_map(
        functools.partial(per_device, mesh.shape["replica"]),
        mesh=mesh,
        in_specs=placed,
        out_specs=P(None, ("groups", "replica"), None),
        check_vma=False,
    )
```

```python
import functools

import jax
import jax.numpy as jnp
from jax import lax
from jax.experimental import pallas as pl
from jax.experimental.pallas import tpu as pltpu
from jax.sharding import PartitionSpec as P

HD = 128
ROWS = 8
HEAD_BLOCK = 8

adapter_scale = 2.0
masked_score = -1e30


def attention_kernel(steps, req_dev, q_ref, k_ref, v_ref, cos_ref, sin_ref, live_ref, kv_ref, out_ref, kn_ref, vn_ref):
    rows = steps * req_dev
    width = q_ref.shape[1]
    lanes = HEAD_BLOCK * HD
    group = rows * HEAD_BLOCK
    cosine = cos_ref[...]
    sine = sin_ref[...]

    def rotated(x):
        pieces = []
        for h in range(HEAD_BLOCK):
            head = x[:, h * HD : (h + 1) * HD]
            pieces.append(head * cosine + pltpu.roll(head, HD // 2, 1) * sine)
        return jnp.concatenate(pieces, axis=1)

    row_head = lax.broadcasted_iota(jnp.int32, (group, lanes), 0) % HEAD_BLOCK
    lane_head = lax.broadcasted_iota(jnp.int32, (group, lanes), 1) // HD
    own_head = row_head == lane_head
    row_j = lax.broadcasted_iota(jnp.int32, (group, 16), 0) // HEAD_BLOCK
    new_j = lax.broadcasted_iota(jnp.int32, (group, 16), 1)
    new_live = (new_j < rows) & (new_j % req_dev == row_j % req_dev) & (new_j // req_dev <= row_j // req_dev)
    live_all = live_ref[...]
    live = jnp.concatenate(
        [
            jnp.broadcast_to(live_all[j % req_dev : j % req_dev + 1], (HEAD_BLOCK, live_all.shape[1]))
            for j in range(rows)
        ],
        axis=0,
    )
    live = live > 0
    kn_ref[...] = jnp.zeros_like(kn_ref)
    vn_ref[...] = jnp.zeros_like(vn_ref)
    contract_lanes = (((1,), (1,)), ((), ()))
    for c in range(width // lanes):
        cols = slice(c * lanes, (c + 1) * lanes)
        query = rotated(q_ref[:, cols].astype(jnp.float32))
        key_new = rotated(k_ref[:, cols].astype(jnp.float32))
        kn_ref[0:8] = key_new
        vn_ref[0:8] = v_ref[:, cols].astype(jnp.float32)
        kn = kn_ref[...].astype(jnp.bfloat16)
        vn = vn_ref[...].astype(jnp.bfloat16)
        spread = jnp.concatenate(
            [jnp.broadcast_to(query[j : j + 1], (HEAD_BLOCK, lanes)) for j in range(rows)], axis=0
        )
        spread = jnp.where(own_head, spread, 0.0).astype(jnp.bfloat16)
        kv = kv_ref[:, cols]
        scores = lax.dot_general(spread, kv, contract_lanes, preferred_element_type=jnp.float32) * (HD**-0.5)
        scores = jnp.where(live, scores, masked_score)
        fresh = lax.dot_general(spread, kn, contract_lanes, preferred_element_type=jnp.float32) * (HD**-0.5)
        fresh = jnp.where(new_live, fresh, masked_score)
        top = jnp.maximum(jnp.max(scores, axis=1, keepdims=True), jnp.max(fresh, axis=1, keepdims=True))
        weights = jnp.where(live, jnp.exp(scores - top), 0.0)
        fresh = jnp.where(new_live, jnp.exp(fresh - top), 0.0)
        totals = jnp.sum(weights, axis=1, keepdims=True) + jnp.sum(fresh, axis=1, keepdims=True)
        weights = pltpu.roll(weights, 1, 1).astype(jnp.bfloat16)
        mixed = jnp.dot(weights, kv, preferred_element_type=jnp.float32)
        mixed = mixed + jnp.dot(fresh.astype(jnp.bfloat16), vn, preferred_element_type=jnp.float32)
        mixed = jnp.where(own_head, mixed / totals, 0.0)
        out = jnp.sum(mixed.reshape(rows, HEAD_BLOCK, lanes), axis=1)
        out_ref[:, cols] = out.astype(out_ref.dtype)


def attention(steps, req_dev, q, k, v, cosine, sine, live, kv):
    rows = steps * req_dev
    width = q.shape[1]
    vmem = pl.BlockSpec(memory_space=pltpu.VMEM)
    return pl.pallas_call(
        functools.partial(attention_kernel, steps, req_dev),
        out_shape=jax.ShapeDtypeStruct((rows, width), jnp.bfloat16),
        in_specs=[vmem] * 7,
        out_specs=vmem,
        scratch_shapes=[pltpu.VMEM((16, HEAD_BLOCK * HD), jnp.float32)] * 2,
        compiler_params=pltpu.CompilerParams(vmem_limit_bytes=32 * 2**20),
        cost_estimate=pl.CostEstimate(flops=10**9, bytes_accessed=6 * 10**6, transcendentals=0),
        name="attention",
    )(q, k, v, cosine, sine, live, kv)


def rotation(my_lengths, steps):
    rows = steps * my_lengths.shape[0]
    positions = (my_lengths[None, :] + jnp.arange(steps, dtype=jnp.int32)[:, None]).reshape(rows)
    positions = jnp.pad(positions, (0, ROWS - rows))
    half = HD // 2
    frequency = jnp.exp(jnp.arange(half, dtype=jnp.float32) * (-2.0 * jnp.log(10000.0) / HD))
    angles = positions.astype(jnp.float32)[:, None] * frequency[None, :]
    cosine = jnp.cos(angles)
    sine = jnp.sin(angles)
    cosine = jnp.concatenate([cosine, cosine], axis=1)
    sine = jnp.concatenate([-sine, sine], axis=1)
    return cosine, sine


def live_tokens(my_lengths, request_page_table, pool_pages, page_len):
    pages = jnp.arange(pool_pages, dtype=jnp.int32)
    max_pages = request_page_table.shape[1]
    place = jnp.max(
        jnp.where(
            request_page_table[:, :, None] == pages[None, None, :],
            jnp.arange(max_pages, dtype=jnp.int32)[None, :, None],
            -1,
        ),
        axis=1,
    )
    token = place[:, :, None] * page_len + jnp.arange(page_len, dtype=jnp.int32)[None, None, :]
    return (place[:, :, None] >= 0) & (token < my_lengths[:, None, None])


def live_rows(my_lengths, request_page_table, pool_pages, page_len):
    alive = live_tokens(my_lengths, request_page_table, pool_pages, page_len)
    live = jnp.stack([alive, jnp.zeros_like(alive)], axis=-1).astype(jnp.int32)
    return live.reshape(request_page_table.shape[0], pool_pages * page_len * 2)


def general_plan(
    replicas,
    hidden,
    query_key_value_weight,
    adapter_down_maps,
    adapter_up_maps,
    adapter_storage_row,
    request_adapter,
    lengths,
    request_page_table,
    key_value_pool,
):
    my_index = lax.axis_index("replica")
    steps, req_dev, width = hidden.shape
    rows = steps * req_dev
    columns = query_key_value_weight.shape[2]
    holder_count, rank, _ = adapter_down_maps.shape
    pool_pages, page_len = key_value_pool.shape[:2]
    adapter_count = adapter_storage_row.shape[0]
    chips = replicas // 2
    total = replicas * ROWS

    block = jnp.pad(hidden.reshape(rows, width), ((0, ROWS - rows), (0, 0)))
    same_core = [[2 * chip + core for chip in range(chips)] for core in range(2)]
    mine = lax.all_to_all(
        jnp.broadcast_to(block[None], (chips, ROWS, width)),
        "replica",
        split_axis=0,
        concat_axis=0,
        axis_index_groups=same_core,
        tiled=True,
    )
    other = lax.ppermute(mine, "replica", [(i, i ^ 1) for i in range(replicas)])
    first = my_index % 2 == 0
    gathered = jnp.stack([jnp.where(first, mine, other), jnp.where(first, other, mine)])
    gathered = gathered.reshape(total, width)

    stored_rows = jnp.sum(
        jnp.where(
            request_adapter[:, None] == jnp.arange(adapter_count, dtype=jnp.int32)[None, :],
            adapter_storage_row[None, :],
            0,
        ),
        axis=1,
    )
    by_block = stored_rows.reshape(chips, 2, 1, req_dev).transpose(1, 0, 2, 3)
    by_block = jnp.broadcast_to(by_block, (2, chips, steps, req_dev)).reshape(2, chips, rows)
    row_stored = jnp.pad(by_block, ((0, 0), (0, 0), (0, ROWS - rows)), constant_values=-1).reshape(total)

    down = jnp.einsum("nd,hfd->nhf", gathered, adapter_down_maps, preferred_element_type=jnp.float32)
    slots = my_index * holder_count + jnp.arange(holder_count, dtype=jnp.int32)
    own = row_stored[:, None] == slots[None, :]
    low = jnp.sum(jnp.where(own[:, :, None], down, 0.0), axis=1).astype(jnp.bfloat16)
    low = jnp.concatenate([low[: total // 2], low[total // 2 :]], axis=1)
    low = lax.all_to_all(
        jnp.broadcast_to(low[None], (replicas,) + low.shape), "replica", split_axis=0, concat_axis=0, tiled=True
    )
    low = jnp.sum(low.astype(jnp.float32), axis=0)
    low = jnp.concatenate([low[:, :rank], low[:, rank:]], axis=0)

    projected = jnp.einsum("nd,idc->nic", gathered, query_key_value_weight, preferred_element_type=jnp.float32)

    def update(first_adapter, maps):
        held = maps.shape[0]
        which = first_adapter + jnp.arange(held, dtype=jnp.int32)
        wide = jnp.where((row_stored[:, None] == which[None, :])[:, :, None], low[:, None, :], 0.0)
        return jnp.dot(
            wide.astype(jnp.bfloat16).reshape(total, held * rank),
            maps.reshape(held * rank, columns),
            preferred_element_type=jnp.float32,
        )

    step_adapters = 64
    if adapter_count <= step_adapters:
        updated = update(0, adapter_up_maps)
    else:
        updated = lax.fori_loop(
            0,
            adapter_count // step_adapters,
            lambda i, sofar: sofar
            + update(
                i * step_adapters,
                lax.dynamic_slice_in_dim(adapter_up_maps, i * step_adapters, step_adapters, 0),
            ),
            jnp.zeros((total, columns), jnp.float32),
        )
    value = projected[:, 2] + adapter_scale * updated
    combined = jnp.concatenate([projected[:, 0], projected[:, 1], value], axis=1).astype(jnp.bfloat16)
    combined = combined.reshape(2, chips, ROWS, 3 * columns).transpose(1, 0, 2, 3)
    combined = combined.reshape(replicas, ROWS, 3 * columns)
    arrived = lax.all_to_all(combined, "replica", split_axis=0, concat_axis=0, tiled=True)
    arrived = arrived.reshape(replicas, ROWS, 3, columns).transpose(2, 1, 0, 3).reshape(3, ROWS, width)

    my_lengths = lax.dynamic_slice_in_dim(lengths, my_index * req_dev, req_dev)
    cosine, sine = rotation(my_lengths, steps)
    live = live_rows(my_lengths, request_page_table, pool_pages, page_len)
    kv = key_value_pool.reshape(pool_pages * page_len * 2, width)
    out = attention(steps, req_dev, arrived[0], arrived[1], arrived[2], cosine, sine, live, kv)
    return out.reshape(steps, req_dev, width)


def trade(value, mask, count):
    return lax.ppermute(value, "replica", [(i, i ^ mask) for i in range(count)])


CONTRACT_LANES = (((1,), (1,)), ((), ()))


def in_hbm(x):
    return pltpu.with_memory_space_constraint(x, pltpu.HBM)


VMEM = pl.BlockSpec(memory_space=pltpu.VMEM)
HBM = pl.BlockSpec(memory_space=pltpu.HBM)
SMEM = pl.BlockSpec(memory_space=pltpu.SMEM)
ANY = pl.BlockSpec(memory_space=pl.ANY)


def start_all(copies):
    for copy in copies:
        copy.start()
    return copies


def wait_all(copies):
    for copy in copies:
        copy.wait()


CACHE_PARTS = 2


def cache_kernel(first, pool_ref, keys_ref, values_ref, raw, values, sem, out_sem):
    heads, tokens = raw.shape[:2]
    copies = start_all([pltpu.make_async_copy(pool_ref.at[:, first + h], raw.at[h], sem.at[h]) for h in range(heads)])
    rows = raw.reshape(heads, 2 * tokens, HD)
    to = lax.broadcasted_iota(jnp.int32, (2 * tokens, 2 * tokens), 0)
    source = lax.broadcasted_iota(jnp.int32, (2 * tokens, 2 * tokens), 1)
    wanted = jnp.where(to < tokens, 2 * to, 2 * (to - tokens) + 1)
    pick = jnp.where(source == wanted, 1.0, 0.0).astype(jnp.bfloat16)
    sent = []
    part = heads // CACHE_PARTS
    for p in range(CACHE_PARTS):
        wait_all(copies[p * part : (p + 1) * part])
        for h in range(p * part, (p + 1) * part, 2):
            both = jnp.concatenate([rows[h], rows[h + 1]], axis=1)
            made = jnp.dot(pick, both, preferred_element_type=jnp.float32).astype(jnp.bfloat16)
            for i in range(2):
                keys_ref[h + i] = made[:tokens, i * HD : (i + 1) * HD]
                values[h + i] = made[tokens:, i * HD : (i + 1) * HD]
        span = slice(p * part, (p + 1) * part)
        sent += start_all([pltpu.make_async_copy(values.at[span], values_ref.at[span], out_sem.at[p])])
    wait_all(sent)


def cache_by_head(pool, first, heads):
    tokens = pool.shape[0]
    return pl.pallas_call(
        functools.partial(cache_kernel, first),
        out_shape=(
            jax.ShapeDtypeStruct((heads, tokens, HD), pool.dtype),
            pltpu.HBM((heads, tokens, HD), pool.dtype),
        ),
        in_specs=[HBM],
        out_specs=(VMEM, HBM),
        scratch_shapes=[
            pltpu.VMEM((heads, tokens, 2, HD), pool.dtype),
            pltpu.VMEM((heads, tokens, HD), pool.dtype),
            pltpu.SemaphoreType.DMA((heads,)),
            pltpu.SemaphoreType.DMA((CACHE_PARTS,)),
        ],
        compiler_params=pltpu.CompilerParams(vmem_limit_bytes=12 * 2**20),
        cost_estimate=pl.CostEstimate(flops=0, bytes_accessed=12 * 10**6, transcendentals=0),
        name="cache_by_head",
    )(in_hbm(pool))


def lanes_of(x):
    return jnp.concatenate([x[c] for c in range(x.shape[0])], axis=1)


def step_rows(x, first, chunks):
    steps, _, count = x.shape[:3]
    flat = x.reshape(steps, x.shape[1], 2 * count, HD)
    return jnp.concatenate(
        [jnp.concatenate([flat[t, c] for c in range(first, first + chunks)], axis=1) for t in range(steps)], axis=0
    )


def index_kernel(me_ref, stored_ref, slot_ref, column_ref):
    requests = stored_ref.shape[1]
    steps = slot_ref.shape[1] // requests
    row = jnp.concatenate([stored_ref[...]] * steps, axis=1)
    slot_ref[...] = row - me_ref[0]
    wide = jnp.concatenate([row, jnp.zeros((1, HD - row.shape[1]), row.dtype)], axis=1)
    column_ref[...] = jnp.broadcast_to(wide.astype(jnp.float32), (HD, HD)).T[: row.shape[1], :1].astype(jnp.int32)


def index_work(first, stored, steps):
    rows = stored.shape[0] * steps
    return pl.pallas_call(
        index_kernel,
        out_shape=(jax.ShapeDtypeStruct((1, rows), jnp.int32), jax.ShapeDtypeStruct((rows, 1), jnp.int32)),
        in_specs=[SMEM, VMEM],
        out_specs=(VMEM, VMEM),
        compiler_params=pltpu.CompilerParams(vmem_limit_bytes=2 * 2**20),
        cost_estimate=pl.CostEstimate(flops=2 * 10**10, bytes_accessed=10**4, transcendentals=0),
        name="index_work",
    )(first, stored[None, :])


def low_kernel(count, me_ref, slot_ref, down_ref, *refs):
    blocks, (x_ref, low_ref, sem) = refs[:count], refs[count:]
    me = me_ref[0]
    holders, rank, width = down_ref.shape
    wait_all(
        start_all(
            [pltpu.make_async_copy(block, x_ref.at[:, :, me ^ k], sem.at[k]) for k, block in enumerate(blocks)]
        )
    )
    x = step_rows(x_ref, 0, x_ref.shape[1])
    rows = x.shape[0]
    made = lax.dot_general(
        down_ref.reshape(holders * rank, width)[...], x, CONTRACT_LANES, preferred_element_type=jnp.float32
    )
    slot = slot_ref[...]
    low = jnp.zeros((rank, rows), jnp.float32)
    for h in range(holders):
        low = low + jnp.where(slot == h, made[h * rank : (h + 1) * rank], 0.0)
    low = low.T
    low_ref[...] = jnp.concatenate([low[: rows // 2], low[rows // 2 :]], axis=1).astype(low_ref.dtype)


def low_of(me, blocks, slot, down):
    count = len(blocks)
    steps, chunks = blocks[0].shape[:2]
    rows = count * steps * 2
    rank = down.shape[1]
    return pl.pallas_call(
        functools.partial(low_kernel, count),
        out_shape=(
            jax.ShapeDtypeStruct((steps, chunks, count, 2, HD), jnp.bfloat16),
            jax.ShapeDtypeStruct((rows // 2, 2 * rank), jnp.bfloat16),
        ),
        in_specs=[SMEM, VMEM, VMEM] + [ANY] * count,
        out_specs=(VMEM, VMEM),
        scratch_shapes=[pltpu.SemaphoreType.DMA((count,))],
        compiler_params=pltpu.CompilerParams(vmem_limit_bytes=12 * 2**20),
        cost_estimate=pl.CostEstimate(flops=10**8, bytes_accessed=4 * 10**6, transcendentals=0),
        name="low_rows",
    )(me, slot, down, *blocks)


def put_chunks(buf, first, value):
    steps, count = buf.shape[1:3]
    flat = buf.reshape(buf.shape[0], steps, 2 * count, HD)
    wide = value.shape[1]
    for c in range(-(-wide // HD)):
        part = value[:, c * HD : min((c + 1) * HD, wide)]
        if part.shape[1] < HD:
            part = jnp.concatenate([part, jnp.zeros((part.shape[0], HD - part.shape[1]), part.dtype)], axis=1)
        part = part.astype(buf.dtype)
        for t in range(steps):
            flat[first + c, t] = part[t * 2 * count : (t + 1) * 2 * count]


def project_kernel(which, x_ref, w_ref, out_ref):
    x = step_rows(x_ref, 0, x_ref.shape[1])
    made = lax.dot_general(w_ref[which], x, CONTRACT_LANES, preferred_element_type=jnp.float32).T
    if which < 2:
        put_chunks(out_ref, 0, made)
    else:
        out_ref[...] = made


def project(which, x, weight):
    steps, _, count = x.shape[:3]
    columns = weight.shape[1]
    chunks = jax.ShapeDtypeStruct((-(-columns // HD), steps, count, 2, HD), jnp.bfloat16)
    base = jax.ShapeDtypeStruct((2 * steps * count, columns), jnp.float32)
    return pl.pallas_call(
        functools.partial(project_kernel, which),
        out_shape=chunks if which < 2 else base,
        in_specs=[VMEM, VMEM],
        out_specs=VMEM,
        compiler_params=pltpu.CompilerParams(vmem_limit_bytes=16 * 2**20),
        cost_estimate=pl.CostEstimate(flops=5 * 10**8, bytes_accessed=4 * 10**6, transcendentals=0),
        name="project",
    )(x, weight)


def update_kernel(stored_ref, query_ref, key_ref, base_ref, up_ref, *refs):
    lows, (send_ref, buf, sem) = refs[:-3], refs[-3:]
    half, packed = lows[0].shape
    rank = packed // 2
    rows = 2 * half
    count = send_ref.shape[0]
    low = lows[0][...].astype(jnp.float32)
    for more in lows[1:]:
        low = low + more[...].astype(jnp.float32)
    low = jnp.concatenate([low[:, :rank], low[:, rank:]], axis=0)
    batch = 256 // rank
    spread = jnp.concatenate([low] * batch, axis=1)
    ahead = stored_ref[...] - lax.broadcasted_iota(jnp.int32, (rows, batch * rank), 1) // rank
    total = jnp.zeros(base_ref.shape, jnp.float32)
    for a in range(0, up_ref.shape[0] // rank, batch):
        wide = jnp.where(ahead == a, spread, 0.0).astype(jnp.bfloat16)
        total = total + jnp.dot(wide, up_ref[a * rank : (a + batch) * rank], preferred_element_type=jnp.float32)
    each = query_ref.shape[0]
    buf[:each] = query_ref[...]
    buf[each : 2 * each] = key_ref[...]
    put_chunks(buf, 2 * each, base_ref[...] + adapter_scale * total)
    wait_all(
        start_all([pltpu.make_async_copy(buf.at[:, :, k], send_ref.at[k], sem.at[k]) for k in range(count)])
    )


def update_values(stored, query, key, base, up, lows):
    chunks, steps, count = query.shape[:3]
    return pl.pallas_call(
        update_kernel,
        out_shape=pltpu.HBM((count, 3 * chunks, steps, 2, HD), query.dtype),
        in_specs=[VMEM] * (5 + len(lows)),
        out_specs=HBM,
        scratch_shapes=[
            pltpu.VMEM((3 * chunks, steps, count, 2, HD), query.dtype),
            pltpu.SemaphoreType.DMA((count,)),
        ],
        compiler_params=pltpu.CompilerParams(vmem_limit_bytes=8 * 2**20),
        cost_estimate=pl.CostEstimate(flops=3 * 10**8, bytes_accessed=4 * 10**6, transcendentals=0),
        name="update_values",
    )(stored, query, key, base, up, *lows)


def attend_kernel(cos_ref, sin_ref, live_ref, pieces_ref, *refs):
    keys_refs, values_refs, (out_ref, values_buf, kn_ref, vn_ref, sem) = refs[:2], refs[2:4], refs[4:]
    count, _, steps = pieces_ref.shape[:3]
    rows = 2 * steps
    each = pieces_ref.shape[1] // 3
    heads = 2 * out_ref.shape[1] // count
    lanes = heads * HD
    group = rows * HEAD_BLOCK
    chips = range(count // 2)
    places = [divmod(c, count // 4) for c in chips]
    fetches = start_all(
        [
            pltpu.make_async_copy(values_refs[half].at[at * heads : (at + 1) * heads], values_buf.at[c], sem.at[c])
            for c, (half, at) in enumerate(places)
        ]
    )
    cosine = cos_ref[...][:rows]
    sine = sin_ref[...][:rows]
    left = lax.broadcasted_iota(jnp.int32, (rows, HD), 1) < HD // 2

    def chip_columns(chip, at):
        low = [pieces_ref[2 * chip, at + c].reshape(rows, HD).astype(jnp.float32) for c in range(each)]
        high = [pieces_ref[2 * chip + 1, at + c].reshape(rows, HD).astype(jnp.float32) for c in range(each)]
        high = [pltpu.roll(x, HD // 2, 1) for x in high]
        whole = low[:-1] + [jnp.where(left, low[-1], high[0])]
        return whole + [jnp.where(left, a, b) for a, b in zip(high[:-1], high[1:])]

    def rotated(parts):
        return [x * cosine + pltpu.roll(x, HD // 2, 1) * sine for x in parts]

    row_head = lax.broadcasted_iota(jnp.int32, (group, lanes), 0) % HEAD_BLOCK
    lane_head = lax.broadcasted_iota(jnp.int32, (group, lanes), 1) // HD
    own_head = row_head == lane_head
    row_j = lax.broadcasted_iota(jnp.int32, (group, 16), 0) // HEAD_BLOCK
    new_j = lax.broadcasted_iota(jnp.int32, (group, 16), 1)
    new_live = (new_j < rows) & (new_j % 2 == row_j % 2) & (new_j // 2 <= row_j // 2)
    live = jnp.concatenate(
        [
            jnp.broadcast_to(live_ref[j % 2 : j % 2 + 1, :], (HEAD_BLOCK, live_ref.shape[1]))
            for j in range(rows)
        ],
        axis=0,
    )
    live = live > 0
    kn_ref[...] = jnp.zeros_like(kn_ref)
    vn_ref[...] = jnp.zeros_like(vn_ref)
    spreads = []
    for c in chips:
        query = jnp.concatenate(rotated(chip_columns(c, 0)), axis=1)
        kn_ref[c, 0:rows] = jnp.concatenate(rotated(chip_columns(c, each)), axis=1)
        vn_ref[c, 0:rows] = jnp.concatenate(chip_columns(c, 2 * each), axis=1)
        spread = jnp.concatenate(
            [jnp.broadcast_to(query[j : j + 1], (HEAD_BLOCK, lanes)) for j in range(rows)], axis=0
        )
        spreads.append(jnp.where(own_head, spread, 0.0).astype(jnp.bfloat16))
    scores, fresh = [], []
    for c in chips:
        half, at = places[c]
        keys = jnp.concatenate([keys_refs[half][at * heads + h] for h in range(heads)], axis=1)
        kn = kn_ref[c].astype(jnp.bfloat16)
        scores.append(lax.dot_general(spreads[c], keys, CONTRACT_LANES, preferred_element_type=jnp.float32))
        fresh.append(lax.dot_general(spreads[c], kn, CONTRACT_LANES, preferred_element_type=jnp.float32))
    weights, fresh_weights, totals = [], [], []
    for c in chips:
        old = jnp.where(live, scores[c] * (HD**-0.5), masked_score)
        new = jnp.where(new_live, fresh[c] * (HD**-0.5), masked_score)
        top = jnp.maximum(jnp.max(old, axis=1, keepdims=True), jnp.max(new, axis=1, keepdims=True))
        old = jnp.where(live, jnp.exp(old - top), 0.0)
        new = jnp.where(new_live, jnp.exp(new - top), 0.0)
        totals.append(jnp.sum(old, axis=1, keepdims=True) + jnp.sum(new, axis=1, keepdims=True))
        weights.append(old.astype(jnp.bfloat16))
        fresh_weights.append(new.astype(jnp.bfloat16))
    wait_all(fetches)
    for c in chips:
        values = lanes_of(values_buf[c])
        vn = vn_ref[c].astype(jnp.bfloat16)
        mixed = jnp.dot(weights[c], values, preferred_element_type=jnp.float32)
        mixed = mixed + jnp.dot(fresh_weights[c], vn, preferred_element_type=jnp.float32)
        mixed = jnp.where(own_head, mixed / totals[c], 0.0)
        out = jnp.sum(mixed.reshape(rows, HEAD_BLOCK, lanes), axis=1).astype(out_ref.dtype)
        for t in range(steps):
            for h in range(heads):
                out_ref[t, c * heads + h] = out[2 * t : 2 * t + 2, h * HD : (h + 1) * HD]


def attend(cosine, sine, live, pieces, keys, values):
    count, _, steps = pieces.shape[:3]
    heads, tokens = 2 * keys[0].shape[0], keys[0].shape[1]
    chips = count // 2
    per = heads // chips
    return pl.pallas_call(
        attend_kernel,
        out_shape=jax.ShapeDtypeStruct((steps, heads, 2, HD), jnp.bfloat16),
        in_specs=[VMEM] * 6 + [HBM] * 2,
        out_specs=VMEM,
        scratch_shapes=[pltpu.VMEM((chips, per, tokens, HD), jnp.bfloat16)]
        + [pltpu.VMEM((chips, 16, per * HD), jnp.float32)] * 2
        + [pltpu.SemaphoreType.DMA((chips,))],
        compiler_params=pltpu.CompilerParams(vmem_limit_bytes=16 * 2**20),
        cost_estimate=pl.CostEstimate(flops=10**9, bytes_accessed=6 * 10**6, transcendentals=0),
        name="attention",
    )(cosine, sine, live, pieces, *keys, *[in_hbm(x) for x in values])


def chip_plan(
    count,
    hidden,
    query_key_value_weight,
    adapter_down_maps,
    adapter_up_maps,
    adapter_storage_row,
    request_adapter,
    lengths,
    request_page_table,
    key_value_pool,
):
    me = lax.axis_index("replica")
    steps, req_dev, width = hidden.shape
    heads = width // HD
    holder_count, rank, _ = adapter_down_maps.shape
    pool_pages, page_len = key_value_pool.shape[:2]
    adapter_count = adapter_storage_row.shape[0]

    tokens = pool_pages * page_len
    pool = key_value_pool.reshape(tokens, 2, heads, HD).transpose(0, 2, 1, 3)

    stored = jnp.sum(
        jnp.where(
            request_adapter[:, None] == jnp.arange(adapter_count, dtype=jnp.int32)[None, :],
            adapter_storage_row[None, :],
            0,
        ),
        axis=1,
    )
    slot, column = index_work((me * holder_count).astype(jnp.int32).reshape(1), stored, steps)

    held = {m: trade(hidden, m, count) for m in range(count - 4, 0, -4)}
    own, slot, column = lax.optimization_barrier((hidden, slot, column))
    held[2] = trade(own, 2, count)
    own, held[4] = lax.optimization_barrier((hidden, held[4]))
    held[1] = trade(own, 1, count)
    held[0] = hidden
    held.update({m | 2: trade(held[m], 2, count) for m in range(4, count, 4)})
    held.update({m | 1: trade(held[m], 1, count) for m in range(2, count, 2)})
    blocks = [held[k].reshape(steps, req_dev, heads, HD).transpose(0, 2, 1, 3) for k in range(count)]
    blocks[0] = in_hbm(blocks[0])

    x, low = low_of(me.astype(jnp.int32).reshape(1), blocks, slot, adapter_down_maps)
    weight = query_key_value_weight.transpose(0, 2, 1)
    arrived = [trade(low, m, count) for m in (1, 2, 3)]
    query, key = project(0, x, weight), project(1, x, weight)
    arrived, query, key, pool = lax.optimization_barrier((arrived, query, key, pool))
    low = (low + arrived[0]) + (arrived[1] + arrived[2])
    arrived = [trade(low, m, count) for m in range(4, count, 4)]
    base = project(2, x, weight)
    early_cache = cache_by_head(pool, 0, heads // 2)
    arrived, base, early_cache = lax.optimization_barrier((arrived, base, early_cache))
    send = update_values(column, query, key, base, adapter_up_maps.reshape(adapter_count * rank, -1), [low, *arrived])
    send, pool = lax.optimization_barrier((send, pool))
    late_cache = cache_by_head(pool, heads // 2, heads // 2)
    pieces = lax.all_to_all(send, "replica", split_axis=0, concat_axis=0, tiled=True)

    my_lengths = lax.dynamic_slice_in_dim(lengths, me * req_dev, req_dev)
    cosine, sine = rotation(my_lengths, steps)
    live = live_tokens(my_lengths, request_page_table, pool_pages, page_len).astype(jnp.int32)
    keys, values = zip(early_cache, late_cache)
    out = attend(cosine, sine, live.reshape(req_dev, tokens), pieces, keys, values)
    return out.transpose(0, 2, 1, 3).reshape(steps, req_dev, width)


def per_device(replicas, *arrays):
    columns = arrays[1].shape[2]
    whole_heads = replicas % 4 == 0 and (2 * columns) % HD == 0 and columns % HD == HD // 2
    plan = chip_plan if whole_heads and arrays[0].shape[1] == 2 else general_plan
    return plan(replicas, *arrays)


def solution(mesh):
    placed = (
        P(None, ("groups", "replica"), None),
        P(None, None, "replica"),
        P("replica", None, None),
        P(None, None, "replica"),
        P(),
        P("groups"),
        P("groups"),
        P(("groups", "replica"), None),
        P(("groups", "replica"), None, None, None),
    )
    return jax.shard_map(
        functools.partial(per_device, mesh.shape["replica"]),
        mesh=mesh,
        in_specs=placed,
        out_specs=P(None, ("groups", "replica"), None),
        check_vma=False,
    )
```

```python
import functools

import jax
import jax.numpy as jnp
from jax import lax
from jax.experimental import pallas as pl
from jax.experimental.pallas import tpu as pltpu
from jax.sharding import PartitionSpec as P

HD = 128
ROWS = 8
HEAD_BLOCK = 8

adapter_scale = 2.0
masked_score = -1e30


def attention_kernel(steps, req_dev, q_ref, k_ref, v_ref, cos_ref, sin_ref, live_ref, kv_ref, out_ref, kn_ref, vn_ref):
    rows = steps * req_dev
    width = q_ref.shape[1]
    lanes = HEAD_BLOCK * HD
    group = rows * HEAD_BLOCK
    cosine = cos_ref[...]
    sine = sin_ref[...]

    def rotated(x):
        pieces = []
        for h in range(HEAD_BLOCK):
            head = x[:, h * HD : (h + 1) * HD]
            pieces.append(head * cosine + pltpu.roll(head, HD // 2, 1) * sine)
        return jnp.concatenate(pieces, axis=1)

    row_head = lax.broadcasted_iota(jnp.int32, (group, lanes), 0) % HEAD_BLOCK
    lane_head = lax.broadcasted_iota(jnp.int32, (group, lanes), 1) // HD
    own_head = row_head == lane_head
    row_j = lax.broadcasted_iota(jnp.int32, (group, 16), 0) // HEAD_BLOCK
    new_j = lax.broadcasted_iota(jnp.int32, (group, 16), 1)
    new_live = (new_j < rows) & (new_j % req_dev == row_j % req_dev) & (new_j // req_dev <= row_j // req_dev)
    live_all = live_ref[...]
    live = jnp.concatenate(
        [
            jnp.broadcast_to(live_all[j % req_dev : j % req_dev + 1], (HEAD_BLOCK, live_all.shape[1]))
            for j in range(rows)
        ],
        axis=0,
    )
    live = live > 0
    kn_ref[...] = jnp.zeros_like(kn_ref)
    vn_ref[...] = jnp.zeros_like(vn_ref)
    contract_lanes = (((1,), (1,)), ((), ()))
    for c in range(width // lanes):
        cols = slice(c * lanes, (c + 1) * lanes)
        query = rotated(q_ref[:, cols].astype(jnp.float32))
        key_new = rotated(k_ref[:, cols].astype(jnp.float32))
        kn_ref[0:8] = key_new
        vn_ref[0:8] = v_ref[:, cols].astype(jnp.float32)
        kn = kn_ref[...].astype(jnp.bfloat16)
        vn = vn_ref[...].astype(jnp.bfloat16)
        spread = jnp.concatenate(
            [jnp.broadcast_to(query[j : j + 1], (HEAD_BLOCK, lanes)) for j in range(rows)], axis=0
        )
        spread = jnp.where(own_head, spread, 0.0).astype(jnp.bfloat16)
        kv = kv_ref[:, cols]
        scores = lax.dot_general(spread, kv, contract_lanes, preferred_element_type=jnp.float32) * (HD**-0.5)
        scores = jnp.where(live, scores, masked_score)
        fresh = lax.dot_general(spread, kn, contract_lanes, preferred_element_type=jnp.float32) * (HD**-0.5)
        fresh = jnp.where(new_live, fresh, masked_score)
        top = jnp.maximum(jnp.max(scores, axis=1, keepdims=True), jnp.max(fresh, axis=1, keepdims=True))
        weights = jnp.where(live, jnp.exp(scores - top), 0.0)
        fresh = jnp.where(new_live, jnp.exp(fresh - top), 0.0)
        totals = jnp.sum(weights, axis=1, keepdims=True) + jnp.sum(fresh, axis=1, keepdims=True)
        weights = pltpu.roll(weights, 1, 1).astype(jnp.bfloat16)
        mixed = jnp.dot(weights, kv, preferred_element_type=jnp.float32)
        mixed = mixed + jnp.dot(fresh.astype(jnp.bfloat16), vn, preferred_element_type=jnp.float32)
        mixed = jnp.where(own_head, mixed / totals, 0.0)
        out = jnp.sum(mixed.reshape(rows, HEAD_BLOCK, lanes), axis=1)
        out_ref[:, cols] = out.astype(out_ref.dtype)


def attention(steps, req_dev, q, k, v, cosine, sine, live, kv):
    rows = steps * req_dev
    width = q.shape[1]
    vmem = pl.BlockSpec(memory_space=pltpu.VMEM)
    return pl.pallas_call(
        functools.partial(attention_kernel, steps, req_dev),
        out_shape=jax.ShapeDtypeStruct((rows, width), jnp.bfloat16),
        in_specs=[vmem] * 7,
        out_specs=vmem,
        scratch_shapes=[pltpu.VMEM((16, HEAD_BLOCK * HD), jnp.float32)] * 2,
        compiler_params=pltpu.CompilerParams(vmem_limit_bytes=32 * 2**20),
        cost_estimate=pl.CostEstimate(flops=10**9, bytes_accessed=6 * 10**6, transcendentals=0),
        name="attention",
    )(q, k, v, cosine, sine, live, kv)


def rotation(my_lengths, steps):
    rows = steps * my_lengths.shape[0]
    positions = (my_lengths[None, :] + jnp.arange(steps, dtype=jnp.int32)[:, None]).reshape(rows)
    positions = jnp.pad(positions, (0, ROWS - rows))
    half = HD // 2
    frequency = jnp.exp(jnp.arange(half, dtype=jnp.float32) * (-2.0 * jnp.log(10000.0) / HD))
    angles = positions.astype(jnp.float32)[:, None] * frequency[None, :]
    cosine = jnp.cos(angles)
    sine = jnp.sin(angles)
    cosine = jnp.concatenate([cosine, cosine], axis=1)
    sine = jnp.concatenate([-sine, sine], axis=1)
    return cosine, sine


def live_tokens(my_lengths, request_page_table, pool_pages, page_len):
    pages = jnp.arange(pool_pages, dtype=jnp.int32)
    max_pages = request_page_table.shape[1]
    place = jnp.max(
        jnp.where(
            request_page_table[:, :, None] == pages[None, None, :],
            jnp.arange(max_pages, dtype=jnp.int32)[None, :, None],
            -1,
        ),
        axis=1,
    )
    token = place[:, :, None] * page_len + jnp.arange(page_len, dtype=jnp.int32)[None, None, :]
    return (place[:, :, None] >= 0) & (token < my_lengths[:, None, None])


def live_rows(my_lengths, request_page_table, pool_pages, page_len):
    alive = live_tokens(my_lengths, request_page_table, pool_pages, page_len)
    live = jnp.stack([alive, jnp.zeros_like(alive)], axis=-1).astype(jnp.int32)
    return live.reshape(request_page_table.shape[0], pool_pages * page_len * 2)


def general_plan(
    replicas,
    hidden,
    query_key_value_weight,
    adapter_down_maps,
    adapter_up_maps,
    adapter_storage_row,
    request_adapter,
    lengths,
    request_page_table,
    key_value_pool,
):
    my_index = lax.axis_index("replica")
    steps, req_dev, width = hidden.shape
    rows = steps * req_dev
    columns = query_key_value_weight.shape[2]
    holder_count, rank, _ = adapter_down_maps.shape
    pool_pages, page_len = key_value_pool.shape[:2]
    adapter_count = adapter_storage_row.shape[0]
    chips = replicas // 2
    total = replicas * ROWS

    block = jnp.pad(hidden.reshape(rows, width), ((0, ROWS - rows), (0, 0)))
    same_core = [[2 * chip + core for chip in range(chips)] for core in range(2)]
    mine = lax.all_to_all(
        jnp.broadcast_to(block[None], (chips, ROWS, width)),
        "replica",
        split_axis=0,
        concat_axis=0,
        axis_index_groups=same_core,
        tiled=True,
    )
    other = lax.ppermute(mine, "replica", [(i, i ^ 1) for i in range(replicas)])
    first = my_index % 2 == 0
    gathered = jnp.stack([jnp.where(first, mine, other), jnp.where(first, other, mine)])
    gathered = gathered.reshape(total, width)

    stored_rows = jnp.sum(
        jnp.where(
            request_adapter[:, None] == jnp.arange(adapter_count, dtype=jnp.int32)[None, :],
            adapter_storage_row[None, :],
            0,
        ),
        axis=1,
    )
    by_block = stored_rows.reshape(chips, 2, 1, req_dev).transpose(1, 0, 2, 3)
    by_block = jnp.broadcast_to(by_block, (2, chips, steps, req_dev)).reshape(2, chips, rows)
    row_stored = jnp.pad(by_block, ((0, 0), (0, 0), (0, ROWS - rows)), constant_values=-1).reshape(total)

    down = jnp.einsum("nd,hfd->nhf", gathered, adapter_down_maps, preferred_element_type=jnp.float32)
    slots = my_index * holder_count + jnp.arange(holder_count, dtype=jnp.int32)
    own = row_stored[:, None] == slots[None, :]
    low = jnp.sum(jnp.where(own[:, :, None], down, 0.0), axis=1).astype(jnp.bfloat16)
    low = jnp.concatenate([low[: total // 2], low[total // 2 :]], axis=1)
    low = lax.all_to_all(
        jnp.broadcast_to(low[None], (replicas,) + low.shape), "replica", split_axis=0, concat_axis=0, tiled=True
    )
    low = jnp.sum(low.astype(jnp.float32), axis=0)
    low = jnp.concatenate([low[:, :rank], low[:, rank:]], axis=0)

    projected = jnp.einsum("nd,idc->nic", gathered, query_key_value_weight, preferred_element_type=jnp.float32)

    def update(first_adapter, maps):
        held = maps.shape[0]
        which = first_adapter + jnp.arange(held, dtype=jnp.int32)
        wide = jnp.where((row_stored[:, None] == which[None, :])[:, :, None], low[:, None, :], 0.0)
        return jnp.dot(
            wide.astype(jnp.bfloat16).reshape(total, held * rank),
            maps.reshape(held * rank, columns),
            preferred_element_type=jnp.float32,
        )

    step_adapters = 64
    if adapter_count <= step_adapters:
        updated = update(0, adapter_up_maps)
    else:
        updated = lax.fori_loop(
            0,
            adapter_count // step_adapters,
            lambda i, sofar: sofar
            + update(
                i * step_adapters,
                lax.dynamic_slice_in_dim(adapter_up_maps, i * step_adapters, step_adapters, 0),
            ),
            jnp.zeros((total, columns), jnp.float32),
        )
    value = projected[:, 2] + adapter_scale * updated
    combined = jnp.concatenate([projected[:, 0], projected[:, 1], value], axis=1).astype(jnp.bfloat16)
    combined = combined.reshape(2, chips, ROWS, 3 * columns).transpose(1, 0, 2, 3)
    combined = combined.reshape(replicas, ROWS, 3 * columns)
    arrived = lax.all_to_all(combined, "replica", split_axis=0, concat_axis=0, tiled=True)
    arrived = arrived.reshape(replicas, ROWS, 3, columns).transpose(2, 1, 0, 3).reshape(3, ROWS, width)

    my_lengths = lax.dynamic_slice_in_dim(lengths, my_index * req_dev, req_dev)
    cosine, sine = rotation(my_lengths, steps)
    live = live_rows(my_lengths, request_page_table, pool_pages, page_len)
    kv = key_value_pool.reshape(pool_pages * page_len * 2, width)
    out = attention(steps, req_dev, arrived[0], arrived[1], arrived[2], cosine, sine, live, kv)
    return out.reshape(steps, req_dev, width)


def rotation_rows(lengths, first, req_dev, steps):
    row = jnp.arange(ROWS, dtype=jnp.int32)
    wanted = first + row % req_dev
    chosen = jnp.where(wanted[:, None] == jnp.arange(lengths.shape[0], dtype=jnp.int32)[None, :], lengths[None, :], 0)
    positions = jnp.sum(chosen, axis=1, keepdims=True) + (row // req_dev)[:, None]
    lane = jnp.arange(HD, dtype=jnp.int32)
    frequency = jnp.exp((lane % (HD // 2)).astype(jnp.float32) * (-2.0 * jnp.log(10000.0) / HD))
    angles = positions.astype(jnp.float32) * frequency[None, :]
    return jnp.cos(angles), jnp.where(lane < HD // 2, -1.0, 1.0)[None, :] * jnp.sin(angles)


def live_lanes(lengths, first, request_page_table, tokens, page_len):
    req_dev, max_pages = request_page_table.shape
    wanted = first + jnp.arange(req_dev, dtype=jnp.int32)
    chosen = jnp.where(wanted[:, None] == jnp.arange(lengths.shape[0], dtype=jnp.int32)[None, :], lengths[None, :], 0)
    lane = jnp.arange(tokens, dtype=jnp.int32)
    page = jnp.arange(max_pages, dtype=jnp.int32)
    place = jnp.max(
        jnp.where(request_page_table[:, :, None] == (lane // page_len)[None, None, :], page[None, :, None], -1),
        axis=1,
    )
    token = place * page_len + (lane % page_len)[None, :]
    return ((place >= 0) & (token < jnp.sum(chosen, axis=1, keepdims=True))).astype(jnp.int32)


def trade(value, mask, count):
    return lax.ppermute(value, "replica", [(i, i ^ mask) for i in range(count)])


CONTRACT_LANES = (((1,), (1,)), ((), ()))


def in_hbm(x):
    return pltpu.with_memory_space_constraint(x, pltpu.HBM)


VMEM = pl.BlockSpec(memory_space=pltpu.VMEM)
HBM = pl.BlockSpec(memory_space=pltpu.HBM)
SMEM = pl.BlockSpec(memory_space=pltpu.SMEM)
ANY = pl.BlockSpec(memory_space=pl.ANY)


def start_all(copies):
    for copy in copies:
        copy.start()
    return copies


def wait_all(copies):
    for copy in copies:
        copy.wait()


CACHE_SECTION = 10


def cache_kernel(first, pool_ref, keys_ref, values_ref, raw, values, sem, out_sem):
    heads, tokens = raw.shape[:2]
    copies = start_all([pltpu.make_async_copy(pool_ref.at[:, first + h], raw.at[h], sem.at[h]) for h in range(heads)])
    rows = raw.reshape(heads, 2 * tokens, HD)
    to = lax.broadcasted_iota(jnp.int32, (2 * tokens, 2 * tokens), 0)
    source = lax.broadcasted_iota(jnp.int32, (2 * tokens, 2 * tokens), 1)
    wanted = jnp.where(to < tokens, 2 * to, 2 * (to - tokens) + 1)
    pick = jnp.where(source == wanted, 1.0, 0.0).astype(jnp.bfloat16)
    sent = []
    part = CACHE_SECTION
    for p in range(heads // part):
        wait_all(copies[p * part : (p + 1) * part])
        for h in range(p * part, (p + 1) * part, 2):
            both = jnp.concatenate([rows[h], rows[h + 1]], axis=1)
            made = jnp.dot(pick, both, preferred_element_type=jnp.float32).astype(jnp.bfloat16)
            for i in range(2):
                keys_ref[h + i] = made[:tokens, i * HD : (i + 1) * HD]
                values[h + i] = made[tokens:, i * HD : (i + 1) * HD]
        span = slice(p * part, (p + 1) * part)
        sent += start_all([pltpu.make_async_copy(values.at[span], values_ref.at[span], out_sem.at[p])])
    wait_all(sent)


def cache_by_head(pool, first, heads):
    tokens = pool.shape[0]
    return pl.pallas_call(
        functools.partial(cache_kernel, first),
        out_shape=(
            jax.ShapeDtypeStruct((heads, tokens, HD), pool.dtype),
            pltpu.HBM((heads, tokens, HD), pool.dtype),
        ),
        in_specs=[HBM],
        out_specs=(VMEM, HBM),
        scratch_shapes=[
            pltpu.VMEM((heads, tokens, 2, HD), pool.dtype),
            pltpu.VMEM((heads, tokens, HD), pool.dtype),
            pltpu.SemaphoreType.DMA((heads,)),
            pltpu.SemaphoreType.DMA((heads // CACHE_SECTION,)),
        ],
        compiler_params=pltpu.CompilerParams(vmem_limit_bytes=12 * 2**20),
        cost_estimate=pl.CostEstimate(flops=0, bytes_accessed=12 * 10**6, transcendentals=0),
        name="cache_by_head",
    )(in_hbm(pool))


def lanes_of(x):
    return jnp.concatenate([x[c] for c in range(x.shape[0])], axis=1)


def step_rows(x, first, chunks):
    steps, _, count = x.shape[:3]
    flat = x.reshape(steps, x.shape[1], 2 * count, HD)
    return jnp.concatenate(
        [jnp.concatenate([flat[t, c] for c in range(first, first + chunks)], axis=1) for t in range(steps)], axis=0
    )


def index_kernel(me_ref, stored_ref, slot_ref, column_ref):
    requests = stored_ref.shape[1]
    steps = slot_ref.shape[1] // requests
    row = jnp.concatenate([stored_ref[...]] * steps, axis=1)
    slot_ref[...] = row - me_ref[0]
    wide = jnp.concatenate([row, jnp.zeros((1, HD - row.shape[1]), row.dtype)], axis=1)
    column_ref[...] = jnp.broadcast_to(wide.astype(jnp.float32), (HD, HD)).T[: row.shape[1], :1].astype(jnp.int32)


def index_work(first, stored, steps):
    rows = stored.shape[0] * steps
    return pl.pallas_call(
        index_kernel,
        out_shape=(jax.ShapeDtypeStruct((1, rows), jnp.int32), jax.ShapeDtypeStruct((rows, 1), jnp.int32)),
        in_specs=[SMEM, VMEM],
        out_specs=(VMEM, VMEM),
        compiler_params=pltpu.CompilerParams(vmem_limit_bytes=2 * 2**20),
        cost_estimate=pl.CostEstimate(flops=2 * 10**10, bytes_accessed=10**4, transcendentals=0),
        name="index_work",
    )(first, stored[None, :])


def low_kernel(count, me_ref, slot_ref, down_ref, *refs):
    blocks, (x_ref, low_ref, sem) = refs[:count], refs[count:]
    me = me_ref[0]
    holders, rank, width = down_ref.shape
    wait_all(
        start_all(
            [pltpu.make_async_copy(block, x_ref.at[:, :, me ^ k], sem.at[k]) for k, block in enumerate(blocks)]
        )
    )
    x = step_rows(x_ref, 0, x_ref.shape[1])
    rows = x.shape[0]
    made = lax.dot_general(
        down_ref.reshape(holders * rank, width)[...], x, CONTRACT_LANES, preferred_element_type=jnp.float32
    )
    slot = slot_ref[...]
    low = jnp.zeros((rank, rows), jnp.float32)
    for h in range(holders):
        low = low + jnp.where(slot == h, made[h * rank : (h + 1) * rank], 0.0)
    low = low.T
    low_ref[...] = jnp.concatenate([low[: rows // 2], low[rows // 2 :]], axis=1).astype(low_ref.dtype)


def low_of(me, blocks, slot, down):
    count = len(blocks)
    steps, chunks = blocks[0].shape[:2]
    rows = count * steps * 2
    rank = down.shape[1]
    return pl.pallas_call(
        functools.partial(low_kernel, count),
        out_shape=(
            jax.ShapeDtypeStruct((steps, chunks, count, 2, HD), jnp.bfloat16),
            jax.ShapeDtypeStruct((rows // 2, 2 * rank), jnp.bfloat16),
        ),
        in_specs=[SMEM, VMEM, VMEM] + [ANY] * count,
        out_specs=(VMEM, VMEM),
        scratch_shapes=[pltpu.SemaphoreType.DMA((count,))],
        compiler_params=pltpu.CompilerParams(vmem_limit_bytes=12 * 2**20),
        cost_estimate=pl.CostEstimate(flops=10**8, bytes_accessed=4 * 10**6, transcendentals=0),
        name="low_rows",
    )(me, slot, down, *blocks)


def put_chunks(buf, first, value):
    steps, count = buf.shape[1:3]
    flat = buf.reshape(buf.shape[0], steps, 2 * count, HD)
    wide = value.shape[1]
    for c in range(-(-wide // HD)):
        part = value[:, c * HD : min((c + 1) * HD, wide)]
        if part.shape[1] < HD:
            part = jnp.concatenate([part, jnp.zeros((part.shape[0], HD - part.shape[1]), part.dtype)], axis=1)
        part = part.astype(buf.dtype)
        for t in range(steps):
            flat[first + c, t] = part[t * 2 * count : (t + 1) * 2 * count]


def project_kernel(which, x_ref, w_ref, out_ref):
    x = step_rows(x_ref, 0, x_ref.shape[1])
    made = lax.dot_general(w_ref[which], x, CONTRACT_LANES, preferred_element_type=jnp.float32).T
    if which < 2:
        put_chunks(out_ref, 0, made)
    else:
        out_ref[...] = made


def project(which, x, weight):
    steps, _, count = x.shape[:3]
    columns = weight.shape[1]
    chunks = jax.ShapeDtypeStruct((-(-columns // HD), steps, count, 2, HD), jnp.bfloat16)
    base = jax.ShapeDtypeStruct((2 * steps * count, columns), jnp.float32)
    return pl.pallas_call(
        functools.partial(project_kernel, which),
        out_shape=chunks if which < 2 else base,
        in_specs=[VMEM, VMEM],
        out_specs=VMEM,
        compiler_params=pltpu.CompilerParams(vmem_limit_bytes=16 * 2**20),
        cost_estimate=pl.CostEstimate(flops=5 * 10**8, bytes_accessed=4 * 10**6, transcendentals=0),
        name="project",
    )(x, weight)


def update_kernel(stored_ref, query_ref, key_ref, base_ref, up_ref, *refs):
    lows, (send_ref, buf, sem) = refs[:-3], refs[-3:]
    half, packed = lows[0].shape
    rank = packed // 2
    rows = 2 * half
    count = send_ref.shape[0]
    low = lows[0][...].astype(jnp.float32)
    for more in lows[1:]:
        low = low + more[...].astype(jnp.float32)
    low = jnp.concatenate([low[:, :rank], low[:, rank:]], axis=0)
    batch = 256 // rank
    spread = jnp.concatenate([low] * batch, axis=1)
    ahead = stored_ref[...] - lax.broadcasted_iota(jnp.int32, (rows, batch * rank), 1) // rank
    total = jnp.zeros(base_ref.shape, jnp.float32)
    for a in range(0, up_ref.shape[0] // rank, batch):
        wide = jnp.where(ahead == a, spread, 0.0).astype(jnp.bfloat16)
        total = total + jnp.dot(wide, up_ref[a * rank : (a + batch) * rank], preferred_element_type=jnp.float32)
    each = query_ref.shape[0]
    buf[:each] = query_ref[...]
    buf[each : 2 * each] = key_ref[...]
    put_chunks(buf, 2 * each, base_ref[...] + adapter_scale * total)
    wait_all(
        start_all([pltpu.make_async_copy(buf.at[:, :, k], send_ref.at[k], sem.at[k]) for k in range(count)])
    )


def update_values(stored, query, key, base, up, lows):
    chunks, steps, count = query.shape[:3]
    return pl.pallas_call(
        update_kernel,
        out_shape=pltpu.HBM((count, 3 * chunks, steps, 2, HD), query.dtype),
        in_specs=[VMEM] * (5 + len(lows)),
        out_specs=HBM,
        scratch_shapes=[
            pltpu.VMEM((3 * chunks, steps, count, 2, HD), query.dtype),
            pltpu.SemaphoreType.DMA((count,)),
        ],
        compiler_params=pltpu.CompilerParams(vmem_limit_bytes=8 * 2**20),
        cost_estimate=pl.CostEstimate(flops=3 * 10**8, bytes_accessed=4 * 10**6, transcendentals=0),
        name="update_values",
    )(stored, query, key, base, up, *lows)


def attend_kernel(cos_ref, sin_ref, live_ref, pieces_ref, *refs):
    keys_refs, values_refs, (out_ref, values_buf, kn_ref, vn_ref, sem) = refs[:2], refs[2:4], refs[4:]
    count, _, steps = pieces_ref.shape[:3]
    rows = 2 * steps
    each = pieces_ref.shape[1] // 3
    heads = 2 * out_ref.shape[1] // count
    lanes = heads * HD
    group = rows * HEAD_BLOCK
    chips = range(count // 2)
    early = keys_refs[0].shape[0] // heads
    places = [(0, c) if c < early else (1, c - early) for c in chips]
    fetches = start_all(
        [
            pltpu.make_async_copy(values_refs[half].at[at * heads : (at + 1) * heads], values_buf.at[c], sem.at[c])
            for c, (half, at) in enumerate(places)
        ]
    )
    cosine = cos_ref[...][:rows]
    sine = sin_ref[...][:rows]
    left = lax.broadcasted_iota(jnp.int32, (rows, HD), 1) < HD // 2

    def chip_columns(chip, at):
        low = [pieces_ref[2 * chip, at + c].reshape(rows, HD).astype(jnp.float32) for c in range(each)]
        high = [pieces_ref[2 * chip + 1, at + c].reshape(rows, HD).astype(jnp.float32) for c in range(each)]
        high = [pltpu.roll(x, HD // 2, 1) for x in high]
        whole = low[:-1] + [jnp.where(left, low[-1], high[0])]
        return whole + [jnp.where(left, a, b) for a, b in zip(high[:-1], high[1:])]

    def rotated(parts):
        return [x * cosine + pltpu.roll(x, HD // 2, 1) * sine for x in parts]

    row_head = lax.broadcasted_iota(jnp.int32, (group, lanes), 0) % HEAD_BLOCK
    lane_head = lax.broadcasted_iota(jnp.int32, (group, lanes), 1) // HD
    own_head = row_head == lane_head
    row_j = lax.broadcasted_iota(jnp.int32, (group, 16), 0) // HEAD_BLOCK
    new_j = lax.broadcasted_iota(jnp.int32, (group, 16), 1)
    new_live = (new_j < rows) & (new_j % 2 == row_j % 2) & (new_j // 2 <= row_j // 2)
    live = jnp.concatenate(
        [
            jnp.broadcast_to(live_ref[j % 2 : j % 2 + 1, :], (HEAD_BLOCK, live_ref.shape[1]))
            for j in range(rows)
        ],
        axis=0,
    )
    live = live > 0
    kn_ref[...] = jnp.zeros_like(kn_ref)
    vn_ref[...] = jnp.zeros_like(vn_ref)
    spreads = []
    for c in chips:
        query = jnp.concatenate(rotated(chip_columns(c, 0)), axis=1)
        kn_ref[c, 0:rows] = jnp.concatenate(rotated(chip_columns(c, each)), axis=1)
        vn_ref[c, 0:rows] = jnp.concatenate(chip_columns(c, 2 * each), axis=1)
        spread = jnp.concatenate(
            [jnp.broadcast_to(query[j : j + 1], (HEAD_BLOCK, lanes)) for j in range(rows)], axis=0
        )
        spreads.append(jnp.where(own_head, spread, 0.0).astype(jnp.bfloat16))
    scores, fresh = [], []
    for c in chips:
        half, at = places[c]
        keys = jnp.concatenate([keys_refs[half][at * heads + h] for h in range(heads)], axis=1)
        kn = kn_ref[c].astype(jnp.bfloat16)
        scores.append(lax.dot_general(spreads[c], keys, CONTRACT_LANES, preferred_element_type=jnp.float32))
        fresh.append(lax.dot_general(spreads[c], kn, CONTRACT_LANES, preferred_element_type=jnp.float32))
    weights, fresh_weights, totals = [], [], []
    for c in chips:
        old = jnp.where(live, scores[c] * (HD**-0.5), masked_score)
        new = jnp.where(new_live, fresh[c] * (HD**-0.5), masked_score)
        top = jnp.maximum(jnp.max(old, axis=1, keepdims=True), jnp.max(new, axis=1, keepdims=True))
        old = jnp.where(live, jnp.exp(old - top), 0.0)
        new = jnp.where(new_live, jnp.exp(new - top), 0.0)
        totals.append(jnp.sum(old, axis=1, keepdims=True) + jnp.sum(new, axis=1, keepdims=True))
        weights.append(old.astype(jnp.bfloat16))
        fresh_weights.append(new.astype(jnp.bfloat16))
    wait_all(fetches)
    for c in chips:
        values = lanes_of(values_buf[c])
        vn = vn_ref[c].astype(jnp.bfloat16)
        mixed = jnp.dot(weights[c], values, preferred_element_type=jnp.float32)
        mixed = mixed + jnp.dot(fresh_weights[c], vn, preferred_element_type=jnp.float32)
        mixed = jnp.where(own_head, mixed / totals[c], 0.0)
        out = jnp.sum(mixed.reshape(rows, HEAD_BLOCK, lanes), axis=1).astype(out_ref.dtype)
        for t in range(steps):
            for h in range(heads):
                out_ref[t, c * heads + h] = out[2 * t : 2 * t + 2, h * HD : (h + 1) * HD]


def attend(cosine, sine, live, pieces, keys, values):
    count, _, steps = pieces.shape[:3]
    heads, tokens = sum(x.shape[0] for x in keys), keys[0].shape[1]
    chips = count // 2
    per = heads // chips
    return pl.pallas_call(
        attend_kernel,
        out_shape=jax.ShapeDtypeStruct((steps, heads, 2, HD), jnp.bfloat16),
        in_specs=[VMEM] * 6 + [HBM] * 2,
        out_specs=VMEM,
        scratch_shapes=[pltpu.VMEM((chips, per, tokens, HD), jnp.bfloat16)]
        + [pltpu.VMEM((chips, 16, per * HD), jnp.float32)] * 2
        + [pltpu.SemaphoreType.DMA((chips,))],
        compiler_params=pltpu.CompilerParams(vmem_limit_bytes=16 * 2**20),
        cost_estimate=pl.CostEstimate(flops=10**9, bytes_accessed=6 * 10**6, transcendentals=0),
        name="attention",
    )(cosine, sine, live, pieces, *keys, *[in_hbm(x) for x in values])


def chip_plan(
    count,
    hidden,
    query_key_value_weight,
    adapter_down_maps,
    adapter_up_maps,
    adapter_storage_row,
    request_adapter,
    lengths,
    request_page_table,
    key_value_pool,
):
    me = lax.axis_index("replica")
    steps, req_dev, width = hidden.shape
    heads = width // HD
    holder_count, rank, _ = adapter_down_maps.shape
    pool_pages, page_len = key_value_pool.shape[:2]
    adapter_count = adapter_storage_row.shape[0]

    tokens = pool_pages * page_len
    pool = key_value_pool.reshape(tokens, 2, heads, HD).transpose(0, 2, 1, 3)

    stored = jnp.sum(
        jnp.where(
            request_adapter[:, None] == jnp.arange(adapter_count, dtype=jnp.int32)[None, :],
            adapter_storage_row[None, :],
            0,
        ),
        axis=1,
    )
    cosine, sine = rotation_rows(lengths, me * req_dev, req_dev, steps)
    live = live_lanes(lengths, me * req_dev, request_page_table, tokens, page_len)
    slot, column = index_work((me * holder_count).astype(jnp.int32).reshape(1), stored, steps)

    held = {m: trade(hidden, m, count) for m in range(count - 4, 0, -4)}
    own, slot, column = lax.optimization_barrier((hidden, slot, column))
    held[2] = trade(own, 2, count)
    held.update({m | 2: trade(held[m], 2, count) for m in range(4, count, 4)})
    held[0] = hidden
    ready = [0, 2, *range(4, count, 4)]
    *waiting, held[count - 2] = lax.optimization_barrier([held[m] for m in ready] + [held[count - 2]])
    held.update(zip(ready, waiting))
    held.update({m | 1: trade(held[m], 1, count) for m in range(0, count, 2)})
    blocks = [held[k].reshape(steps, req_dev, heads, HD).transpose(0, 2, 1, 3) for k in range(count)]
    blocks[0] = in_hbm(blocks[0])

    x, low = low_of(me.astype(jnp.int32).reshape(1), blocks, slot, adapter_down_maps)
    weight = query_key_value_weight.transpose(0, 2, 1)
    arrived = [trade(low, m, count) for m in (1, 2, 3)]
    query, key = project(0, x, weight), project(1, x, weight)
    arrived, query, key, pool = lax.optimization_barrier((arrived, query, key, pool))
    low = (low + arrived[0]) + (arrived[1] + arrived[2])
    arrived = [trade(low, m, count) for m in range(4, count, 4)]
    base = project(2, x, weight)
    early_heads = heads // 4
    early_cache = cache_by_head(pool, 0, early_heads)
    arrived, base, early_cache = lax.optimization_barrier((arrived, base, early_cache))
    send = update_values(column, query, key, base, adapter_up_maps.reshape(adapter_count * rank, -1), [low, *arrived])
    send, pool = lax.optimization_barrier((send, pool))
    late_cache = cache_by_head(pool, early_heads, heads - early_heads)
    pieces = lax.all_to_all(send, "replica", split_axis=0, concat_axis=0, tiled=True)

    keys, values = zip(early_cache, late_cache)
    out = attend(cosine, sine, live, pieces, keys, values)
    return out.transpose(0, 2, 1, 3).reshape(steps, req_dev, width)


def per_device(replicas, *arrays):
    columns = arrays[1].shape[2]
    whole_heads = replicas % 4 == 0 and (2 * columns) % HD == 0 and columns % HD == HD // 2
    plan = chip_plan if whole_heads and arrays[0].shape[1] == 2 else general_plan
    return plan(replicas, *arrays)


def solution(mesh):
    placed = (
        P(None, ("groups", "replica"), None),
        P(None, None, "replica"),
        P("replica", None, None),
        P(None, None, "replica"),
        P(),
        P("groups"),
        P("groups"),
        P(("groups", "replica"), None),
        P(("groups", "replica"), None, None, None),
    )
    return jax.shard_map(
        functools.partial(per_device, mesh.shape["replica"]),
        mesh=mesh,
        in_specs=placed,
        out_specs=P(None, ("groups", "replica"), None),
        check_vma=False,
    )
```

```python
import functools

import jax
import jax.numpy as jnp
from jax import lax
from jax.experimental import pallas as pl
from jax.experimental.pallas import tpu as pltpu
from jax.sharding import PartitionSpec as P

HD = 128
ROWS = 8
HEAD_BLOCK = 8

adapter_scale = 2.0
masked_score = -1e30


def attention_kernel(steps, req_dev, q_ref, k_ref, v_ref, cos_ref, sin_ref, live_ref, kv_ref, out_ref, kn_ref, vn_ref):
    rows = steps * req_dev
    width = q_ref.shape[1]
    lanes = HEAD_BLOCK * HD
    group = rows * HEAD_BLOCK
    cosine = cos_ref[...]
    sine = sin_ref[...]

    def rotated(x):
        pieces = []
        for h in range(HEAD_BLOCK):
            head = x[:, h * HD : (h + 1) * HD]
            pieces.append(head * cosine + pltpu.roll(head, HD // 2, 1) * sine)
        return jnp.concatenate(pieces, axis=1)

    row_head = lax.broadcasted_iota(jnp.int32, (group, lanes), 0) % HEAD_BLOCK
    lane_head = lax.broadcasted_iota(jnp.int32, (group, lanes), 1) // HD
    own_head = row_head == lane_head
    row_j = lax.broadcasted_iota(jnp.int32, (group, 16), 0) // HEAD_BLOCK
    new_j = lax.broadcasted_iota(jnp.int32, (group, 16), 1)
    new_live = (new_j < rows) & (new_j % req_dev == row_j % req_dev) & (new_j // req_dev <= row_j // req_dev)
    live_all = live_ref[...]
    live = jnp.concatenate(
        [
            jnp.broadcast_to(live_all[j % req_dev : j % req_dev + 1], (HEAD_BLOCK, live_all.shape[1]))
            for j in range(rows)
        ],
        axis=0,
    )
    live = live > 0
    kn_ref[...] = jnp.zeros_like(kn_ref)
    vn_ref[...] = jnp.zeros_like(vn_ref)
    contract_lanes = (((1,), (1,)), ((), ()))
    for c in range(width // lanes):
        cols = slice(c * lanes, (c + 1) * lanes)
        query = rotated(q_ref[:, cols].astype(jnp.float32))
        key_new = rotated(k_ref[:, cols].astype(jnp.float32))
        kn_ref[0:8] = key_new
        vn_ref[0:8] = v_ref[:, cols].astype(jnp.float32)
        kn = kn_ref[...].astype(jnp.bfloat16)
        vn = vn_ref[...].astype(jnp.bfloat16)
        spread = jnp.concatenate(
            [jnp.broadcast_to(query[j : j + 1], (HEAD_BLOCK, lanes)) for j in range(rows)], axis=0
        )
        spread = jnp.where(own_head, spread, 0.0).astype(jnp.bfloat16)
        kv = kv_ref[:, cols]
        scores = lax.dot_general(spread, kv, contract_lanes, preferred_element_type=jnp.float32) * (HD**-0.5)
        scores = jnp.where(live, scores, masked_score)
        fresh = lax.dot_general(spread, kn, contract_lanes, preferred_element_type=jnp.float32) * (HD**-0.5)
        fresh = jnp.where(new_live, fresh, masked_score)
        top = jnp.maximum(jnp.max(scores, axis=1, keepdims=True), jnp.max(fresh, axis=1, keepdims=True))
        weights = jnp.where(live, jnp.exp(scores - top), 0.0)
        fresh = jnp.where(new_live, jnp.exp(fresh - top), 0.0)
        totals = jnp.sum(weights, axis=1, keepdims=True) + jnp.sum(fresh, axis=1, keepdims=True)
        weights = pltpu.roll(weights, 1, 1).astype(jnp.bfloat16)
        mixed = jnp.dot(weights, kv, preferred_element_type=jnp.float32)
        mixed = mixed + jnp.dot(fresh.astype(jnp.bfloat16), vn, preferred_element_type=jnp.float32)
        mixed = jnp.where(own_head, mixed / totals, 0.0)
        out = jnp.sum(mixed.reshape(rows, HEAD_BLOCK, lanes), axis=1)
        out_ref[:, cols] = out.astype(out_ref.dtype)


def attention(steps, req_dev, q, k, v, cosine, sine, live, kv):
    rows = steps * req_dev
    width = q.shape[1]
    vmem = pl.BlockSpec(memory_space=pltpu.VMEM)
    return pl.pallas_call(
        functools.partial(attention_kernel, steps, req_dev),
        out_shape=jax.ShapeDtypeStruct((rows, width), jnp.bfloat16),
        in_specs=[vmem] * 7,
        out_specs=vmem,
        scratch_shapes=[pltpu.VMEM((16, HEAD_BLOCK * HD), jnp.float32)] * 2,
        compiler_params=pltpu.CompilerParams(vmem_limit_bytes=32 * 2**20),
        cost_estimate=pl.CostEstimate(flops=10**9, bytes_accessed=6 * 10**6, transcendentals=0),
        name="attention",
    )(q, k, v, cosine, sine, live, kv)


def rotation(my_lengths, steps):
    rows = steps * my_lengths.shape[0]
    positions = (my_lengths[None, :] + jnp.arange(steps, dtype=jnp.int32)[:, None]).reshape(rows)
    positions = jnp.pad(positions, (0, ROWS - rows))
    half = HD // 2
    frequency = jnp.exp(jnp.arange(half, dtype=jnp.float32) * (-2.0 * jnp.log(10000.0) / HD))
    angles = positions.astype(jnp.float32)[:, None] * frequency[None, :]
    cosine = jnp.cos(angles)
    sine = jnp.sin(angles)
    cosine = jnp.concatenate([cosine, cosine], axis=1)
    sine = jnp.concatenate([-sine, sine], axis=1)
    return cosine, sine


def live_tokens(my_lengths, request_page_table, pool_pages, page_len):
    pages = jnp.arange(pool_pages, dtype=jnp.int32)
    max_pages = request_page_table.shape[1]
    place = jnp.max(
        jnp.where(
            request_page_table[:, :, None] == pages[None, None, :],
            jnp.arange(max_pages, dtype=jnp.int32)[None, :, None],
            -1,
        ),
        axis=1,
    )
    token = place[:, :, None] * page_len + jnp.arange(page_len, dtype=jnp.int32)[None, None, :]
    return (place[:, :, None] >= 0) & (token < my_lengths[:, None, None])


def live_rows(my_lengths, request_page_table, pool_pages, page_len):
    alive = live_tokens(my_lengths, request_page_table, pool_pages, page_len)
    live = jnp.stack([alive, jnp.zeros_like(alive)], axis=-1).astype(jnp.int32)
    return live.reshape(request_page_table.shape[0], pool_pages * page_len * 2)


def general_plan(
    replicas,
    hidden,
    query_key_value_weight,
    adapter_down_maps,
    adapter_up_maps,
    adapter_storage_row,
    request_adapter,
    lengths,
    request_page_table,
    key_value_pool,
):
    my_index = lax.axis_index("replica")
    steps, req_dev, width = hidden.shape
    rows = steps * req_dev
    columns = query_key_value_weight.shape[2]
    holder_count, rank, _ = adapter_down_maps.shape
    pool_pages, page_len = key_value_pool.shape[:2]
    adapter_count = adapter_storage_row.shape[0]
    chips = replicas // 2
    total = replicas * ROWS

    block = jnp.pad(hidden.reshape(rows, width), ((0, ROWS - rows), (0, 0)))
    same_core = [[2 * chip + core for chip in range(chips)] for core in range(2)]
    mine = lax.all_to_all(
        jnp.broadcast_to(block[None], (chips, ROWS, width)),
        "replica",
        split_axis=0,
        concat_axis=0,
        axis_index_groups=same_core,
        tiled=True,
    )
    other = lax.ppermute(mine, "replica", [(i, i ^ 1) for i in range(replicas)])
    first = my_index % 2 == 0
    gathered = jnp.stack([jnp.where(first, mine, other), jnp.where(first, other, mine)])
    gathered = gathered.reshape(total, width)

    stored_rows = jnp.sum(
        jnp.where(
            request_adapter[:, None] == jnp.arange(adapter_count, dtype=jnp.int32)[None, :],
            adapter_storage_row[None, :],
            0,
        ),
        axis=1,
    )
    by_block = stored_rows.reshape(chips, 2, 1, req_dev).transpose(1, 0, 2, 3)
    by_block = jnp.broadcast_to(by_block, (2, chips, steps, req_dev)).reshape(2, chips, rows)
    row_stored = jnp.pad(by_block, ((0, 0), (0, 0), (0, ROWS - rows)), constant_values=-1).reshape(total)

    down = jnp.einsum("nd,hfd->nhf", gathered, adapter_down_maps, preferred_element_type=jnp.float32)
    slots = my_index * holder_count + jnp.arange(holder_count, dtype=jnp.int32)
    own = row_stored[:, None] == slots[None, :]
    low = jnp.sum(jnp.where(own[:, :, None], down, 0.0), axis=1).astype(jnp.bfloat16)
    low = jnp.concatenate([low[: total // 2], low[total // 2 :]], axis=1)
    low = lax.all_to_all(
        jnp.broadcast_to(low[None], (replicas,) + low.shape), "replica", split_axis=0, concat_axis=0, tiled=True
    )
    low = jnp.sum(low.astype(jnp.float32), axis=0)
    low = jnp.concatenate([low[:, :rank], low[:, rank:]], axis=0)

    projected = jnp.einsum("nd,idc->nic", gathered, query_key_value_weight, preferred_element_type=jnp.float32)

    def update(first_adapter, maps):
        held = maps.shape[0]
        which = first_adapter + jnp.arange(held, dtype=jnp.int32)
        wide = jnp.where((row_stored[:, None] == which[None, :])[:, :, None], low[:, None, :], 0.0)
        return jnp.dot(
            wide.astype(jnp.bfloat16).reshape(total, held * rank),
            maps.reshape(held * rank, columns),
            preferred_element_type=jnp.float32,
        )

    step_adapters = 64
    if adapter_count <= step_adapters:
        updated = update(0, adapter_up_maps)
    else:
        updated = lax.fori_loop(
            0,
            adapter_count // step_adapters,
            lambda i, sofar: sofar
            + update(
                i * step_adapters,
                lax.dynamic_slice_in_dim(adapter_up_maps, i * step_adapters, step_adapters, 0),
            ),
            jnp.zeros((total, columns), jnp.float32),
        )
    value = projected[:, 2] + adapter_scale * updated
    combined = jnp.concatenate([projected[:, 0], projected[:, 1], value], axis=1).astype(jnp.bfloat16)
    combined = combined.reshape(2, chips, ROWS, 3 * columns).transpose(1, 0, 2, 3)
    combined = combined.reshape(replicas, ROWS, 3 * columns)
    arrived = lax.all_to_all(combined, "replica", split_axis=0, concat_axis=0, tiled=True)
    arrived = arrived.reshape(replicas, ROWS, 3, columns).transpose(2, 1, 0, 3).reshape(3, ROWS, width)

    my_lengths = lax.dynamic_slice_in_dim(lengths, my_index * req_dev, req_dev)
    cosine, sine = rotation(my_lengths, steps)
    live = live_rows(my_lengths, request_page_table, pool_pages, page_len)
    kv = key_value_pool.reshape(pool_pages * page_len * 2, width)
    out = attention(steps, req_dev, arrived[0], arrived[1], arrived[2], cosine, sine, live, kv)
    return out.reshape(steps, req_dev, width)


def rotation_rows(lengths, first, req_dev, steps):
    row = jnp.arange(ROWS, dtype=jnp.int32)
    wanted = first + row % req_dev
    chosen = jnp.where(wanted[:, None] == jnp.arange(lengths.shape[0], dtype=jnp.int32)[None, :], lengths[None, :], 0)
    positions = jnp.sum(chosen, axis=1, keepdims=True) + (row // req_dev)[:, None]
    lane = jnp.arange(HD, dtype=jnp.int32)
    frequency = jnp.exp((lane % (HD // 2)).astype(jnp.float32) * (-2.0 * jnp.log(10000.0) / HD))
    angles = positions.astype(jnp.float32) * frequency[None, :]
    return jnp.cos(angles), jnp.where(lane < HD // 2, -1.0, 1.0)[None, :] * jnp.sin(angles)


def live_lanes(lengths, first, request_page_table, tokens, page_len):
    req_dev, max_pages = request_page_table.shape
    wanted = first + jnp.arange(req_dev, dtype=jnp.int32)
    chosen = jnp.where(wanted[:, None] == jnp.arange(lengths.shape[0], dtype=jnp.int32)[None, :], lengths[None, :], 0)
    lane = jnp.arange(tokens, dtype=jnp.int32)
    page = jnp.arange(max_pages, dtype=jnp.int32)
    place = jnp.max(
        jnp.where(request_page_table[:, :, None] == (lane // page_len)[None, None, :], page[None, :, None], -1),
        axis=1,
    )
    token = place * page_len + (lane % page_len)[None, :]
    return ((place >= 0) & (token < jnp.sum(chosen, axis=1, keepdims=True))).astype(jnp.int32)


def trade(value, mask, count):
    return lax.ppermute(value, "replica", [(i, i ^ mask) for i in range(count)])


CONTRACT_LANES = (((1,), (1,)), ((), ()))


def in_hbm(x):
    return pltpu.with_memory_space_constraint(x, pltpu.HBM)


VMEM = pl.BlockSpec(memory_space=pltpu.VMEM)
HBM = pl.BlockSpec(memory_space=pltpu.HBM)
SMEM = pl.BlockSpec(memory_space=pltpu.SMEM)
ANY = pl.BlockSpec(memory_space=pl.ANY)


def start_all(copies):
    for copy in copies:
        copy.start()
    return copies


def wait_all(copies):
    for copy in copies:
        copy.wait()


CACHE_SECTION = 10


def cache_kernel(first, pool_ref, keys_ref, values_ref, raw, values, sem, out_sem):
    heads, tokens = raw.shape[:2]
    copies = start_all([pltpu.make_async_copy(pool_ref.at[:, first + h], raw.at[h], sem.at[h]) for h in range(heads)])
    rows = raw.reshape(heads, 2 * tokens, HD)
    to = lax.broadcasted_iota(jnp.int32, (2 * tokens, 2 * tokens), 0)
    source = lax.broadcasted_iota(jnp.int32, (2 * tokens, 2 * tokens), 1)
    wanted = jnp.where(to < tokens, 2 * to, 2 * (to - tokens) + 1)
    pick = jnp.where(source == wanted, 1.0, 0.0).astype(jnp.bfloat16)
    sent = []
    part = CACHE_SECTION
    for p in range(heads // part):
        wait_all(copies[p * part : (p + 1) * part])
        for h in range(p * part, (p + 1) * part, 2):
            both = jnp.concatenate([rows[h], rows[h + 1]], axis=1)
            made = jnp.dot(pick, both, preferred_element_type=jnp.float32).astype(jnp.bfloat16)
            for i in range(2):
                keys_ref[h + i] = made[:tokens, i * HD : (i + 1) * HD]
                values[h + i] = made[tokens:, i * HD : (i + 1) * HD]
        span = slice(p * part, (p + 1) * part)
        sent += start_all([pltpu.make_async_copy(values.at[span], values_ref.at[span], out_sem.at[p])])
    wait_all(sent)


def cache_by_head(pool, first, heads):
    tokens = pool.shape[0]
    return pl.pallas_call(
        functools.partial(cache_kernel, first),
        out_shape=(
            jax.ShapeDtypeStruct((heads, tokens, HD), pool.dtype),
            pltpu.HBM((heads, tokens, HD), pool.dtype),
        ),
        in_specs=[HBM],
        out_specs=(VMEM, HBM),
        scratch_shapes=[
            pltpu.VMEM((heads, tokens, 2, HD), pool.dtype),
            pltpu.VMEM((heads, tokens, HD), pool.dtype),
            pltpu.SemaphoreType.DMA((heads,)),
            pltpu.SemaphoreType.DMA((heads // CACHE_SECTION,)),
        ],
        compiler_params=pltpu.CompilerParams(vmem_limit_bytes=12 * 2**20),
        cost_estimate=pl.CostEstimate(flops=0, bytes_accessed=12 * 10**6, transcendentals=0),
        name="cache_by_head",
    )(in_hbm(pool))


def lanes_of(x):
    return jnp.concatenate([x[c] for c in range(x.shape[0])], axis=1)


def step_rows(x, first, chunks):
    steps, _, count = x.shape[:3]
    flat = x.reshape(steps, x.shape[1], 2 * count, HD)
    return jnp.concatenate(
        [jnp.concatenate([flat[t, c] for c in range(first, first + chunks)], axis=1) for t in range(steps)], axis=0
    )


def pack_kernel(*refs):
    blocks, (out_ref, sem) = refs[:-2], refs[-2:]
    wait_all(
        start_all([pltpu.make_async_copy(block, out_ref.at[i], sem.at[i]) for i, block in enumerate(blocks)])
    )


def packed(blocks):
    return pl.pallas_call(
        pack_kernel,
        out_shape=jax.ShapeDtypeStruct((len(blocks),) + blocks[0].shape, blocks[0].dtype),
        in_specs=[ANY] * len(blocks),
        out_specs=VMEM,
        scratch_shapes=[pltpu.SemaphoreType.DMA((len(blocks),))],
        compiler_params=pltpu.CompilerParams(vmem_limit_bytes=2 * 2**20),
        cost_estimate=pl.CostEstimate(flops=0, bytes_accessed=10**6, transcendentals=0),
        name="pack_blocks",
    )(*blocks)


def index_kernel(me_ref, stored_ref, slot_ref, column_ref):
    requests = stored_ref.shape[1]
    steps = slot_ref.shape[1] // requests
    row = jnp.concatenate([stored_ref[...]] * steps, axis=1)
    slot_ref[...] = row - me_ref[0]
    wide = jnp.concatenate([row, jnp.zeros((1, HD - row.shape[1]), row.dtype)], axis=1)
    column_ref[...] = jnp.broadcast_to(wide.astype(jnp.float32), (HD, HD)).T[: row.shape[1], :1].astype(jnp.int32)


def index_work(first, stored, steps):
    rows = stored.shape[0] * steps
    return pl.pallas_call(
        index_kernel,
        out_shape=(jax.ShapeDtypeStruct((1, rows), jnp.int32), jax.ShapeDtypeStruct((rows, 1), jnp.int32)),
        in_specs=[SMEM, VMEM],
        out_specs=(VMEM, VMEM),
        compiler_params=pltpu.CompilerParams(vmem_limit_bytes=2 * 2**20),
        cost_estimate=pl.CostEstimate(flops=2 * 10**10, bytes_accessed=10**4, transcendentals=0),
        name="index_work",
    )(first, stored[None, :])


def low_kernel(places, packs, me_ref, slot_ref, down_ref, pack_ref, *refs):
    blocks, (x_ref, low_ref, sem) = refs[: len(places)], refs[len(places) :]
    me = me_ref[0]
    holders, rank, width = down_ref.shape
    sources = list(zip(places, blocks)) + [(k, pack_ref.at[i]) for i, k in enumerate(packs)]
    wait_all(
        start_all([pltpu.make_async_copy(block, x_ref.at[:, :, me ^ k], sem.at[k]) for k, block in sources])
    )
    x = step_rows(x_ref, 0, x_ref.shape[1])
    rows = x.shape[0]
    made = lax.dot_general(
        down_ref.reshape(holders * rank, width)[...], x, CONTRACT_LANES, preferred_element_type=jnp.float32
    )
    slot = slot_ref[...]
    low = jnp.zeros((rank, rows), jnp.float32)
    for h in range(holders):
        low = low + jnp.where(slot == h, made[h * rank : (h + 1) * rank], 0.0)
    low = low.T
    low_ref[...] = jnp.concatenate([low[: rows // 2], low[rows // 2 :]], axis=1).astype(low_ref.dtype)


def low_of(me, blocks, packs, pack, slot, down):
    count = len(blocks) + len(packs)
    steps, chunks = blocks[0].shape[:2]
    rows = count * steps * 2
    rank = down.shape[1]
    return pl.pallas_call(
        functools.partial(low_kernel, tuple(blocks), packs),
        out_shape=(
            jax.ShapeDtypeStruct((steps, chunks, count, 2, HD), jnp.bfloat16),
            jax.ShapeDtypeStruct((rows // 2, 2 * rank), jnp.bfloat16),
        ),
        in_specs=[SMEM, VMEM, VMEM, ANY] + [ANY] * len(blocks),
        out_specs=(VMEM, VMEM),
        scratch_shapes=[pltpu.SemaphoreType.DMA((count,))],
        compiler_params=pltpu.CompilerParams(vmem_limit_bytes=12 * 2**20),
        cost_estimate=pl.CostEstimate(flops=10**8, bytes_accessed=4 * 10**6, transcendentals=0),
        name="low_rows",
    )(me, slot, down, pack, *blocks.values())


def put_chunks(buf, first, value):
    steps, count = buf.shape[1:3]
    flat = buf.reshape(buf.shape[0], steps, 2 * count, HD)
    wide = value.shape[1]
    for c in range(-(-wide // HD)):
        part = value[:, c * HD : min((c + 1) * HD, wide)]
        if part.shape[1] < HD:
            part = jnp.concatenate([part, jnp.zeros((part.shape[0], HD - part.shape[1]), part.dtype)], axis=1)
        part = part.astype(buf.dtype)
        for t in range(steps):
            flat[first + c, t] = part[t * 2 * count : (t + 1) * 2 * count]


def project_kernel(which, x_ref, w_ref, out_ref):
    x = step_rows(x_ref, 0, x_ref.shape[1])
    made = lax.dot_general(w_ref[which], x, CONTRACT_LANES, preferred_element_type=jnp.float32).T
    if which < 2:
        put_chunks(out_ref, 0, made)
    else:
        out_ref[...] = made


def project(which, x, weight):
    steps, _, count = x.shape[:3]
    columns = weight.shape[1]
    chunks = jax.ShapeDtypeStruct((-(-columns // HD), steps, count, 2, HD), jnp.bfloat16)
    base = jax.ShapeDtypeStruct((2 * steps * count, columns), jnp.float32)
    return pl.pallas_call(
        functools.partial(project_kernel, which),
        out_shape=chunks if which < 2 else base,
        in_specs=[VMEM, VMEM],
        out_specs=VMEM,
        compiler_params=pltpu.CompilerParams(vmem_limit_bytes=16 * 2**20),
        cost_estimate=pl.CostEstimate(flops=5 * 10**8, bytes_accessed=4 * 10**6, transcendentals=0),
        name="project",
    )(x, weight)


def update_kernel(stored_ref, query_ref, key_ref, base_ref, up_ref, *refs):
    lows, (send_ref, buf, sem) = refs[:-3], refs[-3:]
    half, packed = lows[0].shape
    rank = packed // 2
    rows = 2 * half
    count = send_ref.shape[0]
    low = lows[0][...].astype(jnp.float32)
    for more in lows[1:]:
        low = low + more[...].astype(jnp.float32)
    low = jnp.concatenate([low[:, :rank], low[:, rank:]], axis=0)
    batch = 256 // rank
    spread = jnp.concatenate([low] * batch, axis=1)
    ahead = stored_ref[...] - lax.broadcasted_iota(jnp.int32, (rows, batch * rank), 1) // rank
    total = jnp.zeros(base_ref.shape, jnp.float32)
    for a in range(0, up_ref.shape[0] // rank, batch):
        wide = jnp.where(ahead == a, spread, 0.0).astype(jnp.bfloat16)
        total = total + jnp.dot(wide, up_ref[a * rank : (a + batch) * rank], preferred_element_type=jnp.float32)
    each = query_ref.shape[0]
    buf[:each] = query_ref[...]
    buf[each : 2 * each] = key_ref[...]
    put_chunks(buf, 2 * each, base_ref[...] + adapter_scale * total)
    wait_all(
        start_all([pltpu.make_async_copy(buf.at[:, :, k], send_ref.at[k], sem.at[k]) for k in range(count)])
    )


def update_values(stored, query, key, base, up, lows):
    chunks, steps, count = query.shape[:3]
    return pl.pallas_call(
        update_kernel,
        out_shape=pltpu.HBM((count, 3 * chunks, steps, 2, HD), query.dtype),
        in_specs=[VMEM] * (5 + len(lows)),
        out_specs=HBM,
        scratch_shapes=[
            pltpu.VMEM((3 * chunks, steps, count, 2, HD), query.dtype),
            pltpu.SemaphoreType.DMA((count,)),
        ],
        compiler_params=pltpu.CompilerParams(vmem_limit_bytes=8 * 2**20),
        cost_estimate=pl.CostEstimate(flops=3 * 10**8, bytes_accessed=4 * 10**6, transcendentals=0),
        name="update_values",
    )(stored, query, key, base, up, *lows)


def attend_kernel(cos_ref, sin_ref, live_ref, pieces_ref, *refs):
    *parts, out_ref, values_buf, kn_ref, vn_ref, sem = refs
    keys_refs, values_refs = parts[: len(parts) // 2], parts[len(parts) // 2 :]
    count, _, steps = pieces_ref.shape[:3]
    rows = 2 * steps
    each = pieces_ref.shape[1] // 3
    heads = 2 * out_ref.shape[1] // count
    lanes = heads * HD
    group = rows * HEAD_BLOCK
    chips = range(count // 2)
    early = keys_refs[0].shape[0] // heads
    places = [(0, c) if c < early else (1, c - early) for c in chips]
    fetches = start_all(
        [
            pltpu.make_async_copy(values_refs[half].at[at * heads : (at + 1) * heads], values_buf.at[c], sem.at[c])
            for c, (half, at) in enumerate(places)
        ]
    )
    cosine = cos_ref[...][:rows]
    sine = sin_ref[...][:rows]
    left = lax.broadcasted_iota(jnp.int32, (rows, HD), 1) < HD // 2

    def chip_columns(chip, at):
        low = [pieces_ref[2 * chip, at + c].reshape(rows, HD).astype(jnp.float32) for c in range(each)]
        high = [pieces_ref[2 * chip + 1, at + c].reshape(rows, HD).astype(jnp.float32) for c in range(each)]
        high = [pltpu.roll(x, HD // 2, 1) for x in high]
        whole = low[:-1] + [jnp.where(left, low[-1], high[0])]
        return whole + [jnp.where(left, a, b) for a, b in zip(high[:-1], high[1:])]

    def rotated(parts):
        return [x * cosine + pltpu.roll(x, HD // 2, 1) * sine for x in parts]

    row_head = lax.broadcasted_iota(jnp.int32, (group, lanes), 0) % HEAD_BLOCK
    lane_head = lax.broadcasted_iota(jnp.int32, (group, lanes), 1) // HD
    own_head = row_head == lane_head
    row_j = lax.broadcasted_iota(jnp.int32, (group, 16), 0) // HEAD_BLOCK
    new_j = lax.broadcasted_iota(jnp.int32, (group, 16), 1)
    new_live = (new_j < rows) & (new_j % 2 == row_j % 2) & (new_j // 2 <= row_j // 2)
    live = jnp.concatenate(
        [
            jnp.broadcast_to(live_ref[j % 2 : j % 2 + 1, :], (HEAD_BLOCK, live_ref.shape[1]))
            for j in range(rows)
        ],
        axis=0,
    )
    live = live > 0
    kn_ref[...] = jnp.zeros_like(kn_ref)
    vn_ref[...] = jnp.zeros_like(vn_ref)
    spreads = []
    for c in chips:
        query = jnp.concatenate(rotated(chip_columns(c, 0)), axis=1)
        kn_ref[c, 0:rows] = jnp.concatenate(rotated(chip_columns(c, each)), axis=1)
        vn_ref[c, 0:rows] = jnp.concatenate(chip_columns(c, 2 * each), axis=1)
        spread = jnp.concatenate(
            [jnp.broadcast_to(query[j : j + 1], (HEAD_BLOCK, lanes)) for j in range(rows)], axis=0
        )
        spreads.append(jnp.where(own_head, spread, 0.0).astype(jnp.bfloat16))
    scores, fresh = [], []
    for c in chips:
        half, at = places[c]
        keys = jnp.concatenate([keys_refs[half][at * heads + h] for h in range(heads)], axis=1)
        kn = kn_ref[c].astype(jnp.bfloat16)
        scores.append(lax.dot_general(spreads[c], keys, CONTRACT_LANES, preferred_element_type=jnp.float32))
        fresh.append(lax.dot_general(spreads[c], kn, CONTRACT_LANES, preferred_element_type=jnp.float32))
    weights, fresh_weights, totals = [], [], []
    for c in chips:
        old = jnp.where(live, scores[c] * (HD**-0.5), masked_score)
        new = jnp.where(new_live, fresh[c] * (HD**-0.5), masked_score)
        top = jnp.maximum(jnp.max(old, axis=1, keepdims=True), jnp.max(new, axis=1, keepdims=True))
        old = jnp.where(live, jnp.exp(old - top), 0.0)
        new = jnp.where(new_live, jnp.exp(new - top), 0.0)
        totals.append(jnp.sum(old, axis=1, keepdims=True) + jnp.sum(new, axis=1, keepdims=True))
        weights.append(old.astype(jnp.bfloat16))
        fresh_weights.append(new.astype(jnp.bfloat16))
    wait_all(fetches)
    for c in chips:
        values = lanes_of(values_buf[c])
        vn = vn_ref[c].astype(jnp.bfloat16)
        mixed = jnp.dot(weights[c], values, preferred_element_type=jnp.float32)
        mixed = mixed + jnp.dot(fresh_weights[c], vn, preferred_element_type=jnp.float32)
        mixed = jnp.where(own_head, mixed / totals[c], 0.0)
        out = jnp.sum(mixed.reshape(rows, HEAD_BLOCK, lanes), axis=1).astype(out_ref.dtype)
        for t in range(steps):
            for h in range(heads):
                out_ref[t, c * heads + h] = out[2 * t : 2 * t + 2, h * HD : (h + 1) * HD]


def attend(cosine, sine, live, pieces, keys, values):
    count, _, steps = pieces.shape[:3]
    heads, tokens = sum(x.shape[0] for x in keys), keys[0].shape[1]
    chips = count // 2
    per = heads // chips
    return pl.pallas_call(
        attend_kernel,
        out_shape=jax.ShapeDtypeStruct((steps, heads, 2, HD), jnp.bfloat16),
        in_specs=[VMEM] * (4 + len(keys)) + [HBM] * len(values),
        out_specs=VMEM,
        scratch_shapes=[pltpu.VMEM((chips, per, tokens, HD), jnp.bfloat16)]
        + [pltpu.VMEM((chips, 16, per * HD), jnp.float32)] * 2
        + [pltpu.SemaphoreType.DMA((chips,))],
        compiler_params=pltpu.CompilerParams(vmem_limit_bytes=16 * 2**20),
        cost_estimate=pl.CostEstimate(flops=10**9, bytes_accessed=6 * 10**6, transcendentals=0),
        name="attention",
    )(cosine, sine, live, pieces, *keys, *[in_hbm(x) for x in values])


def chip_plan(
    count,
    hidden,
    query_key_value_weight,
    adapter_down_maps,
    adapter_up_maps,
    adapter_storage_row,
    request_adapter,
    lengths,
    request_page_table,
    key_value_pool,
):
    me = lax.axis_index("replica")
    steps, req_dev, width = hidden.shape
    heads = width // HD
    holder_count, rank, _ = adapter_down_maps.shape
    pool_pages, page_len = key_value_pool.shape[:2]
    adapter_count = adapter_storage_row.shape[0]

    tokens = pool_pages * page_len
    pool = key_value_pool.reshape(tokens, 2, heads, HD).transpose(0, 2, 1, 3)

    stored = jnp.sum(
        jnp.where(
            request_adapter[:, None] == jnp.arange(adapter_count, dtype=jnp.int32)[None, :],
            adapter_storage_row[None, :],
            0,
        ),
        axis=1,
    )
    first, slots, here, stored = lax.optimization_barrier(
        (me * req_dev, (me * holder_count).astype(jnp.int32).reshape(1), me.astype(jnp.int32).reshape(1), stored)
    )
    slot, column = index_work(slots, stored, steps)
    cosine, sine = rotation_rows(lengths, first, req_dev, steps)
    live = live_lanes(lengths, first, request_page_table, tokens, page_len)

    whole = hidden.reshape(steps, req_dev, heads, HD).transpose(0, 2, 1, 3)
    held = {m: trade(hidden, m, count) for m in range(4, count, 4)}
    held[2] = trade(hidden, 2, count)
    held.update({m | 2: trade(held[m], 2, count) for m in range(4, count, 4)})
    held = {k: v.reshape(steps, req_dev, heads, HD).transpose(0, 2, 1, 3) for k, v in held.items()}
    held[0] = in_hbm(whole)
    line = tuple(range(0, count, 4))
    near = count // 2 + 2
    *share, held[near] = lax.optimization_barrier([whole] + [held[m] for m in line[1:]] + [held[near]])
    pack = trade(packed(share), 1, count)
    held.update({m | 1: trade(held[m], 1, count) for m in range(2, count, 4)})
    x, low = low_of(here, held, tuple(m | 1 for m in line), pack, slot, adapter_down_maps)
    weight = query_key_value_weight.transpose(0, 2, 1)
    arrived = [trade(low, m, count) for m in (1, 2, 3)]
    query, key = project(0, x, weight), project(1, x, weight)
    arrived, query, key, pool = lax.optimization_barrier((arrived, query, key, pool))
    low = (low + arrived[0]) + (arrived[1] + arrived[2])
    arrived = [trade(low, m, count) for m in range(4, count, 4)]
    base = project(2, x, weight)
    arrived, base = lax.optimization_barrier((arrived, base))
    send = update_values(column, query, key, base, adapter_up_maps.reshape(adapter_count * rank, -1), [low, *arrived])
    send, pool = lax.optimization_barrier((send, pool))
    keys, values = cache_by_head(pool, 0, heads)
    pieces = lax.all_to_all(send, "replica", split_axis=0, concat_axis=0, tiled=True)

    out = attend(cosine, sine, live, pieces, [keys], [values])
    return out.transpose(0, 2, 1, 3).reshape(steps, req_dev, width)


def per_device(replicas, *arrays):
    columns = arrays[1].shape[2]
    whole_heads = replicas % 4 == 0 and (2 * columns) % HD == 0 and columns % HD == HD // 2
    plan = chip_plan if whole_heads and arrays[0].shape[1] == 2 else general_plan
    return plan(replicas, *arrays)


def solution(mesh):
    placed = (
        P(None, ("groups", "replica"), None),
        P(None, None, "replica"),
        P("replica", None, None),
        P(None, None, "replica"),
        P(),
        P("groups"),
        P("groups"),
        P(("groups", "replica"), None),
        P(("groups", "replica"), None, None, None),
    )
    return jax.shard_map(
        functools.partial(per_device, mesh.shape["replica"]),
        mesh=mesh,
        in_specs=placed,
        out_specs=P(None, ("groups", "replica"), None),
        check_vma=False,
    )
```

```python
import functools

import jax
import jax.numpy as jnp
from jax import lax
from jax.experimental import pallas as pl
from jax.experimental.pallas import tpu as pltpu
from jax.sharding import PartitionSpec as P

HD = 128
ROWS = 8
HEAD_BLOCK = 8

adapter_scale = 2.0
masked_score = -1e30


def attention_kernel(steps, req_dev, q_ref, k_ref, v_ref, cos_ref, sin_ref, live_ref, kv_ref, out_ref, kn_ref, vn_ref):
    rows = steps * req_dev
    width = q_ref.shape[1]
    lanes = HEAD_BLOCK * HD
    group = rows * HEAD_BLOCK
    cosine = cos_ref[...]
    sine = sin_ref[...]

    def rotated(x):
        pieces = []
        for h in range(HEAD_BLOCK):
            head = x[:, h * HD : (h + 1) * HD]
            pieces.append(head * cosine + pltpu.roll(head, HD // 2, 1) * sine)
        return jnp.concatenate(pieces, axis=1)

    row_head = lax.broadcasted_iota(jnp.int32, (group, lanes), 0) % HEAD_BLOCK
    lane_head = lax.broadcasted_iota(jnp.int32, (group, lanes), 1) // HD
    own_head = row_head == lane_head
    row_j = lax.broadcasted_iota(jnp.int32, (group, 16), 0) // HEAD_BLOCK
    new_j = lax.broadcasted_iota(jnp.int32, (group, 16), 1)
    new_live = (new_j < rows) & (new_j % req_dev == row_j % req_dev) & (new_j // req_dev <= row_j // req_dev)
    live_all = live_ref[...]
    live = jnp.concatenate(
        [
            jnp.broadcast_to(live_all[j % req_dev : j % req_dev + 1], (HEAD_BLOCK, live_all.shape[1]))
            for j in range(rows)
        ],
        axis=0,
    )
    live = live > 0
    kn_ref[...] = jnp.zeros_like(kn_ref)
    vn_ref[...] = jnp.zeros_like(vn_ref)
    contract_lanes = (((1,), (1,)), ((), ()))
    for c in range(width // lanes):
        cols = slice(c * lanes, (c + 1) * lanes)
        query = rotated(q_ref[:, cols].astype(jnp.float32))
        key_new = rotated(k_ref[:, cols].astype(jnp.float32))
        kn_ref[0:8] = key_new
        vn_ref[0:8] = v_ref[:, cols].astype(jnp.float32)
        kn = kn_ref[...].astype(jnp.bfloat16)
        vn = vn_ref[...].astype(jnp.bfloat16)
        spread = jnp.concatenate(
            [jnp.broadcast_to(query[j : j + 1], (HEAD_BLOCK, lanes)) for j in range(rows)], axis=0
        )
        spread = jnp.where(own_head, spread, 0.0).astype(jnp.bfloat16)
        kv = kv_ref[:, cols]
        scores = lax.dot_general(spread, kv, contract_lanes, preferred_element_type=jnp.float32) * (HD**-0.5)
        scores = jnp.where(live, scores, masked_score)
        fresh = lax.dot_general(spread, kn, contract_lanes, preferred_element_type=jnp.float32) * (HD**-0.5)
        fresh = jnp.where(new_live, fresh, masked_score)
        top = jnp.maximum(jnp.max(scores, axis=1, keepdims=True), jnp.max(fresh, axis=1, keepdims=True))
        weights = jnp.where(live, jnp.exp(scores - top), 0.0)
        fresh = jnp.where(new_live, jnp.exp(fresh - top), 0.0)
        totals = jnp.sum(weights, axis=1, keepdims=True) + jnp.sum(fresh, axis=1, keepdims=True)
        weights = pltpu.roll(weights, 1, 1).astype(jnp.bfloat16)
        mixed = jnp.dot(weights, kv, preferred_element_type=jnp.float32)
        mixed = mixed + jnp.dot(fresh.astype(jnp.bfloat16), vn, preferred_element_type=jnp.float32)
        mixed = jnp.where(own_head, mixed / totals, 0.0)
        out = jnp.sum(mixed.reshape(rows, HEAD_BLOCK, lanes), axis=1)
        out_ref[:, cols] = out.astype(out_ref.dtype)


def attention(steps, req_dev, q, k, v, cosine, sine, live, kv):
    rows = steps * req_dev
    width = q.shape[1]
    vmem = pl.BlockSpec(memory_space=pltpu.VMEM)
    return pl.pallas_call(
        functools.partial(attention_kernel, steps, req_dev),
        out_shape=jax.ShapeDtypeStruct((rows, width), jnp.bfloat16),
        in_specs=[vmem] * 7,
        out_specs=vmem,
        scratch_shapes=[pltpu.VMEM((16, HEAD_BLOCK * HD), jnp.float32)] * 2,
        compiler_params=pltpu.CompilerParams(vmem_limit_bytes=32 * 2**20),
        cost_estimate=pl.CostEstimate(flops=10**9, bytes_accessed=6 * 10**6, transcendentals=0),
        name="attention",
    )(q, k, v, cosine, sine, live, kv)


def rotation(my_lengths, steps):
    rows = steps * my_lengths.shape[0]
    positions = (my_lengths[None, :] + jnp.arange(steps, dtype=jnp.int32)[:, None]).reshape(rows)
    positions = jnp.pad(positions, (0, ROWS - rows))
    half = HD // 2
    frequency = jnp.exp(jnp.arange(half, dtype=jnp.float32) * (-2.0 * jnp.log(10000.0) / HD))
    angles = positions.astype(jnp.float32)[:, None] * frequency[None, :]
    cosine = jnp.cos(angles)
    sine = jnp.sin(angles)
    cosine = jnp.concatenate([cosine, cosine], axis=1)
    sine = jnp.concatenate([-sine, sine], axis=1)
    return cosine, sine


def live_tokens(my_lengths, request_page_table, pool_pages, page_len):
    pages = jnp.arange(pool_pages, dtype=jnp.int32)
    max_pages = request_page_table.shape[1]
    place = jnp.max(
        jnp.where(
            request_page_table[:, :, None] == pages[None, None, :],
            jnp.arange(max_pages, dtype=jnp.int32)[None, :, None],
            -1,
        ),
        axis=1,
    )
    token = place[:, :, None] * page_len + jnp.arange(page_len, dtype=jnp.int32)[None, None, :]
    return (place[:, :, None] >= 0) & (token < my_lengths[:, None, None])


def live_rows(my_lengths, request_page_table, pool_pages, page_len):
    alive = live_tokens(my_lengths, request_page_table, pool_pages, page_len)
    live = jnp.stack([alive, jnp.zeros_like(alive)], axis=-1).astype(jnp.int32)
    return live.reshape(request_page_table.shape[0], pool_pages * page_len * 2)


def general_plan(
    replicas,
    hidden,
    query_key_value_weight,
    adapter_down_maps,
    adapter_up_maps,
    adapter_storage_row,
    request_adapter,
    lengths,
    request_page_table,
    key_value_pool,
):
    my_index = lax.axis_index("replica")
    steps, req_dev, width = hidden.shape
    rows = steps * req_dev
    columns = query_key_value_weight.shape[2]
    holder_count, rank, _ = adapter_down_maps.shape
    pool_pages, page_len = key_value_pool.shape[:2]
    adapter_count = adapter_storage_row.shape[0]
    chips = replicas // 2
    total = replicas * ROWS

    block = jnp.pad(hidden.reshape(rows, width), ((0, ROWS - rows), (0, 0)))
    same_core = [[2 * chip + core for chip in range(chips)] for core in range(2)]
    mine = lax.all_to_all(
        jnp.broadcast_to(block[None], (chips, ROWS, width)),
        "replica",
        split_axis=0,
        concat_axis=0,
        axis_index_groups=same_core,
        tiled=True,
    )
    other = lax.ppermute(mine, "replica", [(i, i ^ 1) for i in range(replicas)])
    first = my_index % 2 == 0
    gathered = jnp.stack([jnp.where(first, mine, other), jnp.where(first, other, mine)])
    gathered = gathered.reshape(total, width)

    stored_rows = jnp.sum(
        jnp.where(
            request_adapter[:, None] == jnp.arange(adapter_count, dtype=jnp.int32)[None, :],
            adapter_storage_row[None, :],
            0,
        ),
        axis=1,
    )
    by_block = stored_rows.reshape(chips, 2, 1, req_dev).transpose(1, 0, 2, 3)
    by_block = jnp.broadcast_to(by_block, (2, chips, steps, req_dev)).reshape(2, chips, rows)
    row_stored = jnp.pad(by_block, ((0, 0), (0, 0), (0, ROWS - rows)), constant_values=-1).reshape(total)

    down = jnp.einsum("nd,hfd->nhf", gathered, adapter_down_maps, preferred_element_type=jnp.float32)
    slots = my_index * holder_count + jnp.arange(holder_count, dtype=jnp.int32)
    own = row_stored[:, None] == slots[None, :]
    low = jnp.sum(jnp.where(own[:, :, None], down, 0.0), axis=1).astype(jnp.bfloat16)
    low = jnp.concatenate([low[: total // 2], low[total // 2 :]], axis=1)
    low = lax.all_to_all(
        jnp.broadcast_to(low[None], (replicas,) + low.shape), "replica", split_axis=0, concat_axis=0, tiled=True
    )
    low = jnp.sum(low.astype(jnp.float32), axis=0)
    low = jnp.concatenate([low[:, :rank], low[:, rank:]], axis=0)

    projected = jnp.einsum("nd,idc->nic", gathered, query_key_value_weight, preferred_element_type=jnp.float32)

    def update(first_adapter, maps):
        held = maps.shape[0]
        which = first_adapter + jnp.arange(held, dtype=jnp.int32)
        wide = jnp.where((row_stored[:, None] == which[None, :])[:, :, None], low[:, None, :], 0.0)
        return jnp.dot(
            wide.astype(jnp.bfloat16).reshape(total, held * rank),
            maps.reshape(held * rank, columns),
            preferred_element_type=jnp.float32,
        )

    step_adapters = 64
    if adapter_count <= step_adapters:
        updated = update(0, adapter_up_maps)
    else:
        updated = lax.fori_loop(
            0,
            adapter_count // step_adapters,
            lambda i, sofar: sofar
            + update(
                i * step_adapters,
                lax.dynamic_slice_in_dim(adapter_up_maps, i * step_adapters, step_adapters, 0),
            ),
            jnp.zeros((total, columns), jnp.float32),
        )
    value = projected[:, 2] + adapter_scale * updated
    combined = jnp.concatenate([projected[:, 0], projected[:, 1], value], axis=1).astype(jnp.bfloat16)
    combined = combined.reshape(2, chips, ROWS, 3 * columns).transpose(1, 0, 2, 3)
    combined = combined.reshape(replicas, ROWS, 3 * columns)
    arrived = lax.all_to_all(combined, "replica", split_axis=0, concat_axis=0, tiled=True)
    arrived = arrived.reshape(replicas, ROWS, 3, columns).transpose(2, 1, 0, 3).reshape(3, ROWS, width)

    my_lengths = lax.dynamic_slice_in_dim(lengths, my_index * req_dev, req_dev)
    cosine, sine = rotation(my_lengths, steps)
    live = live_rows(my_lengths, request_page_table, pool_pages, page_len)
    kv = key_value_pool.reshape(pool_pages * page_len * 2, width)
    out = attention(steps, req_dev, arrived[0], arrived[1], arrived[2], cosine, sine, live, kv)
    return out.reshape(steps, req_dev, width)


def rotation_rows(lengths, first, req_dev, steps):
    row = jnp.arange(ROWS, dtype=jnp.int32)
    wanted = first + row % req_dev
    chosen = jnp.where(wanted[:, None] == jnp.arange(lengths.shape[0], dtype=jnp.int32)[None, :], lengths[None, :], 0)
    positions = jnp.sum(chosen, axis=1, keepdims=True) + (row // req_dev)[:, None]
    lane = jnp.arange(HD, dtype=jnp.int32)
    frequency = jnp.exp((lane % (HD // 2)).astype(jnp.float32) * (-2.0 * jnp.log(10000.0) / HD))
    angles = positions.astype(jnp.float32) * frequency[None, :]
    return jnp.cos(angles), jnp.where(lane < HD // 2, -1.0, 1.0)[None, :] * jnp.sin(angles)


def live_lanes(lengths, first, request_page_table, tokens, page_len):
    req_dev, max_pages = request_page_table.shape
    wanted = first + jnp.arange(req_dev, dtype=jnp.int32)
    chosen = jnp.where(wanted[:, None] == jnp.arange(lengths.shape[0], dtype=jnp.int32)[None, :], lengths[None, :], 0)
    lane = jnp.arange(tokens, dtype=jnp.int32)
    page = jnp.arange(max_pages, dtype=jnp.int32)
    place = jnp.max(
        jnp.where(request_page_table[:, :, None] == (lane // page_len)[None, None, :], page[None, :, None], -1),
        axis=1,
    )
    token = place * page_len + (lane % page_len)[None, :]
    return ((place >= 0) & (token < jnp.sum(chosen, axis=1, keepdims=True))).astype(jnp.int32)


def trade(value, mask, count):
    return lax.ppermute(value, "replica", [(i, i ^ mask) for i in range(count)])


CONTRACT_LANES = (((1,), (1,)), ((), ()))


def in_hbm(x):
    return pltpu.with_memory_space_constraint(x, pltpu.HBM)


VMEM = pl.BlockSpec(memory_space=pltpu.VMEM)
HBM = pl.BlockSpec(memory_space=pltpu.HBM)
SMEM = pl.BlockSpec(memory_space=pltpu.SMEM)
ANY = pl.BlockSpec(memory_space=pl.ANY)


def start_all(copies):
    for copy in copies:
        copy.start()
    return copies


def wait_all(copies):
    for copy in copies:
        copy.wait()


CACHE_SECTION = 10


def cache_kernel(first, pool_ref, keys_ref, values_ref, raw, values, sem, out_sem):
    heads, tokens = raw.shape[:2]
    copies = start_all([pltpu.make_async_copy(pool_ref.at[:, first + h], raw.at[h], sem.at[h]) for h in range(heads)])
    rows = raw.reshape(heads, 2 * tokens, HD)
    to = lax.broadcasted_iota(jnp.int32, (2 * tokens, 2 * tokens), 0)
    source = lax.broadcasted_iota(jnp.int32, (2 * tokens, 2 * tokens), 1)
    wanted = jnp.where(to < tokens, 2 * to, 2 * (to - tokens) + 1)
    pick = jnp.where(source == wanted, 1.0, 0.0).astype(jnp.bfloat16)
    sent = []
    part = CACHE_SECTION
    for p in range(heads // part):
        wait_all(copies[p * part : (p + 1) * part])
        for h in range(p * part, (p + 1) * part, 2):
            both = jnp.concatenate([rows[h], rows[h + 1]], axis=1)
            made = jnp.dot(pick, both, preferred_element_type=jnp.float32).astype(jnp.bfloat16)
            for i in range(2):
                keys_ref[h + i] = made[:tokens, i * HD : (i + 1) * HD]
                values[h + i] = made[tokens:, i * HD : (i + 1) * HD]
        span = slice(p * part, (p + 1) * part)
        sent += start_all([pltpu.make_async_copy(values.at[span], values_ref.at[span], out_sem.at[p])])
    wait_all(sent)


def cache_by_head(pool, first, heads):
    tokens = pool.shape[0]
    return pl.pallas_call(
        functools.partial(cache_kernel, first),
        out_shape=(
            jax.ShapeDtypeStruct((heads, tokens, HD), pool.dtype),
            pltpu.HBM((heads, tokens, HD), pool.dtype),
        ),
        in_specs=[HBM],
        out_specs=(VMEM, HBM),
        scratch_shapes=[
            pltpu.VMEM((heads, tokens, 2, HD), pool.dtype),
            pltpu.VMEM((heads, tokens, HD), pool.dtype),
            pltpu.SemaphoreType.DMA((heads,)),
            pltpu.SemaphoreType.DMA((heads // CACHE_SECTION,)),
        ],
        compiler_params=pltpu.CompilerParams(vmem_limit_bytes=12 * 2**20),
        cost_estimate=pl.CostEstimate(flops=0, bytes_accessed=12 * 10**6, transcendentals=0),
        name="cache_by_head",
    )(in_hbm(pool))


def lanes_of(x):
    return jnp.concatenate([x[c] for c in range(x.shape[0])], axis=1)


def step_rows(x, first, chunks):
    steps, _, count = x.shape[:3]
    flat = x.reshape(steps, x.shape[1], 2 * count, HD)
    return jnp.concatenate(
        [jnp.concatenate([flat[t, c] for c in range(first, first + chunks)], axis=1) for t in range(steps)], axis=0
    )


def index_kernel(me_ref, stored_ref, slot_ref, column_ref):
    requests = stored_ref.shape[1]
    steps = slot_ref.shape[1] // requests
    row = jnp.concatenate([stored_ref[...]] * steps, axis=1)
    slot_ref[...] = row - me_ref[0]
    wide = jnp.concatenate([row, jnp.zeros((1, HD - row.shape[1]), row.dtype)], axis=1)
    column_ref[...] = jnp.broadcast_to(wide.astype(jnp.float32), (HD, HD)).T[: row.shape[1], :1].astype(jnp.int32)


def index_work(first, stored, steps):
    rows = stored.shape[0] * steps
    return pl.pallas_call(
        index_kernel,
        out_shape=(jax.ShapeDtypeStruct((1, rows), jnp.int32), jax.ShapeDtypeStruct((rows, 1), jnp.int32)),
        in_specs=[SMEM, VMEM],
        out_specs=(VMEM, VMEM),
        compiler_params=pltpu.CompilerParams(vmem_limit_bytes=2 * 2**20),
        cost_estimate=pl.CostEstimate(flops=2 * 10**10, bytes_accessed=10**4, transcendentals=0),
        name="index_work",
    )(first, stored[None, :])


def low_kernel(count, me_ref, slot_ref, down_ref, *refs):
    blocks, (x_ref, low_ref, sem) = refs[:count], refs[count:]
    me = me_ref[0]
    holders, rank, width = down_ref.shape
    wait_all(
        start_all(
            [pltpu.make_async_copy(block, x_ref.at[:, :, me ^ k], sem.at[k]) for k, block in enumerate(blocks)]
        )
    )
    x = step_rows(x_ref, 0, x_ref.shape[1])
    rows = x.shape[0]
    made = lax.dot_general(
        down_ref.reshape(holders * rank, width)[...], x, CONTRACT_LANES, preferred_element_type=jnp.float32
    )
    slot = slot_ref[...]
    low = jnp.zeros((rank, rows), jnp.float32)
    for h in range(holders):
        low = low + jnp.where(slot == h, made[h * rank : (h + 1) * rank], 0.0)
    low = low.T
    low_ref[...] = jnp.concatenate([low[: rows // 2], low[rows // 2 :]], axis=1).astype(low_ref.dtype)


def low_of(me, blocks, slot, down):
    count = len(blocks)
    steps, chunks = blocks[0].shape[:2]
    rows = count * steps * 2
    rank = down.shape[1]
    return pl.pallas_call(
        functools.partial(low_kernel, count),
        out_shape=(
            jax.ShapeDtypeStruct((steps, chunks, count, 2, HD), jnp.bfloat16),
            jax.ShapeDtypeStruct((rows // 2, 2 * rank), jnp.bfloat16),
        ),
        in_specs=[SMEM, VMEM, VMEM] + [ANY] * count,
        out_specs=(VMEM, VMEM),
        scratch_shapes=[pltpu.SemaphoreType.DMA((count,))],
        compiler_params=pltpu.CompilerParams(vmem_limit_bytes=12 * 2**20),
        cost_estimate=pl.CostEstimate(flops=10**8, bytes_accessed=4 * 10**6, transcendentals=0),
        name="low_rows",
    )(me, slot, down, *blocks)


def put_chunks(buf, first, value):
    steps, count = buf.shape[1:3]
    flat = buf.reshape(buf.shape[0], steps, 2 * count, HD)
    wide = value.shape[1]
    for c in range(-(-wide // HD)):
        part = value[:, c * HD : min((c + 1) * HD, wide)]
        if part.shape[1] < HD:
            part = jnp.concatenate([part, jnp.zeros((part.shape[0], HD - part.shape[1]), part.dtype)], axis=1)
        part = part.astype(buf.dtype)
        for t in range(steps):
            flat[first + c, t] = part[t * 2 * count : (t + 1) * 2 * count]


def project_kernel(which, x_ref, w_ref, out_ref):
    x = step_rows(x_ref, 0, x_ref.shape[1])
    made = lax.dot_general(w_ref[which], x, CONTRACT_LANES, preferred_element_type=jnp.float32).T
    if which < 2:
        put_chunks(out_ref, 0, made)
    else:
        out_ref[...] = made


def project(which, x, weight):
    steps, _, count = x.shape[:3]
    columns = weight.shape[1]
    chunks = jax.ShapeDtypeStruct((-(-columns // HD), steps, count, 2, HD), jnp.bfloat16)
    base = jax.ShapeDtypeStruct((2 * steps * count, columns), jnp.float32)
    return pl.pallas_call(
        functools.partial(project_kernel, which),
        out_shape=chunks if which < 2 else base,
        in_specs=[VMEM, VMEM],
        out_specs=VMEM,
        compiler_params=pltpu.CompilerParams(vmem_limit_bytes=16 * 2**20),
        cost_estimate=pl.CostEstimate(flops=5 * 10**8, bytes_accessed=4 * 10**6, transcendentals=0),
        name="project",
    )(x, weight)


def update_kernel(stored_ref, query_ref, key_ref, base_ref, up_ref, *refs):
    lows, (send_ref, buf, sem) = refs[:-3], refs[-3:]
    half, packed = lows[0].shape
    rank = packed // 2
    rows = 2 * half
    count = send_ref.shape[0]
    low = lows[0][...].astype(jnp.float32)
    for more in lows[1:]:
        low = low + more[...].astype(jnp.float32)
    low = jnp.concatenate([low[:, :rank], low[:, rank:]], axis=0)
    batch = 256 // rank
    spread = jnp.concatenate([low] * batch, axis=1)
    ahead = stored_ref[...] - lax.broadcasted_iota(jnp.int32, (rows, batch * rank), 1) // rank
    total = jnp.zeros(base_ref.shape, jnp.float32)
    for a in range(0, up_ref.shape[0] // rank, batch):
        wide = jnp.where(ahead == a, spread, 0.0).astype(jnp.bfloat16)
        total = total + jnp.dot(wide, up_ref[a * rank : (a + batch) * rank], preferred_element_type=jnp.float32)
    each = query_ref.shape[0]
    buf[:each] = query_ref[...]
    buf[each : 2 * each] = key_ref[...]
    put_chunks(buf, 2 * each, base_ref[...] + adapter_scale * total)
    wait_all(
        start_all([pltpu.make_async_copy(buf.at[:, :, k], send_ref.at[k], sem.at[k]) for k in range(count)])
    )


def update_values(stored, query, key, base, up, lows):
    chunks, steps, count = query.shape[:3]
    return pl.pallas_call(
        update_kernel,
        out_shape=pltpu.HBM((count, 3 * chunks, steps, 2, HD), query.dtype),
        in_specs=[VMEM] * (5 + len(lows)),
        out_specs=HBM,
        scratch_shapes=[
            pltpu.VMEM((3 * chunks, steps, count, 2, HD), query.dtype),
            pltpu.SemaphoreType.DMA((count,)),
        ],
        compiler_params=pltpu.CompilerParams(vmem_limit_bytes=8 * 2**20),
        cost_estimate=pl.CostEstimate(flops=3 * 10**8, bytes_accessed=4 * 10**6, transcendentals=0),
        name="update_values",
    )(stored, query, key, base, up, *lows)


def attend_kernel(cos_ref, sin_ref, live_ref, pieces_ref, *refs):
    *parts, out_ref, values_buf, kn_ref, vn_ref, sem = refs
    keys_refs, values_refs = parts[: len(parts) // 2], parts[len(parts) // 2 :]
    count, _, steps = pieces_ref.shape[:3]
    rows = 2 * steps
    each = pieces_ref.shape[1] // 3
    heads = 2 * out_ref.shape[1] // count
    lanes = heads * HD
    group = rows * HEAD_BLOCK
    chips = range(count // 2)
    early = keys_refs[0].shape[0] // heads
    places = [(0, c) if c < early else (1, c - early) for c in chips]
    fetches = start_all(
        [
            pltpu.make_async_copy(values_refs[half].at[at * heads : (at + 1) * heads], values_buf.at[c], sem.at[c])
            for c, (half, at) in enumerate(places)
        ]
    )
    cosine = cos_ref[...][:rows]
    sine = sin_ref[...][:rows]
    left = lax.broadcasted_iota(jnp.int32, (rows, HD), 1) < HD // 2

    def chip_columns(chip, at):
        low = [pieces_ref[2 * chip, at + c].reshape(rows, HD).astype(jnp.float32) for c in range(each)]
        high = [pieces_ref[2 * chip + 1, at + c].reshape(rows, HD).astype(jnp.float32) for c in range(each)]
        high = [pltpu.roll(x, HD // 2, 1) for x in high]
        whole = low[:-1] + [jnp.where(left, low[-1], high[0])]
        return whole + [jnp.where(left, a, b) for a, b in zip(high[:-1], high[1:])]

    def rotated(parts):
        return [x * cosine + pltpu.roll(x, HD // 2, 1) * sine for x in parts]

    row_head = lax.broadcasted_iota(jnp.int32, (group, lanes), 0) % HEAD_BLOCK
    lane_head = lax.broadcasted_iota(jnp.int32, (group, lanes), 1) // HD
    own_head = row_head == lane_head
    row_j = lax.broadcasted_iota(jnp.int32, (group, 16), 0) // HEAD_BLOCK
    new_j = lax.broadcasted_iota(jnp.int32, (group, 16), 1)
    new_live = (new_j < rows) & (new_j % 2 == row_j % 2) & (new_j // 2 <= row_j // 2)
    live = jnp.concatenate(
        [
            jnp.broadcast_to(live_ref[j % 2 : j % 2 + 1, :], (HEAD_BLOCK, live_ref.shape[1]))
            for j in range(rows)
        ],
        axis=0,
    )
    live = live > 0
    kn_ref[...] = jnp.zeros_like(kn_ref)
    vn_ref[...] = jnp.zeros_like(vn_ref)
    spreads = []
    for c in chips:
        query = jnp.concatenate(rotated(chip_columns(c, 0)), axis=1)
        kn_ref[c, 0:rows] = jnp.concatenate(rotated(chip_columns(c, each)), axis=1)
        vn_ref[c, 0:rows] = jnp.concatenate(chip_columns(c, 2 * each), axis=1)
        spread = jnp.concatenate(
            [jnp.broadcast_to(query[j : j + 1], (HEAD_BLOCK, lanes)) for j in range(rows)], axis=0
        )
        spreads.append(jnp.where(own_head, spread, 0.0).astype(jnp.bfloat16))
    scores, fresh = [], []
    for c in chips:
        half, at = places[c]
        keys = jnp.concatenate([keys_refs[half][at * heads + h] for h in range(heads)], axis=1)
        kn = kn_ref[c].astype(jnp.bfloat16)
        scores.append(lax.dot_general(spreads[c], keys, CONTRACT_LANES, preferred_element_type=jnp.float32))
        fresh.append(lax.dot_general(spreads[c], kn, CONTRACT_LANES, preferred_element_type=jnp.float32))
    weights, fresh_weights, totals = [], [], []
    for c in chips:
        old = jnp.where(live, scores[c] * (HD**-0.5), masked_score)
        new = jnp.where(new_live, fresh[c] * (HD**-0.5), masked_score)
        top = jnp.maximum(jnp.max(old, axis=1, keepdims=True), jnp.max(new, axis=1, keepdims=True))
        old = jnp.where(live, jnp.exp(old - top), 0.0)
        new = jnp.where(new_live, jnp.exp(new - top), 0.0)
        totals.append(jnp.sum(old, axis=1, keepdims=True) + jnp.sum(new, axis=1, keepdims=True))
        weights.append(old.astype(jnp.bfloat16))
        fresh_weights.append(new.astype(jnp.bfloat16))
    wait_all(fetches)
    for c in chips:
        values = lanes_of(values_buf[c])
        vn = vn_ref[c].astype(jnp.bfloat16)
        mixed = jnp.dot(weights[c], values, preferred_element_type=jnp.float32)
        mixed = mixed + jnp.dot(fresh_weights[c], vn, preferred_element_type=jnp.float32)
        mixed = jnp.where(own_head, mixed / totals[c], 0.0)
        out = jnp.sum(mixed.reshape(rows, HEAD_BLOCK, lanes), axis=1).astype(out_ref.dtype)
        for t in range(steps):
            for h in range(heads):
                out_ref[t, c * heads + h] = out[2 * t : 2 * t + 2, h * HD : (h + 1) * HD]


def attend(cosine, sine, live, pieces, keys, values):
    count, _, steps = pieces.shape[:3]
    heads, tokens = sum(x.shape[0] for x in keys), keys[0].shape[1]
    chips = count // 2
    per = heads // chips
    return pl.pallas_call(
        attend_kernel,
        out_shape=jax.ShapeDtypeStruct((steps, heads, 2, HD), jnp.bfloat16),
        in_specs=[VMEM] * (4 + len(keys)) + [HBM] * len(values),
        out_specs=VMEM,
        scratch_shapes=[pltpu.VMEM((chips, per, tokens, HD), jnp.bfloat16)]
        + [pltpu.VMEM((chips, 16, per * HD), jnp.float32)] * 2
        + [pltpu.SemaphoreType.DMA((chips,))],
        compiler_params=pltpu.CompilerParams(vmem_limit_bytes=16 * 2**20),
        cost_estimate=pl.CostEstimate(flops=10**9, bytes_accessed=6 * 10**6, transcendentals=0),
        name="attention",
    )(cosine, sine, live, pieces, *keys, *[in_hbm(x) for x in values])


def chip_plan(
    count,
    hidden,
    query_key_value_weight,
    adapter_down_maps,
    adapter_up_maps,
    adapter_storage_row,
    request_adapter,
    lengths,
    request_page_table,
    key_value_pool,
):
    me = lax.axis_index("replica")
    steps, req_dev, width = hidden.shape
    heads = width // HD
    holder_count, rank, _ = adapter_down_maps.shape
    pool_pages, page_len = key_value_pool.shape[:2]
    adapter_count = adapter_storage_row.shape[0]

    tokens = pool_pages * page_len
    pool = key_value_pool.reshape(tokens, 2, heads, HD).transpose(0, 2, 1, 3)

    stored = jnp.sum(
        jnp.where(
            request_adapter[:, None] == jnp.arange(adapter_count, dtype=jnp.int32)[None, :],
            adapter_storage_row[None, :],
            0,
        ),
        axis=1,
    )
    first, slots, here, stored = lax.optimization_barrier(
        (me * req_dev, (me * holder_count).astype(jnp.int32).reshape(1), me.astype(jnp.int32).reshape(1), stored)
    )
    slot, column = index_work(slots, stored, steps)

    held = {0: hidden}
    held.update({m: trade(hidden, m, count) for m in range(4, count, 4)})
    _, lengths, request_page_table = lax.optimization_barrier((held[4], lengths, request_page_table))
    cosine, sine = rotation_rows(lengths, first, req_dev, steps)
    live = live_lanes(lengths, first, request_page_table, tokens, page_len)
    for mask in (2, 1):
        held.update({k ^ mask: trade(v, mask, count) for k, v in list(held.items())})
    blocks = [held[k].reshape(steps, req_dev, heads, HD).transpose(0, 2, 1, 3) for k in range(count)]
    blocks[0] = in_hbm(blocks[0])
    x, low = low_of(here, blocks, slot, adapter_down_maps)
    weight = query_key_value_weight.transpose(0, 2, 1)
    arrived = [trade(low, m, count) for m in (1, 2, 3)]
    query, key = project(0, x, weight), project(1, x, weight)
    arrived, query, key, pool = lax.optimization_barrier((arrived, query, key, pool))
    low = (low + arrived[0]) + (arrived[1] + arrived[2])
    arrived = [trade(low, m, count) for m in range(4, count, 4)]
    base = project(2, x, weight)
    arrived, base = lax.optimization_barrier((arrived, base))
    send = update_values(column, query, key, base, adapter_up_maps.reshape(adapter_count * rank, -1), [low, *arrived])
    send, pool = lax.optimization_barrier((send, pool))
    keys, values = cache_by_head(pool, 0, heads)
    pieces = lax.all_to_all(send, "replica", split_axis=0, concat_axis=0, tiled=True)

    out = attend(cosine, sine, live, pieces, [keys], [values])
    return out.transpose(0, 2, 1, 3).reshape(steps, req_dev, width)


def per_device(replicas, *arrays):
    columns = arrays[1].shape[2]
    whole_heads = replicas % 4 == 0 and (2 * columns) % HD == 0 and columns % HD == HD // 2
    plan = chip_plan if whole_heads and arrays[0].shape[1] == 2 else general_plan
    return plan(replicas, *arrays)


def solution(mesh):
    placed = (
        P(None, ("groups", "replica"), None),
        P(None, None, "replica"),
        P("replica", None, None),
        P(None, None, "replica"),
        P(),
        P("groups"),
        P("groups"),
        P(("groups", "replica"), None),
        P(("groups", "replica"), None, None, None),
    )
    return jax.shard_map(
        functools.partial(per_device, mesh.shape["replica"]),
        mesh=mesh,
        in_specs=placed,
        out_specs=P(None, ("groups", "replica"), None),
        check_vma=False,
    )
```

```python
import functools

import jax
import jax.numpy as jnp
from jax import lax
from jax.experimental import pallas as pl
from jax.experimental.pallas import tpu as pltpu
from jax.sharding import PartitionSpec as P

HD = 128
ROWS = 8
HEAD_BLOCK = 8

adapter_scale = 2.0
masked_score = -1e30


def attention_kernel(steps, req_dev, q_ref, k_ref, v_ref, cos_ref, sin_ref, live_ref, kv_ref, out_ref, kn_ref, vn_ref):
    rows = steps * req_dev
    width = q_ref.shape[1]
    lanes = HEAD_BLOCK * HD
    group = rows * HEAD_BLOCK
    cosine = cos_ref[...]
    sine = sin_ref[...]

    def rotated(x):
        pieces = []
        for h in range(HEAD_BLOCK):
            head = x[:, h * HD : (h + 1) * HD]
            pieces.append(head * cosine + pltpu.roll(head, HD // 2, 1) * sine)
        return jnp.concatenate(pieces, axis=1)

    row_head = lax.broadcasted_iota(jnp.int32, (group, lanes), 0) % HEAD_BLOCK
    lane_head = lax.broadcasted_iota(jnp.int32, (group, lanes), 1) // HD
    own_head = row_head == lane_head
    row_j = lax.broadcasted_iota(jnp.int32, (group, 16), 0) // HEAD_BLOCK
    new_j = lax.broadcasted_iota(jnp.int32, (group, 16), 1)
    new_live = (new_j < rows) & (new_j % req_dev == row_j % req_dev) & (new_j // req_dev <= row_j // req_dev)
    live_all = live_ref[...]
    live = jnp.concatenate(
        [
            jnp.broadcast_to(live_all[j % req_dev : j % req_dev + 1], (HEAD_BLOCK, live_all.shape[1]))
            for j in range(rows)
        ],
        axis=0,
    )
    live = live > 0
    kn_ref[...] = jnp.zeros_like(kn_ref)
    vn_ref[...] = jnp.zeros_like(vn_ref)
    contract_lanes = (((1,), (1,)), ((), ()))
    for c in range(width // lanes):
        cols = slice(c * lanes, (c + 1) * lanes)
        query = rotated(q_ref[:, cols].astype(jnp.float32))
        key_new = rotated(k_ref[:, cols].astype(jnp.float32))
        kn_ref[0:8] = key_new
        vn_ref[0:8] = v_ref[:, cols].astype(jnp.float32)
        kn = kn_ref[...].astype(jnp.bfloat16)
        vn = vn_ref[...].astype(jnp.bfloat16)
        spread = jnp.concatenate(
            [jnp.broadcast_to(query[j : j + 1], (HEAD_BLOCK, lanes)) for j in range(rows)], axis=0
        )
        spread = jnp.where(own_head, spread, 0.0).astype(jnp.bfloat16)
        kv = kv_ref[:, cols]
        scores = lax.dot_general(spread, kv, contract_lanes, preferred_element_type=jnp.float32) * (HD**-0.5)
        scores = jnp.where(live, scores, masked_score)
        fresh = lax.dot_general(spread, kn, contract_lanes, preferred_element_type=jnp.float32) * (HD**-0.5)
        fresh = jnp.where(new_live, fresh, masked_score)
        top = jnp.maximum(jnp.max(scores, axis=1, keepdims=True), jnp.max(fresh, axis=1, keepdims=True))
        weights = jnp.where(live, jnp.exp(scores - top), 0.0)
        fresh = jnp.where(new_live, jnp.exp(fresh - top), 0.0)
        totals = jnp.sum(weights, axis=1, keepdims=True) + jnp.sum(fresh, axis=1, keepdims=True)
        weights = pltpu.roll(weights, 1, 1).astype(jnp.bfloat16)
        mixed = jnp.dot(weights, kv, preferred_element_type=jnp.float32)
        mixed = mixed + jnp.dot(fresh.astype(jnp.bfloat16), vn, preferred_element_type=jnp.float32)
        mixed = jnp.where(own_head, mixed / totals, 0.0)
        out = jnp.sum(mixed.reshape(rows, HEAD_BLOCK, lanes), axis=1)
        out_ref[:, cols] = out.astype(out_ref.dtype)


def attention(steps, req_dev, q, k, v, cosine, sine, live, kv):
    rows = steps * req_dev
    width = q.shape[1]
    vmem = pl.BlockSpec(memory_space=pltpu.VMEM)
    return pl.pallas_call(
        functools.partial(attention_kernel, steps, req_dev),
        out_shape=jax.ShapeDtypeStruct((rows, width), jnp.bfloat16),
        in_specs=[vmem] * 7,
        out_specs=vmem,
        scratch_shapes=[pltpu.VMEM((16, HEAD_BLOCK * HD), jnp.float32)] * 2,
        compiler_params=pltpu.CompilerParams(vmem_limit_bytes=32 * 2**20),
        cost_estimate=pl.CostEstimate(flops=10**9, bytes_accessed=6 * 10**6, transcendentals=0),
        name="attention",
    )(q, k, v, cosine, sine, live, kv)


def rotation(my_lengths, steps):
    rows = steps * my_lengths.shape[0]
    positions = (my_lengths[None, :] + jnp.arange(steps, dtype=jnp.int32)[:, None]).reshape(rows)
    positions = jnp.pad(positions, (0, ROWS - rows))
    half = HD // 2
    frequency = jnp.exp(jnp.arange(half, dtype=jnp.float32) * (-2.0 * jnp.log(10000.0) / HD))
    angles = positions.astype(jnp.float32)[:, None] * frequency[None, :]
    cosine = jnp.cos(angles)
    sine = jnp.sin(angles)
    cosine = jnp.concatenate([cosine, cosine], axis=1)
    sine = jnp.concatenate([-sine, sine], axis=1)
    return cosine, sine


def live_tokens(my_lengths, request_page_table, pool_pages, page_len):
    pages = jnp.arange(pool_pages, dtype=jnp.int32)
    max_pages = request_page_table.shape[1]
    place = jnp.max(
        jnp.where(
            request_page_table[:, :, None] == pages[None, None, :],
            jnp.arange(max_pages, dtype=jnp.int32)[None, :, None],
            -1,
        ),
        axis=1,
    )
    token = place[:, :, None] * page_len + jnp.arange(page_len, dtype=jnp.int32)[None, None, :]
    return (place[:, :, None] >= 0) & (token < my_lengths[:, None, None])


def live_rows(my_lengths, request_page_table, pool_pages, page_len):
    alive = live_tokens(my_lengths, request_page_table, pool_pages, page_len)
    live = jnp.stack([alive, jnp.zeros_like(alive)], axis=-1).astype(jnp.int32)
    return live.reshape(request_page_table.shape[0], pool_pages * page_len * 2)


def general_plan(
    replicas,
    hidden,
    query_key_value_weight,
    adapter_down_maps,
    adapter_up_maps,
    adapter_storage_row,
    request_adapter,
    lengths,
    request_page_table,
    key_value_pool,
):
    my_index = lax.axis_index("replica")
    steps, req_dev, width = hidden.shape
    rows = steps * req_dev
    columns = query_key_value_weight.shape[2]
    holder_count, rank, _ = adapter_down_maps.shape
    pool_pages, page_len = key_value_pool.shape[:2]
    adapter_count = adapter_storage_row.shape[0]
    chips = replicas // 2
    total = replicas * ROWS

    block = jnp.pad(hidden.reshape(rows, width), ((0, ROWS - rows), (0, 0)))
    same_core = [[2 * chip + core for chip in range(chips)] for core in range(2)]
    mine = lax.all_to_all(
        jnp.broadcast_to(block[None], (chips, ROWS, width)),
        "replica",
        split_axis=0,
        concat_axis=0,
        axis_index_groups=same_core,
        tiled=True,
    )
    other = lax.ppermute(mine, "replica", [(i, i ^ 1) for i in range(replicas)])
    first = my_index % 2 == 0
    gathered = jnp.stack([jnp.where(first, mine, other), jnp.where(first, other, mine)])
    gathered = gathered.reshape(total, width)

    stored_rows = jnp.sum(
        jnp.where(
            request_adapter[:, None] == jnp.arange(adapter_count, dtype=jnp.int32)[None, :],
            adapter_storage_row[None, :],
            0,
        ),
        axis=1,
    )
    by_block = stored_rows.reshape(chips, 2, 1, req_dev).transpose(1, 0, 2, 3)
    by_block = jnp.broadcast_to(by_block, (2, chips, steps, req_dev)).reshape(2, chips, rows)
    row_stored = jnp.pad(by_block, ((0, 0), (0, 0), (0, ROWS - rows)), constant_values=-1).reshape(total)

    down = jnp.einsum("nd,hfd->nhf", gathered, adapter_down_maps, preferred_element_type=jnp.float32)
    slots = my_index * holder_count + jnp.arange(holder_count, dtype=jnp.int32)
    own = row_stored[:, None] == slots[None, :]
    low = jnp.sum(jnp.where(own[:, :, None], down, 0.0), axis=1).astype(jnp.bfloat16)
    low = jnp.concatenate([low[: total // 2], low[total // 2 :]], axis=1)
    low = lax.all_to_all(
        jnp.broadcast_to(low[None], (replicas,) + low.shape), "replica", split_axis=0, concat_axis=0, tiled=True
    )
    low = jnp.sum(low.astype(jnp.float32), axis=0)
    low = jnp.concatenate([low[:, :rank], low[:, rank:]], axis=0)

    projected = jnp.einsum("nd,idc->nic", gathered, query_key_value_weight, preferred_element_type=jnp.float32)

    def update(first_adapter, maps):
        held = maps.shape[0]
        which = first_adapter + jnp.arange(held, dtype=jnp.int32)
        wide = jnp.where((row_stored[:, None] == which[None, :])[:, :, None], low[:, None, :], 0.0)
        return jnp.dot(
            wide.astype(jnp.bfloat16).reshape(total, held * rank),
            maps.reshape(held * rank, columns),
            preferred_element_type=jnp.float32,
        )

    step_adapters = 64
    if adapter_count <= step_adapters:
        updated = update(0, adapter_up_maps)
    else:
        updated = lax.fori_loop(
            0,
            adapter_count // step_adapters,
            lambda i, sofar: sofar
            + update(
                i * step_adapters,
                lax.dynamic_slice_in_dim(adapter_up_maps, i * step_adapters, step_adapters, 0),
            ),
            jnp.zeros((total, columns), jnp.float32),
        )
    value = projected[:, 2] + adapter_scale * updated
    combined = jnp.concatenate([projected[:, 0], projected[:, 1], value], axis=1).astype(jnp.bfloat16)
    combined = combined.reshape(2, chips, ROWS, 3 * columns).transpose(1, 0, 2, 3)
    combined = combined.reshape(replicas, ROWS, 3 * columns)
    arrived = lax.all_to_all(combined, "replica", split_axis=0, concat_axis=0, tiled=True)
    arrived = arrived.reshape(replicas, ROWS, 3, columns).transpose(2, 1, 0, 3).reshape(3, ROWS, width)

    my_lengths = lax.dynamic_slice_in_dim(lengths, my_index * req_dev, req_dev)
    cosine, sine = rotation(my_lengths, steps)
    live = live_rows(my_lengths, request_page_table, pool_pages, page_len)
    kv = key_value_pool.reshape(pool_pages * page_len * 2, width)
    out = attention(steps, req_dev, arrived[0], arrived[1], arrived[2], cosine, sine, live, kv)
    return out.reshape(steps, req_dev, width)


def rotation_rows(lengths, first, req_dev, steps):
    row = jnp.arange(ROWS, dtype=jnp.int32)
    wanted = first + row % req_dev
    chosen = jnp.where(wanted[:, None] == jnp.arange(lengths.shape[0], dtype=jnp.int32)[None, :], lengths[None, :], 0)
    positions = jnp.sum(chosen, axis=1, keepdims=True) + (row // req_dev)[:, None]
    lane = jnp.arange(HD, dtype=jnp.int32)
    frequency = jnp.exp((lane % (HD // 2)).astype(jnp.float32) * (-2.0 * jnp.log(10000.0) / HD))
    angles = positions.astype(jnp.float32) * frequency[None, :]
    return jnp.cos(angles), jnp.where(lane < HD // 2, -1.0, 1.0)[None, :] * jnp.sin(angles)


def live_lanes(lengths, first, request_page_table, tokens, page_len):
    req_dev, max_pages = request_page_table.shape
    wanted = first + jnp.arange(req_dev, dtype=jnp.int32)
    chosen = jnp.where(wanted[:, None] == jnp.arange(lengths.shape[0], dtype=jnp.int32)[None, :], lengths[None, :], 0)
    lane = jnp.arange(tokens, dtype=jnp.int32)
    page = jnp.arange(max_pages, dtype=jnp.int32)
    place = jnp.max(
        jnp.where(request_page_table[:, :, None] == (lane // page_len)[None, None, :], page[None, :, None], -1),
        axis=1,
    )
    token = place * page_len + (lane % page_len)[None, :]
    return ((place >= 0) & (token < jnp.sum(chosen, axis=1, keepdims=True))).astype(jnp.int32)


def trade(value, mask, count):
    return lax.ppermute(value, "replica", [(i, i ^ mask) for i in range(count)])


CONTRACT_LANES = (((1,), (1,)), ((), ()))


def in_hbm(x):
    return pltpu.with_memory_space_constraint(x, pltpu.HBM)


VMEM = pl.BlockSpec(memory_space=pltpu.VMEM)
HBM = pl.BlockSpec(memory_space=pltpu.HBM)
SMEM = pl.BlockSpec(memory_space=pltpu.SMEM)
ANY = pl.BlockSpec(memory_space=pl.ANY)


def start_all(copies):
    for copy in copies:
        copy.start()
    return copies


def wait_all(copies):
    for copy in copies:
        copy.wait()


CACHE_SECTION = 10
CACHE_AHEAD = 2


def cache_kernel(first, pool_ref, keys_ref, values_ref, raw, values, sem, out_sem):
    heads, tokens = raw.shape[:2]
    copies = [pltpu.make_async_copy(pool_ref.at[:, first + h], raw.at[h], sem.at[h]) for h in range(heads)]
    start_all(copies[: CACHE_AHEAD * CACHE_SECTION])
    rows = raw.reshape(heads, 2 * tokens, HD)
    to = lax.broadcasted_iota(jnp.int32, (2 * tokens, 2 * tokens), 0)
    source = lax.broadcasted_iota(jnp.int32, (2 * tokens, 2 * tokens), 1)
    wanted = jnp.where(to < tokens, 2 * to, 2 * (to - tokens) + 1)
    pick = jnp.where(source == wanted, 1.0, 0.0).astype(jnp.bfloat16)
    sent = []
    part = CACHE_SECTION
    for p in range(heads // part):
        wait_all(copies[p * part : (p + 1) * part])
        start_all(copies[(p + CACHE_AHEAD) * part : (p + CACHE_AHEAD + 1) * part])
        for h in range(p * part, (p + 1) * part, 2):
            both = jnp.concatenate([rows[h], rows[h + 1]], axis=1)
            made = jnp.dot(pick, both, preferred_element_type=jnp.float32).astype(jnp.bfloat16)
            for i in range(2):
                keys_ref[h + i] = made[:tokens, i * HD : (i + 1) * HD]
                values[h + i] = made[tokens:, i * HD : (i + 1) * HD]
        span = slice(p * part, (p + 1) * part)
        sent += start_all([pltpu.make_async_copy(values.at[span], values_ref.at[span], out_sem.at[p])])
    wait_all(sent)


def cache_by_head(pool, first, heads):
    tokens = pool.shape[0]
    return pl.pallas_call(
        functools.partial(cache_kernel, first),
        out_shape=(
            jax.ShapeDtypeStruct((heads, tokens, HD), pool.dtype),
            pltpu.HBM((heads, tokens, HD), pool.dtype),
        ),
        in_specs=[HBM],
        out_specs=(VMEM, HBM),
        scratch_shapes=[
            pltpu.VMEM((heads, tokens, 2, HD), pool.dtype),
            pltpu.VMEM((heads, tokens, HD), pool.dtype),
            pltpu.SemaphoreType.DMA((heads,)),
            pltpu.SemaphoreType.DMA((heads // CACHE_SECTION,)),
        ],
        compiler_params=pltpu.CompilerParams(vmem_limit_bytes=12 * 2**20),
        cost_estimate=pl.CostEstimate(flops=0, bytes_accessed=12 * 10**6, transcendentals=0),
        name="cache_by_head",
    )(in_hbm(pool))


def lanes_of(x):
    return jnp.concatenate([x[c] for c in range(x.shape[0])], axis=1)


def step_rows(x, first, chunks):
    steps, _, count = x.shape[:3]
    flat = x.reshape(steps, x.shape[1], 2 * count, HD)
    return jnp.concatenate(
        [jnp.concatenate([flat[t, c] for c in range(first, first + chunks)], axis=1) for t in range(steps)], axis=0
    )


def index_kernel(me_ref, stored_ref, slot_ref, column_ref):
    requests = stored_ref.shape[1]
    steps = slot_ref.shape[1] // requests
    row = jnp.concatenate([stored_ref[...]] * steps, axis=1)
    slot_ref[...] = row - me_ref[0]
    wide = jnp.concatenate([row, jnp.zeros((1, HD - row.shape[1]), row.dtype)], axis=1)
    column_ref[...] = jnp.broadcast_to(wide.astype(jnp.float32), (HD, HD)).T[: row.shape[1], :1].astype(jnp.int32)


def index_work(first, stored, steps):
    rows = stored.shape[0] * steps
    return pl.pallas_call(
        index_kernel,
        out_shape=(jax.ShapeDtypeStruct((1, rows), jnp.int32), jax.ShapeDtypeStruct((rows, 1), jnp.int32)),
        in_specs=[SMEM, VMEM],
        out_specs=(VMEM, VMEM),
        compiler_params=pltpu.CompilerParams(vmem_limit_bytes=2 * 2**20),
        cost_estimate=pl.CostEstimate(flops=2 * 10**10, bytes_accessed=10**4, transcendentals=0),
        name="index_work",
    )(first, stored[None, :])


def low_kernel(count, me_ref, slot_ref, down_ref, *refs):
    blocks, (x_ref, low_ref, sem) = refs[:count], refs[count:]
    me = me_ref[0]
    holders, rank, width = down_ref.shape
    wait_all(
        start_all(
            [pltpu.make_async_copy(block, x_ref.at[:, :, me ^ k], sem.at[k]) for k, block in enumerate(blocks)]
        )
    )
    x = step_rows(x_ref, 0, x_ref.shape[1])
    rows = x.shape[0]
    made = lax.dot_general(
        down_ref.reshape(holders * rank, width)[...], x, CONTRACT_LANES, preferred_element_type=jnp.float32
    )
    slot = slot_ref[...]
    low = jnp.zeros((rank, rows), jnp.float32)
    for h in range(holders):
        low = low + jnp.where(slot == h, made[h * rank : (h + 1) * rank], 0.0)
    low = low.T
    low_ref[...] = jnp.concatenate([low[: rows // 2], low[rows // 2 :]], axis=1).astype(low_ref.dtype)


def low_of(me, blocks, slot, down):
    count = len(blocks)
    steps, chunks = blocks[0].shape[:2]
    rows = count * steps * 2
    rank = down.shape[1]
    return pl.pallas_call(
        functools.partial(low_kernel, count),
        out_shape=(
            jax.ShapeDtypeStruct((steps, chunks, count, 2, HD), jnp.bfloat16),
            jax.ShapeDtypeStruct((rows // 2, 2 * rank), jnp.bfloat16),
        ),
        in_specs=[SMEM, VMEM, VMEM] + [ANY] * count,
        out_specs=(VMEM, VMEM),
        scratch_shapes=[pltpu.SemaphoreType.DMA((count,))],
        compiler_params=pltpu.CompilerParams(vmem_limit_bytes=12 * 2**20),
        cost_estimate=pl.CostEstimate(flops=10**8, bytes_accessed=4 * 10**6, transcendentals=0),
        name="low_rows",
    )(me, slot, down, *blocks)


def put_chunks(buf, first, value):
    steps, count = buf.shape[1:3]
    flat = buf.reshape(buf.shape[0], steps, 2 * count, HD)
    wide = value.shape[1]
    for c in range(-(-wide // HD)):
        part = value[:, c * HD : min((c + 1) * HD, wide)]
        if part.shape[1] < HD:
            part = jnp.concatenate([part, jnp.zeros((part.shape[0], HD - part.shape[1]), part.dtype)], axis=1)
        part = part.astype(buf.dtype)
        for t in range(steps):
            flat[first + c, t] = part[t * 2 * count : (t + 1) * 2 * count]


def project_kernel(which, x_ref, w_ref, out_ref):
    x = step_rows(x_ref, 0, x_ref.shape[1])
    made = lax.dot_general(w_ref[which], x, CONTRACT_LANES, preferred_element_type=jnp.float32).T
    if which < 2:
        put_chunks(out_ref, 0, made)
    else:
        out_ref[...] = made


def project(which, x, weight):
    steps, _, count = x.shape[:3]
    columns = weight.shape[1]
    chunks = jax.ShapeDtypeStruct((-(-columns // HD), steps, count, 2, HD), jnp.bfloat16)
    base = jax.ShapeDtypeStruct((2 * steps * count, columns), jnp.float32)
    return pl.pallas_call(
        functools.partial(project_kernel, which),
        out_shape=chunks if which < 2 else base,
        in_specs=[VMEM, VMEM],
        out_specs=VMEM,
        compiler_params=pltpu.CompilerParams(vmem_limit_bytes=16 * 2**20),
        cost_estimate=pl.CostEstimate(flops=5 * 10**8, bytes_accessed=4 * 10**6, transcendentals=0),
        name="project",
    )(x, weight)


def update_kernel(stored_ref, query_ref, key_ref, base_ref, up_ref, *refs):
    lows, (send_ref, buf, sem) = refs[:-3], refs[-3:]
    half, packed = lows[0].shape
    rank = packed // 2
    rows = 2 * half
    count = send_ref.shape[0]
    low = lows[0][...].astype(jnp.float32)
    for more in lows[1:]:
        low = low + more[...].astype(jnp.float32)
    low = jnp.concatenate([low[:, :rank], low[:, rank:]], axis=0)
    batch = 256 // rank
    spread = jnp.concatenate([low] * batch, axis=1)
    ahead = stored_ref[...] - lax.broadcasted_iota(jnp.int32, (rows, batch * rank), 1) // rank
    total = jnp.zeros(base_ref.shape, jnp.float32)
    for a in range(0, up_ref.shape[0] // rank, batch):
        wide = jnp.where(ahead == a, spread, 0.0).astype(jnp.bfloat16)
        total = total + jnp.dot(wide, up_ref[a * rank : (a + batch) * rank], preferred_element_type=jnp.float32)
    each = query_ref.shape[0]
    buf[:each] = query_ref[...]
    buf[each : 2 * each] = key_ref[...]
    put_chunks(buf, 2 * each, base_ref[...] + adapter_scale * total)
    wait_all(
        start_all([pltpu.make_async_copy(buf.at[:, :, k], send_ref.at[k], sem.at[k]) for k in range(count)])
    )


def update_values(stored, query, key, base, up, lows):
    chunks, steps, count = query.shape[:3]
    return pl.pallas_call(
        update_kernel,
        out_shape=pltpu.HBM((count, 3 * chunks, steps, 2, HD), query.dtype),
        in_specs=[VMEM] * (5 + len(lows)),
        out_specs=HBM,
        scratch_shapes=[
            pltpu.VMEM((3 * chunks, steps, count, 2, HD), query.dtype),
            pltpu.SemaphoreType.DMA((count,)),
        ],
        compiler_params=pltpu.CompilerParams(vmem_limit_bytes=8 * 2**20),
        cost_estimate=pl.CostEstimate(flops=3 * 10**8, bytes_accessed=4 * 10**6, transcendentals=0),
        name="update_values",
    )(stored, query, key, base, up, *lows)


def attend_kernel(cos_ref, sin_ref, live_ref, pieces_ref, *refs):
    *parts, out_ref, values_buf, kn_ref, vn_ref, sem = refs
    keys_refs, values_refs = parts[: len(parts) // 2], parts[len(parts) // 2 :]
    count, _, steps = pieces_ref.shape[:3]
    rows = 2 * steps
    each = pieces_ref.shape[1] // 3
    heads = 2 * out_ref.shape[1] // count
    lanes = heads * HD
    group = rows * HEAD_BLOCK
    chips = range(count // 2)
    early = keys_refs[0].shape[0] // heads
    places = [(0, c) if c < early else (1, c - early) for c in chips]
    fetches = start_all(
        [
            pltpu.make_async_copy(values_refs[half].at[at * heads : (at + 1) * heads], values_buf.at[c], sem.at[c])
            for c, (half, at) in enumerate(places)
        ]
    )
    cosine = cos_ref[...][:rows]
    sine = sin_ref[...][:rows]
    left = lax.broadcasted_iota(jnp.int32, (rows, HD), 1) < HD // 2

    def chip_columns(chip, at):
        low = [pieces_ref[2 * chip, at + c].reshape(rows, HD).astype(jnp.float32) for c in range(each)]
        high = [pieces_ref[2 * chip + 1, at + c].reshape(rows, HD).astype(jnp.float32) for c in range(each)]
        high = [pltpu.roll(x, HD // 2, 1) for x in high]
        whole = low[:-1] + [jnp.where(left, low[-1], high[0])]
        return whole + [jnp.where(left, a, b) for a, b in zip(high[:-1], high[1:])]

    def rotated(parts):
        return [x * cosine + pltpu.roll(x, HD // 2, 1) * sine for x in parts]

    row_head = lax.broadcasted_iota(jnp.int32, (group, lanes), 0) % HEAD_BLOCK
    lane_head = lax.broadcasted_iota(jnp.int32, (group, lanes), 1) // HD
    own_head = row_head == lane_head
    row_j = lax.broadcasted_iota(jnp.int32, (group, 16), 0) // HEAD_BLOCK
    new_j = lax.broadcasted_iota(jnp.int32, (group, 16), 1)
    new_live = (new_j < rows) & (new_j % 2 == row_j % 2) & (new_j // 2 <= row_j // 2)
    live = jnp.concatenate(
        [
            jnp.broadcast_to(live_ref[j % 2 : j % 2 + 1, :], (HEAD_BLOCK, live_ref.shape[1]))
            for j in range(rows)
        ],
        axis=0,
    )
    live = live > 0
    kn_ref[...] = jnp.zeros_like(kn_ref)
    vn_ref[...] = jnp.zeros_like(vn_ref)
    spreads = []
    for c in chips:
        query = jnp.concatenate(rotated(chip_columns(c, 0)), axis=1)
        kn_ref[c, 0:rows] = jnp.concatenate(rotated(chip_columns(c, each)), axis=1)
        vn_ref[c, 0:rows] = jnp.concatenate(chip_columns(c, 2 * each), axis=1)
        spread = jnp.concatenate(
            [jnp.broadcast_to(query[j : j + 1], (HEAD_BLOCK, lanes)) for j in range(rows)], axis=0
        )
        spreads.append(jnp.where(own_head, spread, 0.0).astype(jnp.bfloat16))
    scores, fresh = [], []
    for c in chips:
        half, at = places[c]
        keys = jnp.concatenate([keys_refs[half][at * heads + h] for h in range(heads)], axis=1)
        kn = kn_ref[c].astype(jnp.bfloat16)
        scores.append(lax.dot_general(spreads[c], keys, CONTRACT_LANES, preferred_element_type=jnp.float32))
        fresh.append(lax.dot_general(spreads[c], kn, CONTRACT_LANES, preferred_element_type=jnp.float32))
    weights, fresh_weights, totals = [], [], []
    for c in chips:
        old = jnp.where(live, scores[c] * (HD**-0.5), masked_score)
        new = jnp.where(new_live, fresh[c] * (HD**-0.5), masked_score)
        top = jnp.maximum(jnp.max(old, axis=1, keepdims=True), jnp.max(new, axis=1, keepdims=True))
        old = jnp.where(live, jnp.exp(old - top), 0.0)
        new = jnp.where(new_live, jnp.exp(new - top), 0.0)
        totals.append(jnp.sum(old, axis=1, keepdims=True) + jnp.sum(new, axis=1, keepdims=True))
        weights.append(old.astype(jnp.bfloat16))
        fresh_weights.append(new.astype(jnp.bfloat16))
    wait_all(fetches)
    for c in chips:
        values = lanes_of(values_buf[c])
        vn = vn_ref[c].astype(jnp.bfloat16)
        mixed = jnp.dot(weights[c], values, preferred_element_type=jnp.float32)
        mixed = mixed + jnp.dot(fresh_weights[c], vn, preferred_element_type=jnp.float32)
        mixed = jnp.where(own_head, mixed / totals[c], 0.0)
        out = jnp.sum(mixed.reshape(rows, HEAD_BLOCK, lanes), axis=1).astype(out_ref.dtype)
        for t in range(steps):
            for h in range(heads):
                out_ref[t, c * heads + h] = out[2 * t : 2 * t + 2, h * HD : (h + 1) * HD]


def attend(cosine, sine, live, pieces, keys, values):
    count, _, steps = pieces.shape[:3]
    heads, tokens = sum(x.shape[0] for x in keys), keys[0].shape[1]
    chips = count // 2
    per = heads // chips
    return pl.pallas_call(
        attend_kernel,
        out_shape=jax.ShapeDtypeStruct((steps, heads, 2, HD), jnp.bfloat16),
        in_specs=[VMEM] * (4 + len(keys)) + [HBM] * len(values),
        out_specs=VMEM,
        scratch_shapes=[pltpu.VMEM((chips, per, tokens, HD), jnp.bfloat16)]
        + [pltpu.VMEM((chips, 16, per * HD), jnp.float32)] * 2
        + [pltpu.SemaphoreType.DMA((chips,))],
        compiler_params=pltpu.CompilerParams(vmem_limit_bytes=16 * 2**20),
        cost_estimate=pl.CostEstimate(flops=10**9, bytes_accessed=6 * 10**6, transcendentals=0),
        name="attention",
    )(cosine, sine, live, pieces, *keys, *[in_hbm(x) for x in values])


def chip_plan(
    count,
    hidden,
    query_key_value_weight,
    adapter_down_maps,
    adapter_up_maps,
    adapter_storage_row,
    request_adapter,
    lengths,
    request_page_table,
    key_value_pool,
):
    me = lax.axis_index("replica")
    steps, req_dev, width = hidden.shape
    heads = width // HD
    holder_count, rank, _ = adapter_down_maps.shape
    pool_pages, page_len = key_value_pool.shape[:2]
    adapter_count = adapter_storage_row.shape[0]

    tokens = pool_pages * page_len
    pool = key_value_pool.reshape(tokens, 2, heads, HD).transpose(0, 2, 1, 3)

    stored = jnp.sum(
        jnp.where(
            request_adapter[:, None] == jnp.arange(adapter_count, dtype=jnp.int32)[None, :],
            adapter_storage_row[None, :],
            0,
        ),
        axis=1,
    )
    first, slots, here, stored = lax.optimization_barrier(
        (me * req_dev, (me * holder_count).astype(jnp.int32).reshape(1), me.astype(jnp.int32).reshape(1), stored)
    )
    slot, column = index_work(slots, stored, steps)

    held = {0: hidden}
    held.update({m: trade(hidden, m, count) for m in range(4, count, 4)})
    _, lengths, request_page_table = lax.optimization_barrier((held[4], lengths, request_page_table))
    cosine, sine = rotation_rows(lengths, first, req_dev, steps)
    live = live_lanes(lengths, first, request_page_table, tokens, page_len)
    held.update({k | 2: trade(v, 2, count) for k, v in list(held.items())})
    ready = [0, 2, 4, 6]
    held.update(zip(ready, lax.optimization_barrier([held[k] for k in ready])))
    held.update({k | 1: trade(v, 1, count) for k, v in list(held.items())})
    blocks = [held[k].reshape(steps, req_dev, heads, HD).transpose(0, 2, 1, 3) for k in range(count)]
    blocks[0] = in_hbm(blocks[0])
    x, low = low_of(here, blocks, slot, adapter_down_maps)
    weight = query_key_value_weight.transpose(0, 2, 1)
    arrived = [trade(low, m, count) for m in (1, 2, 3)]
    query, key = project(0, x, weight), project(1, x, weight)
    arrived, query, key, pool = lax.optimization_barrier((arrived, query, key, pool))
    low = (low + arrived[0]) + (arrived[1] + arrived[2])
    arrived = [trade(low, m, count) for m in range(4, count, 4)]
    base = project(2, x, weight)
    arrived, base = lax.optimization_barrier((arrived, base))
    send = update_values(column, query, key, base, adapter_up_maps.reshape(adapter_count * rank, -1), [low, *arrived])
    send, pool = lax.optimization_barrier((send, pool))
    keys, values = cache_by_head(pool, 0, heads)
    pieces = lax.all_to_all(send, "replica", split_axis=0, concat_axis=0, tiled=True)

    out = attend(cosine, sine, live, pieces, [keys], [values])
    return out.transpose(0, 2, 1, 3).reshape(steps, req_dev, width)


def per_device(replicas, *arrays):
    columns = arrays[1].shape[2]
    whole_heads = replicas % 4 == 0 and (2 * columns) % HD == 0 and columns % HD == HD // 2
    plan = chip_plan if whole_heads and arrays[0].shape[1] == 2 else general_plan
    return plan(replicas, *arrays)


def solution(mesh):
    placed = (
        P(None, ("groups", "replica"), None),
        P(None, None, "replica"),
        P("replica", None, None),
        P(None, None, "replica"),
        P(),
        P("groups"),
        P("groups"),
        P(("groups", "replica"), None),
        P(("groups", "replica"), None, None, None),
    )
    return jax.shard_map(
        functools.partial(per_device, mesh.shape["replica"]),
        mesh=mesh,
        in_specs=placed,
        out_specs=P(None, ("groups", "replica"), None),
        check_vma=False,
    )
```

```python
import functools

import jax
import jax.numpy as jnp
from jax import lax
from jax.experimental import pallas as pl
from jax.experimental.pallas import tpu as pltpu
from jax.sharding import PartitionSpec as P

HD = 128
ROWS = 8
HEAD_BLOCK = 8

adapter_scale = 2.0
masked_score = -1e30


def attention_kernel(steps, req_dev, q_ref, k_ref, v_ref, cos_ref, sin_ref, live_ref, kv_ref, out_ref, kn_ref, vn_ref):
    rows = steps * req_dev
    width = q_ref.shape[1]
    lanes = HEAD_BLOCK * HD
    group = rows * HEAD_BLOCK
    cosine = cos_ref[...]
    sine = sin_ref[...]

    def rotated(x):
        pieces = []
        for h in range(HEAD_BLOCK):
            head = x[:, h * HD : (h + 1) * HD]
            pieces.append(head * cosine + pltpu.roll(head, HD // 2, 1) * sine)
        return jnp.concatenate(pieces, axis=1)

    row_head = lax.broadcasted_iota(jnp.int32, (group, lanes), 0) % HEAD_BLOCK
    lane_head = lax.broadcasted_iota(jnp.int32, (group, lanes), 1) // HD
    own_head = row_head == lane_head
    row_j = lax.broadcasted_iota(jnp.int32, (group, 16), 0) // HEAD_BLOCK
    new_j = lax.broadcasted_iota(jnp.int32, (group, 16), 1)
    new_live = (new_j < rows) & (new_j % req_dev == row_j % req_dev) & (new_j // req_dev <= row_j // req_dev)
    live_all = live_ref[...]
    live = jnp.concatenate(
        [
            jnp.broadcast_to(live_all[j % req_dev : j % req_dev + 1], (HEAD_BLOCK, live_all.shape[1]))
            for j in range(rows)
        ],
        axis=0,
    )
    live = live > 0
    kn_ref[...] = jnp.zeros_like(kn_ref)
    vn_ref[...] = jnp.zeros_like(vn_ref)
    contract_lanes = (((1,), (1,)), ((), ()))
    for c in range(width // lanes):
        cols = slice(c * lanes, (c + 1) * lanes)
        query = rotated(q_ref[:, cols].astype(jnp.float32))
        key_new = rotated(k_ref[:, cols].astype(jnp.float32))
        kn_ref[0:8] = key_new
        vn_ref[0:8] = v_ref[:, cols].astype(jnp.float32)
        kn = kn_ref[...].astype(jnp.bfloat16)
        vn = vn_ref[...].astype(jnp.bfloat16)
        spread = jnp.concatenate(
            [jnp.broadcast_to(query[j : j + 1], (HEAD_BLOCK, lanes)) for j in range(rows)], axis=0
        )
        spread = jnp.where(own_head, spread, 0.0).astype(jnp.bfloat16)
        kv = kv_ref[:, cols]
        scores = lax.dot_general(spread, kv, contract_lanes, preferred_element_type=jnp.float32) * (HD**-0.5)
        scores = jnp.where(live, scores, masked_score)
        fresh = lax.dot_general(spread, kn, contract_lanes, preferred_element_type=jnp.float32) * (HD**-0.5)
        fresh = jnp.where(new_live, fresh, masked_score)
        top = jnp.maximum(jnp.max(scores, axis=1, keepdims=True), jnp.max(fresh, axis=1, keepdims=True))
        weights = jnp.where(live, jnp.exp(scores - top), 0.0)
        fresh = jnp.where(new_live, jnp.exp(fresh - top), 0.0)
        totals = jnp.sum(weights, axis=1, keepdims=True) + jnp.sum(fresh, axis=1, keepdims=True)
        weights = pltpu.roll(weights, 1, 1).astype(jnp.bfloat16)
        mixed = jnp.dot(weights, kv, preferred_element_type=jnp.float32)
        mixed = mixed + jnp.dot(fresh.astype(jnp.bfloat16), vn, preferred_element_type=jnp.float32)
        mixed = jnp.where(own_head, mixed / totals, 0.0)
        out = jnp.sum(mixed.reshape(rows, HEAD_BLOCK, lanes), axis=1)
        out_ref[:, cols] = out.astype(out_ref.dtype)


def attention(steps, req_dev, q, k, v, cosine, sine, live, kv):
    rows = steps * req_dev
    width = q.shape[1]
    vmem = pl.BlockSpec(memory_space=pltpu.VMEM)
    return pl.pallas_call(
        functools.partial(attention_kernel, steps, req_dev),
        out_shape=jax.ShapeDtypeStruct((rows, width), jnp.bfloat16),
        in_specs=[vmem] * 7,
        out_specs=vmem,
        scratch_shapes=[pltpu.VMEM((16, HEAD_BLOCK * HD), jnp.float32)] * 2,
        compiler_params=pltpu.CompilerParams(vmem_limit_bytes=32 * 2**20),
        cost_estimate=pl.CostEstimate(flops=10**9, bytes_accessed=6 * 10**6, transcendentals=0),
        name="attention",
    )(q, k, v, cosine, sine, live, kv)


def rotation(my_lengths, steps):
    rows = steps * my_lengths.shape[0]
    positions = (my_lengths[None, :] + jnp.arange(steps, dtype=jnp.int32)[:, None]).reshape(rows)
    positions = jnp.pad(positions, (0, ROWS - rows))
    half = HD // 2
    frequency = jnp.exp(jnp.arange(half, dtype=jnp.float32) * (-2.0 * jnp.log(10000.0) / HD))
    angles = positions.astype(jnp.float32)[:, None] * frequency[None, :]
    cosine = jnp.cos(angles)
    sine = jnp.sin(angles)
    cosine = jnp.concatenate([cosine, cosine], axis=1)
    sine = jnp.concatenate([-sine, sine], axis=1)
    return cosine, sine


def live_tokens(my_lengths, request_page_table, pool_pages, page_len):
    pages = jnp.arange(pool_pages, dtype=jnp.int32)
    max_pages = request_page_table.shape[1]
    place = jnp.max(
        jnp.where(
            request_page_table[:, :, None] == pages[None, None, :],
            jnp.arange(max_pages, dtype=jnp.int32)[None, :, None],
            -1,
        ),
        axis=1,
    )
    token = place[:, :, None] * page_len + jnp.arange(page_len, dtype=jnp.int32)[None, None, :]
    return (place[:, :, None] >= 0) & (token < my_lengths[:, None, None])


def live_rows(my_lengths, request_page_table, pool_pages, page_len):
    alive = live_tokens(my_lengths, request_page_table, pool_pages, page_len)
    live = jnp.stack([alive, jnp.zeros_like(alive)], axis=-1).astype(jnp.int32)
    return live.reshape(request_page_table.shape[0], pool_pages * page_len * 2)


def general_plan(
    replicas,
    hidden,
    query_key_value_weight,
    adapter_down_maps,
    adapter_up_maps,
    adapter_storage_row,
    request_adapter,
    lengths,
    request_page_table,
    key_value_pool,
):
    my_index = lax.axis_index("replica")
    steps, req_dev, width = hidden.shape
    rows = steps * req_dev
    columns = query_key_value_weight.shape[2]
    holder_count, rank, _ = adapter_down_maps.shape
    pool_pages, page_len = key_value_pool.shape[:2]
    adapter_count = adapter_storage_row.shape[0]
    chips = replicas // 2
    total = replicas * ROWS

    block = jnp.pad(hidden.reshape(rows, width), ((0, ROWS - rows), (0, 0)))
    same_core = [[2 * chip + core for chip in range(chips)] for core in range(2)]
    mine = lax.all_to_all(
        jnp.broadcast_to(block[None], (chips, ROWS, width)),
        "replica",
        split_axis=0,
        concat_axis=0,
        axis_index_groups=same_core,
        tiled=True,
    )
    other = lax.ppermute(mine, "replica", [(i, i ^ 1) for i in range(replicas)])
    first = my_index % 2 == 0
    gathered = jnp.stack([jnp.where(first, mine, other), jnp.where(first, other, mine)])
    gathered = gathered.reshape(total, width)

    stored_rows = jnp.sum(
        jnp.where(
            request_adapter[:, None] == jnp.arange(adapter_count, dtype=jnp.int32)[None, :],
            adapter_storage_row[None, :],
            0,
        ),
        axis=1,
    )
    by_block = stored_rows.reshape(chips, 2, 1, req_dev).transpose(1, 0, 2, 3)
    by_block = jnp.broadcast_to(by_block, (2, chips, steps, req_dev)).reshape(2, chips, rows)
    row_stored = jnp.pad(by_block, ((0, 0), (0, 0), (0, ROWS - rows)), constant_values=-1).reshape(total)

    down = jnp.einsum("nd,hfd->nhf", gathered, adapter_down_maps, preferred_element_type=jnp.float32)
    slots = my_index * holder_count + jnp.arange(holder_count, dtype=jnp.int32)
    own = row_stored[:, None] == slots[None, :]
    low = jnp.sum(jnp.where(own[:, :, None], down, 0.0), axis=1).astype(jnp.bfloat16)
    low = jnp.concatenate([low[: total // 2], low[total // 2 :]], axis=1)
    low = lax.all_to_all(
        jnp.broadcast_to(low[None], (replicas,) + low.shape), "replica", split_axis=0, concat_axis=0, tiled=True
    )
    low = jnp.sum(low.astype(jnp.float32), axis=0)
    low = jnp.concatenate([low[:, :rank], low[:, rank:]], axis=0)

    projected = jnp.einsum("nd,idc->nic", gathered, query_key_value_weight, preferred_element_type=jnp.float32)

    def update(first_adapter, maps):
        held = maps.shape[0]
        which = first_adapter + jnp.arange(held, dtype=jnp.int32)
        wide = jnp.where((row_stored[:, None] == which[None, :])[:, :, None], low[:, None, :], 0.0)
        return jnp.dot(
            wide.astype(jnp.bfloat16).reshape(total, held * rank),
            maps.reshape(held * rank, columns),
            preferred_element_type=jnp.float32,
        )

    step_adapters = 64
    if adapter_count <= step_adapters:
        updated = update(0, adapter_up_maps)
    else:
        updated = lax.fori_loop(
            0,
            adapter_count // step_adapters,
            lambda i, sofar: sofar
            + update(
                i * step_adapters,
                lax.dynamic_slice_in_dim(adapter_up_maps, i * step_adapters, step_adapters, 0),
            ),
            jnp.zeros((total, columns), jnp.float32),
        )
    value = projected[:, 2] + adapter_scale * updated
    combined = jnp.concatenate([projected[:, 0], projected[:, 1], value], axis=1).astype(jnp.bfloat16)
    combined = combined.reshape(2, chips, ROWS, 3 * columns).transpose(1, 0, 2, 3)
    combined = combined.reshape(replicas, ROWS, 3 * columns)
    arrived = lax.all_to_all(combined, "replica", split_axis=0, concat_axis=0, tiled=True)
    arrived = arrived.reshape(replicas, ROWS, 3, columns).transpose(2, 1, 0, 3).reshape(3, ROWS, width)

    my_lengths = lax.dynamic_slice_in_dim(lengths, my_index * req_dev, req_dev)
    cosine, sine = rotation(my_lengths, steps)
    live = live_rows(my_lengths, request_page_table, pool_pages, page_len)
    kv = key_value_pool.reshape(pool_pages * page_len * 2, width)
    out = attention(steps, req_dev, arrived[0], arrived[1], arrived[2], cosine, sine, live, kv)
    return out.reshape(steps, req_dev, width)


def rotation_rows(lengths, first, req_dev, steps):
    row = jnp.arange(ROWS, dtype=jnp.int32)
    wanted = first + row % req_dev
    chosen = jnp.where(wanted[:, None] == jnp.arange(lengths.shape[0], dtype=jnp.int32)[None, :], lengths[None, :], 0)
    positions = jnp.sum(chosen, axis=1, keepdims=True) + (row // req_dev)[:, None]
    lane = jnp.arange(HD, dtype=jnp.int32)
    frequency = jnp.exp((lane % (HD // 2)).astype(jnp.float32) * (-2.0 * jnp.log(10000.0) / HD))
    angles = positions.astype(jnp.float32) * frequency[None, :]
    return jnp.cos(angles), jnp.where(lane < HD // 2, -1.0, 1.0)[None, :] * jnp.sin(angles)


def live_lanes(lengths, first, request_page_table, tokens, page_len):
    req_dev, max_pages = request_page_table.shape
    wanted = first + jnp.arange(req_dev, dtype=jnp.int32)
    chosen = jnp.where(wanted[:, None] == jnp.arange(lengths.shape[0], dtype=jnp.int32)[None, :], lengths[None, :], 0)
    lane = jnp.arange(tokens, dtype=jnp.int32)
    page = jnp.arange(max_pages, dtype=jnp.int32)
    place = jnp.max(
        jnp.where(request_page_table[:, :, None] == (lane // page_len)[None, None, :], page[None, :, None], -1),
        axis=1,
    )
    token = place * page_len + (lane % page_len)[None, :]
    return ((place >= 0) & (token < jnp.sum(chosen, axis=1, keepdims=True))).astype(jnp.int32)


def trade(value, mask, count):
    return lax.ppermute(value, "replica", [(i, i ^ mask) for i in range(count)])


CONTRACT_LANES = (((1,), (1,)), ((), ()))


def in_hbm(x):
    return pltpu.with_memory_space_constraint(x, pltpu.HBM)


VMEM = pl.BlockSpec(memory_space=pltpu.VMEM)
HBM = pl.BlockSpec(memory_space=pltpu.HBM)
SMEM = pl.BlockSpec(memory_space=pltpu.SMEM)
ANY = pl.BlockSpec(memory_space=pl.ANY)


def start_all(copies):
    for copy in copies:
        copy.start()
    return copies


def wait_all(copies):
    for copy in copies:
        copy.wait()


CACHE_SECTION = 10
CACHE_AHEAD = 4
CACHE_TOKENS = 128


def cache_kernel(first, pool_ref, keys_ref, values_ref, raw, values, sem, out_sem):
    heads, tokens = raw.shape[:2]
    copies = [pltpu.make_async_copy(pool_ref.at[:, first + h], raw.at[h], sem.at[h]) for h in range(heads)]
    start_all(copies[: CACHE_AHEAD * CACHE_SECTION])
    rows = raw.reshape(heads, 2 * tokens, HD)
    block = min(tokens, CACHE_TOKENS)
    to = lax.broadcasted_iota(jnp.int32, (2 * block, 2 * block), 0)
    source = lax.broadcasted_iota(jnp.int32, (2 * block, 2 * block), 1)
    wanted = jnp.where(to < block, 2 * to, 2 * (to - block) + 1)
    pick = jnp.where(source == wanted, 1.0, 0.0).astype(jnp.bfloat16)
    sent = []
    part = CACHE_SECTION
    for p in range(heads // part):
        wait_all(copies[p * part : (p + 1) * part])
        start_all(copies[(p + CACHE_AHEAD) * part : (p + CACHE_AHEAD + 1) * part])
        for h in range(p * part, (p + 1) * part, 2):
            for first_token in range(0, tokens, block):
                raw_rows = slice(2 * first_token, 2 * (first_token + block))
                both = jnp.concatenate([rows[h, raw_rows], rows[h + 1, raw_rows]], axis=1)
                made = jnp.dot(pick, both, preferred_element_type=jnp.float32).astype(jnp.bfloat16)
                span = slice(first_token, first_token + block)
                for i in range(2):
                    keys_ref[h + i, span] = made[:block, i * HD : (i + 1) * HD]
                    values[h + i, span] = made[block:, i * HD : (i + 1) * HD]
        span = slice(p * part, (p + 1) * part)
        sent += start_all([pltpu.make_async_copy(values.at[span], values_ref.at[span], out_sem.at[p])])
    wait_all(sent)


def cache_by_head(pool, first, heads):
    tokens = pool.shape[0]
    return pl.pallas_call(
        functools.partial(cache_kernel, first),
        out_shape=(
            jax.ShapeDtypeStruct((heads, tokens, HD), pool.dtype),
            pltpu.HBM((heads, tokens, HD), pool.dtype),
        ),
        in_specs=[HBM],
        out_specs=(VMEM, HBM),
        scratch_shapes=[
            pltpu.VMEM((heads, tokens, 2, HD), pool.dtype),
            pltpu.VMEM((heads, tokens, HD), pool.dtype),
            pltpu.SemaphoreType.DMA((heads,)),
            pltpu.SemaphoreType.DMA((heads // CACHE_SECTION,)),
        ],
        compiler_params=pltpu.CompilerParams(vmem_limit_bytes=12 * 2**20),
        cost_estimate=pl.CostEstimate(flops=0, bytes_accessed=12 * 10**6, transcendentals=0),
        name="cache_by_head",
    )(in_hbm(pool))


def lanes_of(x):
    return jnp.concatenate([x[c] for c in range(x.shape[0])], axis=1)


def step_rows(x, first, chunks):
    steps, _, count = x.shape[:3]
    flat = x.reshape(steps, x.shape[1], 2 * count, HD)
    return jnp.concatenate(
        [jnp.concatenate([flat[t, c] for c in range(first, first + chunks)], axis=1) for t in range(steps)], axis=0
    )


def index_kernel(me_ref, stored_ref, slot_ref, column_ref):
    requests = stored_ref.shape[1]
    steps = slot_ref.shape[1] // requests
    row = jnp.concatenate([stored_ref[...]] * steps, axis=1)
    slot_ref[...] = row - me_ref[0]
    wide = jnp.concatenate([row, jnp.zeros((1, HD - row.shape[1]), row.dtype)], axis=1)
    column_ref[...] = jnp.broadcast_to(wide.astype(jnp.float32), (HD, HD)).T[: row.shape[1], :1].astype(jnp.int32)


def index_work(first, stored, steps):
    rows = stored.shape[0] * steps
    return pl.pallas_call(
        index_kernel,
        out_shape=(jax.ShapeDtypeStruct((1, rows), jnp.int32), jax.ShapeDtypeStruct((rows, 1), jnp.int32)),
        in_specs=[SMEM, VMEM],
        out_specs=(VMEM, VMEM),
        compiler_params=pltpu.CompilerParams(vmem_limit_bytes=2 * 2**20),
        cost_estimate=pl.CostEstimate(flops=2 * 10**10, bytes_accessed=10**4, transcendentals=0),
        name="index_work",
    )(first, stored[None, :])


def low_kernel(count, me_ref, slot_ref, down_ref, *refs):
    blocks, (x_ref, low_ref, sem) = refs[:count], refs[count:]
    me = me_ref[0]
    holders, rank, width = down_ref.shape
    wait_all(
        start_all(
            [pltpu.make_async_copy(block, x_ref.at[:, :, me ^ k], sem.at[k]) for k, block in enumerate(blocks)]
        )
    )
    x = step_rows(x_ref, 0, x_ref.shape[1])
    rows = x.shape[0]
    made = lax.dot_general(
        down_ref.reshape(holders * rank, width)[...], x, CONTRACT_LANES, preferred_element_type=jnp.float32
    )
    slot = slot_ref[...]
    low = jnp.zeros((rank, rows), jnp.float32)
    for h in range(holders):
        low = low + jnp.where(slot == h, made[h * rank : (h + 1) * rank], 0.0)
    low = low.T
    low_ref[...] = jnp.concatenate([low[: rows // 2], low[rows // 2 :]], axis=1).astype(low_ref.dtype)


def low_of(me, blocks, slot, down):
    count = len(blocks)
    steps, chunks = blocks[0].shape[:2]
    rows = count * steps * 2
    rank = down.shape[1]
    return pl.pallas_call(
        functools.partial(low_kernel, count),
        out_shape=(
            jax.ShapeDtypeStruct((steps, chunks, count, 2, HD), jnp.bfloat16),
            jax.ShapeDtypeStruct((rows // 2, 2 * rank), jnp.bfloat16),
        ),
        in_specs=[SMEM, VMEM, VMEM] + [ANY] * count,
        out_specs=(VMEM, VMEM),
        scratch_shapes=[pltpu.SemaphoreType.DMA((count,))],
        compiler_params=pltpu.CompilerParams(vmem_limit_bytes=12 * 2**20),
        cost_estimate=pl.CostEstimate(flops=10**8, bytes_accessed=4 * 10**6, transcendentals=0),
        name="low_rows",
    )(me, slot, down, *blocks)


def put_chunks(buf, first, value):
    steps, count = buf.shape[1:3]
    flat = buf.reshape(buf.shape[0], steps, 2 * count, HD)
    wide = value.shape[1]
    for c in range(-(-wide // HD)):
        part = value[:, c * HD : min((c + 1) * HD, wide)]
        if part.shape[1] < HD:
            part = jnp.concatenate([part, jnp.zeros((part.shape[0], HD - part.shape[1]), part.dtype)], axis=1)
        part = part.astype(buf.dtype)
        for t in range(steps):
            flat[first + c, t] = part[t * 2 * count : (t + 1) * 2 * count]


def project_kernel(which, x_ref, w_ref, out_ref):
    x = step_rows(x_ref, 0, x_ref.shape[1])
    made = lax.dot_general(w_ref[which], x, CONTRACT_LANES, preferred_element_type=jnp.float32).T
    if which < 2:
        pad = jnp.zeros((made.shape[0], HD // 2), made.dtype)
        put_chunks(out_ref, 0, jnp.concatenate([made, pad] if which == 0 else [pad, made], axis=1))
    else:
        out_ref[...] = made


def project(which, x, weight):
    steps, _, count = x.shape[:3]
    columns = weight.shape[1]
    chunks = jax.ShapeDtypeStruct((-(-columns // HD), steps, count, 2, HD), jnp.bfloat16)
    base = jax.ShapeDtypeStruct((2 * steps * count, columns), jnp.float32)
    return pl.pallas_call(
        functools.partial(project_kernel, which),
        out_shape=chunks if which < 2 else base,
        in_specs=[VMEM, VMEM],
        out_specs=VMEM,
        compiler_params=pltpu.CompilerParams(vmem_limit_bytes=16 * 2**20),
        cost_estimate=pl.CostEstimate(flops=5 * 10**8, bytes_accessed=4 * 10**6, transcendentals=0),
        name="project",
    )(x, weight)


def update_kernel(stored_ref, query_ref, key_ref, base_ref, up_ref, *refs):
    lows, (send_ref, buf, sem) = refs[:-3], refs[-3:]
    half, packed = lows[0].shape
    rank = packed // 2
    rows = 2 * half
    count = send_ref.shape[0]
    low = lows[0][...].astype(jnp.float32)
    for more in lows[1:]:
        low = low + more[...].astype(jnp.float32)
    low = jnp.concatenate([low[:, :rank], low[:, rank:]], axis=0)
    batch = 256 // rank
    spread = jnp.concatenate([low] * batch, axis=1)
    ahead = stored_ref[...] - lax.broadcasted_iota(jnp.int32, (rows, batch * rank), 1) // rank
    total = jnp.zeros(base_ref.shape, jnp.float32)
    for a in range(0, up_ref.shape[0] // rank, batch):
        wide = jnp.where(ahead == a, spread, 0.0).astype(jnp.bfloat16)
        total = total + jnp.dot(wide, up_ref[a * rank : (a + batch) * rank], preferred_element_type=jnp.float32)
    each = query_ref.shape[0]
    buf[: each - 1] = query_ref[: each - 1]
    buf[each - 1] = query_ref[each - 1] + key_ref[0]
    buf[each : 2 * each - 1] = key_ref[1:]
    put_chunks(buf, 2 * each - 1, base_ref[...] + adapter_scale * total)
    wait_all(
        start_all([pltpu.make_async_copy(buf.at[:, :, k], send_ref.at[k], sem.at[k]) for k in range(count)])
    )


def update_values(stored, query, key, base, up, lows):
    chunks, steps, count = query.shape[:3]
    return pl.pallas_call(
        update_kernel,
        out_shape=pltpu.HBM((count, 3 * chunks - 1, steps, 2, HD), query.dtype),
        in_specs=[VMEM] * (5 + len(lows)),
        out_specs=HBM,
        scratch_shapes=[
            pltpu.VMEM((3 * chunks - 1, steps, count, 2, HD), query.dtype),
            pltpu.SemaphoreType.DMA((count,)),
        ],
        compiler_params=pltpu.CompilerParams(vmem_limit_bytes=8 * 2**20),
        cost_estimate=pl.CostEstimate(flops=3 * 10**8, bytes_accessed=4 * 10**6, transcendentals=0),
        name="update_values",
    )(stored, query, key, base, up, *lows)


def attend_kernel(cos_ref, sin_ref, live_ref, pieces_ref, *refs):
    *parts, out_ref, values_buf, kn_ref, vn_ref, sem = refs
    keys_refs, values_refs = parts[: len(parts) // 2], parts[len(parts) // 2 :]
    count, _, steps = pieces_ref.shape[:3]
    rows = 2 * steps
    each = (pieces_ref.shape[1] + 1) // 3
    heads = 2 * out_ref.shape[1] // count
    lanes = heads * HD
    group = rows * HEAD_BLOCK
    chips = range(count // 2)
    early = keys_refs[0].shape[0] // heads
    places = [(0, c) if c < early else (1, c - early) for c in chips]
    fetches = start_all(
        [
            pltpu.make_async_copy(values_refs[half].at[at * heads : (at + 1) * heads], values_buf.at[c], sem.at[c])
            for c, (half, at) in enumerate(places)
        ]
    )
    cosine = cos_ref[...][:rows]
    sine = sin_ref[...][:rows]
    left = lax.broadcasted_iota(jnp.int32, (rows, HD), 1) < HD // 2

    def halves(chip, at):
        return [
            [pieces_ref[2 * chip + core, at + c].reshape(rows, HD).astype(jnp.float32) for c in range(each)]
            for core in range(2)
        ]

    def swapped(parts):
        return [pltpu.roll(x, HD // 2, 1) for x in parts]

    def joined(parts):
        return [jnp.where(left, a, b) for a, b in zip(parts[:-1], parts[1:])]

    def chip_columns(chip, at):
        low, high = halves(chip, at)
        high = swapped(high)
        return low[:-1] + [jnp.where(left, low[-1], high[0])] + joined(high)

    def chip_keys(chip):
        low, high = halves(chip, each - 1)
        low = swapped(low)
        return joined(low) + [jnp.where(left, low[-1], high[0])] + high[1:]

    def rotated(parts):
        return [x * cosine + pltpu.roll(x, HD // 2, 1) * sine for x in parts]

    row_head = lax.broadcasted_iota(jnp.int32, (group, lanes), 0) % HEAD_BLOCK
    lane_head = lax.broadcasted_iota(jnp.int32, (group, lanes), 1) // HD
    own_head = row_head == lane_head
    row_j = lax.broadcasted_iota(jnp.int32, (group, 16), 0) // HEAD_BLOCK
    new_j = lax.broadcasted_iota(jnp.int32, (group, 16), 1)
    new_live = (new_j < rows) & (new_j % 2 == row_j % 2) & (new_j // 2 <= row_j // 2)
    live = jnp.concatenate(
        [
            jnp.broadcast_to(live_ref[j % 2 : j % 2 + 1, :], (HEAD_BLOCK, live_ref.shape[1]))
            for j in range(rows)
        ],
        axis=0,
    )
    live = live > 0
    kn_ref[...] = jnp.zeros_like(kn_ref)
    vn_ref[...] = jnp.zeros_like(vn_ref)
    spreads = []
    for c in chips:
        query = jnp.concatenate(rotated(chip_columns(c, 0)), axis=1)
        kn_ref[c, 0:rows] = jnp.concatenate(rotated(chip_keys(c)), axis=1)
        vn_ref[c, 0:rows] = jnp.concatenate(chip_columns(c, 2 * each - 1), axis=1)
        spread = jnp.concatenate(
            [jnp.broadcast_to(query[j : j + 1], (HEAD_BLOCK, lanes)) for j in range(rows)], axis=0
        )
        spreads.append(jnp.where(own_head, spread, 0.0).astype(jnp.bfloat16))
    scores, fresh = [], []
    for c in chips:
        half, at = places[c]
        keys = jnp.concatenate([keys_refs[half][at * heads + h] for h in range(heads)], axis=1)
        kn = kn_ref[c].astype(jnp.bfloat16)
        scores.append(lax.dot_general(spreads[c], keys, CONTRACT_LANES, preferred_element_type=jnp.float32))
        fresh.append(lax.dot_general(spreads[c], kn, CONTRACT_LANES, preferred_element_type=jnp.float32))
    weights, fresh_weights, totals = [], [], []
    for c in chips:
        old = jnp.where(live, scores[c] * (HD**-0.5), masked_score)
        new = jnp.where(new_live, fresh[c] * (HD**-0.5), masked_score)
        top = jnp.maximum(jnp.max(old, axis=1, keepdims=True), jnp.max(new, axis=1, keepdims=True))
        old = jnp.where(live, jnp.exp(old - top), 0.0)
        new = jnp.where(new_live, jnp.exp(new - top), 0.0)
        totals.append(jnp.sum(old, axis=1, keepdims=True) + jnp.sum(new, axis=1, keepdims=True))
        weights.append(old.astype(jnp.bfloat16))
        fresh_weights.append(new.astype(jnp.bfloat16))
    wait_all(fetches)
    for c in chips:
        values = lanes_of(values_buf[c])
        vn = vn_ref[c].astype(jnp.bfloat16)
        mixed = jnp.dot(weights[c], values, preferred_element_type=jnp.float32)
        mixed = mixed + jnp.dot(fresh_weights[c], vn, preferred_element_type=jnp.float32)
        mixed = jnp.where(own_head, mixed / totals[c], 0.0)
        out = jnp.sum(mixed.reshape(rows, HEAD_BLOCK, lanes), axis=1).astype(out_ref.dtype)
        for t in range(steps):
            for h in range(heads):
                out_ref[t, c * heads + h] = out[2 * t : 2 * t + 2, h * HD : (h + 1) * HD]


def attend(cosine, sine, live, pieces, keys, values):
    count, _, steps = pieces.shape[:3]
    heads, tokens = sum(x.shape[0] for x in keys), keys[0].shape[1]
    chips = count // 2
    per = heads // chips
    return pl.pallas_call(
        attend_kernel,
        out_shape=jax.ShapeDtypeStruct((steps, heads, 2, HD), jnp.bfloat16),
        in_specs=[VMEM] * (4 + len(keys)) + [HBM] * len(values),
        out_specs=VMEM,
        scratch_shapes=[pltpu.VMEM((chips, per, tokens, HD), jnp.bfloat16)]
        + [pltpu.VMEM((chips, 16, per * HD), jnp.float32)] * 2
        + [pltpu.SemaphoreType.DMA((chips,))],
        compiler_params=pltpu.CompilerParams(vmem_limit_bytes=16 * 2**20),
        cost_estimate=pl.CostEstimate(flops=10**9, bytes_accessed=6 * 10**6, transcendentals=0),
        name="attention",
    )(cosine, sine, live, pieces, *keys, *[in_hbm(x) for x in values])


def chip_plan(
    count,
    hidden,
    query_key_value_weight,
    adapter_down_maps,
    adapter_up_maps,
    adapter_storage_row,
    request_adapter,
    lengths,
    request_page_table,
    key_value_pool,
):
    me = lax.axis_index("replica")
    steps, req_dev, width = hidden.shape
    heads = width // HD
    holder_count, rank, _ = adapter_down_maps.shape
    pool_pages, page_len = key_value_pool.shape[:2]
    adapter_count = adapter_storage_row.shape[0]

    tokens = pool_pages * page_len
    pool = key_value_pool.reshape(tokens, 2, heads, HD).transpose(0, 2, 1, 3)

    stored = jnp.sum(
        jnp.where(
            request_adapter[:, None] == jnp.arange(adapter_count, dtype=jnp.int32)[None, :],
            adapter_storage_row[None, :],
            0,
        ),
        axis=1,
    )
    first, slots, here, stored = lax.optimization_barrier(
        (me * req_dev, (me * holder_count).astype(jnp.int32).reshape(1), me.astype(jnp.int32).reshape(1), stored)
    )
    slot, column = index_work(slots, stored, steps)

    held = {0: hidden}
    held.update({m: trade(hidden, m, count) for m in range(4, count, 4)})
    _, lengths, request_page_table = lax.optimization_barrier((held[4], lengths, request_page_table))
    cosine, sine = rotation_rows(lengths, first, req_dev, steps)
    live = live_lanes(lengths, first, request_page_table, tokens, page_len)
    held.update({k | 2: trade(v, 2, count) for k, v in list(held.items())})
    ready = [0, 2, 4, 6]
    held.update(zip(ready, lax.optimization_barrier([held[k] for k in ready])))
    held.update({k | 1: trade(v, 1, count) for k, v in list(held.items())})
    blocks = [held[k].reshape(steps, req_dev, heads, HD).transpose(0, 2, 1, 3) for k in range(count)]
    blocks[0] = in_hbm(blocks[0])
    x, low = low_of(here, blocks, slot, adapter_down_maps)
    weight = query_key_value_weight.transpose(0, 2, 1)
    arrived = [trade(low, m, count) for m in (1, 2, 3)]
    query, key = project(0, x, weight), project(1, x, weight)
    arrived, query, key, pool = lax.optimization_barrier((arrived, query, key, pool))
    low = (low + arrived[0]) + (arrived[1] + arrived[2])
    arrived = [trade(low, m, count) for m in range(4, count, 4)]
    base = project(2, x, weight)
    arrived, base = lax.optimization_barrier((arrived, base))
    send = update_values(column, query, key, base, adapter_up_maps.reshape(adapter_count * rank, -1), [low, *arrived])
    send, pool = lax.optimization_barrier((send, pool))
    keys, values = cache_by_head(pool, 0, heads)
    pieces = lax.all_to_all(send, "replica", split_axis=0, concat_axis=0, tiled=True)

    out = attend(cosine, sine, live, pieces, [keys], [values])
    return out.transpose(0, 2, 1, 3).reshape(steps, req_dev, width)


def per_device(replicas, *arrays):
    columns = arrays[1].shape[2]
    whole_heads = replicas % 4 == 0 and (2 * columns) % HD == 0 and columns % HD == HD // 2
    plan = chip_plan if whole_heads and arrays[0].shape[1] == 2 else general_plan
    return plan(replicas, *arrays)


def solution(mesh):
    placed = (
        P(None, ("groups", "replica"), None),
        P(None, None, "replica"),
        P("replica", None, None),
        P(None, None, "replica"),
        P(),
        P("groups"),
        P("groups"),
        P(("groups", "replica"), None),
        P(("groups", "replica"), None, None, None),
    )
    return jax.shard_map(
        functools.partial(per_device, mesh.shape["replica"]),
        mesh=mesh,
        in_specs=placed,
        out_specs=P(None, ("groups", "replica"), None),
        check_vma=False,
    )
```

```python
import functools

import jax
import jax.numpy as jnp
from jax import lax
from jax.experimental import pallas as pl
from jax.experimental.pallas import tpu as pltpu
from jax.sharding import PartitionSpec as P

HD = 128
ROWS = 8
HEAD_BLOCK = 8

adapter_scale = 2.0
masked_score = -1e30


def attention_kernel(steps, req_dev, q_ref, k_ref, v_ref, cos_ref, sin_ref, live_ref, kv_ref, out_ref, kn_ref, vn_ref):
    rows = steps * req_dev
    width = q_ref.shape[1]
    lanes = HEAD_BLOCK * HD
    group = rows * HEAD_BLOCK
    cosine = cos_ref[...]
    sine = sin_ref[...]

    def rotated(x):
        pieces = []
        for h in range(HEAD_BLOCK):
            head = x[:, h * HD : (h + 1) * HD]
            pieces.append(head * cosine + pltpu.roll(head, HD // 2, 1) * sine)
        return jnp.concatenate(pieces, axis=1)

    row_head = lax.broadcasted_iota(jnp.int32, (group, lanes), 0) % HEAD_BLOCK
    lane_head = lax.broadcasted_iota(jnp.int32, (group, lanes), 1) // HD
    own_head = row_head == lane_head
    row_j = lax.broadcasted_iota(jnp.int32, (group, 16), 0) // HEAD_BLOCK
    new_j = lax.broadcasted_iota(jnp.int32, (group, 16), 1)
    new_live = (new_j < rows) & (new_j % req_dev == row_j % req_dev) & (new_j // req_dev <= row_j // req_dev)
    live_all = live_ref[...]
    live = jnp.concatenate(
        [
            jnp.broadcast_to(live_all[j % req_dev : j % req_dev + 1], (HEAD_BLOCK, live_all.shape[1]))
            for j in range(rows)
        ],
        axis=0,
    )
    live = live > 0
    kn_ref[...] = jnp.zeros_like(kn_ref)
    vn_ref[...] = jnp.zeros_like(vn_ref)
    contract_lanes = (((1,), (1,)), ((), ()))
    for c in range(width // lanes):
        cols = slice(c * lanes, (c + 1) * lanes)
        query = rotated(q_ref[:, cols].astype(jnp.float32))
        key_new = rotated(k_ref[:, cols].astype(jnp.float32))
        kn_ref[0:8] = key_new
        vn_ref[0:8] = v_ref[:, cols].astype(jnp.float32)
        kn = kn_ref[...].astype(jnp.bfloat16)
        vn = vn_ref[...].astype(jnp.bfloat16)
        spread = jnp.concatenate(
            [jnp.broadcast_to(query[j : j + 1], (HEAD_BLOCK, lanes)) for j in range(rows)], axis=0
        )
        spread = jnp.where(own_head, spread, 0.0).astype(jnp.bfloat16)
        kv = kv_ref[:, cols]
        scores = lax.dot_general(spread, kv, contract_lanes, preferred_element_type=jnp.float32) * (HD**-0.5)
        scores = jnp.where(live, scores, masked_score)
        fresh = lax.dot_general(spread, kn, contract_lanes, preferred_element_type=jnp.float32) * (HD**-0.5)
        fresh = jnp.where(new_live, fresh, masked_score)
        top = jnp.maximum(jnp.max(scores, axis=1, keepdims=True), jnp.max(fresh, axis=1, keepdims=True))
        weights = jnp.where(live, jnp.exp(scores - top), 0.0)
        fresh = jnp.where(new_live, jnp.exp(fresh - top), 0.0)
        totals = jnp.sum(weights, axis=1, keepdims=True) + jnp.sum(fresh, axis=1, keepdims=True)
        weights = pltpu.roll(weights, 1, 1).astype(jnp.bfloat16)
        mixed = jnp.dot(weights, kv, preferred_element_type=jnp.float32)
        mixed = mixed + jnp.dot(fresh.astype(jnp.bfloat16), vn, preferred_element_type=jnp.float32)
        mixed = jnp.where(own_head, mixed / totals, 0.0)
        out = jnp.sum(mixed.reshape(rows, HEAD_BLOCK, lanes), axis=1)
        out_ref[:, cols] = out.astype(out_ref.dtype)


def attention(steps, req_dev, q, k, v, cosine, sine, live, kv):
    rows = steps * req_dev
    width = q.shape[1]
    vmem = pl.BlockSpec(memory_space=pltpu.VMEM)
    return pl.pallas_call(
        functools.partial(attention_kernel, steps, req_dev),
        out_shape=jax.ShapeDtypeStruct((rows, width), jnp.bfloat16),
        in_specs=[vmem] * 7,
        out_specs=vmem,
        scratch_shapes=[pltpu.VMEM((16, HEAD_BLOCK * HD), jnp.float32)] * 2,
        compiler_params=pltpu.CompilerParams(vmem_limit_bytes=32 * 2**20),
        cost_estimate=pl.CostEstimate(flops=10**9, bytes_accessed=6 * 10**6, transcendentals=0),
        name="attention",
    )(q, k, v, cosine, sine, live, kv)


def rotation(my_lengths, steps):
    rows = steps * my_lengths.shape[0]
    positions = (my_lengths[None, :] + jnp.arange(steps, dtype=jnp.int32)[:, None]).reshape(rows)
    positions = jnp.pad(positions, (0, ROWS - rows))
    half = HD // 2
    frequency = jnp.exp(jnp.arange(half, dtype=jnp.float32) * (-2.0 * jnp.log(10000.0) / HD))
    angles = positions.astype(jnp.float32)[:, None] * frequency[None, :]
    cosine = jnp.cos(angles)
    sine = jnp.sin(angles)
    cosine = jnp.concatenate([cosine, cosine], axis=1)
    sine = jnp.concatenate([-sine, sine], axis=1)
    return cosine, sine


def live_tokens(my_lengths, request_page_table, pool_pages, page_len):
    pages = jnp.arange(pool_pages, dtype=jnp.int32)
    max_pages = request_page_table.shape[1]
    place = jnp.max(
        jnp.where(
            request_page_table[:, :, None] == pages[None, None, :],
            jnp.arange(max_pages, dtype=jnp.int32)[None, :, None],
            -1,
        ),
        axis=1,
    )
    token = place[:, :, None] * page_len + jnp.arange(page_len, dtype=jnp.int32)[None, None, :]
    return (place[:, :, None] >= 0) & (token < my_lengths[:, None, None])


def live_rows(my_lengths, request_page_table, pool_pages, page_len):
    alive = live_tokens(my_lengths, request_page_table, pool_pages, page_len)
    live = jnp.stack([alive, jnp.zeros_like(alive)], axis=-1).astype(jnp.int32)
    return live.reshape(request_page_table.shape[0], pool_pages * page_len * 2)


def general_plan(
    replicas,
    hidden,
    query_key_value_weight,
    adapter_down_maps,
    adapter_up_maps,
    adapter_storage_row,
    request_adapter,
    lengths,
    request_page_table,
    key_value_pool,
):
    my_index = lax.axis_index("replica")
    steps, req_dev, width = hidden.shape
    rows = steps * req_dev
    columns = query_key_value_weight.shape[2]
    holder_count, rank, _ = adapter_down_maps.shape
    pool_pages, page_len = key_value_pool.shape[:2]
    adapter_count = adapter_storage_row.shape[0]
    chips = replicas // 2
    total = replicas * ROWS

    block = jnp.pad(hidden.reshape(rows, width), ((0, ROWS - rows), (0, 0)))
    same_core = [[2 * chip + core for chip in range(chips)] for core in range(2)]
    mine = lax.all_to_all(
        jnp.broadcast_to(block[None], (chips, ROWS, width)),
        "replica",
        split_axis=0,
        concat_axis=0,
        axis_index_groups=same_core,
        tiled=True,
    )
    other = lax.ppermute(mine, "replica", [(i, i ^ 1) for i in range(replicas)])
    first = my_index % 2 == 0
    gathered = jnp.stack([jnp.where(first, mine, other), jnp.where(first, other, mine)])
    gathered = gathered.reshape(total, width)

    stored_rows = jnp.sum(
        jnp.where(
            request_adapter[:, None] == jnp.arange(adapter_count, dtype=jnp.int32)[None, :],
            adapter_storage_row[None, :],
            0,
        ),
        axis=1,
    )
    by_block = stored_rows.reshape(chips, 2, 1, req_dev).transpose(1, 0, 2, 3)
    by_block = jnp.broadcast_to(by_block, (2, chips, steps, req_dev)).reshape(2, chips, rows)
    row_stored = jnp.pad(by_block, ((0, 0), (0, 0), (0, ROWS - rows)), constant_values=-1).reshape(total)

    down = jnp.einsum("nd,hfd->nhf", gathered, adapter_down_maps, preferred_element_type=jnp.float32)
    slots = my_index * holder_count + jnp.arange(holder_count, dtype=jnp.int32)
    own = row_stored[:, None] == slots[None, :]
    low = jnp.sum(jnp.where(own[:, :, None], down, 0.0), axis=1).astype(jnp.bfloat16)
    low = jnp.concatenate([low[: total // 2], low[total // 2 :]], axis=1)
    low = lax.all_to_all(
        jnp.broadcast_to(low[None], (replicas,) + low.shape), "replica", split_axis=0, concat_axis=0, tiled=True
    )
    low = jnp.sum(low.astype(jnp.float32), axis=0)
    low = jnp.concatenate([low[:, :rank], low[:, rank:]], axis=0)

    projected = jnp.einsum("nd,idc->nic", gathered, query_key_value_weight, preferred_element_type=jnp.float32)

    def update(first_adapter, maps):
        held = maps.shape[0]
        which = first_adapter + jnp.arange(held, dtype=jnp.int32)
        wide = jnp.where((row_stored[:, None] == which[None, :])[:, :, None], low[:, None, :], 0.0)
        return jnp.dot(
            wide.astype(jnp.bfloat16).reshape(total, held * rank),
            maps.reshape(held * rank, columns),
            preferred_element_type=jnp.float32,
        )

    step_adapters = 64
    if adapter_count <= step_adapters:
        updated = update(0, adapter_up_maps)
    else:
        updated = lax.fori_loop(
            0,
            adapter_count // step_adapters,
            lambda i, sofar: sofar
            + update(
                i * step_adapters,
                lax.dynamic_slice_in_dim(adapter_up_maps, i * step_adapters, step_adapters, 0),
            ),
            jnp.zeros((total, columns), jnp.float32),
        )
    value = projected[:, 2] + adapter_scale * updated
    combined = jnp.concatenate([projected[:, 0], projected[:, 1], value], axis=1).astype(jnp.bfloat16)
    combined = combined.reshape(2, chips, ROWS, 3 * columns).transpose(1, 0, 2, 3)
    combined = combined.reshape(replicas, ROWS, 3 * columns)
    arrived = lax.all_to_all(combined, "replica", split_axis=0, concat_axis=0, tiled=True)
    arrived = arrived.reshape(replicas, ROWS, 3, columns).transpose(2, 1, 0, 3).reshape(3, ROWS, width)

    my_lengths = lax.dynamic_slice_in_dim(lengths, my_index * req_dev, req_dev)
    cosine, sine = rotation(my_lengths, steps)
    live = live_rows(my_lengths, request_page_table, pool_pages, page_len)
    kv = key_value_pool.reshape(pool_pages * page_len * 2, width)
    out = attention(steps, req_dev, arrived[0], arrived[1], arrived[2], cosine, sine, live, kv)
    return out.reshape(steps, req_dev, width)


def rotation_rows(lengths, first, req_dev, steps):
    row = jnp.arange(ROWS, dtype=jnp.int32)
    wanted = first + row % req_dev
    chosen = jnp.where(wanted[:, None] == jnp.arange(lengths.shape[0], dtype=jnp.int32)[None, :], lengths[None, :], 0)
    positions = jnp.sum(chosen, axis=1, keepdims=True) + (row // req_dev)[:, None]
    lane = jnp.arange(HD, dtype=jnp.int32)
    frequency = jnp.exp((lane % (HD // 2)).astype(jnp.float32) * (-2.0 * jnp.log(10000.0) / HD))
    angles = positions.astype(jnp.float32) * frequency[None, :]
    return jnp.cos(angles), jnp.where(lane < HD // 2, -1.0, 1.0)[None, :] * jnp.sin(angles)


def live_lanes(lengths, first, request_page_table, tokens, page_len):
    req_dev, max_pages = request_page_table.shape
    wanted = first + jnp.arange(req_dev, dtype=jnp.int32)
    chosen = jnp.where(wanted[:, None] == jnp.arange(lengths.shape[0], dtype=jnp.int32)[None, :], lengths[None, :], 0)
    lane = jnp.arange(tokens, dtype=jnp.int32)
    page = jnp.arange(max_pages, dtype=jnp.int32)
    place = jnp.max(
        jnp.where(request_page_table[:, :, None] == (lane // page_len)[None, None, :], page[None, :, None], -1),
        axis=1,
    )
    token = place * page_len + (lane % page_len)[None, :]
    return ((place >= 0) & (token < jnp.sum(chosen, axis=1, keepdims=True))).astype(jnp.int32)


def trade(value, mask, count):
    return lax.ppermute(value, "replica", [(i, i ^ mask) for i in range(count)])


CONTRACT_LANES = (((1,), (1,)), ((), ()))


def in_hbm(x):
    return pltpu.with_memory_space_constraint(x, pltpu.HBM)


VMEM = pl.BlockSpec(memory_space=pltpu.VMEM)
HBM = pl.BlockSpec(memory_space=pltpu.HBM)
SMEM = pl.BlockSpec(memory_space=pltpu.SMEM)
ANY = pl.BlockSpec(memory_space=pl.ANY)


def start_all(copies):
    for copy in copies:
        copy.start()
    return copies


def wait_all(copies):
    for copy in copies:
        copy.wait()


CACHE_SECTION = 10
CACHE_AHEAD = 4
CACHE_TOKENS = 128


def cache_kernel(first, pool_ref, keys_ref, values_ref, raw, values, sem, out_sem):
    heads, tokens = raw.shape[:2]
    copies = [pltpu.make_async_copy(pool_ref.at[:, first + h], raw.at[h], sem.at[h]) for h in range(heads)]
    start_all(copies[: CACHE_AHEAD * CACHE_SECTION])
    rows = raw.reshape(heads, 2 * tokens, HD)
    block = min(tokens, CACHE_TOKENS)
    to = lax.broadcasted_iota(jnp.int32, (2 * block, 2 * block), 0)
    source = lax.broadcasted_iota(jnp.int32, (2 * block, 2 * block), 1)
    wanted = jnp.where(to < block, 2 * to, 2 * (to - block) + 1)
    pick = jnp.where(source == wanted, 1.0, 0.0).astype(jnp.bfloat16)
    sent = []
    part = CACHE_SECTION
    for p in range(heads // part):
        wait_all(copies[p * part : (p + 1) * part])
        start_all(copies[(p + CACHE_AHEAD) * part : (p + CACHE_AHEAD + 1) * part])
        for h in range(p * part, (p + 1) * part, 2):
            for first_token in range(0, tokens, block):
                raw_rows = slice(2 * first_token, 2 * (first_token + block))
                both = jnp.concatenate([rows[h, raw_rows], rows[h + 1, raw_rows]], axis=1)
                made = jnp.dot(pick, both, preferred_element_type=jnp.float32).astype(jnp.bfloat16)
                span = slice(first_token, first_token + block)
                for i in range(2):
                    keys_ref[h + i, span] = made[:block, i * HD : (i + 1) * HD]
                    values[h + i, span] = made[block:, i * HD : (i + 1) * HD]
        span = slice(p * part, (p + 1) * part)
        sent += start_all([pltpu.make_async_copy(values.at[span], values_ref.at[span], out_sem.at[p])])
    wait_all(sent)


def cache_by_head(pool, first, heads):
    tokens = pool.shape[0]
    return pl.pallas_call(
        functools.partial(cache_kernel, first),
        out_shape=(
            jax.ShapeDtypeStruct((heads, tokens, HD), pool.dtype),
            pltpu.HBM((heads, tokens, HD), pool.dtype),
        ),
        in_specs=[HBM],
        out_specs=(VMEM, HBM),
        scratch_shapes=[
            pltpu.VMEM((heads, tokens, 2, HD), pool.dtype),
            pltpu.VMEM((heads, tokens, HD), pool.dtype),
            pltpu.SemaphoreType.DMA((heads,)),
            pltpu.SemaphoreType.DMA((heads // CACHE_SECTION,)),
        ],
        compiler_params=pltpu.CompilerParams(vmem_limit_bytes=12 * 2**20),
        cost_estimate=pl.CostEstimate(flops=0, bytes_accessed=12 * 10**6, transcendentals=0),
        name="cache_by_head",
    )(in_hbm(pool))


def lanes_of(x):
    return jnp.concatenate([x[c] for c in range(x.shape[0])], axis=1)


def step_rows(x, first, chunks):
    steps, _, count = x.shape[:3]
    flat = x.reshape(steps, x.shape[1], 2 * count, HD)
    return jnp.concatenate(
        [jnp.concatenate([flat[t, c] for c in range(first, first + chunks)], axis=1) for t in range(steps)], axis=0
    )


def index_kernel(me_ref, stored_ref, slot_ref, column_ref):
    requests = stored_ref.shape[1]
    steps = slot_ref.shape[1] // requests
    row = jnp.concatenate([stored_ref[...]] * steps, axis=1)
    slot_ref[...] = row - me_ref[0]
    wide = jnp.concatenate([row, jnp.zeros((1, HD - row.shape[1]), row.dtype)], axis=1)
    column_ref[...] = jnp.broadcast_to(wide.astype(jnp.float32), (HD, HD)).T[: row.shape[1], :1].astype(jnp.int32)


def index_work(first, stored, steps):
    rows = stored.shape[0] * steps
    return pl.pallas_call(
        index_kernel,
        out_shape=(jax.ShapeDtypeStruct((1, rows), jnp.int32), jax.ShapeDtypeStruct((rows, 1), jnp.int32)),
        in_specs=[SMEM, VMEM],
        out_specs=(VMEM, VMEM),
        compiler_params=pltpu.CompilerParams(vmem_limit_bytes=2 * 2**20),
        cost_estimate=pl.CostEstimate(flops=2 * 10**10, bytes_accessed=10**4, transcendentals=0),
        name="index_work",
    )(first, stored[None, :])


def low_kernel(count, me_ref, slot_ref, down_ref, *refs):
    blocks, (x_ref, low_ref, sem) = refs[:count], refs[count:]
    me = me_ref[0]
    holders, rank, width = down_ref.shape
    wait_all(
        start_all(
            [pltpu.make_async_copy(block, x_ref.at[:, :, me ^ k], sem.at[k]) for k, block in enumerate(blocks)]
        )
    )
    x = step_rows(x_ref, 0, x_ref.shape[1])
    rows = x.shape[0]
    made = lax.dot_general(
        down_ref.reshape(holders * rank, width)[...], x, CONTRACT_LANES, preferred_element_type=jnp.float32
    )
    slot = slot_ref[...]
    low = jnp.zeros((rank, rows), jnp.float32)
    for h in range(holders):
        low = low + jnp.where(slot == h, made[h * rank : (h + 1) * rank], 0.0)
    low = low.T
    low_ref[...] = jnp.concatenate([low[: rows // 2], low[rows // 2 :]], axis=1).astype(low_ref.dtype)


def low_of(me, blocks, slot, down):
    count = len(blocks)
    steps, chunks = blocks[0].shape[:2]
    rows = count * steps * 2
    rank = down.shape[1]
    return pl.pallas_call(
        functools.partial(low_kernel, count),
        out_shape=(
            jax.ShapeDtypeStruct((steps, chunks, count, 2, HD), jnp.bfloat16),
            jax.ShapeDtypeStruct((rows // 2, 2 * rank), jnp.bfloat16),
        ),
        in_specs=[SMEM, VMEM, VMEM] + [ANY] * count,
        out_specs=(VMEM, VMEM),
        scratch_shapes=[pltpu.SemaphoreType.DMA((count,))],
        compiler_params=pltpu.CompilerParams(vmem_limit_bytes=12 * 2**20),
        cost_estimate=pl.CostEstimate(flops=10**8, bytes_accessed=4 * 10**6, transcendentals=0),
        name="low_rows",
    )(me, slot, down, *blocks)


def put_chunks(buf, first, value):
    steps, count = buf.shape[1:3]
    flat = buf.reshape(buf.shape[0], steps, 2 * count, HD)
    wide = value.shape[1]
    for c in range(-(-wide // HD)):
        part = value[:, c * HD : min((c + 1) * HD, wide)]
        if part.shape[1] < HD:
            part = jnp.concatenate([part, jnp.zeros((part.shape[0], HD - part.shape[1]), part.dtype)], axis=1)
        part = part.astype(buf.dtype)
        for t in range(steps):
            flat[first + c, t] = part[t * 2 * count : (t + 1) * 2 * count]


def project_kernel(which, x_ref, w_ref, out_ref):
    x = step_rows(x_ref, 0, x_ref.shape[1])
    made = lax.dot_general(w_ref[which], x, CONTRACT_LANES, preferred_element_type=jnp.float32).T
    if which < 2:
        pad = jnp.zeros((made.shape[0], HD // 2), made.dtype)
        put_chunks(out_ref, 0, jnp.concatenate([made, pad] if which == 0 else [pad, made], axis=1))
    else:
        out_ref[...] = made


def project(which, x, weight):
    steps, _, count = x.shape[:3]
    columns = weight.shape[1]
    chunks = jax.ShapeDtypeStruct((-(-columns // HD), steps, count, 2, HD), jnp.bfloat16)
    base = jax.ShapeDtypeStruct((2 * steps * count, columns), jnp.float32)
    return pl.pallas_call(
        functools.partial(project_kernel, which),
        out_shape=chunks if which < 2 else base,
        in_specs=[VMEM, VMEM],
        out_specs=VMEM,
        compiler_params=pltpu.CompilerParams(vmem_limit_bytes=16 * 2**20),
        cost_estimate=pl.CostEstimate(flops=5 * 10**8, bytes_accessed=4 * 10**6, transcendentals=0),
        name="project",
    )(x, weight)


def update_kernel(stored_ref, query_ref, key_ref, base_ref, up_ref, *refs):
    lows, (send_ref, buf, sem) = refs[:-3], refs[-3:]
    half, packed = lows[0].shape
    rank = packed // 2
    rows = 2 * half
    count = send_ref.shape[0]
    low = lows[0][...].astype(jnp.float32)
    for more in lows[1:]:
        low = low + more[...].astype(jnp.float32)
    low = jnp.concatenate([low[:, :rank], low[:, rank:]], axis=0)
    batch = 256 // rank
    spread = jnp.concatenate([low] * batch, axis=1)
    ahead = stored_ref[...] - lax.broadcasted_iota(jnp.int32, (rows, batch * rank), 1) // rank
    total = jnp.zeros(base_ref.shape, jnp.float32)
    for a in range(0, up_ref.shape[0] // rank, batch):
        wide = jnp.where(ahead == a, spread, 0.0).astype(jnp.bfloat16)
        total = total + jnp.dot(wide, up_ref[a * rank : (a + batch) * rank], preferred_element_type=jnp.float32)
    each = query_ref.shape[0]
    buf[: each - 1] = query_ref[: each - 1]
    buf[each - 1] = query_ref[each - 1] + key_ref[0]
    buf[each : 2 * each - 1] = key_ref[1:]
    put_chunks(buf, 2 * each - 1, base_ref[...] + adapter_scale * total)
    wait_all(
        start_all([pltpu.make_async_copy(buf.at[:, :, k], send_ref.at[k], sem.at[k]) for k in range(count)])
    )


def update_values(stored, query, key, base, up, lows):
    chunks, steps, count = query.shape[:3]
    return pl.pallas_call(
        update_kernel,
        out_shape=pltpu.HBM((count, 3 * chunks - 1, steps, 2, HD), query.dtype),
        in_specs=[VMEM] * (5 + len(lows)),
        out_specs=HBM,
        scratch_shapes=[
            pltpu.VMEM((3 * chunks - 1, steps, count, 2, HD), query.dtype),
            pltpu.SemaphoreType.DMA((count,)),
        ],
        compiler_params=pltpu.CompilerParams(vmem_limit_bytes=8 * 2**20),
        cost_estimate=pl.CostEstimate(flops=3 * 10**8, bytes_accessed=4 * 10**6, transcendentals=0),
        name="update_values",
    )(stored, query, key, base, up, *lows)


def attend_kernel(cos_ref, sin_ref, live_ref, pieces_ref, *refs):
    *parts, out_ref, values_buf, kn_ref, vn_ref, sem = refs
    keys_refs, values_refs = parts[: len(parts) // 2], parts[len(parts) // 2 :]
    count, _, steps = pieces_ref.shape[:3]
    rows = 2 * steps
    each = (pieces_ref.shape[1] + 1) // 3
    heads = 2 * out_ref.shape[1] // count
    lanes = heads * HD
    group = rows * HEAD_BLOCK
    chips = range(count // 2)
    early = keys_refs[0].shape[0] // heads
    places = [(0, c) if c < early else (1, c - early) for c in chips]
    fetches = start_all(
        [
            pltpu.make_async_copy(values_refs[half].at[at * heads : (at + 1) * heads], values_buf.at[c], sem.at[c])
            for c, (half, at) in enumerate(places)
        ]
    )
    cosine = cos_ref[...][:rows]
    sine = sin_ref[...][:rows]
    left = lax.broadcasted_iota(jnp.int32, (rows, HD), 1) < HD // 2

    flat = pieces_ref.reshape(count, pieces_ref.shape[1], rows, HD)

    def halves(chip, at):
        return [
            [flat[2 * chip + core, at + c].astype(jnp.float32) for c in range(each)]
            for core in range(2)
        ]

    def swapped(parts):
        return [pltpu.roll(x, HD // 2, 1) for x in parts]

    def joined(parts):
        return [jnp.where(left, a, b) for a, b in zip(parts[:-1], parts[1:])]

    def chip_columns(chip, at):
        low, high = halves(chip, at)
        high = swapped(high)
        return low[:-1] + [jnp.where(left, low[-1], high[0])] + joined(high)

    def chip_keys(chip):
        low, high = halves(chip, each - 1)
        low = swapped(low)
        return joined(low) + [jnp.where(left, low[-1], high[0])] + high[1:]

    def rotated(parts):
        return [x * cosine + pltpu.roll(x, HD // 2, 1) * sine for x in parts]

    row_head = lax.broadcasted_iota(jnp.int32, (group, lanes), 0) % HEAD_BLOCK
    lane_head = lax.broadcasted_iota(jnp.int32, (group, lanes), 1) // HD
    own_head = row_head == lane_head
    row_j = lax.broadcasted_iota(jnp.int32, (group, 16), 0) // HEAD_BLOCK
    new_j = lax.broadcasted_iota(jnp.int32, (group, 16), 1)
    new_live = (new_j < rows) & (new_j % 2 == row_j % 2) & (new_j // 2 <= row_j // 2)
    live = jnp.concatenate(
        [
            jnp.broadcast_to(live_ref[j % 2 : j % 2 + 1, :], (HEAD_BLOCK, live_ref.shape[1]))
            for j in range(rows)
        ],
        axis=0,
    )
    live = live > 0
    kn_ref[...] = jnp.zeros_like(kn_ref)
    vn_ref[...] = jnp.zeros_like(vn_ref)
    spreads = []
    for c in chips:
        query = jnp.concatenate(rotated(chip_columns(c, 0)), axis=1)
        kn_ref[c, 0:rows] = jnp.concatenate(rotated(chip_keys(c)), axis=1)
        vn_ref[c, 0:rows] = jnp.concatenate(chip_columns(c, 2 * each - 1), axis=1)
        spread = jnp.concatenate(
            [jnp.broadcast_to(query[j : j + 1], (HEAD_BLOCK, lanes)) for j in range(rows)], axis=0
        )
        spreads.append(jnp.where(own_head, spread, 0.0).astype(jnp.bfloat16))
    scores, fresh = [], []
    for c in chips:
        half, at = places[c]
        keys = jnp.concatenate([keys_refs[half][at * heads + h] for h in range(heads)], axis=1)
        kn = kn_ref[c].astype(jnp.bfloat16)
        scores.append(lax.dot_general(spreads[c], keys, CONTRACT_LANES, preferred_element_type=jnp.float32))
        fresh.append(lax.dot_general(spreads[c], kn, CONTRACT_LANES, preferred_element_type=jnp.float32))
    weights, fresh_weights, totals = [], [], []
    for c in chips:
        old = jnp.where(live, scores[c] * (HD**-0.5), masked_score)
        new = jnp.where(new_live, fresh[c] * (HD**-0.5), masked_score)
        top = jnp.maximum(jnp.max(old, axis=1, keepdims=True), jnp.max(new, axis=1, keepdims=True))
        old = jnp.exp(old - top)
        new = jnp.exp(new - top)
        totals.append(jnp.sum(old, axis=1, keepdims=True) + jnp.sum(new, axis=1, keepdims=True))
        weights.append(old.astype(jnp.bfloat16))
        fresh_weights.append(new.astype(jnp.bfloat16))
    wait_all(fetches)
    for c in chips:
        values = lanes_of(values_buf[c])
        vn = vn_ref[c].astype(jnp.bfloat16)
        mixed = jnp.dot(weights[c], values, preferred_element_type=jnp.float32)
        mixed = mixed + jnp.dot(fresh_weights[c], vn, preferred_element_type=jnp.float32)
        mixed = jnp.sum(jnp.where(own_head, mixed, 0.0).reshape(rows, HEAD_BLOCK, lanes), axis=1)
        total = jnp.sum(jnp.where(own_head, totals[c], 0.0).reshape(rows, HEAD_BLOCK, lanes), axis=1)
        out = (mixed / total).astype(out_ref.dtype)
        for t in range(steps):
            for h in range(heads):
                out_ref[t, c * heads + h] = out[2 * t : 2 * t + 2, h * HD : (h + 1) * HD]


def attend(cosine, sine, live, pieces, keys, values):
    count, _, steps = pieces.shape[:3]
    heads, tokens = sum(x.shape[0] for x in keys), keys[0].shape[1]
    chips = count // 2
    per = heads // chips
    return pl.pallas_call(
        attend_kernel,
        out_shape=jax.ShapeDtypeStruct((steps, heads, 2, HD), jnp.bfloat16),
        in_specs=[VMEM] * (4 + len(keys)) + [HBM] * len(values),
        out_specs=VMEM,
        scratch_shapes=[pltpu.VMEM((chips, per, tokens, HD), jnp.bfloat16)]
        + [pltpu.VMEM((chips, 16, per * HD), jnp.float32)] * 2
        + [pltpu.SemaphoreType.DMA((chips,))],
        compiler_params=pltpu.CompilerParams(vmem_limit_bytes=16 * 2**20),
        cost_estimate=pl.CostEstimate(flops=10**9, bytes_accessed=6 * 10**6, transcendentals=0),
        name="attention",
    )(cosine, sine, live, pieces, *keys, *[in_hbm(x) for x in values])


def chip_plan(
    count,
    hidden,
    query_key_value_weight,
    adapter_down_maps,
    adapter_up_maps,
    adapter_storage_row,
    request_adapter,
    lengths,
    request_page_table,
    key_value_pool,
):
    me = lax.axis_index("replica")
    steps, req_dev, width = hidden.shape
    heads = width // HD
    holder_count, rank, _ = adapter_down_maps.shape
    pool_pages, page_len = key_value_pool.shape[:2]
    adapter_count = adapter_storage_row.shape[0]

    tokens = pool_pages * page_len
    pool = key_value_pool.reshape(tokens, 2, heads, HD).transpose(0, 2, 1, 3)

    stored = jnp.sum(
        jnp.where(
            request_adapter[:, None] == jnp.arange(adapter_count, dtype=jnp.int32)[None, :],
            adapter_storage_row[None, :],
            0,
        ),
        axis=1,
    )
    first, slots, here, stored = lax.optimization_barrier(
        (me * req_dev, (me * holder_count).astype(jnp.int32).reshape(1), me.astype(jnp.int32).reshape(1), stored)
    )
    slot, column = index_work(slots, stored, steps)

    held = {0: hidden}
    held.update({m: trade(hidden, m, count) for m in range(4, count, 4)})
    _, lengths, request_page_table = lax.optimization_barrier((held[4], lengths, request_page_table))
    cosine, sine = rotation_rows(lengths, first, req_dev, steps)
    live = live_lanes(lengths, first, request_page_table, tokens, page_len)
    held.update({k | 2: trade(v, 2, count) for k, v in list(held.items())})
    ready = [0, 2, 4, 6]
    held.update(zip(ready, lax.optimization_barrier([held[k] for k in ready])))
    held.update({k | 1: trade(v, 1, count) for k, v in list(held.items())})
    blocks = [held[k].reshape(steps, req_dev, heads, HD).transpose(0, 2, 1, 3) for k in range(count)]
    blocks[0] = in_hbm(blocks[0])
    x, low = low_of(here, blocks, slot, adapter_down_maps)
    weight = query_key_value_weight.transpose(0, 2, 1)
    arrived = [trade(low, m, count) for m in (1, 2, 3)]
    query, key = project(0, x, weight), project(1, x, weight)
    arrived, query, key, pool = lax.optimization_barrier((arrived, query, key, pool))
    low = (low + arrived[0]) + (arrived[1] + arrived[2])
    arrived = [trade(low, m, count) for m in range(4, count, 4)]
    base = project(2, x, weight)
    arrived, base = lax.optimization_barrier((arrived, base))
    send = update_values(column, query, key, base, adapter_up_maps.reshape(adapter_count * rank, -1), [low, *arrived])
    send, pool = lax.optimization_barrier((send, pool))
    keys, values = cache_by_head(pool, 0, heads)
    pieces = lax.all_to_all(send, "replica", split_axis=0, concat_axis=0, tiled=True)

    out = attend(cosine, sine, live, pieces, [keys], [values])
    return out.transpose(0, 2, 1, 3).reshape(steps, req_dev, width)


def per_device(replicas, *arrays):
    columns = arrays[1].shape[2]
    whole_heads = replicas % 4 == 0 and (2 * columns) % HD == 0 and columns % HD == HD // 2
    plan = chip_plan if whole_heads and arrays[0].shape[1] == 2 else general_plan
    return plan(replicas, *arrays)


def solution(mesh):
    placed = (
        P(None, ("groups", "replica"), None),
        P(None, None, "replica"),
        P("replica", None, None),
        P(None, None, "replica"),
        P(),
        P("groups"),
        P("groups"),
        P(("groups", "replica"), None),
        P(("groups", "replica"), None, None, None),
    )
    return jax.shard_map(
        functools.partial(per_device, mesh.shape["replica"]),
        mesh=mesh,
        in_specs=placed,
        out_specs=P(None, ("groups", "replica"), None),
        check_vma=False,
    )
```

```python
import functools

import jax
import jax.numpy as jnp
from jax import lax
from jax.experimental import pallas as pl
from jax.experimental.pallas import tpu as pltpu
from jax.sharding import PartitionSpec as P

HD = 128
ROWS = 8
HEAD_BLOCK = 8

adapter_scale = 2.0
masked_score = -1e30


def attention_kernel(steps, req_dev, q_ref, k_ref, v_ref, cos_ref, sin_ref, live_ref, kv_ref, out_ref, kn_ref, vn_ref):
    rows = steps * req_dev
    width = q_ref.shape[1]
    lanes = HEAD_BLOCK * HD
    group = rows * HEAD_BLOCK
    cosine = cos_ref[...]
    sine = sin_ref[...]

    def rotated(x):
        pieces = []
        for h in range(HEAD_BLOCK):
            head = x[:, h * HD : (h + 1) * HD]
            pieces.append(head * cosine + pltpu.roll(head, HD // 2, 1) * sine)
        return jnp.concatenate(pieces, axis=1)

    row_head = lax.broadcasted_iota(jnp.int32, (group, lanes), 0) % HEAD_BLOCK
    lane_head = lax.broadcasted_iota(jnp.int32, (group, lanes), 1) // HD
    own_head = row_head == lane_head
    row_j = lax.broadcasted_iota(jnp.int32, (group, 16), 0) // HEAD_BLOCK
    new_j = lax.broadcasted_iota(jnp.int32, (group, 16), 1)
    new_live = (new_j < rows) & (new_j % req_dev == row_j % req_dev) & (new_j // req_dev <= row_j // req_dev)
    live_all = live_ref[...]
    live = jnp.concatenate(
        [
            jnp.broadcast_to(live_all[j % req_dev : j % req_dev + 1], (HEAD_BLOCK, live_all.shape[1]))
            for j in range(rows)
        ],
        axis=0,
    )
    live = live > 0
    kn_ref[...] = jnp.zeros_like(kn_ref)
    vn_ref[...] = jnp.zeros_like(vn_ref)
    contract_lanes = (((1,), (1,)), ((), ()))
    for c in range(width // lanes):
        cols = slice(c * lanes, (c + 1) * lanes)
        query = rotated(q_ref[:, cols].astype(jnp.float32))
        key_new = rotated(k_ref[:, cols].astype(jnp.float32))
        kn_ref[0:8] = key_new
        vn_ref[0:8] = v_ref[:, cols].astype(jnp.float32)
        kn = kn_ref[...].astype(jnp.bfloat16)
        vn = vn_ref[...].astype(jnp.bfloat16)
        spread = jnp.concatenate(
            [jnp.broadcast_to(query[j : j + 1], (HEAD_BLOCK, lanes)) for j in range(rows)], axis=0
        )
        spread = jnp.where(own_head, spread, 0.0).astype(jnp.bfloat16)
        kv = kv_ref[:, cols]
        scores = lax.dot_general(spread, kv, contract_lanes, preferred_element_type=jnp.float32) * (HD**-0.5)
        scores = jnp.where(live, scores, masked_score)
        fresh = lax.dot_general(spread, kn, contract_lanes, preferred_element_type=jnp.float32) * (HD**-0.5)
        fresh = jnp.where(new_live, fresh, masked_score)
        top = jnp.maximum(jnp.max(scores, axis=1, keepdims=True), jnp.max(fresh, axis=1, keepdims=True))
        weights = jnp.where(live, jnp.exp(scores - top), 0.0)
        fresh = jnp.where(new_live, jnp.exp(fresh - top), 0.0)
        totals = jnp.sum(weights, axis=1, keepdims=True) + jnp.sum(fresh, axis=1, keepdims=True)
        weights = pltpu.roll(weights, 1, 1).astype(jnp.bfloat16)
        mixed = jnp.dot(weights, kv, preferred_element_type=jnp.float32)
        mixed = mixed + jnp.dot(fresh.astype(jnp.bfloat16), vn, preferred_element_type=jnp.float32)
        mixed = jnp.where(own_head, mixed / totals, 0.0)
        out = jnp.sum(mixed.reshape(rows, HEAD_BLOCK, lanes), axis=1)
        out_ref[:, cols] = out.astype(out_ref.dtype)


def attention(steps, req_dev, q, k, v, cosine, sine, live, kv):
    rows = steps * req_dev
    width = q.shape[1]
    vmem = pl.BlockSpec(memory_space=pltpu.VMEM)
    return pl.pallas_call(
        functools.partial(attention_kernel, steps, req_dev),
        out_shape=jax.ShapeDtypeStruct((rows, width), jnp.bfloat16),
        in_specs=[vmem] * 7,
        out_specs=vmem,
        scratch_shapes=[pltpu.VMEM((16, HEAD_BLOCK * HD), jnp.float32)] * 2,
        compiler_params=pltpu.CompilerParams(vmem_limit_bytes=32 * 2**20),
        cost_estimate=pl.CostEstimate(flops=10**9, bytes_accessed=6 * 10**6, transcendentals=0),
        name="attention",
    )(q, k, v, cosine, sine, live, kv)


def rotation(my_lengths, steps):
    rows = steps * my_lengths.shape[0]
    positions = (my_lengths[None, :] + jnp.arange(steps, dtype=jnp.int32)[:, None]).reshape(rows)
    positions = jnp.pad(positions, (0, ROWS - rows))
    half = HD // 2
    frequency = jnp.exp(jnp.arange(half, dtype=jnp.float32) * (-2.0 * jnp.log(10000.0) / HD))
    angles = positions.astype(jnp.float32)[:, None] * frequency[None, :]
    cosine = jnp.cos(angles)
    sine = jnp.sin(angles)
    cosine = jnp.concatenate([cosine, cosine], axis=1)
    sine = jnp.concatenate([-sine, sine], axis=1)
    return cosine, sine


def live_tokens(my_lengths, request_page_table, pool_pages, page_len):
    pages = jnp.arange(pool_pages, dtype=jnp.int32)
    max_pages = request_page_table.shape[1]
    place = jnp.max(
        jnp.where(
            request_page_table[:, :, None] == pages[None, None, :],
            jnp.arange(max_pages, dtype=jnp.int32)[None, :, None],
            -1,
        ),
        axis=1,
    )
    token = place[:, :, None] * page_len + jnp.arange(page_len, dtype=jnp.int32)[None, None, :]
    return (place[:, :, None] >= 0) & (token < my_lengths[:, None, None])


def live_rows(my_lengths, request_page_table, pool_pages, page_len):
    alive = live_tokens(my_lengths, request_page_table, pool_pages, page_len)
    live = jnp.stack([alive, jnp.zeros_like(alive)], axis=-1).astype(jnp.int32)
    return live.reshape(request_page_table.shape[0], pool_pages * page_len * 2)


def general_plan(
    replicas,
    hidden,
    query_key_value_weight,
    adapter_down_maps,
    adapter_up_maps,
    adapter_storage_row,
    request_adapter,
    lengths,
    request_page_table,
    key_value_pool,
):
    my_index = lax.axis_index("replica")
    steps, req_dev, width = hidden.shape
    rows = steps * req_dev
    columns = query_key_value_weight.shape[2]
    holder_count, rank, _ = adapter_down_maps.shape
    pool_pages, page_len = key_value_pool.shape[:2]
    adapter_count = adapter_storage_row.shape[0]
    chips = replicas // 2
    total = replicas * ROWS

    block = jnp.pad(hidden.reshape(rows, width), ((0, ROWS - rows), (0, 0)))
    same_core = [[2 * chip + core for chip in range(chips)] for core in range(2)]
    mine = lax.all_to_all(
        jnp.broadcast_to(block[None], (chips, ROWS, width)),
        "replica",
        split_axis=0,
        concat_axis=0,
        axis_index_groups=same_core,
        tiled=True,
    )
    other = lax.ppermute(mine, "replica", [(i, i ^ 1) for i in range(replicas)])
    first = my_index % 2 == 0
    gathered = jnp.stack([jnp.where(first, mine, other), jnp.where(first, other, mine)])
    gathered = gathered.reshape(total, width)

    stored_rows = jnp.sum(
        jnp.where(
            request_adapter[:, None] == jnp.arange(adapter_count, dtype=jnp.int32)[None, :],
            adapter_storage_row[None, :],
            0,
        ),
        axis=1,
    )
    by_block = stored_rows.reshape(chips, 2, 1, req_dev).transpose(1, 0, 2, 3)
    by_block = jnp.broadcast_to(by_block, (2, chips, steps, req_dev)).reshape(2, chips, rows)
    row_stored = jnp.pad(by_block, ((0, 0), (0, 0), (0, ROWS - rows)), constant_values=-1).reshape(total)

    down = jnp.einsum("nd,hfd->nhf", gathered, adapter_down_maps, preferred_element_type=jnp.float32)
    slots = my_index * holder_count + jnp.arange(holder_count, dtype=jnp.int32)
    own = row_stored[:, None] == slots[None, :]
    low = jnp.sum(jnp.where(own[:, :, None], down, 0.0), axis=1).astype(jnp.bfloat16)
    low = jnp.concatenate([low[: total // 2], low[total // 2 :]], axis=1)
    low = lax.all_to_all(
        jnp.broadcast_to(low[None], (replicas,) + low.shape), "replica", split_axis=0, concat_axis=0, tiled=True
    )
    low = jnp.sum(low.astype(jnp.float32), axis=0)
    low = jnp.concatenate([low[:, :rank], low[:, rank:]], axis=0)

    projected = jnp.einsum("nd,idc->nic", gathered, query_key_value_weight, preferred_element_type=jnp.float32)

    def update(first_adapter, maps):
        held = maps.shape[0]
        which = first_adapter + jnp.arange(held, dtype=jnp.int32)
        wide = jnp.where((row_stored[:, None] == which[None, :])[:, :, None], low[:, None, :], 0.0)
        return jnp.dot(
            wide.astype(jnp.bfloat16).reshape(total, held * rank),
            maps.reshape(held * rank, columns),
            preferred_element_type=jnp.float32,
        )

    step_adapters = 64
    if adapter_count <= step_adapters:
        updated = update(0, adapter_up_maps)
    else:
        updated = lax.fori_loop(
            0,
            adapter_count // step_adapters,
            lambda i, sofar: sofar
            + update(
                i * step_adapters,
                lax.dynamic_slice_in_dim(adapter_up_maps, i * step_adapters, step_adapters, 0),
            ),
            jnp.zeros((total, columns), jnp.float32),
        )
    value = projected[:, 2] + adapter_scale * updated
    combined = jnp.concatenate([projected[:, 0], projected[:, 1], value], axis=1).astype(jnp.bfloat16)
    combined = combined.reshape(2, chips, ROWS, 3 * columns).transpose(1, 0, 2, 3)
    combined = combined.reshape(replicas, ROWS, 3 * columns)
    arrived = lax.all_to_all(combined, "replica", split_axis=0, concat_axis=0, tiled=True)
    arrived = arrived.reshape(replicas, ROWS, 3, columns).transpose(2, 1, 0, 3).reshape(3, ROWS, width)

    my_lengths = lax.dynamic_slice_in_dim(lengths, my_index * req_dev, req_dev)
    cosine, sine = rotation(my_lengths, steps)
    live = live_rows(my_lengths, request_page_table, pool_pages, page_len)
    kv = key_value_pool.reshape(pool_pages * page_len * 2, width)
    out = attention(steps, req_dev, arrived[0], arrived[1], arrived[2], cosine, sine, live, kv)
    return out.reshape(steps, req_dev, width)


def rotation_rows(lengths, first, req_dev, steps):
    row = jnp.arange(ROWS, dtype=jnp.int32)
    wanted = first + row % req_dev
    chosen = jnp.where(wanted[:, None] == jnp.arange(lengths.shape[0], dtype=jnp.int32)[None, :], lengths[None, :], 0)
    positions = jnp.sum(chosen, axis=1, keepdims=True) + (row // req_dev)[:, None]
    lane = jnp.arange(HD, dtype=jnp.int32)
    frequency = jnp.exp((lane % (HD // 2)).astype(jnp.float32) * (-2.0 * jnp.log(10000.0) / HD))
    angles = positions.astype(jnp.float32) * frequency[None, :]
    return jnp.cos(angles), jnp.where(lane < HD // 2, -1.0, 1.0)[None, :] * jnp.sin(angles)


def live_lanes(lengths, first, request_page_table, tokens, page_len):
    req_dev, max_pages = request_page_table.shape
    wanted = first + jnp.arange(req_dev, dtype=jnp.int32)
    chosen = jnp.where(wanted[:, None] == jnp.arange(lengths.shape[0], dtype=jnp.int32)[None, :], lengths[None, :], 0)
    lane = jnp.arange(tokens, dtype=jnp.int32)
    page = jnp.arange(max_pages, dtype=jnp.int32)
    place = jnp.max(
        jnp.where(request_page_table[:, :, None] == (lane // page_len)[None, None, :], page[None, :, None], -1),
        axis=1,
    )
    token = place * page_len + (lane % page_len)[None, :]
    return ((place >= 0) & (token < jnp.sum(chosen, axis=1, keepdims=True))).astype(jnp.int32)


def trade(value, mask, count):
    return lax.ppermute(value, "replica", [(i, i ^ mask) for i in range(count)])


CONTRACT_LANES = (((1,), (1,)), ((), ()))


def in_hbm(x):
    return pltpu.with_memory_space_constraint(x, pltpu.HBM)


VMEM = pl.BlockSpec(memory_space=pltpu.VMEM)
HBM = pl.BlockSpec(memory_space=pltpu.HBM)
SMEM = pl.BlockSpec(memory_space=pltpu.SMEM)
ANY = pl.BlockSpec(memory_space=pl.ANY)


def start_all(copies):
    for copy in copies:
        copy.start()
    return copies


def wait_all(copies):
    for copy in copies:
        copy.wait()


CACHE_SECTION = 10
CACHE_AHEAD = 4
CACHE_TOKENS = 128


def cache_kernel(first, pool_ref, keys_ref, values_ref, raw, values, sem, out_sem):
    heads, tokens = raw.shape[:2]
    copies = [pltpu.make_async_copy(pool_ref.at[:, first + h], raw.at[h], sem.at[h]) for h in range(heads)]
    start_all(copies[: CACHE_AHEAD * CACHE_SECTION])
    rows = raw.reshape(heads, 2 * tokens, HD)
    block = min(tokens, CACHE_TOKENS)
    to = lax.broadcasted_iota(jnp.int32, (2 * block, 2 * block), 0)
    source = lax.broadcasted_iota(jnp.int32, (2 * block, 2 * block), 1)
    wanted = jnp.where(to < block, 2 * to, 2 * (to - block) + 1)
    pick = jnp.where(source == wanted, 1.0, 0.0).astype(jnp.bfloat16)
    sent = []
    part = CACHE_SECTION
    for p in range(heads // part):
        wait_all(copies[p * part : (p + 1) * part])
        start_all(copies[(p + CACHE_AHEAD) * part : (p + CACHE_AHEAD + 1) * part])
        for h in range(p * part, (p + 1) * part, 2):
            for first_token in range(0, tokens, block):
                raw_rows = slice(2 * first_token, 2 * (first_token + block))
                both = jnp.concatenate([rows[h, raw_rows], rows[h + 1, raw_rows]], axis=1)
                made = jnp.dot(pick, both, preferred_element_type=jnp.float32).astype(jnp.bfloat16)
                span = slice(first_token, first_token + block)
                for i in range(2):
                    keys_ref[h + i, span] = made[:block, i * HD : (i + 1) * HD]
                    values[h + i, span] = made[block:, i * HD : (i + 1) * HD]
        span = slice(p * part, (p + 1) * part)
        sent += start_all([pltpu.make_async_copy(values.at[span], values_ref.at[span], out_sem.at[p])])
    wait_all(sent)


def cache_by_head(pool, first, heads):
    tokens = pool.shape[0]
    return pl.pallas_call(
        functools.partial(cache_kernel, first),
        out_shape=(
            jax.ShapeDtypeStruct((heads, tokens, HD), pool.dtype),
            pltpu.HBM((heads, tokens, HD), pool.dtype),
        ),
        in_specs=[HBM],
        out_specs=(VMEM, HBM),
        scratch_shapes=[
            pltpu.VMEM((heads, tokens, 2, HD), pool.dtype),
            pltpu.VMEM((heads, tokens, HD), pool.dtype),
            pltpu.SemaphoreType.DMA((heads,)),
            pltpu.SemaphoreType.DMA((heads // CACHE_SECTION,)),
        ],
        compiler_params=pltpu.CompilerParams(vmem_limit_bytes=12 * 2**20),
        cost_estimate=pl.CostEstimate(flops=0, bytes_accessed=12 * 10**6, transcendentals=0),
        name="cache_by_head",
    )(in_hbm(pool))


def lanes_of(x):
    return jnp.concatenate([x[c] for c in range(x.shape[0])], axis=1)


def step_rows(x, first, chunks):
    steps, _, count = x.shape[:3]
    flat = x.reshape(steps, x.shape[1], 2 * count, HD)
    return jnp.concatenate(
        [jnp.concatenate([flat[t, c] for c in range(first, first + chunks)], axis=1) for t in range(steps)], axis=0
    )


def index_kernel(holders, me_ref, stored_ref, slot_ref, column_ref):
    me = me_ref[0]
    requests = stored_ref.shape[1]
    half = requests // 2
    steps = slot_ref.shape[1] // requests
    wide = jnp.concatenate([stored_ref[...], jnp.zeros((1, HD - requests), jnp.int32)], axis=1)
    by_row = jnp.broadcast_to(wide.astype(jnp.float32), (HD, HD)).T[:requests]
    lane = lax.broadcasted_iota(jnp.int32, (requests, HD), 1)
    core = (me % 2) ^ (lane // half)
    wanted = ((lane % half) // 2 * 2 + core) * 2 + lane % 2
    place = lax.broadcasted_iota(jnp.int32, (requests, HD), 0)
    chosen = jnp.sum(jnp.where(place == wanted, by_row, 0.0), axis=0, keepdims=True)
    row = jnp.concatenate([chosen[:, :half]] * steps + [chosen[:, half:requests]] * steps, axis=1)
    slot_ref[...] = row.astype(jnp.int32) - me * holders
    wide = jnp.concatenate([row, jnp.zeros((1, HD - row.shape[1]), row.dtype)], axis=1)
    column_ref[...] = jnp.broadcast_to(wide, (HD, HD)).T[: row.shape[1], :1].astype(jnp.int32)


def index_work(me, holders, stored, steps):
    rows = stored.shape[0] * steps
    return pl.pallas_call(
        functools.partial(index_kernel, holders),
        out_shape=(jax.ShapeDtypeStruct((1, rows), jnp.int32), jax.ShapeDtypeStruct((rows, 1), jnp.int32)),
        in_specs=[SMEM, VMEM],
        out_specs=(VMEM, VMEM),
        compiler_params=pltpu.CompilerParams(vmem_limit_bytes=2 * 2**20),
        cost_estimate=pl.CostEstimate(flops=2 * 10**10, bytes_accessed=10**4, transcendentals=0),
        name="index_work",
    )(me, stored[None, :])


def line_copies(me, blocks, x_ref, sem):
    return [
        pltpu.make_async_copy(block, x_ref.at[:, :, (me // 2) ^ i], sem.at[i]) for i, block in enumerate(blocks)
    ]


def line_kernel(chips, me_ref, *refs):
    blocks, (x_ref, sem) = refs[:chips], refs[chips:]
    wait_all(start_all(line_copies(me_ref[0], blocks, x_ref, sem)))


def line_rows(me, blocks):
    chips = len(blocks)
    steps, chunks = blocks[0].shape[:2]
    return pl.pallas_call(
        functools.partial(line_kernel, chips),
        out_shape=jax.ShapeDtypeStruct((steps, chunks, chips, 2, HD), jnp.bfloat16),
        in_specs=[SMEM] + [ANY] * chips,
        out_specs=VMEM,
        scratch_shapes=[pltpu.SemaphoreType.DMA((chips,))],
        compiler_params=pltpu.CompilerParams(vmem_limit_bytes=4 * 2**20),
        cost_estimate=pl.CostEstimate(flops=0, bytes_accessed=10**6, transcendentals=0),
        name="line_rows",
    )(me, *blocks)


def low_kernel(chips, me_ref, slot_ref, down_ref, other_ref, *refs):
    blocks, (x_ref, near_ref, far_ref, sem) = refs[:chips], refs[chips:]
    me = me_ref[0]
    holders, rank, width = down_ref.shape
    wait_all(start_all(line_copies(me, blocks, x_ref, sem)))
    x = step_rows(x_ref, 0, x_ref.shape[1])
    rows = x.shape[0]
    slot = slot_ref[...][:, :rows]
    low = jnp.zeros((rank, rows), jnp.float32)
    for maps_ref, first in ((down_ref, 0), (other_ref, holders * (1 - 2 * (me % 2)))):
        made = lax.dot_general(
            maps_ref.reshape(holders * rank, width)[...], x, CONTRACT_LANES, preferred_element_type=jnp.float32
        )
        for h in range(holders):
            low = low + jnp.where(slot == first + h, made[h * rank : (h + 1) * rank], 0.0)
    low = low.T.astype(near_ref.dtype)
    none = jnp.zeros((rows, HD - rank), near_ref.dtype)
    near_ref[...] = jnp.concatenate([low, none], axis=1)
    far_ref[...] = jnp.concatenate([none, low], axis=1)


def low_of(me, blocks, slot, down, other):
    chips = len(blocks)
    steps, chunks = blocks[0].shape[:2]
    rows = chips * steps * 2
    low = jax.ShapeDtypeStruct((rows, HD), jnp.bfloat16)
    return pl.pallas_call(
        functools.partial(low_kernel, chips),
        out_shape=(jax.ShapeDtypeStruct((steps, chunks, chips, 2, HD), jnp.bfloat16), low, low),
        in_specs=[SMEM, VMEM, VMEM, VMEM] + [ANY] * chips,
        out_specs=(VMEM, VMEM, VMEM),
        scratch_shapes=[pltpu.SemaphoreType.DMA((chips,))],
        compiler_params=pltpu.CompilerParams(vmem_limit_bytes=12 * 2**20),
        cost_estimate=pl.CostEstimate(flops=10**8, bytes_accessed=4 * 10**6, transcendentals=0),
        name="low_rows",
    )(me, slot, down, other, *blocks)


def put_chunks(buf, first, value):
    steps, count = buf.shape[1:3]
    flat = buf.reshape(buf.shape[0], steps, 2 * count, HD)
    wide = value.shape[1]
    for c in range(-(-wide // HD)):
        part = value[:, c * HD : min((c + 1) * HD, wide)]
        if part.shape[1] < HD:
            part = jnp.concatenate([part, jnp.zeros((part.shape[0], HD - part.shape[1]), part.dtype)], axis=1)
        part = part.astype(buf.dtype)
        for t in range(steps):
            flat[first + c, t] = part[t * 2 * count : (t + 1) * 2 * count]


def project_kernel(which, own_ref, other_ref, w_ref, out_ref):
    x = jnp.concatenate([step_rows(x_ref, 0, x_ref.shape[1]) for x_ref in (own_ref, other_ref)], axis=0)
    made = lax.dot_general(w_ref[which], x, CONTRACT_LANES, preferred_element_type=jnp.float32).T
    if which < 2:
        pad = jnp.zeros((made.shape[0], HD // 2), made.dtype)
        put_chunks(out_ref, 0, jnp.concatenate([made, pad] if which == 0 else [pad, made], axis=1))
    else:
        out_ref[...] = made


def project(which, own, other, weight):
    steps, _, chips = own.shape[:3]
    columns = weight.shape[1]
    chunks = jax.ShapeDtypeStruct((-(-columns // HD), 2 * steps, chips, 2, HD), jnp.bfloat16)
    base = jax.ShapeDtypeStruct((4 * steps * chips, columns), jnp.float32)
    return pl.pallas_call(
        functools.partial(project_kernel, which),
        out_shape=chunks if which < 2 else base,
        in_specs=[VMEM, VMEM, VMEM],
        out_specs=VMEM,
        compiler_params=pltpu.CompilerParams(vmem_limit_bytes=16 * 2**20),
        cost_estimate=pl.CostEstimate(flops=5 * 10**8, bytes_accessed=4 * 10**6, transcendentals=0),
        name="project",
    )(own, other, weight)


def update_kernel(me_ref, stored_ref, query_ref, key_ref, base_ref, up_ref, *refs):
    lows, (send_ref, buf, sem) = refs[:-3], refs[-3:]
    half, packed = lows[0].shape
    rank = packed // 2
    rows = 2 * half
    count = send_ref.shape[0]
    low = lows[0][...].astype(jnp.float32)
    for more in lows[1:]:
        low = low + more[...].astype(jnp.float32)
    low = jnp.concatenate([low[:, :rank], low[:, rank:]], axis=0)
    batch = 256 // rank
    spread = jnp.concatenate([low] * batch, axis=1)
    ahead = stored_ref[...] - lax.broadcasted_iota(jnp.int32, (rows, batch * rank), 1) // rank
    total = jnp.zeros(base_ref.shape, jnp.float32)
    for a in range(0, up_ref.shape[0] // rank, batch):
        wide = jnp.where(ahead == a, spread, 0.0).astype(jnp.bfloat16)
        total = total + jnp.dot(wide, up_ref[a * rank : (a + batch) * rank], preferred_element_type=jnp.float32)
    each = query_ref.shape[0]
    buf[: each - 1] = query_ref[: each - 1]
    buf[each - 1] = query_ref[each - 1] + key_ref[0]
    buf[each : 2 * each - 1] = key_ref[1:]
    put_chunks(buf, 2 * each - 1, base_ref[...] + adapter_scale * total)
    core = me_ref[0] % 2
    steps = send_ref.shape[2]
    copies = []
    for half in range(2):
        for chip in range(count // 2):
            part = buf.at[:, half * steps : (half + 1) * steps, chip]
            copies.append(pltpu.make_async_copy(part, send_ref.at[2 * chip + (core ^ half)], sem.at[half, chip]))
    wait_all(start_all(copies))


def update_values(me, stored, query, key, base, up, lows):
    chunks, halves, chips = query.shape[:3]
    return pl.pallas_call(
        update_kernel,
        out_shape=pltpu.HBM((2 * chips, 3 * chunks - 1, halves // 2, 2, HD), query.dtype),
        in_specs=[SMEM] + [VMEM] * (5 + len(lows)),
        out_specs=HBM,
        scratch_shapes=[
            pltpu.VMEM((3 * chunks - 1, halves, chips, 2, HD), query.dtype),
            pltpu.SemaphoreType.DMA((2, chips)),
        ],
        compiler_params=pltpu.CompilerParams(vmem_limit_bytes=8 * 2**20),
        cost_estimate=pl.CostEstimate(flops=3 * 10**8, bytes_accessed=4 * 10**6, transcendentals=0),
        name="update_values",
    )(me, stored, query, key, base, up, *lows)


def attend_kernel(cos_ref, sin_ref, live_ref, pieces_ref, *refs):
    *parts, out_ref, values_buf, kn_ref, vn_ref, sem = refs
    keys_refs, values_refs = parts[: len(parts) // 2], parts[len(parts) // 2 :]
    count, _, steps = pieces_ref.shape[:3]
    rows = 2 * steps
    each = (pieces_ref.shape[1] + 1) // 3
    heads = 2 * out_ref.shape[1] // count
    lanes = heads * HD
    group = rows * HEAD_BLOCK
    chips = range(count // 2)
    early = keys_refs[0].shape[0] // heads
    places = [(0, c) if c < early else (1, c - early) for c in chips]
    fetches = start_all(
        [
            pltpu.make_async_copy(values_refs[half].at[at * heads : (at + 1) * heads], values_buf.at[c], sem.at[c])
            for c, (half, at) in enumerate(places)
        ]
    )
    cosine = cos_ref[...][:rows]
    sine = sin_ref[...][:rows]
    left = lax.broadcasted_iota(jnp.int32, (rows, HD), 1) < HD // 2

    def halves(chip, at):
        return [
            [pieces_ref[2 * chip + core, at + c].reshape(rows, HD).astype(jnp.float32) for c in range(each)]
            for core in range(2)
        ]

    def swapped(parts):
        return [pltpu.roll(x, HD // 2, 1) for x in parts]

    def joined(parts):
        return [jnp.where(left, a, b) for a, b in zip(parts[:-1], parts[1:])]

    def chip_columns(chip, at):
        low, high = halves(chip, at)
        high = swapped(high)
        return low[:-1] + [jnp.where(left, low[-1], high[0])] + joined(high)

    def chip_keys(chip):
        low, high = halves(chip, each - 1)
        low = swapped(low)
        return joined(low) + [jnp.where(left, low[-1], high[0])] + high[1:]

    def rotated(parts):
        return [x * cosine + pltpu.roll(x, HD // 2, 1) * sine for x in parts]

    row_head = lax.broadcasted_iota(jnp.int32, (group, lanes), 0) % HEAD_BLOCK
    lane_head = lax.broadcasted_iota(jnp.int32, (group, lanes), 1) // HD
    own_head = row_head == lane_head
    row_j = lax.broadcasted_iota(jnp.int32, (group, 16), 0) // HEAD_BLOCK
    new_j = lax.broadcasted_iota(jnp.int32, (group, 16), 1)
    new_live = (new_j < rows) & (new_j % 2 == row_j % 2) & (new_j // 2 <= row_j // 2)
    live = jnp.concatenate(
        [
            jnp.broadcast_to(live_ref[j % 2 : j % 2 + 1, :], (HEAD_BLOCK, live_ref.shape[1]))
            for j in range(rows)
        ],
        axis=0,
    )
    live = live > 0
    kn_ref[...] = jnp.zeros_like(kn_ref)
    vn_ref[...] = jnp.zeros_like(vn_ref)
    spreads = []
    for c in chips:
        query = jnp.concatenate(rotated(chip_columns(c, 0)), axis=1)
        kn_ref[c, 0:rows] = jnp.concatenate(rotated(chip_keys(c)), axis=1)
        vn_ref[c, 0:rows] = jnp.concatenate(chip_columns(c, 2 * each - 1), axis=1)
        spread = jnp.concatenate(
            [jnp.broadcast_to(query[j : j + 1], (HEAD_BLOCK, lanes)) for j in range(rows)], axis=0
        )
        spreads.append(jnp.where(own_head, spread, 0.0).astype(jnp.bfloat16))
    scores, fresh = [], []
    for c in chips:
        half, at = places[c]
        keys = jnp.concatenate([keys_refs[half][at * heads + h] for h in range(heads)], axis=1)
        kn = kn_ref[c].astype(jnp.bfloat16)
        scores.append(lax.dot_general(spreads[c], keys, CONTRACT_LANES, preferred_element_type=jnp.float32))
        fresh.append(lax.dot_general(spreads[c], kn, CONTRACT_LANES, preferred_element_type=jnp.float32))
    weights, fresh_weights, totals = [], [], []
    for c in chips:
        old = jnp.where(live, scores[c] * (HD**-0.5), masked_score)
        new = jnp.where(new_live, fresh[c] * (HD**-0.5), masked_score)
        top = jnp.maximum(jnp.max(old, axis=1, keepdims=True), jnp.max(new, axis=1, keepdims=True))
        old = jnp.where(live, jnp.exp(old - top), 0.0)
        new = jnp.where(new_live, jnp.exp(new - top), 0.0)
        totals.append(jnp.sum(old, axis=1, keepdims=True) + jnp.sum(new, axis=1, keepdims=True))
        weights.append(old.astype(jnp.bfloat16))
        fresh_weights.append(new.astype(jnp.bfloat16))
    wait_all(fetches)
    for c in chips:
        values = lanes_of(values_buf[c])
        vn = vn_ref[c].astype(jnp.bfloat16)
        mixed = jnp.dot(weights[c], values, preferred_element_type=jnp.float32)
        mixed = mixed + jnp.dot(fresh_weights[c], vn, preferred_element_type=jnp.float32)
        mixed = jnp.where(own_head, mixed / totals[c], 0.0)
        out = jnp.sum(mixed.reshape(rows, HEAD_BLOCK, lanes), axis=1).astype(out_ref.dtype)
        for t in range(steps):
            for h in range(heads):
                out_ref[t, c * heads + h] = out[2 * t : 2 * t + 2, h * HD : (h + 1) * HD]


def attend(cosine, sine, live, pieces, keys, values):
    count, _, steps = pieces.shape[:3]
    heads, tokens = sum(x.shape[0] for x in keys), keys[0].shape[1]
    chips = count // 2
    per = heads // chips
    return pl.pallas_call(
        attend_kernel,
        out_shape=jax.ShapeDtypeStruct((steps, heads, 2, HD), jnp.bfloat16),
        in_specs=[VMEM] * (4 + len(keys)) + [HBM] * len(values),
        out_specs=VMEM,
        scratch_shapes=[pltpu.VMEM((chips, per, tokens, HD), jnp.bfloat16)]
        + [pltpu.VMEM((chips, 16, per * HD), jnp.float32)] * 2
        + [pltpu.SemaphoreType.DMA((chips,))],
        compiler_params=pltpu.CompilerParams(vmem_limit_bytes=16 * 2**20),
        cost_estimate=pl.CostEstimate(flops=10**9, bytes_accessed=6 * 10**6, transcendentals=0),
        name="attention",
    )(cosine, sine, live, pieces, *keys, *[in_hbm(x) for x in values])


def chip_plan(
    count,
    hidden,
    query_key_value_weight,
    adapter_down_maps,
    adapter_up_maps,
    adapter_storage_row,
    request_adapter,
    lengths,
    request_page_table,
    key_value_pool,
):
    me = lax.axis_index("replica")
    steps, req_dev, width = hidden.shape
    heads = width // HD
    holder_count, rank, _ = adapter_down_maps.shape
    pool_pages, page_len = key_value_pool.shape[:2]
    adapter_count = adapter_storage_row.shape[0]

    tokens = pool_pages * page_len
    pool = key_value_pool.reshape(tokens, 2, heads, HD).transpose(0, 2, 1, 3)

    stored = jnp.sum(
        jnp.where(
            request_adapter[:, None] == jnp.arange(adapter_count, dtype=jnp.int32)[None, :],
            adapter_storage_row[None, :],
            0,
        ),
        axis=1,
    )
    first, here, stored = lax.optimization_barrier((me * req_dev, me.astype(jnp.int32).reshape(1), stored))
    slot, column = index_work(here, holder_count, stored, steps)

    other_maps = trade(adapter_down_maps, 1, count)
    held = {0: hidden}
    held.update({m: trade(hidden, m, count) for m in range(4, count, 4)})
    _, lengths, request_page_table = lax.optimization_barrier((held[4], lengths, request_page_table))
    cosine, sine = rotation_rows(lengths, first, req_dev, steps)
    live = live_lanes(lengths, first, request_page_table, tokens, page_len)
    held.update({k | 2: trade(v, 2, count) for k, v in list(held.items())})
    ready = [0, 2, 4, 6, *range(8, count, 4)]
    held.update(zip(ready, lax.optimization_barrier([held[k] for k in ready])))
    held.update({k | 1: trade(v, 1, count) for k, v in list(held.items())})
    blocks = [held[k].reshape(steps, req_dev, heads, HD).transpose(0, 2, 1, 3) for k in range(count)]
    blocks[0] = in_hbm(blocks[0])
    own, near, far = low_of(here, blocks[0::2], slot, adapter_down_maps, other_maps)
    *late, near = lax.optimization_barrier(blocks[1::2] + [near])
    other = line_rows(here, late)
    weight = query_key_value_weight.transpose(0, 2, 1)
    arrived = [trade(far, 1, count), trade(near, 2, count), trade(far, 3, count)]
    query, key = project(0, own, other, weight), project(1, own, other, weight)
    arrived, query, key, pool = lax.optimization_barrier((arrived, query, key, pool))
    low = (near + arrived[0]) + (arrived[1] + arrived[2])
    arrived = [trade(low, m, count) for m in range(4, count, 4)]
    base = project(2, own, other, weight)
    arrived, base = lax.optimization_barrier((arrived, base))
    send = update_values(here, column, query, key, base, adapter_up_maps.reshape(adapter_count * rank, -1), [low, *arrived])
    send, pool = lax.optimization_barrier((send, pool))
    keys, values = cache_by_head(pool, 0, heads)
    pieces = lax.all_to_all(send, "replica", split_axis=0, concat_axis=0, tiled=True)

    out = attend(cosine, sine, live, pieces, [keys], [values])
    return out.transpose(0, 2, 1, 3).reshape(steps, req_dev, width)


def per_device(replicas, *arrays):
    columns = arrays[1].shape[2]
    whole_heads = replicas % 4 == 0 and (2 * columns) % HD == 0 and columns % HD == HD // 2
    plan = chip_plan if whole_heads and arrays[0].shape[1] == 2 else general_plan
    return plan(replicas, *arrays)


def solution(mesh):
    placed = (
        P(None, ("groups", "replica"), None),
        P(None, None, "replica"),
        P("replica", None, None),
        P(None, None, "replica"),
        P(),
        P("groups"),
        P("groups"),
        P(("groups", "replica"), None),
        P(("groups", "replica"), None, None, None),
    )
    return jax.shard_map(
        functools.partial(per_device, mesh.shape["replica"]),
        mesh=mesh,
        in_specs=placed,
        out_specs=P(None, ("groups", "replica"), None),
        check_vma=False,
    )
```

```python
import functools

import jax
import jax.numpy as jnp
from jax import lax
from jax.experimental import pallas as pl
from jax.experimental.pallas import tpu as pltpu
from jax.sharding import PartitionSpec as P

HD = 128
ROWS = 8
HEAD_BLOCK = 8

adapter_scale = 2.0
masked_score = -1e30


def attention_kernel(steps, req_dev, q_ref, k_ref, v_ref, cos_ref, sin_ref, live_ref, kv_ref, out_ref, kn_ref, vn_ref):
    rows = steps * req_dev
    width = q_ref.shape[1]
    lanes = HEAD_BLOCK * HD
    group = rows * HEAD_BLOCK
    cosine = cos_ref[...]
    sine = sin_ref[...]

    def rotated(x):
        pieces = []
        for h in range(HEAD_BLOCK):
            head = x[:, h * HD : (h + 1) * HD]
            pieces.append(head * cosine + pltpu.roll(head, HD // 2, 1) * sine)
        return jnp.concatenate(pieces, axis=1)

    row_head = lax.broadcasted_iota(jnp.int32, (group, lanes), 0) % HEAD_BLOCK
    lane_head = lax.broadcasted_iota(jnp.int32, (group, lanes), 1) // HD
    own_head = row_head == lane_head
    row_j = lax.broadcasted_iota(jnp.int32, (group, 16), 0) // HEAD_BLOCK
    new_j = lax.broadcasted_iota(jnp.int32, (group, 16), 1)
    new_live = (new_j < rows) & (new_j % req_dev == row_j % req_dev) & (new_j // req_dev <= row_j // req_dev)
    live_all = live_ref[...]
    live = jnp.concatenate(
        [
            jnp.broadcast_to(live_all[j % req_dev : j % req_dev + 1], (HEAD_BLOCK, live_all.shape[1]))
            for j in range(rows)
        ],
        axis=0,
    )
    live = live > 0
    kn_ref[...] = jnp.zeros_like(kn_ref)
    vn_ref[...] = jnp.zeros_like(vn_ref)
    contract_lanes = (((1,), (1,)), ((), ()))
    for c in range(width // lanes):
        cols = slice(c * lanes, (c + 1) * lanes)
        query = rotated(q_ref[:, cols].astype(jnp.float32))
        key_new = rotated(k_ref[:, cols].astype(jnp.float32))
        kn_ref[0:8] = key_new
        vn_ref[0:8] = v_ref[:, cols].astype(jnp.float32)
        kn = kn_ref[...].astype(jnp.bfloat16)
        vn = vn_ref[...].astype(jnp.bfloat16)
        spread = jnp.concatenate(
            [jnp.broadcast_to(query[j : j + 1], (HEAD_BLOCK, lanes)) for j in range(rows)], axis=0
        )
        spread = jnp.where(own_head, spread, 0.0).astype(jnp.bfloat16)
        kv = kv_ref[:, cols]
        scores = lax.dot_general(spread, kv, contract_lanes, preferred_element_type=jnp.float32) * (HD**-0.5)
        scores = jnp.where(live, scores, masked_score)
        fresh = lax.dot_general(spread, kn, contract_lanes, preferred_element_type=jnp.float32) * (HD**-0.5)
        fresh = jnp.where(new_live, fresh, masked_score)
        top = jnp.maximum(jnp.max(scores, axis=1, keepdims=True), jnp.max(fresh, axis=1, keepdims=True))
        weights = jnp.where(live, jnp.exp(scores - top), 0.0)
        fresh = jnp.where(new_live, jnp.exp(fresh - top), 0.0)
        totals = jnp.sum(weights, axis=1, keepdims=True) + jnp.sum(fresh, axis=1, keepdims=True)
        weights = pltpu.roll(weights, 1, 1).astype(jnp.bfloat16)
        mixed = jnp.dot(weights, kv, preferred_element_type=jnp.float32)
        mixed = mixed + jnp.dot(fresh.astype(jnp.bfloat16), vn, preferred_element_type=jnp.float32)
        mixed = jnp.where(own_head, mixed / totals, 0.0)
        out = jnp.sum(mixed.reshape(rows, HEAD_BLOCK, lanes), axis=1)
        out_ref[:, cols] = out.astype(out_ref.dtype)


def attention(steps, req_dev, q, k, v, cosine, sine, live, kv):
    rows = steps * req_dev
    width = q.shape[1]
    vmem = pl.BlockSpec(memory_space=pltpu.VMEM)
    return pl.pallas_call(
        functools.partial(attention_kernel, steps, req_dev),
        out_shape=jax.ShapeDtypeStruct((rows, width), jnp.bfloat16),
        in_specs=[vmem] * 7,
        out_specs=vmem,
        scratch_shapes=[pltpu.VMEM((16, HEAD_BLOCK * HD), jnp.float32)] * 2,
        compiler_params=pltpu.CompilerParams(vmem_limit_bytes=32 * 2**20),
        cost_estimate=pl.CostEstimate(flops=10**9, bytes_accessed=6 * 10**6, transcendentals=0),
        name="attention",
    )(q, k, v, cosine, sine, live, kv)


def rotation(my_lengths, steps):
    rows = steps * my_lengths.shape[0]
    positions = (my_lengths[None, :] + jnp.arange(steps, dtype=jnp.int32)[:, None]).reshape(rows)
    positions = jnp.pad(positions, (0, ROWS - rows))
    half = HD // 2
    frequency = jnp.exp(jnp.arange(half, dtype=jnp.float32) * (-2.0 * jnp.log(10000.0) / HD))
    angles = positions.astype(jnp.float32)[:, None] * frequency[None, :]
    cosine = jnp.cos(angles)
    sine = jnp.sin(angles)
    cosine = jnp.concatenate([cosine, cosine], axis=1)
    sine = jnp.concatenate([-sine, sine], axis=1)
    return cosine, sine


def live_tokens(my_lengths, request_page_table, pool_pages, page_len):
    pages = jnp.arange(pool_pages, dtype=jnp.int32)
    max_pages = request_page_table.shape[1]
    place = jnp.max(
        jnp.where(
            request_page_table[:, :, None] == pages[None, None, :],
            jnp.arange(max_pages, dtype=jnp.int32)[None, :, None],
            -1,
        ),
        axis=1,
    )
    token = place[:, :, None] * page_len + jnp.arange(page_len, dtype=jnp.int32)[None, None, :]
    return (place[:, :, None] >= 0) & (token < my_lengths[:, None, None])


def live_rows(my_lengths, request_page_table, pool_pages, page_len):
    alive = live_tokens(my_lengths, request_page_table, pool_pages, page_len)
    live = jnp.stack([alive, jnp.zeros_like(alive)], axis=-1).astype(jnp.int32)
    return live.reshape(request_page_table.shape[0], pool_pages * page_len * 2)


def general_plan(
    replicas,
    hidden,
    query_key_value_weight,
    adapter_down_maps,
    adapter_up_maps,
    adapter_storage_row,
    request_adapter,
    lengths,
    request_page_table,
    key_value_pool,
):
    my_index = lax.axis_index("replica")
    steps, req_dev, width = hidden.shape
    rows = steps * req_dev
    columns = query_key_value_weight.shape[2]
    holder_count, rank, _ = adapter_down_maps.shape
    pool_pages, page_len = key_value_pool.shape[:2]
    adapter_count = adapter_storage_row.shape[0]
    chips = replicas // 2
    total = replicas * ROWS

    block = jnp.pad(hidden.reshape(rows, width), ((0, ROWS - rows), (0, 0)))
    same_core = [[2 * chip + core for chip in range(chips)] for core in range(2)]
    mine = lax.all_to_all(
        jnp.broadcast_to(block[None], (chips, ROWS, width)),
        "replica",
        split_axis=0,
        concat_axis=0,
        axis_index_groups=same_core,
        tiled=True,
    )
    other = lax.ppermute(mine, "replica", [(i, i ^ 1) for i in range(replicas)])
    first = my_index % 2 == 0
    gathered = jnp.stack([jnp.where(first, mine, other), jnp.where(first, other, mine)])
    gathered = gathered.reshape(total, width)

    stored_rows = jnp.sum(
        jnp.where(
            request_adapter[:, None] == jnp.arange(adapter_count, dtype=jnp.int32)[None, :],
            adapter_storage_row[None, :],
            0,
        ),
        axis=1,
    )
    by_block = stored_rows.reshape(chips, 2, 1, req_dev).transpose(1, 0, 2, 3)
    by_block = jnp.broadcast_to(by_block, (2, chips, steps, req_dev)).reshape(2, chips, rows)
    row_stored = jnp.pad(by_block, ((0, 0), (0, 0), (0, ROWS - rows)), constant_values=-1).reshape(total)

    down = jnp.einsum("nd,hfd->nhf", gathered, adapter_down_maps, preferred_element_type=jnp.float32)
    slots = my_index * holder_count + jnp.arange(holder_count, dtype=jnp.int32)
    own = row_stored[:, None] == slots[None, :]
    low = jnp.sum(jnp.where(own[:, :, None], down, 0.0), axis=1).astype(jnp.bfloat16)
    low = jnp.concatenate([low[: total // 2], low[total // 2 :]], axis=1)
    low = lax.all_to_all(
        jnp.broadcast_to(low[None], (replicas,) + low.shape), "replica", split_axis=0, concat_axis=0, tiled=True
    )
    low = jnp.sum(low.astype(jnp.float32), axis=0)
    low = jnp.concatenate([low[:, :rank], low[:, rank:]], axis=0)

    projected = jnp.einsum("nd,idc->nic", gathered, query_key_value_weight, preferred_element_type=jnp.float32)

    def update(first_adapter, maps):
        held = maps.shape[0]
        which = first_adapter + jnp.arange(held, dtype=jnp.int32)
        wide = jnp.where((row_stored[:, None] == which[None, :])[:, :, None], low[:, None, :], 0.0)
        return jnp.dot(
            wide.astype(jnp.bfloat16).reshape(total, held * rank),
            maps.reshape(held * rank, columns),
            preferred_element_type=jnp.float32,
        )

    step_adapters = 64
    if adapter_count <= step_adapters:
        updated = update(0, adapter_up_maps)
    else:
        updated = lax.fori_loop(
            0,
            adapter_count // step_adapters,
            lambda i, sofar: sofar
            + update(
                i * step_adapters,
                lax.dynamic_slice_in_dim(adapter_up_maps, i * step_adapters, step_adapters, 0),
            ),
            jnp.zeros((total, columns), jnp.float32),
        )
    value = projected[:, 2] + adapter_scale * updated
    combined = jnp.concatenate([projected[:, 0], projected[:, 1], value], axis=1).astype(jnp.bfloat16)
    combined = combined.reshape(2, chips, ROWS, 3 * columns).transpose(1, 0, 2, 3)
    combined = combined.reshape(replicas, ROWS, 3 * columns)
    arrived = lax.all_to_all(combined, "replica", split_axis=0, concat_axis=0, tiled=True)
    arrived = arrived.reshape(replicas, ROWS, 3, columns).transpose(2, 1, 0, 3).reshape(3, ROWS, width)

    my_lengths = lax.dynamic_slice_in_dim(lengths, my_index * req_dev, req_dev)
    cosine, sine = rotation(my_lengths, steps)
    live = live_rows(my_lengths, request_page_table, pool_pages, page_len)
    kv = key_value_pool.reshape(pool_pages * page_len * 2, width)
    out = attention(steps, req_dev, arrived[0], arrived[1], arrived[2], cosine, sine, live, kv)
    return out.reshape(steps, req_dev, width)


def rotation_rows(lengths, first, req_dev, steps):
    row = jnp.arange(ROWS, dtype=jnp.int32)
    wanted = first + row % req_dev
    chosen = jnp.where(wanted[:, None] == jnp.arange(lengths.shape[0], dtype=jnp.int32)[None, :], lengths[None, :], 0)
    positions = jnp.sum(chosen, axis=1, keepdims=True) + (row // req_dev)[:, None]
    lane = jnp.arange(HD, dtype=jnp.int32)
    frequency = jnp.exp((lane % (HD // 2)).astype(jnp.float32) * (-2.0 * jnp.log(10000.0) / HD))
    angles = positions.astype(jnp.float32) * frequency[None, :]
    return jnp.cos(angles), jnp.where(lane < HD // 2, -1.0, 1.0)[None, :] * jnp.sin(angles)


def live_lanes(lengths, first, request_page_table, tokens, page_len):
    req_dev, max_pages = request_page_table.shape
    wanted = first + jnp.arange(req_dev, dtype=jnp.int32)
    chosen = jnp.where(wanted[:, None] == jnp.arange(lengths.shape[0], dtype=jnp.int32)[None, :], lengths[None, :], 0)
    lane = jnp.arange(tokens, dtype=jnp.int32)
    page = jnp.arange(max_pages, dtype=jnp.int32)
    place = jnp.max(
        jnp.where(request_page_table[:, :, None] == (lane // page_len)[None, None, :], page[None, :, None], -1),
        axis=1,
    )
    token = place * page_len + (lane % page_len)[None, :]
    return ((place >= 0) & (token < jnp.sum(chosen, axis=1, keepdims=True))).astype(jnp.int32)


def trade(value, mask, count):
    return lax.ppermute(value, "replica", [(i, i ^ mask) for i in range(count)])


CONTRACT_LANES = (((1,), (1,)), ((), ()))


def in_hbm(x):
    return pltpu.with_memory_space_constraint(x, pltpu.HBM)


VMEM = pl.BlockSpec(memory_space=pltpu.VMEM)
HBM = pl.BlockSpec(memory_space=pltpu.HBM)
SMEM = pl.BlockSpec(memory_space=pltpu.SMEM)
ANY = pl.BlockSpec(memory_space=pl.ANY)


def start_all(copies):
    for copy in copies:
        copy.start()
    return copies


def wait_all(copies):
    for copy in copies:
        copy.wait()


CACHE_SECTION = 10
CACHE_AHEAD = 4
CACHE_TOKENS = 128


def cache_kernel(first, pool_ref, keys_ref, values_ref, raw, values, sem, out_sem):
    heads, tokens = raw.shape[:2]
    copies = [pltpu.make_async_copy(pool_ref.at[:, first + h], raw.at[h], sem.at[h]) for h in range(heads)]
    start_all(copies[: CACHE_AHEAD * CACHE_SECTION])
    rows = raw.reshape(heads, 2 * tokens, HD)
    block = min(tokens, CACHE_TOKENS)
    to = lax.broadcasted_iota(jnp.int32, (2 * block, 2 * block), 0)
    source = lax.broadcasted_iota(jnp.int32, (2 * block, 2 * block), 1)
    wanted = jnp.where(to < block, 2 * to, 2 * (to - block) + 1)
    pick = jnp.where(source == wanted, 1.0, 0.0).astype(jnp.bfloat16)
    sent = []
    part = CACHE_SECTION
    for p in range(heads // part):
        wait_all(copies[p * part : (p + 1) * part])
        start_all(copies[(p + CACHE_AHEAD) * part : (p + CACHE_AHEAD + 1) * part])
        for h in range(p * part, (p + 1) * part, 2):
            for first_token in range(0, tokens, block):
                raw_rows = slice(2 * first_token, 2 * (first_token + block))
                both = jnp.concatenate([rows[h, raw_rows], rows[h + 1, raw_rows]], axis=1)
                made = jnp.dot(pick, both, preferred_element_type=jnp.float32).astype(jnp.bfloat16)
                span = slice(first_token, first_token + block)
                for i in range(2):
                    keys_ref[h + i, span] = made[:block, i * HD : (i + 1) * HD]
                    values[h + i, span] = made[block:, i * HD : (i + 1) * HD]
        span = slice(p * part, (p + 1) * part)
        sent += start_all([pltpu.make_async_copy(values.at[span], values_ref.at[span], out_sem.at[p])])
    wait_all(sent)


def cache_by_head(pool, first, heads):
    tokens = pool.shape[0]
    return pl.pallas_call(
        functools.partial(cache_kernel, first),
        out_shape=(
            jax.ShapeDtypeStruct((heads, tokens, HD), pool.dtype),
            pltpu.HBM((heads, tokens, HD), pool.dtype),
        ),
        in_specs=[HBM],
        out_specs=(VMEM, HBM),
        scratch_shapes=[
            pltpu.VMEM((heads, tokens, 2, HD), pool.dtype),
            pltpu.VMEM((heads, tokens, HD), pool.dtype),
            pltpu.SemaphoreType.DMA((heads,)),
            pltpu.SemaphoreType.DMA((heads // CACHE_SECTION,)),
        ],
        compiler_params=pltpu.CompilerParams(vmem_limit_bytes=12 * 2**20),
        cost_estimate=pl.CostEstimate(flops=0, bytes_accessed=12 * 10**6, transcendentals=0),
        name="cache_by_head",
    )(in_hbm(pool))


def lanes_of(x):
    return jnp.concatenate([x[c] for c in range(x.shape[0])], axis=1)


def step_rows(x, first, chunks):
    steps, _, count = x.shape[:3]
    flat = x.reshape(steps, x.shape[1], 2 * count, HD)
    return jnp.concatenate(
        [jnp.concatenate([flat[t, c] for c in range(first, first + chunks)], axis=1) for t in range(steps)], axis=0
    )


def pack_kernel(*refs):
    blocks, (out_ref, sem) = refs[:-2], refs[-2:]
    wait_all(
        start_all([pltpu.make_async_copy(block, out_ref.at[i], sem.at[i]) for i, block in enumerate(blocks)])
    )


def packed(blocks):
    return pl.pallas_call(
        pack_kernel,
        out_shape=jax.ShapeDtypeStruct((len(blocks),) + blocks[0].shape, blocks[0].dtype),
        in_specs=[ANY] * len(blocks),
        out_specs=VMEM,
        scratch_shapes=[pltpu.SemaphoreType.DMA((len(blocks),))],
        compiler_params=pltpu.CompilerParams(vmem_limit_bytes=2 * 2**20),
        cost_estimate=pl.CostEstimate(flops=0, bytes_accessed=10**6, transcendentals=0),
        name="pack_blocks",
    )(*blocks)


def index_kernel(me_ref, stored_ref, slot_ref, column_ref):
    requests = stored_ref.shape[1]
    steps = slot_ref.shape[1] // requests
    row = jnp.concatenate([stored_ref[...]] * steps, axis=1)
    slot_ref[...] = row - me_ref[0]
    wide = jnp.concatenate([row, jnp.zeros((1, HD - row.shape[1]), row.dtype)], axis=1)
    column_ref[...] = jnp.broadcast_to(wide.astype(jnp.float32), (HD, HD)).T[: row.shape[1], :1].astype(jnp.int32)


def index_work(first, stored, steps):
    rows = stored.shape[0] * steps
    return pl.pallas_call(
        index_kernel,
        out_shape=(jax.ShapeDtypeStruct((1, rows), jnp.int32), jax.ShapeDtypeStruct((rows, 1), jnp.int32)),
        in_specs=[SMEM, VMEM],
        out_specs=(VMEM, VMEM),
        compiler_params=pltpu.CompilerParams(vmem_limit_bytes=2 * 2**20),
        cost_estimate=pl.CostEstimate(flops=2 * 10**10, bytes_accessed=10**4, transcendentals=0),
        name="index_work",
    )(first, stored[None, :])


def low_kernel(places, packs, me_ref, slot_ref, down_ref, pack_ref, *refs):
    blocks, (x_ref, low_ref, sem) = refs[: len(places)], refs[len(places) :]
    me = me_ref[0]
    holders, rank, width = down_ref.shape
    sources = list(zip(places, blocks)) + [(k, pack_ref.at[i]) for i, k in enumerate(packs)]
    wait_all(
        start_all([pltpu.make_async_copy(block, x_ref.at[:, :, me ^ k], sem.at[k]) for k, block in sources])
    )
    x = step_rows(x_ref, 0, x_ref.shape[1])
    rows = x.shape[0]
    made = lax.dot_general(
        down_ref.reshape(holders * rank, width)[...], x, CONTRACT_LANES, preferred_element_type=jnp.float32
    )
    slot = slot_ref[...]
    low = jnp.zeros((rank, rows), jnp.float32)
    for h in range(holders):
        low = low + jnp.where(slot == h, made[h * rank : (h + 1) * rank], 0.0)
    low = low.T
    low_ref[...] = jnp.concatenate([low[: rows // 2], low[rows // 2 :]], axis=1).astype(low_ref.dtype)


def low_of(me, blocks, packs, pack, slot, down):
    count = len(blocks) + len(packs)
    steps, chunks = blocks[0].shape[:2]
    rows = count * steps * 2
    rank = down.shape[1]
    return pl.pallas_call(
        functools.partial(low_kernel, tuple(blocks), packs),
        out_shape=(
            jax.ShapeDtypeStruct((steps, chunks, count, 2, HD), jnp.bfloat16),
            jax.ShapeDtypeStruct((rows // 2, 2 * rank), jnp.bfloat16),
        ),
        in_specs=[SMEM, VMEM, VMEM, ANY] + [ANY] * len(blocks),
        out_specs=(VMEM, VMEM),
        scratch_shapes=[pltpu.SemaphoreType.DMA((count,))],
        compiler_params=pltpu.CompilerParams(vmem_limit_bytes=12 * 2**20),
        cost_estimate=pl.CostEstimate(flops=10**8, bytes_accessed=4 * 10**6, transcendentals=0),
        name="low_rows",
    )(me, slot, down, pack, *blocks.values())


def put_chunks(buf, first, value):
    steps, count = buf.shape[1:3]
    flat = buf.reshape(buf.shape[0], steps, 2 * count, HD)
    wide = value.shape[1]
    for c in range(-(-wide // HD)):
        part = value[:, c * HD : min((c + 1) * HD, wide)]
        if part.shape[1] < HD:
            part = jnp.concatenate([part, jnp.zeros((part.shape[0], HD - part.shape[1]), part.dtype)], axis=1)
        part = part.astype(buf.dtype)
        for t in range(steps):
            flat[first + c, t] = part[t * 2 * count : (t + 1) * 2 * count]


def project_kernel(which, x_ref, w_ref, out_ref):
    x = step_rows(x_ref, 0, x_ref.shape[1])
    made = lax.dot_general(w_ref[which], x, CONTRACT_LANES, preferred_element_type=jnp.float32).T
    if which < 2:
        pad = jnp.zeros((made.shape[0], HD // 2), made.dtype)
        put_chunks(out_ref, 0, jnp.concatenate([made, pad] if which == 0 else [pad, made], axis=1))
    else:
        out_ref[...] = made


def project(which, x, weight):
    steps, _, count = x.shape[:3]
    columns = weight.shape[1]
    chunks = jax.ShapeDtypeStruct((-(-columns // HD), steps, count, 2, HD), jnp.bfloat16)
    base = jax.ShapeDtypeStruct((2 * steps * count, columns), jnp.float32)
    return pl.pallas_call(
        functools.partial(project_kernel, which),
        out_shape=chunks if which < 2 else base,
        in_specs=[VMEM, VMEM],
        out_specs=VMEM,
        compiler_params=pltpu.CompilerParams(vmem_limit_bytes=16 * 2**20),
        cost_estimate=pl.CostEstimate(flops=5 * 10**8, bytes_accessed=4 * 10**6, transcendentals=0),
        name="project",
    )(x, weight)


def update_kernel(stored_ref, query_ref, key_ref, base_ref, up_ref, *refs):
    lows, (send_ref, buf, sem) = refs[:-3], refs[-3:]
    half, packed = lows[0].shape
    rank = packed // 2
    rows = 2 * half
    count = send_ref.shape[0]
    low = lows[0][...].astype(jnp.float32)
    for more in lows[1:]:
        low = low + more[...].astype(jnp.float32)
    low = jnp.concatenate([low[:, :rank], low[:, rank:]], axis=0)
    batch = 256 // rank
    spread = jnp.concatenate([low] * batch, axis=1)
    ahead = stored_ref[...] - lax.broadcasted_iota(jnp.int32, (rows, batch * rank), 1) // rank
    total = jnp.zeros(base_ref.shape, jnp.float32)
    for a in range(0, up_ref.shape[0] // rank, batch):
        wide = jnp.where(ahead == a, spread, 0.0).astype(jnp.bfloat16)
        total = total + jnp.dot(wide, up_ref[a * rank : (a + batch) * rank], preferred_element_type=jnp.float32)
    each = query_ref.shape[0]
    buf[: each - 1] = query_ref[: each - 1]
    buf[each - 1] = query_ref[each - 1] + key_ref[0]
    buf[each : 2 * each - 1] = key_ref[1:]
    put_chunks(buf, 2 * each - 1, base_ref[...] + adapter_scale * total)
    wait_all(
        start_all([pltpu.make_async_copy(buf.at[:, :, k], send_ref.at[k], sem.at[k]) for k in range(count)])
    )


def update_values(stored, query, key, base, up, lows):
    chunks, steps, count = query.shape[:3]
    return pl.pallas_call(
        update_kernel,
        out_shape=pltpu.HBM((count, 3 * chunks - 1, steps, 2, HD), query.dtype),
        in_specs=[VMEM] * (5 + len(lows)),
        out_specs=HBM,
        scratch_shapes=[
            pltpu.VMEM((3 * chunks - 1, steps, count, 2, HD), query.dtype),
            pltpu.SemaphoreType.DMA((count,)),
        ],
        compiler_params=pltpu.CompilerParams(vmem_limit_bytes=8 * 2**20),
        cost_estimate=pl.CostEstimate(flops=3 * 10**8, bytes_accessed=4 * 10**6, transcendentals=0),
        name="update_values",
    )(stored, query, key, base, up, *lows)


def attend_kernel(cos_ref, sin_ref, live_ref, pieces_ref, *refs):
    *parts, out_ref, values_buf, kn_ref, vn_ref, sem = refs
    keys_refs, values_refs = parts[: len(parts) // 2], parts[len(parts) // 2 :]
    count, _, steps = pieces_ref.shape[:3]
    rows = 2 * steps
    each = (pieces_ref.shape[1] + 1) // 3
    heads = 2 * out_ref.shape[1] // count
    lanes = heads * HD
    group = rows * HEAD_BLOCK
    chips = range(count // 2)
    early = keys_refs[0].shape[0] // heads
    places = [(0, c) if c < early else (1, c - early) for c in chips]
    fetches = start_all(
        [
            pltpu.make_async_copy(values_refs[half].at[at * heads : (at + 1) * heads], values_buf.at[c], sem.at[c])
            for c, (half, at) in enumerate(places)
        ]
    )
    cosine = cos_ref[...][:rows]
    sine = sin_ref[...][:rows]
    left = lax.broadcasted_iota(jnp.int32, (rows, HD), 1) < HD // 2

    def halves(chip, at):
        return [
            [pieces_ref[2 * chip + core, at + c].reshape(rows, HD).astype(jnp.float32) for c in range(each)]
            for core in range(2)
        ]

    def swapped(parts):
        return [pltpu.roll(x, HD // 2, 1) for x in parts]

    def joined(parts):
        return [jnp.where(left, a, b) for a, b in zip(parts[:-1], parts[1:])]

    def chip_columns(chip, at):
        low, high = halves(chip, at)
        high = swapped(high)
        return low[:-1] + [jnp.where(left, low[-1], high[0])] + joined(high)

    def chip_keys(chip):
        low, high = halves(chip, each - 1)
        low = swapped(low)
        return joined(low) + [jnp.where(left, low[-1], high[0])] + high[1:]

    def rotated(parts):
        return [x * cosine + pltpu.roll(x, HD // 2, 1) * sine for x in parts]

    row_head = lax.broadcasted_iota(jnp.int32, (group, lanes), 0) % HEAD_BLOCK
    lane_head = lax.broadcasted_iota(jnp.int32, (group, lanes), 1) // HD
    own_head = row_head == lane_head
    row_j = lax.broadcasted_iota(jnp.int32, (group, 16), 0) // HEAD_BLOCK
    new_j = lax.broadcasted_iota(jnp.int32, (group, 16), 1)
    new_live = (new_j < rows) & (new_j % 2 == row_j % 2) & (new_j // 2 <= row_j // 2)
    live = jnp.concatenate(
        [
            jnp.broadcast_to(live_ref[j % 2 : j % 2 + 1, :], (HEAD_BLOCK, live_ref.shape[1]))
            for j in range(rows)
        ],
        axis=0,
    )
    live = live > 0
    kn_ref[...] = jnp.zeros_like(kn_ref)
    vn_ref[...] = jnp.zeros_like(vn_ref)
    spreads = []
    for c in chips:
        query = jnp.concatenate(rotated(chip_columns(c, 0)), axis=1)
        kn_ref[c, 0:rows] = jnp.concatenate(rotated(chip_keys(c)), axis=1)
        vn_ref[c, 0:rows] = jnp.concatenate(chip_columns(c, 2 * each - 1), axis=1)
        spread = jnp.concatenate(
            [jnp.broadcast_to(query[j : j + 1], (HEAD_BLOCK, lanes)) for j in range(rows)], axis=0
        )
        spreads.append(jnp.where(own_head, spread, 0.0).astype(jnp.bfloat16))
    scores, fresh = [], []
    for c in chips:
        half, at = places[c]
        keys = jnp.concatenate([keys_refs[half][at * heads + h] for h in range(heads)], axis=1)
        kn = kn_ref[c].astype(jnp.bfloat16)
        scores.append(lax.dot_general(spreads[c], keys, CONTRACT_LANES, preferred_element_type=jnp.float32))
        fresh.append(lax.dot_general(spreads[c], kn, CONTRACT_LANES, preferred_element_type=jnp.float32))
    weights, fresh_weights, totals = [], [], []
    for c in chips:
        old = jnp.where(live, scores[c] * (HD**-0.5), masked_score)
        new = jnp.where(new_live, fresh[c] * (HD**-0.5), masked_score)
        top = jnp.maximum(jnp.max(old, axis=1, keepdims=True), jnp.max(new, axis=1, keepdims=True))
        old = jnp.where(live, jnp.exp(old - top), 0.0)
        new = jnp.where(new_live, jnp.exp(new - top), 0.0)
        totals.append(jnp.sum(old, axis=1, keepdims=True) + jnp.sum(new, axis=1, keepdims=True))
        weights.append(old.astype(jnp.bfloat16))
        fresh_weights.append(new.astype(jnp.bfloat16))
    for c in chips:
        fetches[c].wait()
        values = lanes_of(values_buf[c])
        vn = vn_ref[c].astype(jnp.bfloat16)
        mixed = jnp.dot(weights[c], values, preferred_element_type=jnp.float32)
        mixed = mixed + jnp.dot(fresh_weights[c], vn, preferred_element_type=jnp.float32)
        mixed = jnp.where(own_head, mixed / totals[c], 0.0)
        out = jnp.sum(mixed.reshape(rows, HEAD_BLOCK, lanes), axis=1).astype(out_ref.dtype)
        for t in range(steps):
            for h in range(heads):
                out_ref[t, c * heads + h] = out[2 * t : 2 * t + 2, h * HD : (h + 1) * HD]


def attend(cosine, sine, live, pieces, keys, values):
    count, _, steps = pieces.shape[:3]
    heads, tokens = sum(x.shape[0] for x in keys), keys[0].shape[1]
    chips = count // 2
    per = heads // chips
    return pl.pallas_call(
        attend_kernel,
        out_shape=jax.ShapeDtypeStruct((steps, heads, 2, HD), jnp.bfloat16),
        in_specs=[VMEM] * (4 + len(keys)) + [HBM] * len(values),
        out_specs=VMEM,
        scratch_shapes=[pltpu.VMEM((chips, per, tokens, HD), jnp.bfloat16)]
        + [pltpu.VMEM((chips, 16, per * HD), jnp.float32)] * 2
        + [pltpu.SemaphoreType.DMA((chips,))],
        compiler_params=pltpu.CompilerParams(vmem_limit_bytes=16 * 2**20),
        cost_estimate=pl.CostEstimate(flops=10**9, bytes_accessed=6 * 10**6, transcendentals=0),
        name="attention",
    )(cosine, sine, live, pieces, *keys, *[in_hbm(x) for x in values])


def chip_plan(
    count,
    hidden,
    query_key_value_weight,
    adapter_down_maps,
    adapter_up_maps,
    adapter_storage_row,
    request_adapter,
    lengths,
    request_page_table,
    key_value_pool,
):
    me = lax.axis_index("replica")
    steps, req_dev, width = hidden.shape
    heads = width // HD
    holder_count, rank, _ = adapter_down_maps.shape
    pool_pages, page_len = key_value_pool.shape[:2]
    adapter_count = adapter_storage_row.shape[0]

    tokens = pool_pages * page_len
    pool = key_value_pool.reshape(tokens, 2, heads, HD).transpose(0, 2, 1, 3)

    stored = jnp.sum(
        jnp.where(
            request_adapter[:, None] == jnp.arange(adapter_count, dtype=jnp.int32)[None, :],
            adapter_storage_row[None, :],
            0,
        ),
        axis=1,
    )
    first, slots, here, stored = lax.optimization_barrier(
        (me * req_dev, (me * holder_count).astype(jnp.int32).reshape(1), me.astype(jnp.int32).reshape(1), stored)
    )
    slot, column = index_work(slots, stored, steps)

    held = {0: hidden}
    held.update({m: trade(hidden, m, count) for m in range(4, count, 4)})
    _, lengths, request_page_table = lax.optimization_barrier((held[4], lengths, request_page_table))
    cosine, sine = rotation_rows(lengths, first, req_dev, steps)
    live = live_lanes(lengths, first, request_page_table, tokens, page_len)
    held.update({k | 2: trade(v, 2, count) for k, v in list(held.items())})
    held = {k: v.reshape(steps, req_dev, heads, HD).transpose(0, 2, 1, 3) for k, v in held.items()}
    line = tuple(range(0, count, 4))
    *share, held[2], held[6] = lax.optimization_barrier([held[k] for k in line] + [held[2], held[6]])
    pack = trade(packed(share), 1, count)
    held.update({k | 1: trade(held[k], 1, count) for k in range(2, count, 4)})
    held[0] = in_hbm(held[0])
    x, low = low_of(here, held, tuple(k | 1 for k in line), pack, slot, adapter_down_maps)
    weight = query_key_value_weight.transpose(0, 2, 1)
    arrived = [trade(low, m, count) for m in (1, 2, 3)]
    query, key = project(0, x, weight), project(1, x, weight)
    arrived, query, key, pool = lax.optimization_barrier((arrived, query, key, pool))
    low = (low + arrived[0]) + (arrived[1] + arrived[2])
    arrived = [trade(low, m, count) for m in range(4, count, 4)]
    base = project(2, x, weight)
    arrived, base = lax.optimization_barrier((arrived, base))
    send = update_values(column, query, key, base, adapter_up_maps.reshape(adapter_count * rank, -1), [low, *arrived])
    send, pool = lax.optimization_barrier((send, pool))
    keys, values = cache_by_head(pool, 0, heads)
    pieces = lax.all_to_all(send, "replica", split_axis=0, concat_axis=0, tiled=True)

    out = attend(cosine, sine, live, pieces, [keys], [values])
    return out.transpose(0, 2, 1, 3).reshape(steps, req_dev, width)


def per_device(replicas, *arrays):
    columns = arrays[1].shape[2]
    whole_heads = replicas % 4 == 0 and (2 * columns) % HD == 0 and columns % HD == HD // 2
    plan = chip_plan if whole_heads and arrays[0].shape[1] == 2 else general_plan
    return plan(replicas, *arrays)


def solution(mesh):
    placed = (
        P(None, ("groups", "replica"), None),
        P(None, None, "replica"),
        P("replica", None, None),
        P(None, None, "replica"),
        P(),
        P("groups"),
        P("groups"),
        P(("groups", "replica"), None),
        P(("groups", "replica"), None, None, None),
    )
    return jax.shard_map(
        functools.partial(per_device, mesh.shape["replica"]),
        mesh=mesh,
        in_specs=placed,
        out_specs=P(None, ("groups", "replica"), None),
        check_vma=False,
    )
```

```python
import functools

import jax
import jax.numpy as jnp
from jax import lax
from jax.experimental import pallas as pl
from jax.experimental.pallas import tpu as pltpu
from jax.sharding import PartitionSpec as P

HD = 128
ROWS = 8
HEAD_BLOCK = 8

adapter_scale = 2.0
masked_score = -1e30


def attention_kernel(steps, req_dev, q_ref, k_ref, v_ref, cos_ref, sin_ref, live_ref, kv_ref, out_ref, kn_ref, vn_ref):
    rows = steps * req_dev
    width = q_ref.shape[1]
    lanes = HEAD_BLOCK * HD
    group = rows * HEAD_BLOCK
    cosine = cos_ref[...]
    sine = sin_ref[...]

    def rotated(x):
        pieces = []
        for h in range(HEAD_BLOCK):
            head = x[:, h * HD : (h + 1) * HD]
            pieces.append(head * cosine + pltpu.roll(head, HD // 2, 1) * sine)
        return jnp.concatenate(pieces, axis=1)

    row_head = lax.broadcasted_iota(jnp.int32, (group, lanes), 0) % HEAD_BLOCK
    lane_head = lax.broadcasted_iota(jnp.int32, (group, lanes), 1) // HD
    own_head = row_head == lane_head
    row_j = lax.broadcasted_iota(jnp.int32, (group, 16), 0) // HEAD_BLOCK
    new_j = lax.broadcasted_iota(jnp.int32, (group, 16), 1)
    new_live = (new_j < rows) & (new_j % req_dev == row_j % req_dev) & (new_j // req_dev <= row_j // req_dev)
    live_all = live_ref[...]
    live = jnp.concatenate(
        [
            jnp.broadcast_to(live_all[j % req_dev : j % req_dev + 1], (HEAD_BLOCK, live_all.shape[1]))
            for j in range(rows)
        ],
        axis=0,
    )
    live = live > 0
    kn_ref[...] = jnp.zeros_like(kn_ref)
    vn_ref[...] = jnp.zeros_like(vn_ref)
    contract_lanes = (((1,), (1,)), ((), ()))
    for c in range(width // lanes):
        cols = slice(c * lanes, (c + 1) * lanes)
        query = rotated(q_ref[:, cols].astype(jnp.float32))
        key_new = rotated(k_ref[:, cols].astype(jnp.float32))
        kn_ref[0:8] = key_new
        vn_ref[0:8] = v_ref[:, cols].astype(jnp.float32)
        kn = kn_ref[...].astype(jnp.bfloat16)
        vn = vn_ref[...].astype(jnp.bfloat16)
        spread = jnp.concatenate(
            [jnp.broadcast_to(query[j : j + 1], (HEAD_BLOCK, lanes)) for j in range(rows)], axis=0
        )
        spread = jnp.where(own_head, spread, 0.0).astype(jnp.bfloat16)
        kv = kv_ref[:, cols]
        scores = lax.dot_general(spread, kv, contract_lanes, preferred_element_type=jnp.float32) * (HD**-0.5)
        scores = jnp.where(live, scores, masked_score)
        fresh = lax.dot_general(spread, kn, contract_lanes, preferred_element_type=jnp.float32) * (HD**-0.5)
        fresh = jnp.where(new_live, fresh, masked_score)
        top = jnp.maximum(jnp.max(scores, axis=1, keepdims=True), jnp.max(fresh, axis=1, keepdims=True))
        weights = jnp.where(live, jnp.exp(scores - top), 0.0)
        fresh = jnp.where(new_live, jnp.exp(fresh - top), 0.0)
        totals = jnp.sum(weights, axis=1, keepdims=True) + jnp.sum(fresh, axis=1, keepdims=True)
        weights = pltpu.roll(weights, 1, 1).astype(jnp.bfloat16)
        mixed = jnp.dot(weights, kv, preferred_element_type=jnp.float32)
        mixed = mixed + jnp.dot(fresh.astype(jnp.bfloat16), vn, preferred_element_type=jnp.float32)
        mixed = jnp.where(own_head, mixed / totals, 0.0)
        out = jnp.sum(mixed.reshape(rows, HEAD_BLOCK, lanes), axis=1)
        out_ref[:, cols] = out.astype(out_ref.dtype)


def attention(steps, req_dev, q, k, v, cosine, sine, live, kv):
    rows = steps * req_dev
    width = q.shape[1]
    vmem = pl.BlockSpec(memory_space=pltpu.VMEM)
    return pl.pallas_call(
        functools.partial(attention_kernel, steps, req_dev),
        out_shape=jax.ShapeDtypeStruct((rows, width), jnp.bfloat16),
        in_specs=[vmem] * 7,
        out_specs=vmem,
        scratch_shapes=[pltpu.VMEM((16, HEAD_BLOCK * HD), jnp.float32)] * 2,
        compiler_params=pltpu.CompilerParams(vmem_limit_bytes=32 * 2**20),
        cost_estimate=pl.CostEstimate(flops=10**9, bytes_accessed=6 * 10**6, transcendentals=0),
        name="attention",
    )(q, k, v, cosine, sine, live, kv)


def rotation(my_lengths, steps):
    rows = steps * my_lengths.shape[0]
    positions = (my_lengths[None, :] + jnp.arange(steps, dtype=jnp.int32)[:, None]).reshape(rows)
    positions = jnp.pad(positions, (0, ROWS - rows))
    half = HD // 2
    frequency = jnp.exp(jnp.arange(half, dtype=jnp.float32) * (-2.0 * jnp.log(10000.0) / HD))
    angles = positions.astype(jnp.float32)[:, None] * frequency[None, :]
    cosine = jnp.cos(angles)
    sine = jnp.sin(angles)
    cosine = jnp.concatenate([cosine, cosine], axis=1)
    sine = jnp.concatenate([-sine, sine], axis=1)
    return cosine, sine


def live_tokens(my_lengths, request_page_table, pool_pages, page_len):
    pages = jnp.arange(pool_pages, dtype=jnp.int32)
    max_pages = request_page_table.shape[1]
    place = jnp.max(
        jnp.where(
            request_page_table[:, :, None] == pages[None, None, :],
            jnp.arange(max_pages, dtype=jnp.int32)[None, :, None],
            -1,
        ),
        axis=1,
    )
    token = place[:, :, None] * page_len + jnp.arange(page_len, dtype=jnp.int32)[None, None, :]
    return (place[:, :, None] >= 0) & (token < my_lengths[:, None, None])


def live_rows(my_lengths, request_page_table, pool_pages, page_len):
    alive = live_tokens(my_lengths, request_page_table, pool_pages, page_len)
    live = jnp.stack([alive, jnp.zeros_like(alive)], axis=-1).astype(jnp.int32)
    return live.reshape(request_page_table.shape[0], pool_pages * page_len * 2)


def general_plan(
    replicas,
    hidden,
    query_key_value_weight,
    adapter_down_maps,
    adapter_up_maps,
    adapter_storage_row,
    request_adapter,
    lengths,
    request_page_table,
    key_value_pool,
):
    my_index = lax.axis_index("replica")
    steps, req_dev, width = hidden.shape
    rows = steps * req_dev
    columns = query_key_value_weight.shape[2]
    holder_count, rank, _ = adapter_down_maps.shape
    pool_pages, page_len = key_value_pool.shape[:2]
    adapter_count = adapter_storage_row.shape[0]
    chips = replicas // 2
    total = replicas * ROWS

    block = jnp.pad(hidden.reshape(rows, width), ((0, ROWS - rows), (0, 0)))
    same_core = [[2 * chip + core for chip in range(chips)] for core in range(2)]
    mine = lax.all_to_all(
        jnp.broadcast_to(block[None], (chips, ROWS, width)),
        "replica",
        split_axis=0,
        concat_axis=0,
        axis_index_groups=same_core,
        tiled=True,
    )
    other = lax.ppermute(mine, "replica", [(i, i ^ 1) for i in range(replicas)])
    first = my_index % 2 == 0
    gathered = jnp.stack([jnp.where(first, mine, other), jnp.where(first, other, mine)])
    gathered = gathered.reshape(total, width)

    stored_rows = jnp.sum(
        jnp.where(
            request_adapter[:, None] == jnp.arange(adapter_count, dtype=jnp.int32)[None, :],
            adapter_storage_row[None, :],
            0,
        ),
        axis=1,
    )
    by_block = stored_rows.reshape(chips, 2, 1, req_dev).transpose(1, 0, 2, 3)
    by_block = jnp.broadcast_to(by_block, (2, chips, steps, req_dev)).reshape(2, chips, rows)
    row_stored = jnp.pad(by_block, ((0, 0), (0, 0), (0, ROWS - rows)), constant_values=-1).reshape(total)

    down = jnp.einsum("nd,hfd->nhf", gathered, adapter_down_maps, preferred_element_type=jnp.float32)
    slots = my_index * holder_count + jnp.arange(holder_count, dtype=jnp.int32)
    own = row_stored[:, None] == slots[None, :]
    low = jnp.sum(jnp.where(own[:, :, None], down, 0.0), axis=1).astype(jnp.bfloat16)
    low = jnp.concatenate([low[: total // 2], low[total // 2 :]], axis=1)
    low = lax.all_to_all(
        jnp.broadcast_to(low[None], (replicas,) + low.shape), "replica", split_axis=0, concat_axis=0, tiled=True
    )
    low = jnp.sum(low.astype(jnp.float32), axis=0)
    low = jnp.concatenate([low[:, :rank], low[:, rank:]], axis=0)

    projected = jnp.einsum("nd,idc->nic", gathered, query_key_value_weight, preferred_element_type=jnp.float32)

    def update(first_adapter, maps):
        held = maps.shape[0]
        which = first_adapter + jnp.arange(held, dtype=jnp.int32)
        wide = jnp.where((row_stored[:, None] == which[None, :])[:, :, None], low[:, None, :], 0.0)
        return jnp.dot(
            wide.astype(jnp.bfloat16).reshape(total, held * rank),
            maps.reshape(held * rank, columns),
            preferred_element_type=jnp.float32,
        )

    step_adapters = 64
    if adapter_count <= step_adapters:
        updated = update(0, adapter_up_maps)
    else:
        updated = lax.fori_loop(
            0,
            adapter_count // step_adapters,
            lambda i, sofar: sofar
            + update(
                i * step_adapters,
                lax.dynamic_slice_in_dim(adapter_up_maps, i * step_adapters, step_adapters, 0),
            ),
            jnp.zeros((total, columns), jnp.float32),
        )
    value = projected[:, 2] + adapter_scale * updated
    combined = jnp.concatenate([projected[:, 0], projected[:, 1], value], axis=1).astype(jnp.bfloat16)
    combined = combined.reshape(2, chips, ROWS, 3 * columns).transpose(1, 0, 2, 3)
    combined = combined.reshape(replicas, ROWS, 3 * columns)
    arrived = lax.all_to_all(combined, "replica", split_axis=0, concat_axis=0, tiled=True)
    arrived = arrived.reshape(replicas, ROWS, 3, columns).transpose(2, 1, 0, 3).reshape(3, ROWS, width)

    my_lengths = lax.dynamic_slice_in_dim(lengths, my_index * req_dev, req_dev)
    cosine, sine = rotation(my_lengths, steps)
    live = live_rows(my_lengths, request_page_table, pool_pages, page_len)
    kv = key_value_pool.reshape(pool_pages * page_len * 2, width)
    out = attention(steps, req_dev, arrived[0], arrived[1], arrived[2], cosine, sine, live, kv)
    return out.reshape(steps, req_dev, width)


def rotation_rows(lengths, first, req_dev, steps):
    row = jnp.arange(ROWS, dtype=jnp.int32)
    wanted = first + row % req_dev
    chosen = jnp.where(wanted[:, None] == jnp.arange(lengths.shape[0], dtype=jnp.int32)[None, :], lengths[None, :], 0)
    positions = jnp.sum(chosen, axis=1, keepdims=True) + (row // req_dev)[:, None]
    lane = jnp.arange(HD, dtype=jnp.int32)
    frequency = jnp.exp((lane % (HD // 2)).astype(jnp.float32) * (-2.0 * jnp.log(10000.0) / HD))
    angles = positions.astype(jnp.float32) * frequency[None, :]
    return jnp.cos(angles), jnp.where(lane < HD // 2, -1.0, 1.0)[None, :] * jnp.sin(angles)


def live_lanes(lengths, first, request_page_table, tokens, page_len):
    req_dev, max_pages = request_page_table.shape
    wanted = first + jnp.arange(req_dev, dtype=jnp.int32)
    chosen = jnp.where(wanted[:, None] == jnp.arange(lengths.shape[0], dtype=jnp.int32)[None, :], lengths[None, :], 0)
    lane = jnp.arange(tokens, dtype=jnp.int32)
    page = jnp.arange(max_pages, dtype=jnp.int32)
    place = jnp.max(
        jnp.where(request_page_table[:, :, None] == (lane // page_len)[None, None, :], page[None, :, None], -1),
        axis=1,
    )
    token = place * page_len + (lane % page_len)[None, :]
    return ((place >= 0) & (token < jnp.sum(chosen, axis=1, keepdims=True))).astype(jnp.int32)


def trade(value, mask, count):
    return lax.ppermute(value, "replica", [(i, i ^ mask) for i in range(count)])


CONTRACT_LANES = (((1,), (1,)), ((), ()))


def in_hbm(x):
    return pltpu.with_memory_space_constraint(x, pltpu.HBM)


VMEM = pl.BlockSpec(memory_space=pltpu.VMEM)
HBM = pl.BlockSpec(memory_space=pltpu.HBM)
SMEM = pl.BlockSpec(memory_space=pltpu.SMEM)
ANY = pl.BlockSpec(memory_space=pl.ANY)


def start_all(copies):
    for copy in copies:
        copy.start()
    return copies


def wait_all(copies):
    for copy in copies:
        copy.wait()


CACHE_SECTION = 10
CACHE_AHEAD = 4
CACHE_TOKENS = 128


def cache_kernel(first, pool_ref, keys_ref, values_ref, raw, values, sem, out_sem):
    heads, tokens = raw.shape[:2]
    copies = [pltpu.make_async_copy(pool_ref.at[:, first + h], raw.at[h], sem.at[h]) for h in range(heads)]
    start_all(copies[: CACHE_AHEAD * CACHE_SECTION])
    rows = raw.reshape(heads, 2 * tokens, HD)
    block = min(tokens, CACHE_TOKENS)
    to = lax.broadcasted_iota(jnp.int32, (2 * block, 2 * block), 0)
    source = lax.broadcasted_iota(jnp.int32, (2 * block, 2 * block), 1)
    wanted = jnp.where(to < block, 2 * to, 2 * (to - block) + 1)
    pick = jnp.where(source == wanted, 1.0, 0.0).astype(jnp.bfloat16)
    sent = []
    part = CACHE_SECTION
    for p in range(heads // part):
        wait_all(copies[p * part : (p + 1) * part])
        start_all(copies[(p + CACHE_AHEAD) * part : (p + CACHE_AHEAD + 1) * part])
        for h in range(p * part, (p + 1) * part, 2):
            for first_token in range(0, tokens, block):
                raw_rows = slice(2 * first_token, 2 * (first_token + block))
                both = jnp.concatenate([rows[h, raw_rows], rows[h + 1, raw_rows]], axis=1)
                made = jnp.dot(pick, both, preferred_element_type=jnp.float32).astype(jnp.bfloat16)
                span = slice(first_token, first_token + block)
                for i in range(2):
                    keys_ref[h + i, span] = made[:block, i * HD : (i + 1) * HD]
                    values[h + i, span] = made[block:, i * HD : (i + 1) * HD]
        span = slice(p * part, (p + 1) * part)
        sent += start_all([pltpu.make_async_copy(values.at[span], values_ref.at[span], out_sem.at[p])])
    wait_all(sent)


def cache_by_head(pool, first, heads):
    tokens = pool.shape[0]
    return pl.pallas_call(
        functools.partial(cache_kernel, first),
        out_shape=(
            jax.ShapeDtypeStruct((heads, tokens, HD), pool.dtype),
            pltpu.HBM((heads, tokens, HD), pool.dtype),
        ),
        in_specs=[HBM],
        out_specs=(VMEM, HBM),
        scratch_shapes=[
            pltpu.VMEM((heads, tokens, 2, HD), pool.dtype),
            pltpu.VMEM((heads, tokens, HD), pool.dtype),
            pltpu.SemaphoreType.DMA((heads,)),
            pltpu.SemaphoreType.DMA((heads // CACHE_SECTION,)),
        ],
        compiler_params=pltpu.CompilerParams(vmem_limit_bytes=12 * 2**20),
        cost_estimate=pl.CostEstimate(flops=0, bytes_accessed=12 * 10**6, transcendentals=0),
        name="cache_by_head",
    )(in_hbm(pool))


def lanes_of(x):
    return jnp.concatenate([x[c] for c in range(x.shape[0])], axis=1)


def step_rows(x, first, chunks):
    steps, _, count = x.shape[:3]
    flat = x.reshape(steps, x.shape[1], 2 * count, HD)
    return jnp.concatenate(
        [jnp.concatenate([flat[t, c] for c in range(first, first + chunks)], axis=1) for t in range(steps)], axis=0
    )


def pack_kernel(*refs):
    blocks, (out_ref, sem) = refs[:-2], refs[-2:]
    wait_all(
        start_all([pltpu.make_async_copy(block, out_ref.at[i], sem.at[i]) for i, block in enumerate(blocks)])
    )


def packed(blocks):
    return pl.pallas_call(
        pack_kernel,
        out_shape=jax.ShapeDtypeStruct((len(blocks),) + blocks[0].shape, blocks[0].dtype),
        in_specs=[ANY] * len(blocks),
        out_specs=VMEM,
        scratch_shapes=[pltpu.SemaphoreType.DMA((len(blocks),))],
        compiler_params=pltpu.CompilerParams(vmem_limit_bytes=2 * 2**20),
        cost_estimate=pl.CostEstimate(flops=0, bytes_accessed=10**6, transcendentals=0),
        name="pack_blocks",
    )(*blocks)


def index_kernel(me_ref, stored_ref, slot_ref, column_ref):
    requests = stored_ref.shape[1]
    steps = slot_ref.shape[1] // requests
    row = jnp.concatenate([stored_ref[...]] * steps, axis=1)
    slot_ref[...] = row - me_ref[0]
    wide = jnp.concatenate([row, jnp.zeros((1, HD - row.shape[1]), row.dtype)], axis=1)
    column_ref[...] = jnp.broadcast_to(wide.astype(jnp.float32), (HD, HD)).T[: row.shape[1], :1].astype(jnp.int32)


def index_work(first, stored, steps):
    rows = stored.shape[0] * steps
    return pl.pallas_call(
        index_kernel,
        out_shape=(jax.ShapeDtypeStruct((1, rows), jnp.int32), jax.ShapeDtypeStruct((rows, 1), jnp.int32)),
        in_specs=[SMEM, VMEM],
        out_specs=(VMEM, VMEM),
        compiler_params=pltpu.CompilerParams(vmem_limit_bytes=2 * 2**20),
        cost_estimate=pl.CostEstimate(flops=2 * 10**10, bytes_accessed=10**4, transcendentals=0),
        name="index_work",
    )(first, stored[None, :])


def low_kernel(places, packs, me_ref, slot_ref, down_ref, pack_ref, *refs):
    blocks, (x_ref, low_ref, sem) = refs[: len(places)], refs[len(places) :]
    me = me_ref[0]
    holders, rank, width = down_ref.shape
    sources = list(zip(places, blocks)) + [(k, pack_ref.at[i]) for i, k in enumerate(packs)]
    wait_all(
        start_all([pltpu.make_async_copy(block, x_ref.at[:, :, me ^ k], sem.at[k]) for k, block in sources])
    )
    x = step_rows(x_ref, 0, x_ref.shape[1])
    rows = x.shape[0]
    made = lax.dot_general(
        down_ref.reshape(holders * rank, width)[...], x, CONTRACT_LANES, preferred_element_type=jnp.float32
    )
    slot = slot_ref[...]
    low = jnp.zeros((rank, rows), jnp.float32)
    for h in range(holders):
        low = low + jnp.where(slot == h, made[h * rank : (h + 1) * rank], 0.0)
    low = low.T
    low_ref[...] = jnp.concatenate([low[: rows // 2], low[rows // 2 :]], axis=1).astype(low_ref.dtype)


def low_of(me, blocks, packs, pack, slot, down):
    count = len(blocks) + len(packs)
    steps, chunks = blocks[0].shape[:2]
    rows = count * steps * 2
    rank = down.shape[1]
    return pl.pallas_call(
        functools.partial(low_kernel, tuple(blocks), packs),
        out_shape=(
            jax.ShapeDtypeStruct((steps, chunks, count, 2, HD), jnp.bfloat16),
            jax.ShapeDtypeStruct((rows // 2, 2 * rank), jnp.bfloat16),
        ),
        in_specs=[SMEM, VMEM, VMEM, ANY] + [ANY] * len(blocks),
        out_specs=(VMEM, VMEM),
        scratch_shapes=[pltpu.SemaphoreType.DMA((count,))],
        compiler_params=pltpu.CompilerParams(vmem_limit_bytes=12 * 2**20),
        cost_estimate=pl.CostEstimate(flops=10**8, bytes_accessed=4 * 10**6, transcendentals=0),
        name="low_rows",
    )(me, slot, down, pack, *blocks.values())


def put_chunks(buf, first, value):
    steps, count = buf.shape[1:3]
    flat = buf.reshape(buf.shape[0], steps, 2 * count, HD)
    wide = value.shape[1]
    for c in range(-(-wide // HD)):
        part = value[:, c * HD : min((c + 1) * HD, wide)]
        if part.shape[1] < HD:
            part = jnp.concatenate([part, jnp.zeros((part.shape[0], HD - part.shape[1]), part.dtype)], axis=1)
        part = part.astype(buf.dtype)
        for t in range(steps):
            flat[first + c, t] = part[t * 2 * count : (t + 1) * 2 * count]


def project_kernel(which, x_ref, w_ref, out_ref):
    x = step_rows(x_ref, 0, x_ref.shape[1])
    made = lax.dot_general(w_ref[which], x, CONTRACT_LANES, preferred_element_type=jnp.float32).T
    if which < 2:
        pad = jnp.zeros((made.shape[0], HD // 2), made.dtype)
        put_chunks(out_ref, 0, jnp.concatenate([made, pad] if which == 0 else [pad, made], axis=1))
    else:
        out_ref[...] = made


def project(which, x, weight):
    steps, _, count = x.shape[:3]
    columns = weight.shape[1]
    chunks = jax.ShapeDtypeStruct((-(-columns // HD), steps, count, 2, HD), jnp.bfloat16)
    base = jax.ShapeDtypeStruct((2 * steps * count, columns), jnp.float32)
    return pl.pallas_call(
        functools.partial(project_kernel, which),
        out_shape=chunks if which < 2 else base,
        in_specs=[VMEM, VMEM],
        out_specs=VMEM,
        compiler_params=pltpu.CompilerParams(vmem_limit_bytes=16 * 2**20),
        cost_estimate=pl.CostEstimate(flops=5 * 10**8, bytes_accessed=4 * 10**6, transcendentals=0),
        name="project",
    )(x, weight)


def update_kernel(stored_ref, query_ref, key_ref, base_ref, up_ref, *refs):
    lows, (send_ref, buf, sem) = refs[:-3], refs[-3:]
    half, packed = lows[0].shape
    rank = packed // 2
    rows = 2 * half
    count = send_ref.shape[0]
    low = lows[0][...].astype(jnp.float32)
    for more in lows[1:]:
        low = low + more[...].astype(jnp.float32)
    low = jnp.concatenate([low[:, :rank], low[:, rank:]], axis=0)
    batch = 256 // rank
    spread = jnp.concatenate([low] * batch, axis=1)
    ahead = stored_ref[...] - lax.broadcasted_iota(jnp.int32, (rows, batch * rank), 1) // rank
    total = jnp.zeros(base_ref.shape, jnp.float32)
    for a in range(0, up_ref.shape[0] // rank, batch):
        wide = jnp.where(ahead == a, spread, 0.0).astype(jnp.bfloat16)
        total = total + jnp.dot(wide, up_ref[a * rank : (a + batch) * rank], preferred_element_type=jnp.float32)
    each = query_ref.shape[0]
    buf[: each - 1] = query_ref[: each - 1]
    buf[each - 1] = query_ref[each - 1] + key_ref[0]
    buf[each : 2 * each - 1] = key_ref[1:]
    put_chunks(buf, 2 * each - 1, base_ref[...] + adapter_scale * total)
    wait_all(
        start_all([pltpu.make_async_copy(buf.at[:, :, k], send_ref.at[k], sem.at[k]) for k in range(count)])
    )


def update_values(stored, query, key, base, up, lows):
    chunks, steps, count = query.shape[:3]
    return pl.pallas_call(
        update_kernel,
        out_shape=pltpu.HBM((count, 3 * chunks - 1, steps, 2, HD), query.dtype),
        in_specs=[VMEM] * (5 + len(lows)),
        out_specs=HBM,
        scratch_shapes=[
            pltpu.VMEM((3 * chunks - 1, steps, count, 2, HD), query.dtype),
            pltpu.SemaphoreType.DMA((count,)),
        ],
        compiler_params=pltpu.CompilerParams(vmem_limit_bytes=8 * 2**20),
        cost_estimate=pl.CostEstimate(flops=3 * 10**8, bytes_accessed=4 * 10**6, transcendentals=0),
        name="update_values",
    )(stored, query, key, base, up, *lows)


def attend_kernel(cos_ref, sin_ref, live_ref, pieces_ref, *refs):
    *parts, out_ref, values_buf, kn_ref, vn_ref, sem = refs
    keys_refs, values_refs = parts[: len(parts) // 2], parts[len(parts) // 2 :]
    count, _, steps = pieces_ref.shape[:3]
    rows = 2 * steps
    each = (pieces_ref.shape[1] + 1) // 3
    heads = 2 * out_ref.shape[1] // count
    lanes = heads * HD
    group = rows * HEAD_BLOCK
    chips = range(count // 2)
    early = keys_refs[0].shape[0] // heads
    places = [(0, c) if c < early else (1, c - early) for c in chips]
    fetches = start_all(
        [
            pltpu.make_async_copy(values_refs[half].at[at * heads : (at + 1) * heads], values_buf.at[c], sem.at[c])
            for c, (half, at) in enumerate(places)
        ]
    )
    cosine = cos_ref[...][:rows]
    sine = sin_ref[...][:rows]
    left = lax.broadcasted_iota(jnp.int32, (rows, HD), 1) < HD // 2

    def halves(chip, at):
        return [
            [pieces_ref[2 * chip + core, at + c].reshape(rows, HD).astype(jnp.float32) for c in range(each)]
            for core in range(2)
        ]

    def swapped(parts):
        return [pltpu.roll(x, HD // 2, 1) for x in parts]

    def joined(parts):
        return [jnp.where(left, a, b) for a, b in zip(parts[:-1], parts[1:])]

    def chip_columns(chip, at):
        low, high = halves(chip, at)
        high = swapped(high)
        return low[:-1] + [jnp.where(left, low[-1], high[0])] + joined(high)

    def chip_keys(chip):
        low, high = halves(chip, each - 1)
        low = swapped(low)
        return joined(low) + [jnp.where(left, low[-1], high[0])] + high[1:]

    def rotated(parts):
        return [x * cosine + pltpu.roll(x, HD // 2, 1) * sine for x in parts]

    row_head = lax.broadcasted_iota(jnp.int32, (group, lanes), 0) % HEAD_BLOCK
    lane_head = lax.broadcasted_iota(jnp.int32, (group, lanes), 1) // HD
    own_head = row_head == lane_head
    row_j = lax.broadcasted_iota(jnp.int32, (group, 16), 0) // HEAD_BLOCK
    new_j = lax.broadcasted_iota(jnp.int32, (group, 16), 1)
    new_live = (new_j < rows) & (new_j % 2 == row_j % 2) & (new_j // 2 <= row_j // 2)
    live = jnp.concatenate(
        [
            jnp.broadcast_to(live_ref[j % 2 : j % 2 + 1, :], (HEAD_BLOCK, live_ref.shape[1]))
            for j in range(rows)
        ],
        axis=0,
    )
    live = live > 0
    kn_ref[...] = jnp.zeros_like(kn_ref)
    vn_ref[...] = jnp.zeros_like(vn_ref)
    spreads = []
    for c in chips:
        query = jnp.concatenate(rotated(chip_columns(c, 0)), axis=1)
        kn_ref[c, 0:rows] = jnp.concatenate(rotated(chip_keys(c)), axis=1)
        vn_ref[c, 0:rows] = jnp.concatenate(chip_columns(c, 2 * each - 1), axis=1)
        spread = jnp.concatenate(
            [jnp.broadcast_to(query[j : j + 1], (HEAD_BLOCK, lanes)) for j in range(rows)], axis=0
        )
        spreads.append(jnp.where(own_head, spread, 0.0).astype(jnp.bfloat16))
    scores, fresh = [], []
    for c in chips:
        half, at = places[c]
        keys = jnp.concatenate([keys_refs[half][at * heads + h] for h in range(heads)], axis=1)
        kn = kn_ref[c].astype(jnp.bfloat16)
        scores.append(lax.dot_general(spreads[c], keys, CONTRACT_LANES, preferred_element_type=jnp.float32))
        fresh.append(lax.dot_general(spreads[c], kn, CONTRACT_LANES, preferred_element_type=jnp.float32))
    weights, fresh_weights, totals = [], [], []
    for c in chips:
        old = jnp.where(live, scores[c] * (HD**-0.5), masked_score)
        new = jnp.where(new_live, fresh[c] * (HD**-0.5), masked_score)
        top = jnp.maximum(jnp.max(old, axis=1, keepdims=True), jnp.max(new, axis=1, keepdims=True))
        old = jnp.where(live, jnp.exp(old - top), 0.0)
        new = jnp.where(new_live, jnp.exp(new - top), 0.0)
        totals.append(jnp.sum(old, axis=1, keepdims=True) + jnp.sum(new, axis=1, keepdims=True))
        weights.append(old.astype(jnp.bfloat16))
        fresh_weights.append(new.astype(jnp.bfloat16))
    wait_all(fetches)
    for c in chips:
        values = lanes_of(values_buf[c])
        vn = vn_ref[c].astype(jnp.bfloat16)
        mixed = jnp.dot(weights[c], values, preferred_element_type=jnp.float32)
        mixed = mixed + jnp.dot(fresh_weights[c], vn, preferred_element_type=jnp.float32)
        mixed = jnp.where(own_head, mixed / totals[c], 0.0)
        out = jnp.sum(mixed.reshape(rows, HEAD_BLOCK, lanes), axis=1).astype(out_ref.dtype)
        for t in range(steps):
            for h in range(heads):
                out_ref[t, c * heads + h] = out[2 * t : 2 * t + 2, h * HD : (h + 1) * HD]


def attend(cosine, sine, live, pieces, keys, values):
    count, _, steps = pieces.shape[:3]
    heads, tokens = sum(x.shape[0] for x in keys), keys[0].shape[1]
    chips = count // 2
    per = heads // chips
    return pl.pallas_call(
        attend_kernel,
        out_shape=jax.ShapeDtypeStruct((steps, heads, 2, HD), jnp.bfloat16),
        in_specs=[VMEM] * (4 + len(keys)) + [HBM] * len(values),
        out_specs=VMEM,
        scratch_shapes=[pltpu.VMEM((chips, per, tokens, HD), jnp.bfloat16)]
        + [pltpu.VMEM((chips, 16, per * HD), jnp.float32)] * 2
        + [pltpu.SemaphoreType.DMA((chips,))],
        compiler_params=pltpu.CompilerParams(vmem_limit_bytes=16 * 2**20),
        cost_estimate=pl.CostEstimate(flops=10**9, bytes_accessed=6 * 10**6, transcendentals=0),
        name="attention",
    )(cosine, sine, live, pieces, *keys, *[in_hbm(x) for x in values])


def chip_plan(
    count,
    hidden,
    query_key_value_weight,
    adapter_down_maps,
    adapter_up_maps,
    adapter_storage_row,
    request_adapter,
    lengths,
    request_page_table,
    key_value_pool,
):
    me = lax.axis_index("replica")
    steps, req_dev, width = hidden.shape
    heads = width // HD
    holder_count, rank, _ = adapter_down_maps.shape
    pool_pages, page_len = key_value_pool.shape[:2]
    adapter_count = adapter_storage_row.shape[0]

    tokens = pool_pages * page_len
    pool = key_value_pool.reshape(tokens, 2, heads, HD).transpose(0, 2, 1, 3)

    stored = jnp.sum(
        jnp.where(
            request_adapter[:, None] == jnp.arange(adapter_count, dtype=jnp.int32)[None, :],
            adapter_storage_row[None, :],
            0,
        ),
        axis=1,
    )
    first, slots, here, stored = lax.optimization_barrier(
        (me * req_dev, (me * holder_count).astype(jnp.int32).reshape(1), me.astype(jnp.int32).reshape(1), stored)
    )
    slot, column = index_work(slots, stored, steps)

    held = {0: hidden}
    held.update({m: trade(hidden, m, count) for m in range(4, count, 4)})
    _, lengths, request_page_table = lax.optimization_barrier((held[4], lengths, request_page_table))
    cosine, sine = rotation_rows(lengths, first, req_dev, steps)
    live = live_lanes(lengths, first, request_page_table, tokens, page_len)
    held.update({k | 2: trade(v, 2, count) for k, v in list(held.items())})
    held = {k: v.reshape(steps, req_dev, heads, HD).transpose(0, 2, 1, 3) for k, v in held.items()}
    line = tuple(range(0, count, 4))
    *share, held[2], held[6] = lax.optimization_barrier([held[k] for k in line] + [held[2], held[6]])
    pack = trade(packed(share), 1, count)
    held.update({k | 1: trade(held[k], 1, count) for k in range(2, count, 4)})
    held[0] = in_hbm(held[0])
    x, low = low_of(here, held, tuple(k | 1 for k in line), pack, slot, adapter_down_maps)
    weight = query_key_value_weight.transpose(0, 2, 1)
    arrived = [trade(low, m, count) for m in (1, 2, 3)]
    query, key = project(0, x, weight), project(1, x, weight)
    arrived, query, key, pool = lax.optimization_barrier((arrived, query, key, pool))
    low = (low + arrived[0]) + (arrived[1] + arrived[2])
    arrived = [trade(low, m, count) for m in range(4, count, 4)]
    base = project(2, x, weight)
    arrived, base = lax.optimization_barrier((arrived, base))
    send = update_values(column, query, key, base, adapter_up_maps.reshape(adapter_count * rank, -1), [low, *arrived])
    send, pool = lax.optimization_barrier((send, pool))
    keys, values = cache_by_head(pool, 0, heads)
    pieces = lax.all_to_all(send, "replica", split_axis=0, concat_axis=0, tiled=True)

    out = attend(cosine, sine, live, pieces, [keys], [values])
    return out.transpose(0, 2, 1, 3).reshape(steps, req_dev, width)


def per_device(replicas, *arrays):
    columns = arrays[1].shape[2]
    whole_heads = replicas % 4 == 0 and (2 * columns) % HD == 0 and columns % HD == HD // 2
    plan = chip_plan if whole_heads and arrays[0].shape[1] == 2 else general_plan
    return plan(replicas, *arrays)


def solution(mesh):
    placed = (
        P(None, ("groups", "replica"), None),
        P(None, None, "replica"),
        P("replica", None, None),
        P(None, None, "replica"),
        P(),
        P("groups"),
        P("groups"),
        P(("groups", "replica"), None),
        P(("groups", "replica"), None, None, None),
    )
    return jax.shard_map(
        functools.partial(per_device, mesh.shape["replica"]),
        mesh=mesh,
        in_specs=placed,
        out_specs=P(None, ("groups", "replica"), None),
        check_vma=False,
    )
```

```python
import functools

import jax
import jax.numpy as jnp
from jax import lax
from jax.experimental import pallas as pl
from jax.experimental.pallas import tpu as pltpu
from jax.sharding import PartitionSpec as P

HD = 128
ROWS = 8
HEAD_BLOCK = 8

adapter_scale = 2.0
masked_score = -1e30


def attention_kernel(steps, req_dev, q_ref, k_ref, v_ref, cos_ref, sin_ref, live_ref, kv_ref, out_ref, kn_ref, vn_ref):
    rows = steps * req_dev
    width = q_ref.shape[1]
    lanes = HEAD_BLOCK * HD
    group = rows * HEAD_BLOCK
    cosine = cos_ref[...]
    sine = sin_ref[...]

    def rotated(x):
        pieces = []
        for h in range(HEAD_BLOCK):
            head = x[:, h * HD : (h + 1) * HD]
            pieces.append(head * cosine + pltpu.roll(head, HD // 2, 1) * sine)
        return jnp.concatenate(pieces, axis=1)

    row_head = lax.broadcasted_iota(jnp.int32, (group, lanes), 0) % HEAD_BLOCK
    lane_head = lax.broadcasted_iota(jnp.int32, (group, lanes), 1) // HD
    own_head = row_head == lane_head
    row_j = lax.broadcasted_iota(jnp.int32, (group, 16), 0) // HEAD_BLOCK
    new_j = lax.broadcasted_iota(jnp.int32, (group, 16), 1)
    new_live = (new_j < rows) & (new_j % req_dev == row_j % req_dev) & (new_j // req_dev <= row_j // req_dev)
    live_all = live_ref[...]
    live = jnp.concatenate(
        [
            jnp.broadcast_to(live_all[j % req_dev : j % req_dev + 1], (HEAD_BLOCK, live_all.shape[1]))
            for j in range(rows)
        ],
        axis=0,
    )
    live = live > 0
    kn_ref[...] = jnp.zeros_like(kn_ref)
    vn_ref[...] = jnp.zeros_like(vn_ref)
    contract_lanes = (((1,), (1,)), ((), ()))
    for c in range(width // lanes):
        cols = slice(c * lanes, (c + 1) * lanes)
        query = rotated(q_ref[:, cols].astype(jnp.float32))
        key_new = rotated(k_ref[:, cols].astype(jnp.float32))
        kn_ref[0:8] = key_new
        vn_ref[0:8] = v_ref[:, cols].astype(jnp.float32)
        kn = kn_ref[...].astype(jnp.bfloat16)
        vn = vn_ref[...].astype(jnp.bfloat16)
        spread = jnp.concatenate(
            [jnp.broadcast_to(query[j : j + 1], (HEAD_BLOCK, lanes)) for j in range(rows)], axis=0
        )
        spread = jnp.where(own_head, spread, 0.0).astype(jnp.bfloat16)
        kv = kv_ref[:, cols]
        scores = lax.dot_general(spread, kv, contract_lanes, preferred_element_type=jnp.float32) * (HD**-0.5)
        scores = jnp.where(live, scores, masked_score)
        fresh = lax.dot_general(spread, kn, contract_lanes, preferred_element_type=jnp.float32) * (HD**-0.5)
        fresh = jnp.where(new_live, fresh, masked_score)
        top = jnp.maximum(jnp.max(scores, axis=1, keepdims=True), jnp.max(fresh, axis=1, keepdims=True))
        weights = jnp.where(live, jnp.exp(scores - top), 0.0)
        fresh = jnp.where(new_live, jnp.exp(fresh - top), 0.0)
        totals = jnp.sum(weights, axis=1, keepdims=True) + jnp.sum(fresh, axis=1, keepdims=True)
        weights = pltpu.roll(weights, 1, 1).astype(jnp.bfloat16)
        mixed = jnp.dot(weights, kv, preferred_element_type=jnp.float32)
        mixed = mixed + jnp.dot(fresh.astype(jnp.bfloat16), vn, preferred_element_type=jnp.float32)
        mixed = jnp.where(own_head, mixed / totals, 0.0)
        out = jnp.sum(mixed.reshape(rows, HEAD_BLOCK, lanes), axis=1)
        out_ref[:, cols] = out.astype(out_ref.dtype)


def attention(steps, req_dev, q, k, v, cosine, sine, live, kv):
    rows = steps * req_dev
    width = q.shape[1]
    vmem = pl.BlockSpec(memory_space=pltpu.VMEM)
    return pl.pallas_call(
        functools.partial(attention_kernel, steps, req_dev),
        out_shape=jax.ShapeDtypeStruct((rows, width), jnp.bfloat16),
        in_specs=[vmem] * 7,
        out_specs=vmem,
        scratch_shapes=[pltpu.VMEM((16, HEAD_BLOCK * HD), jnp.float32)] * 2,
        compiler_params=pltpu.CompilerParams(vmem_limit_bytes=32 * 2**20),
        cost_estimate=pl.CostEstimate(flops=10**9, bytes_accessed=6 * 10**6, transcendentals=0),
        name="attention",
    )(q, k, v, cosine, sine, live, kv)


def rotation(my_lengths, steps):
    rows = steps * my_lengths.shape[0]
    positions = (my_lengths[None, :] + jnp.arange(steps, dtype=jnp.int32)[:, None]).reshape(rows)
    positions = jnp.pad(positions, (0, ROWS - rows))
    half = HD // 2
    frequency = jnp.exp(jnp.arange(half, dtype=jnp.float32) * (-2.0 * jnp.log(10000.0) / HD))
    angles = positions.astype(jnp.float32)[:, None] * frequency[None, :]
    cosine = jnp.cos(angles)
    sine = jnp.sin(angles)
    cosine = jnp.concatenate([cosine, cosine], axis=1)
    sine = jnp.concatenate([-sine, sine], axis=1)
    return cosine, sine


def live_tokens(my_lengths, request_page_table, pool_pages, page_len):
    pages = jnp.arange(pool_pages, dtype=jnp.int32)
    max_pages = request_page_table.shape[1]
    place = jnp.max(
        jnp.where(
            request_page_table[:, :, None] == pages[None, None, :],
            jnp.arange(max_pages, dtype=jnp.int32)[None, :, None],
            -1,
        ),
        axis=1,
    )
    token = place[:, :, None] * page_len + jnp.arange(page_len, dtype=jnp.int32)[None, None, :]
    return (place[:, :, None] >= 0) & (token < my_lengths[:, None, None])


def live_rows(my_lengths, request_page_table, pool_pages, page_len):
    alive = live_tokens(my_lengths, request_page_table, pool_pages, page_len)
    live = jnp.stack([alive, jnp.zeros_like(alive)], axis=-1).astype(jnp.int32)
    return live.reshape(request_page_table.shape[0], pool_pages * page_len * 2)


def general_plan(
    replicas,
    hidden,
    query_key_value_weight,
    adapter_down_maps,
    adapter_up_maps,
    adapter_storage_row,
    request_adapter,
    lengths,
    request_page_table,
    key_value_pool,
):
    my_index = lax.axis_index("replica")
    steps, req_dev, width = hidden.shape
    rows = steps * req_dev
    columns = query_key_value_weight.shape[2]
    holder_count, rank, _ = adapter_down_maps.shape
    pool_pages, page_len = key_value_pool.shape[:2]
    adapter_count = adapter_storage_row.shape[0]
    chips = replicas // 2
    total = replicas * ROWS

    block = jnp.pad(hidden.reshape(rows, width), ((0, ROWS - rows), (0, 0)))
    same_core = [[2 * chip + core for chip in range(chips)] for core in range(2)]
    mine = lax.all_to_all(
        jnp.broadcast_to(block[None], (chips, ROWS, width)),
        "replica",
        split_axis=0,
        concat_axis=0,
        axis_index_groups=same_core,
        tiled=True,
    )
    other = lax.ppermute(mine, "replica", [(i, i ^ 1) for i in range(replicas)])
    first = my_index % 2 == 0
    gathered = jnp.stack([jnp.where(first, mine, other), jnp.where(first, other, mine)])
    gathered = gathered.reshape(total, width)

    stored_rows = jnp.sum(
        jnp.where(
            request_adapter[:, None] == jnp.arange(adapter_count, dtype=jnp.int32)[None, :],
            adapter_storage_row[None, :],
            0,
        ),
        axis=1,
    )
    by_block = stored_rows.reshape(chips, 2, 1, req_dev).transpose(1, 0, 2, 3)
    by_block = jnp.broadcast_to(by_block, (2, chips, steps, req_dev)).reshape(2, chips, rows)
    row_stored = jnp.pad(by_block, ((0, 0), (0, 0), (0, ROWS - rows)), constant_values=-1).reshape(total)

    down = jnp.einsum("nd,hfd->nhf", gathered, adapter_down_maps, preferred_element_type=jnp.float32)
    slots = my_index * holder_count + jnp.arange(holder_count, dtype=jnp.int32)
    own = row_stored[:, None] == slots[None, :]
    low = jnp.sum(jnp.where(own[:, :, None], down, 0.0), axis=1).astype(jnp.bfloat16)
    low = jnp.concatenate([low[: total // 2], low[total // 2 :]], axis=1)
    low = lax.all_to_all(
        jnp.broadcast_to(low[None], (replicas,) + low.shape), "replica", split_axis=0, concat_axis=0, tiled=True
    )
    low = jnp.sum(low.astype(jnp.float32), axis=0)
    low = jnp.concatenate([low[:, :rank], low[:, rank:]], axis=0)

    projected = jnp.einsum("nd,idc->nic", gathered, query_key_value_weight, preferred_element_type=jnp.float32)

    def update(first_adapter, maps):
        held = maps.shape[0]
        which = first_adapter + jnp.arange(held, dtype=jnp.int32)
        wide = jnp.where((row_stored[:, None] == which[None, :])[:, :, None], low[:, None, :], 0.0)
        return jnp.dot(
            wide.astype(jnp.bfloat16).reshape(total, held * rank),
            maps.reshape(held * rank, columns),
            preferred_element_type=jnp.float32,
        )

    step_adapters = 64
    if adapter_count <= step_adapters:
        updated = update(0, adapter_up_maps)
    else:
        updated = lax.fori_loop(
            0,
            adapter_count // step_adapters,
            lambda i, sofar: sofar
            + update(
                i * step_adapters,
                lax.dynamic_slice_in_dim(adapter_up_maps, i * step_adapters, step_adapters, 0),
            ),
            jnp.zeros((total, columns), jnp.float32),
        )
    value = projected[:, 2] + adapter_scale * updated
    combined = jnp.concatenate([projected[:, 0], projected[:, 1], value], axis=1).astype(jnp.bfloat16)
    combined = combined.reshape(2, chips, ROWS, 3 * columns).transpose(1, 0, 2, 3)
    combined = combined.reshape(replicas, ROWS, 3 * columns)
    arrived = lax.all_to_all(combined, "replica", split_axis=0, concat_axis=0, tiled=True)
    arrived = arrived.reshape(replicas, ROWS, 3, columns).transpose(2, 1, 0, 3).reshape(3, ROWS, width)

    my_lengths = lax.dynamic_slice_in_dim(lengths, my_index * req_dev, req_dev)
    cosine, sine = rotation(my_lengths, steps)
    live = live_rows(my_lengths, request_page_table, pool_pages, page_len)
    kv = key_value_pool.reshape(pool_pages * page_len * 2, width)
    out = attention(steps, req_dev, arrived[0], arrived[1], arrived[2], cosine, sine, live, kv)
    return out.reshape(steps, req_dev, width)


def rotation_rows(lengths, first, req_dev, steps):
    row = jnp.arange(ROWS, dtype=jnp.int32)
    wanted = first + row % req_dev
    chosen = jnp.where(wanted[:, None] == jnp.arange(lengths.shape[0], dtype=jnp.int32)[None, :], lengths[None, :], 0)
    positions = jnp.sum(chosen, axis=1, keepdims=True) + (row // req_dev)[:, None]
    lane = jnp.arange(HD, dtype=jnp.int32)
    frequency = jnp.exp((lane % (HD // 2)).astype(jnp.float32) * (-2.0 * jnp.log(10000.0) / HD))
    angles = positions.astype(jnp.float32) * frequency[None, :]
    return jnp.cos(angles), jnp.where(lane < HD // 2, -1.0, 1.0)[None, :] * jnp.sin(angles)


def live_lanes(lengths, first, request_page_table, tokens, page_len):
    req_dev, max_pages = request_page_table.shape
    wanted = first + jnp.arange(req_dev, dtype=jnp.int32)
    chosen = jnp.where(wanted[:, None] == jnp.arange(lengths.shape[0], dtype=jnp.int32)[None, :], lengths[None, :], 0)
    lane = jnp.arange(tokens, dtype=jnp.int32)
    page = jnp.arange(max_pages, dtype=jnp.int32)
    place = jnp.max(
        jnp.where(request_page_table[:, :, None] == (lane // page_len)[None, None, :], page[None, :, None], -1),
        axis=1,
    )
    token = place * page_len + (lane % page_len)[None, :]
    return ((place >= 0) & (token < jnp.sum(chosen, axis=1, keepdims=True))).astype(jnp.int32)


def trade(value, mask, count):
    return lax.ppermute(value, "replica", [(i, i ^ mask) for i in range(count)])


CONTRACT_LANES = (((1,), (1,)), ((), ()))


def in_hbm(x):
    return pltpu.with_memory_space_constraint(x, pltpu.HBM)


VMEM = pl.BlockSpec(memory_space=pltpu.VMEM)
HBM = pl.BlockSpec(memory_space=pltpu.HBM)
SMEM = pl.BlockSpec(memory_space=pltpu.SMEM)
ANY = pl.BlockSpec(memory_space=pl.ANY)


def start_all(copies):
    for copy in copies:
        copy.start()
    return copies


def wait_all(copies):
    for copy in copies:
        copy.wait()


CACHE_SECTION = 10
CACHE_AHEAD = 4
CACHE_TOKENS = 128


def cache_kernel(first, pool_ref, keys_ref, values_ref, raw, values, sem, out_sem):
    heads, tokens = raw.shape[:2]
    copies = [pltpu.make_async_copy(pool_ref.at[:, first + h], raw.at[h], sem.at[h]) for h in range(heads)]
    start_all(copies[: CACHE_AHEAD * CACHE_SECTION])
    rows = raw.reshape(heads, 2 * tokens, HD)
    block = min(tokens, CACHE_TOKENS)
    to = lax.broadcasted_iota(jnp.int32, (2 * block, 2 * block), 0)
    source = lax.broadcasted_iota(jnp.int32, (2 * block, 2 * block), 1)
    wanted = jnp.where(to < block, 2 * to, 2 * (to - block) + 1)
    pick = jnp.where(source == wanted, 1.0, 0.0).astype(jnp.bfloat16)
    sent = []
    part = CACHE_SECTION
    for p in range(heads // part):
        wait_all(copies[p * part : (p + 1) * part])
        start_all(copies[(p + CACHE_AHEAD) * part : (p + CACHE_AHEAD + 1) * part])
        for h in range(p * part, (p + 1) * part, 2):
            for first_token in range(0, tokens, block):
                raw_rows = slice(2 * first_token, 2 * (first_token + block))
                both = jnp.concatenate([rows[h, raw_rows], rows[h + 1, raw_rows]], axis=1)
                made = jnp.dot(pick, both, preferred_element_type=jnp.float32).astype(jnp.bfloat16)
                span = slice(first_token, first_token + block)
                for i in range(2):
                    keys_ref[h + i, span] = made[:block, i * HD : (i + 1) * HD]
                    values[h + i, span] = made[block:, i * HD : (i + 1) * HD]
        span = slice(p * part, (p + 1) * part)
        sent += start_all([pltpu.make_async_copy(values.at[span], values_ref.at[span], out_sem.at[p])])
    wait_all(sent)


def cache_by_head(pool, first, heads):
    tokens = pool.shape[0]
    return pl.pallas_call(
        functools.partial(cache_kernel, first),
        out_shape=(
            jax.ShapeDtypeStruct((heads, tokens, HD), pool.dtype),
            pltpu.HBM((heads, tokens, HD), pool.dtype),
        ),
        in_specs=[HBM],
        out_specs=(VMEM, HBM),
        scratch_shapes=[
            pltpu.VMEM((heads, tokens, 2, HD), pool.dtype),
            pltpu.VMEM((heads, tokens, HD), pool.dtype),
            pltpu.SemaphoreType.DMA((heads,)),
            pltpu.SemaphoreType.DMA((heads // CACHE_SECTION,)),
        ],
        compiler_params=pltpu.CompilerParams(vmem_limit_bytes=12 * 2**20),
        cost_estimate=pl.CostEstimate(flops=0, bytes_accessed=12 * 10**6, transcendentals=0),
        name="cache_by_head",
    )(in_hbm(pool))


def lanes_of(x):
    return jnp.concatenate([x[c] for c in range(x.shape[0])], axis=1)


def step_rows(x, first, chunks):
    steps, _, count = x.shape[:3]
    flat = x.reshape(steps, x.shape[1], 2 * count, HD)
    return jnp.concatenate(
        [jnp.concatenate([flat[t, c] for c in range(first, first + chunks)], axis=1) for t in range(steps)], axis=0
    )


def pack_kernel(*refs):
    blocks, (out_ref, sem) = refs[:-2], refs[-2:]
    wait_all(
        start_all([pltpu.make_async_copy(block, out_ref.at[i], sem.at[i]) for i, block in enumerate(blocks)])
    )


def packed(blocks):
    return pl.pallas_call(
        pack_kernel,
        out_shape=jax.ShapeDtypeStruct((len(blocks),) + blocks[0].shape, blocks[0].dtype),
        in_specs=[ANY] * len(blocks),
        out_specs=VMEM,
        scratch_shapes=[pltpu.SemaphoreType.DMA((len(blocks),))],
        compiler_params=pltpu.CompilerParams(vmem_limit_bytes=2 * 2**20),
        cost_estimate=pl.CostEstimate(flops=0, bytes_accessed=10**6, transcendentals=0),
        name="pack_blocks",
    )(*blocks)


def index_kernel(me_ref, stored_ref, slot_ref, column_ref):
    requests = stored_ref.shape[1]
    steps = slot_ref.shape[1] // requests
    row = jnp.concatenate([stored_ref[...]] * steps, axis=1)
    slot_ref[...] = row - me_ref[0]
    wide = jnp.concatenate([row, jnp.zeros((1, HD - row.shape[1]), row.dtype)], axis=1)
    column_ref[...] = jnp.broadcast_to(wide.astype(jnp.float32), (HD, HD)).T[: row.shape[1], :1].astype(jnp.int32)


def index_work(first, stored, steps):
    rows = stored.shape[0] * steps
    return pl.pallas_call(
        index_kernel,
        out_shape=(jax.ShapeDtypeStruct((1, rows), jnp.int32), jax.ShapeDtypeStruct((rows, 1), jnp.int32)),
        in_specs=[SMEM, VMEM],
        out_specs=(VMEM, VMEM),
        compiler_params=pltpu.CompilerParams(vmem_limit_bytes=2 * 2**20),
        cost_estimate=pl.CostEstimate(flops=2 * 10**10, bytes_accessed=10**4, transcendentals=0),
        name="index_work",
    )(first, stored[None, :])


def low_kernel(places, packs, me_ref, slot_ref, down_ref, pack_ref, *refs):
    blocks, (x_ref, low_ref, sem) = refs[: len(places)], refs[len(places) :]
    me = me_ref[0]
    holders, rank, width = down_ref.shape
    sources = list(zip(places, blocks)) + [(k, pack_ref.at[i]) for i, k in enumerate(packs)]
    wait_all(
        start_all([pltpu.make_async_copy(block, x_ref.at[:, :, me ^ k], sem.at[k]) for k, block in sources])
    )
    x = step_rows(x_ref, 0, x_ref.shape[1])
    rows = x.shape[0]
    made = lax.dot_general(
        down_ref.reshape(holders * rank, width)[...], x, CONTRACT_LANES, preferred_element_type=jnp.float32
    )
    slot = slot_ref[...]
    low = jnp.zeros((rank, rows), jnp.float32)
    for h in range(holders):
        low = low + jnp.where(slot == h, made[h * rank : (h + 1) * rank], 0.0)
    low = low.T
    low_ref[...] = jnp.concatenate([low[: rows // 2], low[rows // 2 :]], axis=1).astype(low_ref.dtype)


def low_of(me, blocks, packs, pack, slot, down):
    count = len(blocks) + len(packs)
    steps, chunks = blocks[0].shape[:2]
    rows = count * steps * 2
    rank = down.shape[1]
    return pl.pallas_call(
        functools.partial(low_kernel, tuple(blocks), packs),
        out_shape=(
            jax.ShapeDtypeStruct((steps, chunks, count, 2, HD), jnp.bfloat16),
            jax.ShapeDtypeStruct((rows // 2, 2 * rank), jnp.bfloat16),
        ),
        in_specs=[SMEM, VMEM, VMEM, ANY] + [ANY] * len(blocks),
        out_specs=(VMEM, VMEM),
        scratch_shapes=[pltpu.SemaphoreType.DMA((count,))],
        compiler_params=pltpu.CompilerParams(vmem_limit_bytes=12 * 2**20),
        cost_estimate=pl.CostEstimate(flops=10**8, bytes_accessed=4 * 10**6, transcendentals=0),
        name="low_rows",
    )(me, slot, down, pack, *blocks.values())


def put_chunks(buf, first, value):
    steps, count = buf.shape[1:3]
    flat = buf.reshape(buf.shape[0], steps, 2 * count, HD)
    wide = value.shape[1]
    for c in range(-(-wide // HD)):
        part = value[:, c * HD : min((c + 1) * HD, wide)]
        if part.shape[1] < HD:
            part = jnp.concatenate([part, jnp.zeros((part.shape[0], HD - part.shape[1]), part.dtype)], axis=1)
        part = part.astype(buf.dtype)
        for t in range(steps):
            flat[first + c, t] = part[t * 2 * count : (t + 1) * 2 * count]


def project_kernel(which, x_ref, w_ref, out_ref):
    x = step_rows(x_ref, 0, x_ref.shape[1])
    made = lax.dot_general(w_ref[which], x, CONTRACT_LANES, preferred_element_type=jnp.float32).T
    if which < 2:
        pad = jnp.zeros((made.shape[0], HD // 2), made.dtype)
        put_chunks(out_ref, 0, jnp.concatenate([made, pad] if which == 0 else [pad, made], axis=1))
    else:
        out_ref[...] = made


def project(which, x, weight):
    steps, _, count = x.shape[:3]
    columns = weight.shape[1]
    chunks = jax.ShapeDtypeStruct((-(-columns // HD), steps, count, 2, HD), jnp.bfloat16)
    base = jax.ShapeDtypeStruct((2 * steps * count, columns), jnp.float32)
    return pl.pallas_call(
        functools.partial(project_kernel, which),
        out_shape=chunks if which < 2 else base,
        in_specs=[VMEM, VMEM],
        out_specs=VMEM,
        compiler_params=pltpu.CompilerParams(vmem_limit_bytes=16 * 2**20),
        cost_estimate=pl.CostEstimate(flops=5 * 10**8, bytes_accessed=4 * 10**6, transcendentals=0),
        name="project",
    )(x, weight)


def update_kernel(stored_ref, query_ref, key_ref, base_ref, up_ref, *refs):
    lows, (send_ref, buf, sem) = refs[:-3], refs[-3:]
    half, packed = lows[0].shape
    rank = packed // 2
    rows = 2 * half
    count = send_ref.shape[0]
    low = lows[0][...].astype(jnp.float32)
    for more in lows[1:]:
        low = low + more[...].astype(jnp.float32)
    low = jnp.concatenate([low[:, :rank], low[:, rank:]], axis=0)
    batch = 256 // rank
    spread = jnp.concatenate([low] * batch, axis=1)
    ahead = stored_ref[...] - lax.broadcasted_iota(jnp.int32, (rows, batch * rank), 1) // rank
    total = jnp.zeros(base_ref.shape, jnp.float32)
    for a in range(0, up_ref.shape[0] // rank, batch):
        wide = jnp.where(ahead == a, spread, 0.0).astype(jnp.bfloat16)
        total = total + jnp.dot(wide, up_ref[a * rank : (a + batch) * rank], preferred_element_type=jnp.float32)
    each = query_ref.shape[0]
    buf[: each - 1] = query_ref[: each - 1]
    buf[each - 1] = query_ref[each - 1] + key_ref[0]
    buf[each : 2 * each - 1] = key_ref[1:]
    put_chunks(buf, 2 * each - 1, base_ref[...] + adapter_scale * total)
    wait_all(
        start_all([pltpu.make_async_copy(buf.at[:, :, k], send_ref.at[k], sem.at[k]) for k in range(count)])
    )


def update_values(stored, query, key, base, up, lows):
    chunks, steps, count = query.shape[:3]
    return pl.pallas_call(
        update_kernel,
        out_shape=pltpu.HBM((count, 3 * chunks - 1, steps, 2, HD), query.dtype),
        in_specs=[VMEM] * (5 + len(lows)),
        out_specs=HBM,
        scratch_shapes=[
            pltpu.VMEM((3 * chunks - 1, steps, count, 2, HD), query.dtype),
            pltpu.SemaphoreType.DMA((count,)),
        ],
        compiler_params=pltpu.CompilerParams(vmem_limit_bytes=8 * 2**20),
        cost_estimate=pl.CostEstimate(flops=3 * 10**8, bytes_accessed=4 * 10**6, transcendentals=0),
        name="update_values",
    )(stored, query, key, base, up, *lows)


def attend_kernel(cos_ref, sin_ref, live_ref, pieces_ref, *refs):
    *parts, out_ref, values_buf, kn_ref, vn_ref, sem = refs
    keys_refs, values_refs = parts[: len(parts) // 2], parts[len(parts) // 2 :]
    count, _, steps = pieces_ref.shape[:3]
    rows = 2 * steps
    each = (pieces_ref.shape[1] + 1) // 3
    heads = 2 * out_ref.shape[1] // count
    lanes = heads * HD
    group = rows * HEAD_BLOCK
    chips = range(count // 2)
    early = keys_refs[0].shape[0] // heads
    places = [(0, c) if c < early else (1, c - early) for c in chips]
    fetches = start_all(
        [
            pltpu.make_async_copy(values_refs[half].at[at * heads : (at + 1) * heads], values_buf.at[c], sem.at[c])
            for c, (half, at) in enumerate(places)
        ]
    )
    cosine = cos_ref[...][:rows]
    sine = sin_ref[...][:rows]
    left = lax.broadcasted_iota(jnp.int32, (rows, HD), 1) < HD // 2

    def halves(chip, at):
        return [
            [pieces_ref[2 * chip + core, at + c].reshape(rows, HD).astype(jnp.float32) for c in range(each)]
            for core in range(2)
        ]

    def swapped(parts):
        return [pltpu.roll(x, HD // 2, 1) for x in parts]

    def joined(parts):
        return [jnp.where(left, a, b) for a, b in zip(parts[:-1], parts[1:])]

    def chip_columns(chip, at):
        low, high = halves(chip, at)
        high = swapped(high)
        return low[:-1] + [jnp.where(left, low[-1], high[0])] + joined(high)

    def chip_keys(chip):
        low, high = halves(chip, each - 1)
        low = swapped(low)
        return joined(low) + [jnp.where(left, low[-1], high[0])] + high[1:]

    def rotated(parts):
        return [x * cosine + pltpu.roll(x, HD // 2, 1) * sine for x in parts]

    row_head = lax.broadcasted_iota(jnp.int32, (group, lanes), 0) % HEAD_BLOCK
    lane_head = lax.broadcasted_iota(jnp.int32, (group, lanes), 1) // HD
    own_head = row_head == lane_head
    row_j = lax.broadcasted_iota(jnp.int32, (group, 16), 0) // HEAD_BLOCK
    new_j = lax.broadcasted_iota(jnp.int32, (group, 16), 1)
    new_live = (new_j < rows) & (new_j % 2 == row_j % 2) & (new_j // 2 <= row_j // 2)
    live = jnp.concatenate(
        [
            jnp.broadcast_to(live_ref[j % 2 : j % 2 + 1, :], (HEAD_BLOCK, live_ref.shape[1]))
            for j in range(rows)
        ],
        axis=0,
    )
    live = live > 0
    kn_ref[...] = jnp.zeros_like(kn_ref)
    vn_ref[...] = jnp.zeros_like(vn_ref)
    spreads = []
    for c in chips:
        query = jnp.concatenate(rotated(chip_columns(c, 0)), axis=1)
        kn_ref[c, 0:rows] = jnp.concatenate(rotated(chip_keys(c)), axis=1)
        vn_ref[c, 0:rows] = jnp.concatenate(chip_columns(c, 2 * each - 1), axis=1)
        spread = jnp.concatenate(
            [jnp.broadcast_to(query[j : j + 1], (HEAD_BLOCK, lanes)) for j in range(rows)], axis=0
        )
        spreads.append(jnp.where(own_head, spread, 0.0).astype(jnp.bfloat16))
    scores, fresh = [], []
    for c in chips:
        half, at = places[c]
        keys = jnp.concatenate([keys_refs[half][at * heads + h] for h in range(heads)], axis=1)
        kn = kn_ref[c].astype(jnp.bfloat16)
        scores.append(lax.dot_general(spreads[c], keys, CONTRACT_LANES, preferred_element_type=jnp.float32))
        fresh.append(lax.dot_general(spreads[c], kn, CONTRACT_LANES, preferred_element_type=jnp.float32))
    weights, fresh_weights, totals = [], [], []
    for c in chips:
        old = jnp.where(live, scores[c] * (HD**-0.5), masked_score)
        new = jnp.where(new_live, fresh[c] * (HD**-0.5), masked_score)
        top = jnp.maximum(jnp.max(old, axis=1, keepdims=True), jnp.max(new, axis=1, keepdims=True))
        old = jnp.where(live, jnp.exp(old - top), 0.0)
        new = jnp.where(new_live, jnp.exp(new - top), 0.0)
        totals.append(jnp.sum(old, axis=1, keepdims=True) + jnp.sum(new, axis=1, keepdims=True))
        weights.append(old.astype(jnp.bfloat16))
        fresh_weights.append(new.astype(jnp.bfloat16))
    wait_all(fetches)
    for c in chips:
        values = lanes_of(values_buf[c])
        vn = vn_ref[c].astype(jnp.bfloat16)
        mixed = jnp.dot(weights[c], values, preferred_element_type=jnp.float32)
        mixed = mixed + jnp.dot(fresh_weights[c], vn, preferred_element_type=jnp.float32)
        mixed = jnp.where(own_head, mixed / totals[c], 0.0)
        out = jnp.sum(mixed.reshape(rows, HEAD_BLOCK, lanes), axis=1).astype(out_ref.dtype)
        for t in range(steps):
            for h in range(heads):
                out_ref[t, c * heads + h] = out[2 * t : 2 * t + 2, h * HD : (h + 1) * HD]


def attend(cosine, sine, live, pieces, keys, values):
    count, _, steps = pieces.shape[:3]
    heads, tokens = sum(x.shape[0] for x in keys), keys[0].shape[1]
    chips = count // 2
    per = heads // chips
    return pl.pallas_call(
        attend_kernel,
        out_shape=jax.ShapeDtypeStruct((steps, heads, 2, HD), jnp.bfloat16),
        in_specs=[VMEM] * (4 + len(keys)) + [HBM] * len(values),
        out_specs=VMEM,
        scratch_shapes=[pltpu.VMEM((chips, per, tokens, HD), jnp.bfloat16)]
        + [pltpu.VMEM((chips, 16, per * HD), jnp.float32)] * 2
        + [pltpu.SemaphoreType.DMA((chips,))],
        compiler_params=pltpu.CompilerParams(vmem_limit_bytes=16 * 2**20),
        cost_estimate=pl.CostEstimate(flops=10**9, bytes_accessed=6 * 10**6, transcendentals=0),
        name="attention",
    )(cosine, sine, live, pieces, *keys, *[in_hbm(x) for x in values])


def chip_plan(
    count,
    hidden,
    query_key_value_weight,
    adapter_down_maps,
    adapter_up_maps,
    adapter_storage_row,
    request_adapter,
    lengths,
    request_page_table,
    key_value_pool,
):
    me = lax.axis_index("replica")
    steps, req_dev, width = hidden.shape
    heads = width // HD
    holder_count, rank, _ = adapter_down_maps.shape
    pool_pages, page_len = key_value_pool.shape[:2]
    adapter_count = adapter_storage_row.shape[0]

    tokens = pool_pages * page_len
    pool = key_value_pool.reshape(tokens, 2, heads, HD).transpose(0, 2, 1, 3)

    stored = jnp.sum(
        jnp.where(
            request_adapter[:, None] == jnp.arange(adapter_count, dtype=jnp.int32)[None, :],
            adapter_storage_row[None, :],
            0,
        ),
        axis=1,
    )
    first, slots, here, stored = lax.optimization_barrier(
        (me * req_dev, (me * holder_count).astype(jnp.int32).reshape(1), me.astype(jnp.int32).reshape(1), stored)
    )
    slot, column = index_work(slots, stored, steps)

    held = {0: hidden}
    held.update({m: trade(hidden, m, count) for m in range(4, count, 4)})
    _, lengths, request_page_table = lax.optimization_barrier((held[4], lengths, request_page_table))
    cosine, sine = rotation_rows(lengths, first, req_dev, steps)
    live = live_lanes(lengths, first, request_page_table, tokens, page_len)
    far = count - 4
    held[4], held[far] = lax.optimization_barrier((held[4], held[far]))
    held.update({k | 2: trade(v, 2, count) for k, v in list(held.items())})
    held = {k: v.reshape(steps, req_dev, heads, HD).transpose(0, 2, 1, 3) for k, v in held.items()}
    line = tuple(range(0, count, 4))
    *share, held[2], held[6] = lax.optimization_barrier([held[k] for k in line] + [held[2], held[6]])
    pack = trade(packed(share), 1, count)
    held.update({k | 1: trade(held[k], 1, count) for k in range(2, count, 4)})
    held[0] = in_hbm(held[0])
    x, low = low_of(here, held, tuple(k | 1 for k in line), pack, slot, adapter_down_maps)
    weight = query_key_value_weight.transpose(0, 2, 1)
    arrived = [trade(low, m, count) for m in (1, 2, 3)]
    query, key = project(0, x, weight), project(1, x, weight)
    arrived, query, key, pool = lax.optimization_barrier((arrived, query, key, pool))
    low = (low + arrived[0]) + (arrived[1] + arrived[2])
    arrived = [trade(low, m, count) for m in range(4, count, 4)]
    base = project(2, x, weight)
    arrived, base = lax.optimization_barrier((arrived, base))
    send = update_values(column, query, key, base, adapter_up_maps.reshape(adapter_count * rank, -1), [low, *arrived])
    send, pool = lax.optimization_barrier((send, pool))
    keys, values = cache_by_head(pool, 0, heads)
    pieces = lax.all_to_all(send, "replica", split_axis=0, concat_axis=0, tiled=True)

    out = attend(cosine, sine, live, pieces, [keys], [values])
    return out.transpose(0, 2, 1, 3).reshape(steps, req_dev, width)


def per_device(replicas, *arrays):
    columns = arrays[1].shape[2]
    whole_heads = replicas % 4 == 0 and (2 * columns) % HD == 0 and columns % HD == HD // 2
    plan = chip_plan if whole_heads and arrays[0].shape[1] == 2 else general_plan
    return plan(replicas, *arrays)


def solution(mesh):
    placed = (
        P(None, ("groups", "replica"), None),
        P(None, None, "replica"),
        P("replica", None, None),
        P(None, None, "replica"),
        P(),
        P("groups"),
        P("groups"),
        P(("groups", "replica"), None),
        P(("groups", "replica"), None, None, None),
    )
    return jax.shard_map(
        functools.partial(per_device, mesh.shape["replica"]),
        mesh=mesh,
        in_specs=placed,
        out_specs=P(None, ("groups", "replica"), None),
        check_vma=False,
    )
```

```python
import functools

import jax
import jax.numpy as jnp
from jax import lax
from jax.experimental import pallas as pl
from jax.experimental.pallas import tpu as pltpu
from jax.sharding import PartitionSpec as P

HD = 128
ROWS = 8
HEAD_BLOCK = 8

adapter_scale = 2.0
masked_score = -1e30


def attention_kernel(steps, req_dev, q_ref, k_ref, v_ref, cos_ref, sin_ref, live_ref, kv_ref, out_ref, kn_ref, vn_ref):
    rows = steps * req_dev
    width = q_ref.shape[1]
    lanes = HEAD_BLOCK * HD
    group = rows * HEAD_BLOCK
    cosine = cos_ref[...]
    sine = sin_ref[...]

    def rotated(x):
        pieces = []
        for h in range(HEAD_BLOCK):
            head = x[:, h * HD : (h + 1) * HD]
            pieces.append(head * cosine + pltpu.roll(head, HD // 2, 1) * sine)
        return jnp.concatenate(pieces, axis=1)

    row_head = lax.broadcasted_iota(jnp.int32, (group, lanes), 0) % HEAD_BLOCK
    lane_head = lax.broadcasted_iota(jnp.int32, (group, lanes), 1) // HD
    own_head = row_head == lane_head
    row_j = lax.broadcasted_iota(jnp.int32, (group, 16), 0) // HEAD_BLOCK
    new_j = lax.broadcasted_iota(jnp.int32, (group, 16), 1)
    new_live = (new_j < rows) & (new_j % req_dev == row_j % req_dev) & (new_j // req_dev <= row_j // req_dev)
    live_all = live_ref[...]
    live = jnp.concatenate(
        [
            jnp.broadcast_to(live_all[j % req_dev : j % req_dev + 1], (HEAD_BLOCK, live_all.shape[1]))
            for j in range(rows)
        ],
        axis=0,
    )
    live = live > 0
    kn_ref[...] = jnp.zeros_like(kn_ref)
    vn_ref[...] = jnp.zeros_like(vn_ref)
    contract_lanes = (((1,), (1,)), ((), ()))
    for c in range(width // lanes):
        cols = slice(c * lanes, (c + 1) * lanes)
        query = rotated(q_ref[:, cols].astype(jnp.float32))
        key_new = rotated(k_ref[:, cols].astype(jnp.float32))
        kn_ref[0:8] = key_new
        vn_ref[0:8] = v_ref[:, cols].astype(jnp.float32)
        kn = kn_ref[...].astype(jnp.bfloat16)
        vn = vn_ref[...].astype(jnp.bfloat16)
        spread = jnp.concatenate(
            [jnp.broadcast_to(query[j : j + 1], (HEAD_BLOCK, lanes)) for j in range(rows)], axis=0
        )
        spread = jnp.where(own_head, spread, 0.0).astype(jnp.bfloat16)
        kv = kv_ref[:, cols]
        scores = lax.dot_general(spread, kv, contract_lanes, preferred_element_type=jnp.float32) * (HD**-0.5)
        scores = jnp.where(live, scores, masked_score)
        fresh = lax.dot_general(spread, kn, contract_lanes, preferred_element_type=jnp.float32) * (HD**-0.5)
        fresh = jnp.where(new_live, fresh, masked_score)
        top = jnp.maximum(jnp.max(scores, axis=1, keepdims=True), jnp.max(fresh, axis=1, keepdims=True))
        weights = jnp.where(live, jnp.exp(scores - top), 0.0)
        fresh = jnp.where(new_live, jnp.exp(fresh - top), 0.0)
        totals = jnp.sum(weights, axis=1, keepdims=True) + jnp.sum(fresh, axis=1, keepdims=True)
        weights = pltpu.roll(weights, 1, 1).astype(jnp.bfloat16)
        mixed = jnp.dot(weights, kv, preferred_element_type=jnp.float32)
        mixed = mixed + jnp.dot(fresh.astype(jnp.bfloat16), vn, preferred_element_type=jnp.float32)
        mixed = jnp.where(own_head, mixed / totals, 0.0)
        out = jnp.sum(mixed.reshape(rows, HEAD_BLOCK, lanes), axis=1)
        out_ref[:, cols] = out.astype(out_ref.dtype)


def attention(steps, req_dev, q, k, v, cosine, sine, live, kv):
    rows = steps * req_dev
    width = q.shape[1]
    vmem = pl.BlockSpec(memory_space=pltpu.VMEM)
    return pl.pallas_call(
        functools.partial(attention_kernel, steps, req_dev),
        out_shape=jax.ShapeDtypeStruct((rows, width), jnp.bfloat16),
        in_specs=[vmem] * 7,
        out_specs=vmem,
        scratch_shapes=[pltpu.VMEM((16, HEAD_BLOCK * HD), jnp.float32)] * 2,
        compiler_params=pltpu.CompilerParams(vmem_limit_bytes=32 * 2**20),
        cost_estimate=pl.CostEstimate(flops=10**9, bytes_accessed=6 * 10**6, transcendentals=0),
        name="attention",
    )(q, k, v, cosine, sine, live, kv)


def rotation(my_lengths, steps):
    rows = steps * my_lengths.shape[0]
    positions = (my_lengths[None, :] + jnp.arange(steps, dtype=jnp.int32)[:, None]).reshape(rows)
    positions = jnp.pad(positions, (0, ROWS - rows))
    half = HD // 2
    frequency = jnp.exp(jnp.arange(half, dtype=jnp.float32) * (-2.0 * jnp.log(10000.0) / HD))
    angles = positions.astype(jnp.float32)[:, None] * frequency[None, :]
    cosine = jnp.cos(angles)
    sine = jnp.sin(angles)
    cosine = jnp.concatenate([cosine, cosine], axis=1)
    sine = jnp.concatenate([-sine, sine], axis=1)
    return cosine, sine


def live_tokens(my_lengths, request_page_table, pool_pages, page_len):
    pages = jnp.arange(pool_pages, dtype=jnp.int32)
    max_pages = request_page_table.shape[1]
    place = jnp.max(
        jnp.where(
            request_page_table[:, :, None] == pages[None, None, :],
            jnp.arange(max_pages, dtype=jnp.int32)[None, :, None],
            -1,
        ),
        axis=1,
    )
    token = place[:, :, None] * page_len + jnp.arange(page_len, dtype=jnp.int32)[None, None, :]
    return (place[:, :, None] >= 0) & (token < my_lengths[:, None, None])


def live_rows(my_lengths, request_page_table, pool_pages, page_len):
    alive = live_tokens(my_lengths, request_page_table, pool_pages, page_len)
    live = jnp.stack([alive, jnp.zeros_like(alive)], axis=-1).astype(jnp.int32)
    return live.reshape(request_page_table.shape[0], pool_pages * page_len * 2)


def general_plan(
    replicas,
    hidden,
    query_key_value_weight,
    adapter_down_maps,
    adapter_up_maps,
    adapter_storage_row,
    request_adapter,
    lengths,
    request_page_table,
    key_value_pool,
):
    my_index = lax.axis_index("replica")
    steps, req_dev, width = hidden.shape
    rows = steps * req_dev
    columns = query_key_value_weight.shape[2]
    holder_count, rank, _ = adapter_down_maps.shape
    pool_pages, page_len = key_value_pool.shape[:2]
    adapter_count = adapter_storage_row.shape[0]
    chips = replicas // 2
    total = replicas * ROWS

    block = jnp.pad(hidden.reshape(rows, width), ((0, ROWS - rows), (0, 0)))
    same_core = [[2 * chip + core for chip in range(chips)] for core in range(2)]
    mine = lax.all_to_all(
        jnp.broadcast_to(block[None], (chips, ROWS, width)),
        "replica",
        split_axis=0,
        concat_axis=0,
        axis_index_groups=same_core,
        tiled=True,
    )
    other = lax.ppermute(mine, "replica", [(i, i ^ 1) for i in range(replicas)])
    first = my_index % 2 == 0
    gathered = jnp.stack([jnp.where(first, mine, other), jnp.where(first, other, mine)])
    gathered = gathered.reshape(total, width)

    stored_rows = jnp.sum(
        jnp.where(
            request_adapter[:, None] == jnp.arange(adapter_count, dtype=jnp.int32)[None, :],
            adapter_storage_row[None, :],
            0,
        ),
        axis=1,
    )
    by_block = stored_rows.reshape(chips, 2, 1, req_dev).transpose(1, 0, 2, 3)
    by_block = jnp.broadcast_to(by_block, (2, chips, steps, req_dev)).reshape(2, chips, rows)
    row_stored = jnp.pad(by_block, ((0, 0), (0, 0), (0, ROWS - rows)), constant_values=-1).reshape(total)

    down = jnp.einsum("nd,hfd->nhf", gathered, adapter_down_maps, preferred_element_type=jnp.float32)
    slots = my_index * holder_count + jnp.arange(holder_count, dtype=jnp.int32)
    own = row_stored[:, None] == slots[None, :]
    low = jnp.sum(jnp.where(own[:, :, None], down, 0.0), axis=1).astype(jnp.bfloat16)
    low = jnp.concatenate([low[: total // 2], low[total // 2 :]], axis=1)
    low = lax.all_to_all(
        jnp.broadcast_to(low[None], (replicas,) + low.shape), "replica", split_axis=0, concat_axis=0, tiled=True
    )
    low = jnp.sum(low.astype(jnp.float32), axis=0)
    low = jnp.concatenate([low[:, :rank], low[:, rank:]], axis=0)

    projected = jnp.einsum("nd,idc->nic", gathered, query_key_value_weight, preferred_element_type=jnp.float32)

    def update(first_adapter, maps):
        held = maps.shape[0]
        which = first_adapter + jnp.arange(held, dtype=jnp.int32)
        wide = jnp.where((row_stored[:, None] == which[None, :])[:, :, None], low[:, None, :], 0.0)
        return jnp.dot(
            wide.astype(jnp.bfloat16).reshape(total, held * rank),
            maps.reshape(held * rank, columns),
            preferred_element_type=jnp.float32,
        )

    step_adapters = 64
    if adapter_count <= step_adapters:
        updated = update(0, adapter_up_maps)
    else:
        updated = lax.fori_loop(
            0,
            adapter_count // step_adapters,
            lambda i, sofar: sofar
            + update(
                i * step_adapters,
                lax.dynamic_slice_in_dim(adapter_up_maps, i * step_adapters, step_adapters, 0),
            ),
            jnp.zeros((total, columns), jnp.float32),
        )
    value = projected[:, 2] + adapter_scale * updated
    combined = jnp.concatenate([projected[:, 0], projected[:, 1], value], axis=1).astype(jnp.bfloat16)
    combined = combined.reshape(2, chips, ROWS, 3 * columns).transpose(1, 0, 2, 3)
    combined = combined.reshape(replicas, ROWS, 3 * columns)
    arrived = lax.all_to_all(combined, "replica", split_axis=0, concat_axis=0, tiled=True)
    arrived = arrived.reshape(replicas, ROWS, 3, columns).transpose(2, 1, 0, 3).reshape(3, ROWS, width)

    my_lengths = lax.dynamic_slice_in_dim(lengths, my_index * req_dev, req_dev)
    cosine, sine = rotation(my_lengths, steps)
    live = live_rows(my_lengths, request_page_table, pool_pages, page_len)
    kv = key_value_pool.reshape(pool_pages * page_len * 2, width)
    out = attention(steps, req_dev, arrived[0], arrived[1], arrived[2], cosine, sine, live, kv)
    return out.reshape(steps, req_dev, width)


def rotation_rows(lengths, first, req_dev, steps):
    row = jnp.arange(ROWS, dtype=jnp.int32)
    wanted = first + row % req_dev
    chosen = jnp.where(wanted[:, None] == jnp.arange(lengths.shape[0], dtype=jnp.int32)[None, :], lengths[None, :], 0)
    positions = jnp.sum(chosen, axis=1, keepdims=True) + (row // req_dev)[:, None]
    lane = jnp.arange(HD, dtype=jnp.int32)
    frequency = jnp.exp((lane % (HD // 2)).astype(jnp.float32) * (-2.0 * jnp.log(10000.0) / HD))
    angles = positions.astype(jnp.float32) * frequency[None, :]
    return jnp.cos(angles), jnp.where(lane < HD // 2, -1.0, 1.0)[None, :] * jnp.sin(angles)


def live_lanes(lengths, first, request_page_table, tokens, page_len):
    req_dev, max_pages = request_page_table.shape
    wanted = first + jnp.arange(req_dev, dtype=jnp.int32)
    chosen = jnp.where(wanted[:, None] == jnp.arange(lengths.shape[0], dtype=jnp.int32)[None, :], lengths[None, :], 0)
    lane = jnp.arange(tokens, dtype=jnp.int32)
    page = jnp.arange(max_pages, dtype=jnp.int32)
    place = jnp.max(
        jnp.where(request_page_table[:, :, None] == (lane // page_len)[None, None, :], page[None, :, None], -1),
        axis=1,
    )
    token = place * page_len + (lane % page_len)[None, :]
    return ((place >= 0) & (token < jnp.sum(chosen, axis=1, keepdims=True))).astype(jnp.int32)


def trade(value, mask, count):
    return lax.ppermute(value, "replica", [(i, i ^ mask) for i in range(count)])


CONTRACT_LANES = (((1,), (1,)), ((), ()))


def in_hbm(x):
    return pltpu.with_memory_space_constraint(x, pltpu.HBM)


VMEM = pl.BlockSpec(memory_space=pltpu.VMEM)
HBM = pl.BlockSpec(memory_space=pltpu.HBM)
SMEM = pl.BlockSpec(memory_space=pltpu.SMEM)
ANY = pl.BlockSpec(memory_space=pl.ANY)


def start_all(copies):
    for copy in copies:
        copy.start()
    return copies


def wait_all(copies):
    for copy in copies:
        copy.wait()


CACHE_SECTION = 10
CACHE_AHEAD = 4
CACHE_TOKENS = 128


def cache_kernel(first, pool_ref, keys_ref, values_ref, raw, values, sem, out_sem):
    heads, tokens = raw.shape[:2]
    copies = [pltpu.make_async_copy(pool_ref.at[:, first + h], raw.at[h], sem.at[h]) for h in range(heads)]
    start_all(copies[: CACHE_AHEAD * CACHE_SECTION])
    rows = raw.reshape(heads, 2 * tokens, HD)
    block = min(tokens, CACHE_TOKENS)
    to = lax.broadcasted_iota(jnp.int32, (2 * block, 2 * block), 0)
    source = lax.broadcasted_iota(jnp.int32, (2 * block, 2 * block), 1)
    wanted = jnp.where(to < block, 2 * to, 2 * (to - block) + 1)
    pick = jnp.where(source == wanted, 1.0, 0.0).astype(jnp.bfloat16)
    sent = []
    part = CACHE_SECTION
    for p in range(heads // part):
        wait_all(copies[p * part : (p + 1) * part])
        start_all(copies[(p + CACHE_AHEAD) * part : (p + CACHE_AHEAD + 1) * part])
        for h in range(p * part, (p + 1) * part, 2):
            for first_token in range(0, tokens, block):
                raw_rows = slice(2 * first_token, 2 * (first_token + block))
                both = jnp.concatenate([rows[h, raw_rows], rows[h + 1, raw_rows]], axis=1)
                made = jnp.dot(pick, both, preferred_element_type=jnp.float32).astype(jnp.bfloat16)
                span = slice(first_token, first_token + block)
                for i in range(2):
                    keys_ref[h + i, span] = made[:block, i * HD : (i + 1) * HD]
                    values[h + i, span] = made[block:, i * HD : (i + 1) * HD]
        span = slice(p * part, (p + 1) * part)
        sent += start_all([pltpu.make_async_copy(values.at[span], values_ref.at[span], out_sem.at[p])])
    wait_all(sent)


def cache_by_head(pool, first, heads):
    tokens = pool.shape[0]
    return pl.pallas_call(
        functools.partial(cache_kernel, first),
        out_shape=(
            jax.ShapeDtypeStruct((heads, tokens, HD), pool.dtype),
            pltpu.HBM((heads, tokens, HD), pool.dtype),
        ),
        in_specs=[HBM],
        out_specs=(VMEM, HBM),
        scratch_shapes=[
            pltpu.VMEM((heads, tokens, 2, HD), pool.dtype),
            pltpu.VMEM((heads, tokens, HD), pool.dtype),
            pltpu.SemaphoreType.DMA((heads,)),
            pltpu.SemaphoreType.DMA((heads // CACHE_SECTION,)),
        ],
        compiler_params=pltpu.CompilerParams(vmem_limit_bytes=12 * 2**20),
        cost_estimate=pl.CostEstimate(flops=0, bytes_accessed=12 * 10**6, transcendentals=0),
        name="cache_by_head",
    )(in_hbm(pool))


def lanes_of(x):
    return jnp.concatenate([x[c] for c in range(x.shape[0])], axis=1)


def step_rows(x, first, chunks):
    steps, _, count = x.shape[:3]
    flat = x.reshape(steps, x.shape[1], 2 * count, HD)
    return jnp.concatenate(
        [jnp.concatenate([flat[t, c] for c in range(first, first + chunks)], axis=1) for t in range(steps)], axis=0
    )


def pack_kernel(*refs):
    blocks, (out_ref, sem) = refs[:-2], refs[-2:]
    wait_all(
        start_all([pltpu.make_async_copy(block, out_ref.at[i], sem.at[i]) for i, block in enumerate(blocks)])
    )


def packed(blocks):
    return pl.pallas_call(
        pack_kernel,
        out_shape=jax.ShapeDtypeStruct((len(blocks),) + blocks[0].shape, blocks[0].dtype),
        in_specs=[ANY] * len(blocks),
        out_specs=VMEM,
        scratch_shapes=[pltpu.SemaphoreType.DMA((len(blocks),))],
        compiler_params=pltpu.CompilerParams(vmem_limit_bytes=2 * 2**20),
        cost_estimate=pl.CostEstimate(flops=0, bytes_accessed=10**6, transcendentals=0),
        name="pack_blocks",
    )(*blocks)


def index_kernel(me_ref, stored_ref, slot_ref, column_ref):
    requests = stored_ref.shape[1]
    steps = slot_ref.shape[1] // requests
    row = jnp.concatenate([stored_ref[...]] * steps, axis=1)
    slot_ref[...] = row - me_ref[0]
    wide = jnp.concatenate([row, jnp.zeros((1, HD - row.shape[1]), row.dtype)], axis=1)
    column_ref[...] = jnp.broadcast_to(wide.astype(jnp.float32), (HD, HD)).T[: row.shape[1], :1].astype(jnp.int32)


def index_work(first, stored, steps):
    rows = stored.shape[0] * steps
    return pl.pallas_call(
        index_kernel,
        out_shape=(jax.ShapeDtypeStruct((1, rows), jnp.int32), jax.ShapeDtypeStruct((rows, 1), jnp.int32)),
        in_specs=[SMEM, VMEM],
        out_specs=(VMEM, VMEM),
        compiler_params=pltpu.CompilerParams(vmem_limit_bytes=2 * 2**20),
        cost_estimate=pl.CostEstimate(flops=2 * 10**10, bytes_accessed=10**4, transcendentals=0),
        name="index_work",
    )(first, stored[None, :])


def low_kernel(places, packs, me_ref, slot_ref, down_ref, pack_ref, *refs):
    blocks, (x_ref, low_ref, sem) = refs[: len(places)], refs[len(places) :]
    me = me_ref[0]
    holders, rank, width = down_ref.shape
    sources = list(zip(places, blocks)) + [(k, pack_ref.at[i]) for i, k in enumerate(packs)]
    wait_all(
        start_all([pltpu.make_async_copy(block, x_ref.at[:, :, me ^ k], sem.at[k]) for k, block in sources])
    )
    x = step_rows(x_ref, 0, x_ref.shape[1])
    rows = x.shape[0]
    made = lax.dot_general(
        down_ref.reshape(holders * rank, width)[...], x, CONTRACT_LANES, preferred_element_type=jnp.float32
    )
    slot = slot_ref[...]
    low = jnp.zeros((rank, rows), jnp.float32)
    for h in range(holders):
        low = low + jnp.where(slot == h, made[h * rank : (h + 1) * rank], 0.0)
    low = low.T
    low_ref[...] = jnp.concatenate([low[: rows // 2], low[rows // 2 :]], axis=1).astype(low_ref.dtype)


def low_of(me, blocks, packs, pack, slot, down):
    count = len(blocks) + len(packs)
    steps, chunks = blocks[0].shape[:2]
    rows = count * steps * 2
    rank = down.shape[1]
    return pl.pallas_call(
        functools.partial(low_kernel, tuple(blocks), packs),
        out_shape=(
            jax.ShapeDtypeStruct((steps, chunks, count, 2, HD), jnp.bfloat16),
            jax.ShapeDtypeStruct((rows // 2, 2 * rank), jnp.bfloat16),
        ),
        in_specs=[SMEM, VMEM, VMEM, ANY] + [ANY] * len(blocks),
        out_specs=(VMEM, VMEM),
        scratch_shapes=[pltpu.SemaphoreType.DMA((count,))],
        compiler_params=pltpu.CompilerParams(vmem_limit_bytes=12 * 2**20),
        cost_estimate=pl.CostEstimate(flops=10**8, bytes_accessed=4 * 10**6, transcendentals=0),
        name="low_rows",
    )(me, slot, down, pack, *blocks.values())


def put_chunks(buf, first, value):
    steps, count = buf.shape[1:3]
    flat = buf.reshape(buf.shape[0], steps, 2 * count, HD)
    wide = value.shape[1]
    for c in range(-(-wide // HD)):
        part = value[:, c * HD : min((c + 1) * HD, wide)]
        if part.shape[1] < HD:
            part = jnp.concatenate([part, jnp.zeros((part.shape[0], HD - part.shape[1]), part.dtype)], axis=1)
        part = part.astype(buf.dtype)
        for t in range(steps):
            flat[first + c, t] = part[t * 2 * count : (t + 1) * 2 * count]


def project_kernel(which, x_ref, w_ref, out_ref):
    x = step_rows(x_ref, 0, x_ref.shape[1])
    made = lax.dot_general(w_ref[which], x, CONTRACT_LANES, preferred_element_type=jnp.float32).T
    if which < 2:
        pad = jnp.zeros((made.shape[0], HD // 2), made.dtype)
        put_chunks(out_ref, 0, jnp.concatenate([made, pad] if which == 0 else [pad, made], axis=1))
    else:
        out_ref[...] = made


def project(which, x, weight):
    steps, _, count = x.shape[:3]
    columns = weight.shape[1]
    chunks = jax.ShapeDtypeStruct((-(-columns // HD), steps, count, 2, HD), jnp.bfloat16)
    base = jax.ShapeDtypeStruct((2 * steps * count, columns), jnp.float32)
    return pl.pallas_call(
        functools.partial(project_kernel, which),
        out_shape=chunks if which < 2 else base,
        in_specs=[VMEM, VMEM],
        out_specs=VMEM,
        compiler_params=pltpu.CompilerParams(vmem_limit_bytes=16 * 2**20),
        cost_estimate=pl.CostEstimate(flops=5 * 10**8, bytes_accessed=4 * 10**6, transcendentals=0),
        name="project",
    )(x, weight)


def update_kernel(stored_ref, query_ref, key_ref, base_ref, up_ref, *refs):
    lows, (send_ref, buf, sem) = refs[:-3], refs[-3:]
    half, packed = lows[0].shape
    rank = packed // 2
    rows = 2 * half
    count = send_ref.shape[0]
    low = lows[0][...].astype(jnp.float32)
    for more in lows[1:]:
        low = low + more[...].astype(jnp.float32)
    low = jnp.concatenate([low[:, :rank], low[:, rank:]], axis=0)
    batch = 256 // rank
    spread = jnp.concatenate([low] * batch, axis=1)
    ahead = stored_ref[...] - lax.broadcasted_iota(jnp.int32, (rows, batch * rank), 1) // rank
    total = jnp.zeros(base_ref.shape, jnp.float32)
    for a in range(0, up_ref.shape[0] // rank, batch):
        wide = jnp.where(ahead == a, spread, 0.0).astype(jnp.bfloat16)
        total = total + jnp.dot(wide, up_ref[a * rank : (a + batch) * rank], preferred_element_type=jnp.float32)
    each = query_ref.shape[0]
    buf[: each - 1] = query_ref[: each - 1]
    buf[each - 1] = query_ref[each - 1] + key_ref[0]
    buf[each : 2 * each - 1] = key_ref[1:]
    put_chunks(buf, 2 * each - 1, base_ref[...] + adapter_scale * total)
    wait_all(
        start_all([pltpu.make_async_copy(buf.at[:, :, k], send_ref.at[k], sem.at[k]) for k in range(count)])
    )


def update_values(stored, query, key, base, up, lows):
    chunks, steps, count = query.shape[:3]
    return pl.pallas_call(
        update_kernel,
        out_shape=pltpu.HBM((count, 3 * chunks - 1, steps, 2, HD), query.dtype),
        in_specs=[VMEM] * (5 + len(lows)),
        out_specs=HBM,
        scratch_shapes=[
            pltpu.VMEM((3 * chunks - 1, steps, count, 2, HD), query.dtype),
            pltpu.SemaphoreType.DMA((count,)),
        ],
        compiler_params=pltpu.CompilerParams(vmem_limit_bytes=8 * 2**20),
        cost_estimate=pl.CostEstimate(flops=3 * 10**8, bytes_accessed=4 * 10**6, transcendentals=0),
        name="update_values",
    )(stored, query, key, base, up, *lows)


def attend_kernel(cos_ref, sin_ref, live_ref, pieces_ref, *refs):
    *parts, out_ref, values_buf, kn_ref, vn_ref, sem = refs
    keys_refs, values_refs = parts[: len(parts) // 2], parts[len(parts) // 2 :]
    count, _, steps = pieces_ref.shape[:3]
    rows = 2 * steps
    each = (pieces_ref.shape[1] + 1) // 3
    heads = 4 * out_ref.shape[1] // count
    block = -(-heads // 8) * 8
    lanes = heads * HD
    group = rows * block
    chips = range(count // 4)
    early = keys_refs[0].shape[0] // heads
    places = [(0, c) if c < early else (1, c - early) for c in chips]
    fetches = start_all(
        [
            pltpu.make_async_copy(values_refs[half].at[at * heads : (at + 1) * heads], values_buf.at[c], sem.at[c])
            for c, (half, at) in enumerate(places)
        ]
    )
    cosine = cos_ref[...][:rows]
    sine = sin_ref[...][:rows]
    left = lax.broadcasted_iota(jnp.int32, (rows, HD), 1) < HD // 2

    def halves(chip, at):
        return [
            [pieces_ref[2 * chip + core, at + c].reshape(rows, HD).astype(jnp.float32) for c in range(each)]
            for core in range(2)
        ]

    def swapped(parts):
        return [pltpu.roll(x, HD // 2, 1) for x in parts]

    def joined(parts):
        return [jnp.where(left, a, b) for a, b in zip(parts[:-1], parts[1:])]

    def chip_columns(chip, at):
        low, high = halves(chip, at)
        high = swapped(high)
        return low[:-1] + [jnp.where(left, low[-1], high[0])] + joined(high)

    def chip_keys(chip):
        low, high = halves(chip, each - 1)
        low = swapped(low)
        return joined(low) + [jnp.where(left, low[-1], high[0])] + high[1:]

    def rotated(parts):
        return [x * cosine + pltpu.roll(x, HD // 2, 1) * sine for x in parts]

    row_head = lax.broadcasted_iota(jnp.int32, (group, lanes), 0) % block
    lane_head = lax.broadcasted_iota(jnp.int32, (group, lanes), 1) // HD
    own_head = row_head == lane_head
    row_j = lax.broadcasted_iota(jnp.int32, (group, 16), 0) // block
    new_j = lax.broadcasted_iota(jnp.int32, (group, 16), 1)
    new_live = (new_j < rows) & (new_j % 2 == row_j % 2) & (new_j // 2 <= row_j // 2)
    live = jnp.concatenate(
        [
            jnp.broadcast_to(live_ref[j % 2 : j % 2 + 1, :], (block, live_ref.shape[1]))
            for j in range(rows)
        ],
        axis=0,
    )
    live = live > 0
    kn_ref[...] = jnp.zeros_like(kn_ref)
    vn_ref[...] = jnp.zeros_like(vn_ref)
    spreads = []
    for c in chips:
        query = jnp.concatenate(rotated(chip_columns(2 * c, 0) + chip_columns(2 * c + 1, 0)), axis=1)
        kn_ref[c, 0:rows] = jnp.concatenate(rotated(chip_keys(2 * c) + chip_keys(2 * c + 1)), axis=1)
        fresh_columns = chip_columns(2 * c, 2 * each - 1) + chip_columns(2 * c + 1, 2 * each - 1)
        vn_ref[c, 0:rows] = jnp.concatenate(fresh_columns, axis=1)
        spread = jnp.concatenate(
            [jnp.broadcast_to(query[j : j + 1], (block, lanes)) for j in range(rows)], axis=0
        )
        spreads.append(jnp.where(own_head, spread, 0.0).astype(jnp.bfloat16))
    scores, fresh = [], []
    for c in chips:
        half, at = places[c]
        keys = jnp.concatenate([keys_refs[half][at * heads + h] for h in range(heads)], axis=1)
        kn = kn_ref[c].astype(jnp.bfloat16)
        scores.append(lax.dot_general(spreads[c], keys, CONTRACT_LANES, preferred_element_type=jnp.float32))
        fresh.append(lax.dot_general(spreads[c], kn, CONTRACT_LANES, preferred_element_type=jnp.float32))
    weights, fresh_weights, totals = [], [], []
    for c in chips:
        old = jnp.where(live, scores[c] * (HD**-0.5), masked_score)
        new = jnp.where(new_live, fresh[c] * (HD**-0.5), masked_score)
        top = jnp.maximum(jnp.max(old, axis=1, keepdims=True), jnp.max(new, axis=1, keepdims=True))
        old = jnp.where(live, jnp.exp(old - top), 0.0)
        new = jnp.where(new_live, jnp.exp(new - top), 0.0)
        totals.append(jnp.sum(old, axis=1, keepdims=True) + jnp.sum(new, axis=1, keepdims=True))
        weights.append(old.astype(jnp.bfloat16))
        fresh_weights.append(new.astype(jnp.bfloat16))
    wait_all(fetches)
    for c in chips:
        values = lanes_of(values_buf[c])
        vn = vn_ref[c].astype(jnp.bfloat16)
        mixed = jnp.dot(weights[c], values, preferred_element_type=jnp.float32)
        mixed = mixed + jnp.dot(fresh_weights[c], vn, preferred_element_type=jnp.float32)
        mixed = jnp.sum(jnp.where(own_head, mixed, 0.0).reshape(rows, block, lanes), axis=1)
        total = jnp.sum(jnp.where(own_head, totals[c], 0.0).reshape(rows, block, lanes), axis=1)
        out = (mixed / total).astype(out_ref.dtype)
        for t in range(steps):
            for h in range(heads):
                out_ref[t, c * heads + h] = out[2 * t : 2 * t + 2, h * HD : (h + 1) * HD]


def attend(cosine, sine, live, pieces, keys, values):
    count, _, steps = pieces.shape[:3]
    heads, tokens = sum(x.shape[0] for x in keys), keys[0].shape[1]
    chips = count // 4
    per = heads // chips
    return pl.pallas_call(
        attend_kernel,
        out_shape=jax.ShapeDtypeStruct((steps, heads, 2, HD), jnp.bfloat16),
        in_specs=[VMEM] * (4 + len(keys)) + [HBM] * len(values),
        out_specs=VMEM,
        scratch_shapes=[pltpu.VMEM((chips, per, tokens, HD), jnp.bfloat16)]
        + [pltpu.VMEM((chips, 16, per * HD), jnp.float32)] * 2
        + [pltpu.SemaphoreType.DMA((chips,))],
        compiler_params=pltpu.CompilerParams(vmem_limit_bytes=16 * 2**20),
        cost_estimate=pl.CostEstimate(flops=10**9, bytes_accessed=6 * 10**6, transcendentals=0),
        name="attention",
    )(cosine, sine, live, pieces, *keys, *[in_hbm(x) for x in values])


def chip_plan(
    count,
    hidden,
    query_key_value_weight,
    adapter_down_maps,
    adapter_up_maps,
    adapter_storage_row,
    request_adapter,
    lengths,
    request_page_table,
    key_value_pool,
):
    me = lax.axis_index("replica")
    steps, req_dev, width = hidden.shape
    heads = width // HD
    holder_count, rank, _ = adapter_down_maps.shape
    pool_pages, page_len = key_value_pool.shape[:2]
    adapter_count = adapter_storage_row.shape[0]

    tokens = pool_pages * page_len
    pool = key_value_pool.reshape(tokens, 2, heads, HD).transpose(0, 2, 1, 3)

    stored = jnp.sum(
        jnp.where(
            request_adapter[:, None] == jnp.arange(adapter_count, dtype=jnp.int32)[None, :],
            adapter_storage_row[None, :],
            0,
        ),
        axis=1,
    )
    first, slots, here, stored = lax.optimization_barrier(
        (me * req_dev, (me * holder_count).astype(jnp.int32).reshape(1), me.astype(jnp.int32).reshape(1), stored)
    )
    slot, column = index_work(slots, stored, steps)

    held = {0: hidden}
    held.update({m: trade(hidden, m, count) for m in range(4, count, 4)})
    _, lengths, request_page_table = lax.optimization_barrier((held[4], lengths, request_page_table))
    cosine, sine = rotation_rows(lengths, first, req_dev, steps)
    live = live_lanes(lengths, first, request_page_table, tokens, page_len)
    far = count - 4
    held[4], held[far] = lax.optimization_barrier((held[4], held[far]))
    held.update({k | 2: trade(v, 2, count) for k, v in list(held.items())})
    held = {k: v.reshape(steps, req_dev, heads, HD).transpose(0, 2, 1, 3) for k, v in held.items()}
    line = tuple(range(0, count, 4))
    *share, held[2], held[6] = lax.optimization_barrier([held[k] for k in line] + [held[2], held[6]])
    pack = trade(packed(share), 1, count)
    held.update({k | 1: trade(held[k], 1, count) for k in range(2, count, 4)})
    held[0] = in_hbm(held[0])
    x, low = low_of(here, held, tuple(k | 1 for k in line), pack, slot, adapter_down_maps)
    weight = query_key_value_weight.transpose(0, 2, 1)
    arrived = [trade(low, m, count) for m in (1, 2, 3)]
    query, key = project(0, x, weight), project(1, x, weight)
    arrived, query, key, pool = lax.optimization_barrier((arrived, query, key, pool))
    low = (low + arrived[0]) + (arrived[1] + arrived[2])
    arrived = [trade(low, m, count) for m in range(4, count, 4)]
    base = project(2, x, weight)
    arrived, base = lax.optimization_barrier((arrived, base))
    send = update_values(column, query, key, base, adapter_up_maps.reshape(adapter_count * rank, -1), [low, *arrived])
    send, pool = lax.optimization_barrier((send, pool))
    keys, values = cache_by_head(pool, 0, heads)
    pieces = lax.all_to_all(send, "replica", split_axis=0, concat_axis=0, tiled=True)

    out = attend(cosine, sine, live, pieces, [keys], [values])
    return out.transpose(0, 2, 1, 3).reshape(steps, req_dev, width)


def per_device(replicas, *arrays):
    columns = arrays[1].shape[2]
    whole_heads = replicas % 4 == 0 and (2 * columns) % HD == 0 and columns % HD == HD // 2
    plan = chip_plan if whole_heads and arrays[0].shape[1] == 2 else general_plan
    return plan(replicas, *arrays)


def solution(mesh):
    placed = (
        P(None, ("groups", "replica"), None),
        P(None, None, "replica"),
        P("replica", None, None),
        P(None, None, "replica"),
        P(),
        P("groups"),
        P("groups"),
        P(("groups", "replica"), None),
        P(("groups", "replica"), None, None, None),
    )
    return jax.shard_map(
        functools.partial(per_device, mesh.shape["replica"]),
        mesh=mesh,
        in_specs=placed,
        out_specs=P(None, ("groups", "replica"), None),
        check_vma=False,
    )
```

```python
import functools

import jax
import jax.numpy as jnp
from jax import lax
from jax.experimental import pallas as pl
from jax.experimental.pallas import tpu as pltpu
from jax.sharding import PartitionSpec as P

HD = 128
ROWS = 8
HEAD_BLOCK = 8

adapter_scale = 2.0
masked_score = -1e30


def attention_kernel(steps, req_dev, q_ref, k_ref, v_ref, cos_ref, sin_ref, live_ref, kv_ref, out_ref, kn_ref, vn_ref):
    rows = steps * req_dev
    width = q_ref.shape[1]
    lanes = HEAD_BLOCK * HD
    group = rows * HEAD_BLOCK
    cosine = cos_ref[...]
    sine = sin_ref[...]

    def rotated(x):
        pieces = []
        for h in range(HEAD_BLOCK):
            head = x[:, h * HD : (h + 1) * HD]
            pieces.append(head * cosine + pltpu.roll(head, HD // 2, 1) * sine)
        return jnp.concatenate(pieces, axis=1)

    row_head = lax.broadcasted_iota(jnp.int32, (group, lanes), 0) % HEAD_BLOCK
    lane_head = lax.broadcasted_iota(jnp.int32, (group, lanes), 1) // HD
    own_head = row_head == lane_head
    row_j = lax.broadcasted_iota(jnp.int32, (group, 16), 0) // HEAD_BLOCK
    new_j = lax.broadcasted_iota(jnp.int32, (group, 16), 1)
    new_live = (new_j < rows) & (new_j % req_dev == row_j % req_dev) & (new_j // req_dev <= row_j // req_dev)
    live_all = live_ref[...]
    live = jnp.concatenate(
        [
            jnp.broadcast_to(live_all[j % req_dev : j % req_dev + 1], (HEAD_BLOCK, live_all.shape[1]))
            for j in range(rows)
        ],
        axis=0,
    )
    live = live > 0
    kn_ref[...] = jnp.zeros_like(kn_ref)
    vn_ref[...] = jnp.zeros_like(vn_ref)
    contract_lanes = (((1,), (1,)), ((), ()))
    for c in range(width // lanes):
        cols = slice(c * lanes, (c + 1) * lanes)
        query = rotated(q_ref[:, cols].astype(jnp.float32))
        key_new = rotated(k_ref[:, cols].astype(jnp.float32))
        kn_ref[0:8] = key_new
        vn_ref[0:8] = v_ref[:, cols].astype(jnp.float32)
        kn = kn_ref[...].astype(jnp.bfloat16)
        vn = vn_ref[...].astype(jnp.bfloat16)
        spread = jnp.concatenate(
            [jnp.broadcast_to(query[j : j + 1], (HEAD_BLOCK, lanes)) for j in range(rows)], axis=0
        )
        spread = jnp.where(own_head, spread, 0.0).astype(jnp.bfloat16)
        kv = kv_ref[:, cols]
        scores = lax.dot_general(spread, kv, contract_lanes, preferred_element_type=jnp.float32) * (HD**-0.5)
        scores = jnp.where(live, scores, masked_score)
        fresh = lax.dot_general(spread, kn, contract_lanes, preferred_element_type=jnp.float32) * (HD**-0.5)
        fresh = jnp.where(new_live, fresh, masked_score)
        top = jnp.maximum(jnp.max(scores, axis=1, keepdims=True), jnp.max(fresh, axis=1, keepdims=True))
        weights = jnp.where(live, jnp.exp(scores - top), 0.0)
        fresh = jnp.where(new_live, jnp.exp(fresh - top), 0.0)
        totals = jnp.sum(weights, axis=1, keepdims=True) + jnp.sum(fresh, axis=1, keepdims=True)
        weights = pltpu.roll(weights, 1, 1).astype(jnp.bfloat16)
        mixed = jnp.dot(weights, kv, preferred_element_type=jnp.float32)
        mixed = mixed + jnp.dot(fresh.astype(jnp.bfloat16), vn, preferred_element_type=jnp.float32)
        mixed = jnp.where(own_head, mixed / totals, 0.0)
        out = jnp.sum(mixed.reshape(rows, HEAD_BLOCK, lanes), axis=1)
        out_ref[:, cols] = out.astype(out_ref.dtype)


def attention(steps, req_dev, q, k, v, cosine, sine, live, kv):
    rows = steps * req_dev
    width = q.shape[1]
    vmem = pl.BlockSpec(memory_space=pltpu.VMEM)
    return pl.pallas_call(
        functools.partial(attention_kernel, steps, req_dev),
        out_shape=jax.ShapeDtypeStruct((rows, width), jnp.bfloat16),
        in_specs=[vmem] * 7,
        out_specs=vmem,
        scratch_shapes=[pltpu.VMEM((16, HEAD_BLOCK * HD), jnp.float32)] * 2,
        compiler_params=pltpu.CompilerParams(vmem_limit_bytes=32 * 2**20),
        cost_estimate=pl.CostEstimate(flops=10**9, bytes_accessed=6 * 10**6, transcendentals=0),
        name="attention",
    )(q, k, v, cosine, sine, live, kv)


def rotation(my_lengths, steps):
    rows = steps * my_lengths.shape[0]
    positions = (my_lengths[None, :] + jnp.arange(steps, dtype=jnp.int32)[:, None]).reshape(rows)
    positions = jnp.pad(positions, (0, ROWS - rows))
    half = HD // 2
    frequency = jnp.exp(jnp.arange(half, dtype=jnp.float32) * (-2.0 * jnp.log(10000.0) / HD))
    angles = positions.astype(jnp.float32)[:, None] * frequency[None, :]
    cosine = jnp.cos(angles)
    sine = jnp.sin(angles)
    cosine = jnp.concatenate([cosine, cosine], axis=1)
    sine = jnp.concatenate([-sine, sine], axis=1)
    return cosine, sine


def live_tokens(my_lengths, request_page_table, pool_pages, page_len):
    pages = jnp.arange(pool_pages, dtype=jnp.int32)
    max_pages = request_page_table.shape[1]
    place = jnp.max(
        jnp.where(
            request_page_table[:, :, None] == pages[None, None, :],
            jnp.arange(max_pages, dtype=jnp.int32)[None, :, None],
            -1,
        ),
        axis=1,
    )
    token = place[:, :, None] * page_len + jnp.arange(page_len, dtype=jnp.int32)[None, None, :]
    return (place[:, :, None] >= 0) & (token < my_lengths[:, None, None])


def live_rows(my_lengths, request_page_table, pool_pages, page_len):
    alive = live_tokens(my_lengths, request_page_table, pool_pages, page_len)
    live = jnp.stack([alive, jnp.zeros_like(alive)], axis=-1).astype(jnp.int32)
    return live.reshape(request_page_table.shape[0], pool_pages * page_len * 2)


def general_plan(
    replicas,
    hidden,
    query_key_value_weight,
    adapter_down_maps,
    adapter_up_maps,
    adapter_storage_row,
    request_adapter,
    lengths,
    request_page_table,
    key_value_pool,
):
    my_index = lax.axis_index("replica")
    steps, req_dev, width = hidden.shape
    rows = steps * req_dev
    columns = query_key_value_weight.shape[2]
    holder_count, rank, _ = adapter_down_maps.shape
    pool_pages, page_len = key_value_pool.shape[:2]
    adapter_count = adapter_storage_row.shape[0]
    chips = replicas // 2
    total = replicas * ROWS

    block = jnp.pad(hidden.reshape(rows, width), ((0, ROWS - rows), (0, 0)))
    same_core = [[2 * chip + core for chip in range(chips)] for core in range(2)]
    mine = lax.all_to_all(
        jnp.broadcast_to(block[None], (chips, ROWS, width)),
        "replica",
        split_axis=0,
        concat_axis=0,
        axis_index_groups=same_core,
        tiled=True,
    )
    other = lax.ppermute(mine, "replica", [(i, i ^ 1) for i in range(replicas)])
    first = my_index % 2 == 0
    gathered = jnp.stack([jnp.where(first, mine, other), jnp.where(first, other, mine)])
    gathered = gathered.reshape(total, width)

    stored_rows = jnp.sum(
        jnp.where(
            request_adapter[:, None] == jnp.arange(adapter_count, dtype=jnp.int32)[None, :],
            adapter_storage_row[None, :],
            0,
        ),
        axis=1,
    )
    by_block = stored_rows.reshape(chips, 2, 1, req_dev).transpose(1, 0, 2, 3)
    by_block = jnp.broadcast_to(by_block, (2, chips, steps, req_dev)).reshape(2, chips, rows)
    row_stored = jnp.pad(by_block, ((0, 0), (0, 0), (0, ROWS - rows)), constant_values=-1).reshape(total)

    down = jnp.einsum("nd,hfd->nhf", gathered, adapter_down_maps, preferred_element_type=jnp.float32)
    slots = my_index * holder_count + jnp.arange(holder_count, dtype=jnp.int32)
    own = row_stored[:, None] == slots[None, :]
    low = jnp.sum(jnp.where(own[:, :, None], down, 0.0), axis=1).astype(jnp.bfloat16)
    low = jnp.concatenate([low[: total // 2], low[total // 2 :]], axis=1)
    low = lax.all_to_all(
        jnp.broadcast_to(low[None], (replicas,) + low.shape), "replica", split_axis=0, concat_axis=0, tiled=True
    )
    low = jnp.sum(low.astype(jnp.float32), axis=0)
    low = jnp.concatenate([low[:, :rank], low[:, rank:]], axis=0)

    projected = jnp.einsum("nd,idc->nic", gathered, query_key_value_weight, preferred_element_type=jnp.float32)

    def update(first_adapter, maps):
        held = maps.shape[0]
        which = first_adapter + jnp.arange(held, dtype=jnp.int32)
        wide = jnp.where((row_stored[:, None] == which[None, :])[:, :, None], low[:, None, :], 0.0)
        return jnp.dot(
            wide.astype(jnp.bfloat16).reshape(total, held * rank),
            maps.reshape(held * rank, columns),
            preferred_element_type=jnp.float32,
        )

    step_adapters = 64
    if adapter_count <= step_adapters:
        updated = update(0, adapter_up_maps)
    else:
        updated = lax.fori_loop(
            0,
            adapter_count // step_adapters,
            lambda i, sofar: sofar
            + update(
                i * step_adapters,
                lax.dynamic_slice_in_dim(adapter_up_maps, i * step_adapters, step_adapters, 0),
            ),
            jnp.zeros((total, columns), jnp.float32),
        )
    value = projected[:, 2] + adapter_scale * updated
    combined = jnp.concatenate([projected[:, 0], projected[:, 1], value], axis=1).astype(jnp.bfloat16)
    combined = combined.reshape(2, chips, ROWS, 3 * columns).transpose(1, 0, 2, 3)
    combined = combined.reshape(replicas, ROWS, 3 * columns)
    arrived = lax.all_to_all(combined, "replica", split_axis=0, concat_axis=0, tiled=True)
    arrived = arrived.reshape(replicas, ROWS, 3, columns).transpose(2, 1, 0, 3).reshape(3, ROWS, width)

    my_lengths = lax.dynamic_slice_in_dim(lengths, my_index * req_dev, req_dev)
    cosine, sine = rotation(my_lengths, steps)
    live = live_rows(my_lengths, request_page_table, pool_pages, page_len)
    kv = key_value_pool.reshape(pool_pages * page_len * 2, width)
    out = attention(steps, req_dev, arrived[0], arrived[1], arrived[2], cosine, sine, live, kv)
    return out.reshape(steps, req_dev, width)


def rotation_rows(lengths, first, req_dev, steps):
    row = jnp.arange(ROWS, dtype=jnp.int32)
    wanted = first + row % req_dev
    chosen = jnp.where(wanted[:, None] == jnp.arange(lengths.shape[0], dtype=jnp.int32)[None, :], lengths[None, :], 0)
    positions = jnp.sum(chosen, axis=1, keepdims=True) + (row // req_dev)[:, None]
    lane = jnp.arange(HD, dtype=jnp.int32)
    frequency = jnp.exp((lane % (HD // 2)).astype(jnp.float32) * (-2.0 * jnp.log(10000.0) / HD))
    angles = positions.astype(jnp.float32) * frequency[None, :]
    return jnp.cos(angles), jnp.where(lane < HD // 2, -1.0, 1.0)[None, :] * jnp.sin(angles)


def live_lanes(lengths, first, request_page_table, tokens, page_len):
    req_dev, max_pages = request_page_table.shape
    wanted = first + jnp.arange(req_dev, dtype=jnp.int32)
    chosen = jnp.where(wanted[:, None] == jnp.arange(lengths.shape[0], dtype=jnp.int32)[None, :], lengths[None, :], 0)
    lane = jnp.arange(tokens, dtype=jnp.int32)
    page = jnp.arange(max_pages, dtype=jnp.int32)
    place = jnp.max(
        jnp.where(request_page_table[:, :, None] == (lane // page_len)[None, None, :], page[None, :, None], -1),
        axis=1,
    )
    token = place * page_len + (lane % page_len)[None, :]
    return ((place >= 0) & (token < jnp.sum(chosen, axis=1, keepdims=True))).astype(jnp.int32)


def trade(value, mask, count):
    return lax.ppermute(value, "replica", [(i, i ^ mask) for i in range(count)])


CONTRACT_LANES = (((1,), (1,)), ((), ()))


def in_hbm(x):
    return pltpu.with_memory_space_constraint(x, pltpu.HBM)


VMEM = pl.BlockSpec(memory_space=pltpu.VMEM)
HBM = pl.BlockSpec(memory_space=pltpu.HBM)
SMEM = pl.BlockSpec(memory_space=pltpu.SMEM)
ANY = pl.BlockSpec(memory_space=pl.ANY)


def start_all(copies):
    for copy in copies:
        copy.start()
    return copies


def wait_all(copies):
    for copy in copies:
        copy.wait()


CACHE_SECTION = 10
CACHE_AHEAD = 4
CACHE_TOKENS = 128


def cache_kernel(first, pool_ref, keys_ref, values_ref, raw, values, sem, out_sem):
    heads, tokens = raw.shape[:2]
    copies = [pltpu.make_async_copy(pool_ref.at[:, first + h], raw.at[h], sem.at[h]) for h in range(heads)]
    start_all(copies[: CACHE_AHEAD * CACHE_SECTION])
    rows = raw.reshape(heads, 2 * tokens, HD)
    block = min(tokens, CACHE_TOKENS)
    to = lax.broadcasted_iota(jnp.int32, (2 * block, 2 * block), 0)
    source = lax.broadcasted_iota(jnp.int32, (2 * block, 2 * block), 1)
    wanted = jnp.where(to < block, 2 * to, 2 * (to - block) + 1)
    pick = jnp.where(source == wanted, 1.0, 0.0).astype(jnp.bfloat16)
    sent = []
    part = CACHE_SECTION
    for p in range(heads // part):
        wait_all(copies[p * part : (p + 1) * part])
        start_all(copies[(p + CACHE_AHEAD) * part : (p + CACHE_AHEAD + 1) * part])
        for h in range(p * part, (p + 1) * part, 2):
            for first_token in range(0, tokens, block):
                raw_rows = slice(2 * first_token, 2 * (first_token + block))
                both = jnp.concatenate([rows[h, raw_rows], rows[h + 1, raw_rows]], axis=1)
                made = jnp.dot(pick, both, preferred_element_type=jnp.float32).astype(jnp.bfloat16)
                span = slice(first_token, first_token + block)
                for i in range(2):
                    keys_ref[h + i, span] = made[:block, i * HD : (i + 1) * HD]
                    values[h + i, span] = made[block:, i * HD : (i + 1) * HD]
        span = slice(p * part, (p + 1) * part)
        sent += start_all([pltpu.make_async_copy(values.at[span], values_ref.at[span], out_sem.at[p])])
    wait_all(sent)


def cache_by_head(pool, first, heads):
    tokens = pool.shape[0]
    return pl.pallas_call(
        functools.partial(cache_kernel, first),
        out_shape=(
            jax.ShapeDtypeStruct((heads, tokens, HD), pool.dtype),
            pltpu.HBM((heads, tokens, HD), pool.dtype),
        ),
        in_specs=[HBM],
        out_specs=(VMEM, HBM),
        scratch_shapes=[
            pltpu.VMEM((heads, tokens, 2, HD), pool.dtype),
            pltpu.VMEM((heads, tokens, HD), pool.dtype),
            pltpu.SemaphoreType.DMA((heads,)),
            pltpu.SemaphoreType.DMA((heads // CACHE_SECTION,)),
        ],
        compiler_params=pltpu.CompilerParams(vmem_limit_bytes=12 * 2**20),
        cost_estimate=pl.CostEstimate(flops=0, bytes_accessed=12 * 10**6, transcendentals=0),
        name="cache_by_head",
    )(in_hbm(pool))


def lanes_of(x):
    return jnp.concatenate([x[c] for c in range(x.shape[0])], axis=1)


def step_rows(x, first, chunks):
    steps, _, count = x.shape[:3]
    flat = x.reshape(steps, x.shape[1], 2 * count, HD)
    return jnp.concatenate(
        [jnp.concatenate([flat[t, c] for c in range(first, first + chunks)], axis=1) for t in range(steps)], axis=0
    )


def pack_kernel(*refs):
    blocks, (out_ref, sem) = refs[:-2], refs[-2:]
    wait_all(
        start_all([pltpu.make_async_copy(block, out_ref.at[i], sem.at[i]) for i, block in enumerate(blocks)])
    )


def packed(blocks):
    return pl.pallas_call(
        pack_kernel,
        out_shape=jax.ShapeDtypeStruct((len(blocks),) + blocks[0].shape, blocks[0].dtype),
        in_specs=[ANY] * len(blocks),
        out_specs=VMEM,
        scratch_shapes=[pltpu.SemaphoreType.DMA((len(blocks),))],
        compiler_params=pltpu.CompilerParams(vmem_limit_bytes=2 * 2**20),
        cost_estimate=pl.CostEstimate(flops=0, bytes_accessed=10**6, transcendentals=0),
        name="pack_blocks",
    )(*blocks)


def index_kernel(me_ref, stored_ref, slot_ref, column_ref):
    requests = stored_ref.shape[1]
    steps = slot_ref.shape[1] // requests
    row = jnp.concatenate([stored_ref[...]] * steps, axis=1)
    slot_ref[...] = row - me_ref[0]
    wide = jnp.concatenate([row, jnp.zeros((1, HD - row.shape[1]), row.dtype)], axis=1)
    column_ref[...] = jnp.broadcast_to(wide.astype(jnp.float32), (HD, HD)).T[: row.shape[1], :1].astype(jnp.int32)


def index_work(first, stored, steps):
    rows = stored.shape[0] * steps
    return pl.pallas_call(
        index_kernel,
        out_shape=(jax.ShapeDtypeStruct((1, rows), jnp.int32), jax.ShapeDtypeStruct((rows, 1), jnp.int32)),
        in_specs=[SMEM, VMEM],
        out_specs=(VMEM, VMEM),
        compiler_params=pltpu.CompilerParams(vmem_limit_bytes=2 * 2**20),
        cost_estimate=pl.CostEstimate(flops=2 * 10**10, bytes_accessed=10**4, transcendentals=0),
        name="index_work",
    )(first, stored[None, :])


def low_kernel(places, packs, me_ref, slot_ref, down_ref, pack_ref, *refs):
    blocks, (x_ref, low_ref, sem) = refs[: len(places)], refs[len(places) :]
    me = me_ref[0]
    holders, rank, width = down_ref.shape
    sources = list(zip(places, blocks)) + [(k, pack_ref.at[i]) for i, k in enumerate(packs)]
    wait_all(
        start_all([pltpu.make_async_copy(block, x_ref.at[:, :, me ^ k], sem.at[k]) for k, block in sources])
    )
    x = step_rows(x_ref, 0, x_ref.shape[1])
    rows = x.shape[0]
    made = lax.dot_general(
        down_ref.reshape(holders * rank, width)[...], x, CONTRACT_LANES, preferred_element_type=jnp.float32
    )
    slot = slot_ref[...]
    low = jnp.zeros((rank, rows), jnp.float32)
    for h in range(holders):
        low = low + jnp.where(slot == h, made[h * rank : (h + 1) * rank], 0.0)
    low = low.T
    low_ref[...] = jnp.concatenate([low[: rows // 2], low[rows // 2 :]], axis=1).astype(low_ref.dtype)


def low_of(me, blocks, packs, pack, slot, down):
    count = len(blocks) + len(packs)
    steps, chunks = blocks[0].shape[:2]
    rows = count * steps * 2
    rank = down.shape[1]
    return pl.pallas_call(
        functools.partial(low_kernel, tuple(blocks), packs),
        out_shape=(
            jax.ShapeDtypeStruct((steps, chunks, count, 2, HD), jnp.bfloat16),
            jax.ShapeDtypeStruct((rows // 2, 2 * rank), jnp.bfloat16),
        ),
        in_specs=[SMEM, VMEM, VMEM, ANY] + [ANY] * len(blocks),
        out_specs=(VMEM, VMEM),
        scratch_shapes=[pltpu.SemaphoreType.DMA((count,))],
        compiler_params=pltpu.CompilerParams(vmem_limit_bytes=12 * 2**20),
        cost_estimate=pl.CostEstimate(flops=10**8, bytes_accessed=4 * 10**6, transcendentals=0),
        name="low_rows",
    )(me, slot, down, pack, *blocks.values())


def put_chunks(buf, first, value):
    steps, count = buf.shape[1:3]
    flat = buf.reshape(buf.shape[0], steps, 2 * count, HD)
    wide = value.shape[1]
    for c in range(-(-wide // HD)):
        part = value[:, c * HD : min((c + 1) * HD, wide)]
        if part.shape[1] < HD:
            part = jnp.concatenate([part, jnp.zeros((part.shape[0], HD - part.shape[1]), part.dtype)], axis=1)
        part = part.astype(buf.dtype)
        for t in range(steps):
            flat[first + c, t] = part[t * 2 * count : (t + 1) * 2 * count]


def project_kernel(which, x_ref, w_ref, out_ref):
    x = step_rows(x_ref, 0, x_ref.shape[1])
    made = lax.dot_general(w_ref[which], x, CONTRACT_LANES, preferred_element_type=jnp.float32).T
    if which < 2:
        pad = jnp.zeros((made.shape[0], HD // 2), made.dtype)
        put_chunks(out_ref, 0, jnp.concatenate([made, pad] if which == 0 else [pad, made], axis=1))
    else:
        out_ref[...] = made


def project(which, x, weight):
    steps, _, count = x.shape[:3]
    columns = weight.shape[1]
    chunks = jax.ShapeDtypeStruct((-(-columns // HD), steps, count, 2, HD), jnp.bfloat16)
    base = jax.ShapeDtypeStruct((2 * steps * count, columns), jnp.float32)
    return pl.pallas_call(
        functools.partial(project_kernel, which),
        out_shape=chunks if which < 2 else base,
        in_specs=[VMEM, VMEM],
        out_specs=VMEM,
        compiler_params=pltpu.CompilerParams(vmem_limit_bytes=16 * 2**20),
        cost_estimate=pl.CostEstimate(flops=5 * 10**8, bytes_accessed=4 * 10**6, transcendentals=0),
        name="project",
    )(x, weight)


def update_kernel(stored_ref, query_ref, key_ref, base_ref, up_ref, *refs):
    lows, (send_ref, buf, sem) = refs[:-3], refs[-3:]
    half, packed = lows[0].shape
    rank = packed // 2
    rows = 2 * half
    count = send_ref.shape[0]
    low = lows[0][...].astype(jnp.float32)
    for more in lows[1:]:
        low = low + more[...].astype(jnp.float32)
    low = jnp.concatenate([low[:, :rank], low[:, rank:]], axis=0)
    batch = 256 // rank
    spread = jnp.concatenate([low] * batch, axis=1)
    ahead = stored_ref[...] - lax.broadcasted_iota(jnp.int32, (rows, batch * rank), 1) // rank
    total = jnp.zeros(base_ref.shape, jnp.float32)
    for a in range(0, up_ref.shape[0] // rank, batch):
        wide = jnp.where(ahead == a, spread, 0.0).astype(jnp.bfloat16)
        total = total + jnp.dot(wide, up_ref[a * rank : (a + batch) * rank], preferred_element_type=jnp.float32)
    each = query_ref.shape[0]
    buf[: each - 1] = query_ref[: each - 1]
    buf[each - 1] = query_ref[each - 1] + key_ref[0]
    buf[each : 2 * each - 1] = key_ref[1:]
    put_chunks(buf, 2 * each - 1, base_ref[...] + adapter_scale * total)
    wait_all(
        start_all([pltpu.make_async_copy(buf.at[:, :, k], send_ref.at[k], sem.at[k]) for k in range(count)])
    )


def update_values(stored, query, key, base, up, lows):
    chunks, steps, count = query.shape[:3]
    return pl.pallas_call(
        update_kernel,
        out_shape=pltpu.HBM((count, 3 * chunks - 1, steps, 2, HD), query.dtype),
        in_specs=[VMEM] * (5 + len(lows)),
        out_specs=HBM,
        scratch_shapes=[
            pltpu.VMEM((3 * chunks - 1, steps, count, 2, HD), query.dtype),
            pltpu.SemaphoreType.DMA((count,)),
        ],
        compiler_params=pltpu.CompilerParams(vmem_limit_bytes=8 * 2**20),
        cost_estimate=pl.CostEstimate(flops=3 * 10**8, bytes_accessed=4 * 10**6, transcendentals=0),
        name="update_values",
    )(stored, query, key, base, up, *lows)


def attend_kernel(cos_ref, sin_ref, live_ref, pieces_ref, *refs):
    *parts, out_ref, values_buf, kn_ref, vn_ref, sem = refs
    keys_refs, values_refs = parts[: len(parts) // 2], parts[len(parts) // 2 :]
    count, _, steps = pieces_ref.shape[:3]
    rows = 2 * steps
    each = (pieces_ref.shape[1] + 1) // 3
    heads = 2 * out_ref.shape[1] // count
    lanes = heads * HD
    group = rows * HEAD_BLOCK
    chips = range(count // 2)
    early = keys_refs[0].shape[0] // heads
    places = [(0, c) if c < early else (1, c - early) for c in chips]
    fetches = start_all(
        [
            pltpu.make_async_copy(values_refs[half].at[at * heads : (at + 1) * heads], values_buf.at[c], sem.at[c])
            for c, (half, at) in enumerate(places)
        ]
    )
    cosine = cos_ref[...][:rows]
    sine = sin_ref[...][:rows]
    left = lax.broadcasted_iota(jnp.int32, (rows, HD), 1) < HD // 2

    def halves(chip, at):
        return [
            [pieces_ref[2 * chip + core, at + c].reshape(rows, HD).astype(jnp.float32) for c in range(each)]
            for core in range(2)
        ]

    def swapped(parts):
        return [pltpu.roll(x, HD // 2, 1) for x in parts]

    def joined(parts):
        return [jnp.where(left, a, b) for a, b in zip(parts[:-1], parts[1:])]

    def chip_columns(chip, at):
        low, high = halves(chip, at)
        high = swapped(high)
        return low[:-1] + [jnp.where(left, low[-1], high[0])] + joined(high)

    def chip_keys(chip):
        low, high = halves(chip, each - 1)
        low = swapped(low)
        return joined(low) + [jnp.where(left, low[-1], high[0])] + high[1:]

    def rotated(parts):
        return [x * cosine + pltpu.roll(x, HD // 2, 1) * sine for x in parts]

    row_head = lax.broadcasted_iota(jnp.int32, (group, lanes), 0) % HEAD_BLOCK
    lane_head = lax.broadcasted_iota(jnp.int32, (group, lanes), 1) // HD
    own_head = row_head == lane_head
    row_j = lax.broadcasted_iota(jnp.int32, (group, 16), 0) // HEAD_BLOCK
    new_j = lax.broadcasted_iota(jnp.int32, (group, 16), 1)
    new_live = (new_j < rows) & (new_j % 2 == row_j % 2) & (new_j // 2 <= row_j // 2)
    live = jnp.concatenate(
        [
            jnp.broadcast_to(live_ref[j % 2 : j % 2 + 1, :], (HEAD_BLOCK, live_ref.shape[1]))
            for j in range(rows)
        ],
        axis=0,
    )
    live = live > 0
    kn_ref[...] = jnp.zeros_like(kn_ref)
    vn_ref[...] = jnp.zeros_like(vn_ref)
    spreads = []
    for c in chips:
        query = jnp.concatenate(rotated(chip_columns(c, 0)), axis=1)
        kn_ref[c, 0:rows] = jnp.concatenate(rotated(chip_keys(c)), axis=1)
        vn_ref[c, 0:rows] = jnp.concatenate(chip_columns(c, 2 * each - 1), axis=1)
        spread = jnp.concatenate(
            [jnp.broadcast_to(query[j : j + 1], (HEAD_BLOCK, lanes)) for j in range(rows)], axis=0
        )
        spreads.append(jnp.where(own_head, spread, 0.0).astype(jnp.bfloat16))
    scores, fresh = [], []
    for c in chips:
        half, at = places[c]
        keys = jnp.concatenate([keys_refs[half][at * heads + h] for h in range(heads)], axis=1)
        kn = kn_ref[c].astype(jnp.bfloat16)
        scores.append(lax.dot_general(spreads[c], keys, CONTRACT_LANES, preferred_element_type=jnp.float32))
        fresh.append(lax.dot_general(spreads[c], kn, CONTRACT_LANES, preferred_element_type=jnp.float32))
    weights, fresh_weights, totals = [], [], []
    for c in chips:
        old = jnp.where(live, scores[c] * (HD**-0.5), masked_score)
        new = jnp.where(new_live, fresh[c] * (HD**-0.5), masked_score)
        top = jnp.maximum(jnp.max(old, axis=1, keepdims=True), jnp.max(new, axis=1, keepdims=True))
        old = jnp.where(live, jnp.exp(old - top), 0.0)
        new = jnp.where(new_live, jnp.exp(new - top), 0.0)
        totals.append(jnp.sum(old, axis=1, keepdims=True) + jnp.sum(new, axis=1, keepdims=True))
        weights.append(old.astype(jnp.bfloat16))
        fresh_weights.append(new.astype(jnp.bfloat16))
    wait_all(fetches)
    for c in chips:
        values = lanes_of(values_buf[c])
        vn = vn_ref[c].astype(jnp.bfloat16)
        mixed = jnp.dot(weights[c], values, preferred_element_type=jnp.float32)
        mixed = mixed + jnp.dot(fresh_weights[c], vn, preferred_element_type=jnp.float32)
        mixed = jnp.where(own_head, mixed / totals[c], 0.0)
        out = jnp.sum(mixed.reshape(rows, HEAD_BLOCK, lanes), axis=1).astype(out_ref.dtype)
        for t in range(steps):
            for h in range(heads):
                out_ref[t, c * heads + h] = out[2 * t : 2 * t + 2, h * HD : (h + 1) * HD]


def attend(cosine, sine, live, pieces, keys, values):
    count, _, steps = pieces.shape[:3]
    heads, tokens = sum(x.shape[0] for x in keys), keys[0].shape[1]
    chips = count // 2
    per = heads // chips
    return pl.pallas_call(
        attend_kernel,
        out_shape=jax.ShapeDtypeStruct((steps, heads, 2, HD), jnp.bfloat16),
        in_specs=[VMEM] * (4 + len(keys)) + [HBM] * len(values),
        out_specs=VMEM,
        scratch_shapes=[pltpu.VMEM((chips, per, tokens, HD), jnp.bfloat16)]
        + [pltpu.VMEM((chips, 16, per * HD), jnp.float32)] * 2
        + [pltpu.SemaphoreType.DMA((chips,))],
        compiler_params=pltpu.CompilerParams(vmem_limit_bytes=16 * 2**20),
        cost_estimate=pl.CostEstimate(flops=10**9, bytes_accessed=6 * 10**6, transcendentals=0),
        name="attention",
    )(cosine, sine, live, pieces, *keys, *[in_hbm(x) for x in values])


def chip_plan(
    count,
    hidden,
    query_key_value_weight,
    adapter_down_maps,
    adapter_up_maps,
    adapter_storage_row,
    request_adapter,
    lengths,
    request_page_table,
    key_value_pool,
):
    me = lax.axis_index("replica")
    steps, req_dev, width = hidden.shape
    heads = width // HD
    holder_count, rank, _ = adapter_down_maps.shape
    pool_pages, page_len = key_value_pool.shape[:2]
    adapter_count = adapter_storage_row.shape[0]

    tokens = pool_pages * page_len
    pool = key_value_pool.reshape(tokens, 2, heads, HD).transpose(0, 2, 1, 3)

    stored = jnp.sum(
        jnp.where(
            request_adapter[:, None] == jnp.arange(adapter_count, dtype=jnp.int32)[None, :],
            adapter_storage_row[None, :],
            0,
        ),
        axis=1,
    )
    first, slots, here, stored = lax.optimization_barrier(
        (me * req_dev, (me * holder_count).astype(jnp.int32).reshape(1), me.astype(jnp.int32).reshape(1), stored)
    )
    slot, column = index_work(slots, stored, steps)

    held = {0: hidden}
    held.update({m: trade(hidden, m, count) for m in range(4, count, 4)})
    _, lengths, request_page_table = lax.optimization_barrier((held[count - 4], lengths, request_page_table))
    cosine, sine = rotation_rows(lengths, first, req_dev, steps)
    live = live_lanes(lengths, first, request_page_table, tokens, page_len)
    held.update({k | 2: trade(v, 2, count) for k, v in list(held.items())})
    held = {k: v.reshape(steps, req_dev, heads, HD).transpose(0, 2, 1, 3) for k, v in held.items()}
    line = tuple(range(0, count, 4))
    *share, held[2], held[6] = lax.optimization_barrier([held[k] for k in line] + [held[2], held[6]])
    pack = trade(packed(share), 1, count)
    held.update({k | 1: trade(held[k], 1, count) for k in range(2, count, 4)})
    held[0] = in_hbm(held[0])
    x, low = low_of(here, held, tuple(k | 1 for k in line), pack, slot, adapter_down_maps)
    weight = query_key_value_weight.transpose(0, 2, 1)
    arrived = [trade(low, m, count) for m in (1, 2, 3)]
    query, key = project(0, x, weight), project(1, x, weight)
    arrived, query, key, pool = lax.optimization_barrier((arrived, query, key, pool))
    low = (low + arrived[0]) + (arrived[1] + arrived[2])
    arrived = [trade(low, m, count) for m in range(4, count, 4)]
    base = project(2, x, weight)
    arrived, base = lax.optimization_barrier((arrived, base))
    send = update_values(column, query, key, base, adapter_up_maps.reshape(adapter_count * rank, -1), [low, *arrived])
    send, pool = lax.optimization_barrier((send, pool))
    keys, values = cache_by_head(pool, 0, heads)
    pieces = lax.all_to_all(send, "replica", split_axis=0, concat_axis=0, tiled=True)

    out = attend(cosine, sine, live, pieces, [keys], [values])
    return out.transpose(0, 2, 1, 3).reshape(steps, req_dev, width)


def per_device(replicas, *arrays):
    columns = arrays[1].shape[2]
    whole_heads = replicas % 4 == 0 and (2 * columns) % HD == 0 and columns % HD == HD // 2
    plan = chip_plan if whole_heads and arrays[0].shape[1] == 2 else general_plan
    return plan(replicas, *arrays)


def solution(mesh):
    placed = (
        P(None, ("groups", "replica"), None),
        P(None, None, "replica"),
        P("replica", None, None),
        P(None, None, "replica"),
        P(),
        P("groups"),
        P("groups"),
        P(("groups", "replica"), None),
        P(("groups", "replica"), None, None, None),
    )
    return jax.shard_map(
        functools.partial(per_device, mesh.shape["replica"]),
        mesh=mesh,
        in_specs=placed,
        out_specs=P(None, ("groups", "replica"), None),
        check_vma=False,
    )
```
